32 devices in a mesh: brick: 4 (over y, core), grp: 8 (over z, x).
Axes of the slice: x: 2, y: 2, z: 4, core: 2. Of those that a mesh axis runs over, the one named last changes fastest.
Arguments:
- source: float32 [8, 4, 2, 32, 1024], P('grp', 'brick'), may hold values from -21 to 21
- uptake: float32 [8, 4, 2, 32, 1024], P('grp', 'brick'), may hold values from 0.00015 to 0.006
- conductance: float32 [8, 4, 6, 2, 32, 1024], P('grp', 'brick'), may hold values from 0 to 3, as said below
- occupancy: int32 [8, 2, 4], replicated, may hold values from 0 to 1, as said below
- assignment: int32 [4], replicated, may hold values from 0 to 3, as said below
Outputs:
- solution_field: float32 [8, 4, 2, 32, 1024], P('grp', 'brick')
- residual: float32 [8, 4, 2, 32, 1024], P('grp', 'brick')
The draws below stay inside these ranges and needn't reach their ends.
Inputs may be any that keep to these rules, and one draw needn't show every extreme that they name: `occupancy`: 1 marks an occupied brick; in every draw one patch of some slab has all its bricks occupied. `assignment`: each patch is held by exactly one index of brick. `conductance`: equal at both ends of a bond: the value toward +x at a cell is the value toward -x at its +x neighbour, likewise for y and z, the lattice being read cyclically; values toward +z and -z are 0.3 or more.
All inputs are finite; a program needn't handle non-finite values.
Results may differ from the reference program's by a relative error of at most 0.0003.
Values sent between devices are 32-bit elements; how exact they have to be, the bound alone decides.
No kernel may reach another device: no remote copies, remote signals or barrier semaphores. Data moves between devices by JAX's collectives and lax.ppermute only.
A program may use at most 128 MiB of HBM per device.

```python
import math
import jax
import jax.numpy as jnp
from jax import lax

BS = 32
PATCH_X = 1
PATCH_Y = 2
ITERS = 3
SWEEPS = 2
SLOTS = 2
NSLAB = 8
NPATCH = 4
PGY = 2
LXB = 2
LYB = 4
COARSE = 16


def patch_order(key):
    return jax.random.permutation(jax.random.fold_in(key, 11), NPATCH).astype(jnp.int32)


def draw_assignment(key, part):
    return patch_order(key)


def draw_occupancy(key, part):
    subkeys = jax.random.split(jax.random.fold_in(key, 23), 4)
    density = jax.random.randint(subkeys[0], (NSLAB, 2, PGY), 30, 101)
    density = jnp.repeat(jnp.repeat(density, PATCH_X, axis=1), PATCH_Y, axis=2)
    chances = jax.random.randint(subkeys[1], (NSLAB, LXB, LYB), 0, 100)
    chosen_slab = jax.random.randint(subkeys[2], (), 0, NSLAB)
    chosen_patch = jax.random.randint(subkeys[3], (), 0, NPATCH)
    slab_ids = jnp.arange(NSLAB)[:, None, None]
    row_ids = (jnp.arange(LXB) // PATCH_X)[None, :, None]
    column_ids = (jnp.arange(LYB) // PATCH_Y)[None, None, :]
    forced = (slab_ids == chosen_slab) & (row_ids == chosen_patch // PGY) & (column_ids == chosen_patch % PGY)
    return ((chances < density) | forced).astype(jnp.int32)


def to_devices_drawn(lattice, layout_order):
    shaped = lattice.reshape(NSLAB, BS, 2, PATCH_X, BS, PGY, PATCH_Y, BS)
    ordered = jnp.transpose(shaped, (0, 2, 5, 3, 6, 4, 7, 1)).reshape(NSLAB, NPATCH, SLOTS, BS, BS * BS)
    return jnp.take(ordered, layout_order, axis=1)


def strength(subkey, extent):
    return jnp.exp(jax.random.uniform(subkey, extent, jnp.float32, math.log(0.3), math.log(3.0)))


def draw_conductance(key, part):
    layout_order = patch_order(key)
    subkeys = jax.random.split(jax.random.fold_in(key, 31), 5)
    extent = (NSLAB * BS, LXB * BS, LYB * BS)
    dilution = 0.3
    kept_first = (jax.random.uniform(subkeys[1], extent, jnp.float32) >= dilution).astype(jnp.float32)
    kept_second = (jax.random.uniform(subkeys[3], extent, jnp.float32) >= dilution).astype(jnp.float32)
    along_first = strength(subkeys[0], extent) * kept_first
    along_second = strength(subkeys[2], extent) * kept_second
    along_third = strength(subkeys[4], extent)
    pieces = [along_first, jnp.roll(along_first, 1, axis=1), along_second, jnp.roll(along_second, 1, axis=2), along_third, jnp.roll(along_third, 1, axis=0)]
    return jnp.stack([to_devices_drawn(piece, layout_order) for piece in pieces], axis=2)


def draw_source(key, part):
    subkeys = jax.random.split(jax.random.fold_in(key, 41), 1)
    extent = (NSLAB, NPATCH, SLOTS, BS, BS * BS)
    rising = (1.0 + 2.0 * jnp.arange(NSLAB, dtype=jnp.float32) / max(NSLAB - 1, 1)).reshape(NSLAB, 1, 1, 1, 1)
    values = jnp.clip(jax.random.normal(subkeys[0], extent, jnp.float32), -7.0, 7.0)
    return values * rising


def draw_uptake(key, part):
    subkeys = jax.random.split(jax.random.fold_in(key, 53), 2)
    extent = (NSLAB, NPATCH, SLOTS, BS, BS * BS)
    per_brick = jnp.exp(jax.random.uniform(subkeys[0], (NSLAB, NPATCH, SLOTS, 1, 1), jnp.float32, math.log(0.0003), math.log(0.003)))
    per_cell = jnp.exp(jax.random.uniform(subkeys[1], extent, jnp.float32, math.log(0.5), math.log(2.0)))
    return per_brick * per_cell


def setup_inputs(seed: int = 0) -> dict:
    key_list = jax.random.split(jax.random.key(seed), 6)
    return {
        "source": draw_source(jax.random.fold_in(key_list[5], 71), 0),
        "uptake": draw_uptake(jax.random.fold_in(key_list[5], 71), 0),
        "conductance": draw_conductance(jax.random.fold_in(key_list[5], 71), 0),
        "occupancy": draw_occupancy(jax.random.fold_in(key_list[5], 71), 0),
        "assignment": draw_assignment(jax.random.fold_in(key_list[5], 71), 0),
    }


OMEGA = 0.6

def assemble(coarse_diag, couplings, strides):
    extent = coarse_diag.shape[0]
    matrix = jnp.diag(coarse_diag)
    for coupling, stride in zip(couplings, strides):
        if stride < extent:
            banded = coupling[:extent - stride]
            matrix = matrix - jnp.diag(banded, stride) - jnp.diag(banded, -stride)
    return matrix

def to_lattice(field, owners):
    ordered = jnp.take(field, owners, axis=1)
    shaped = ordered.reshape(NSLAB, 2, PGY, PATCH_X, PATCH_Y, BS, BS, BS)
    return jnp.transpose(shaped, (0, 7, 1, 3, 5, 2, 4, 6)).reshape(NSLAB * BS, LXB * BS, LYB * BS)

def to_devices(lattice, assignment):
    shaped = lattice.reshape(NSLAB, BS, 2, PATCH_X, BS, PGY, PATCH_Y, BS)
    ordered = jnp.transpose(shaped, (0, 2, 5, 3, 6, 4, 7, 1)).reshape(NSLAB, NPATCH, SLOTS, BS, BS * BS)
    return jnp.take(ordered, assignment, axis=1)

def ahead(field, axis):
    extent = field.shape[axis]
    rest = lax.slice_in_dim(field, 1, extent, axis=axis)
    zeros = jnp.zeros_like(lax.slice_in_dim(field, 0, 1, axis=axis))
    return jnp.concatenate([rest, zeros], axis=axis)

def behind(field, axis):
    extent = field.shape[axis]
    rest = lax.slice_in_dim(field, 0, extent - 1, axis=axis)
    zeros = jnp.zeros_like(lax.slice_in_dim(field, 0, 1, axis=axis))
    return jnp.concatenate([zeros, rest], axis=axis)
MOVES = ((1, True), (1, False), (2, True), (2, False), (0, True), (0, False))

def neighbour(field, move):
    if move[1]:
        return ahead(field, move[0])
    return behind(field, move[0])

def brick_sums(field):
    return field.reshape(NSLAB, BS, LXB, BS, LYB, BS).sum(axis=(1, 3, 5))

def per_patch(grid):
    return jnp.transpose(grid.reshape(NSLAB, 2, PATCH_X, PGY, PATCH_Y), (1, 3, 0, 2, 4)).reshape(NPATCH, COARSE)

def from_patches(vectors):
    return jnp.transpose(vectors.reshape(2, PGY, NSLAB, PATCH_X, PATCH_Y), (2, 0, 3, 1, 4)).reshape(NSLAB, LXB, LYB)

def build(coarse_diag, first, second, third):
    return assemble(coarse_diag, (first, second, third), (PATCH_Y, 1, SLOTS))

def reference(source, uptake, conductance, occupancy, assignment):
    owners = jnp.zeros((NPATCH,), jnp.int32).at[assignment].set(jnp.arange(NPATCH, dtype=jnp.int32))
    live = occupancy.astype(jnp.float32)
    cube_shape = (NSLAB * BS, LXB * BS, LYB * BS)
    live_cells = jnp.broadcast_to(live[:, None, :, None, :, None], (NSLAB, BS, LXB, BS, LYB, BS)).reshape(cube_shape)
    effective = []
    for direction in range(6):
        bonds = to_lattice(conductance[:, :, direction], owners)
        effective.append(bonds * live_cells * neighbour(live_cells, MOVES[direction]))
    absorb = to_lattice(uptake, owners)
    diagonal = absorb
    for direction in range(6):
        diagonal = diagonal + effective[direction]

    def operate(field):
        total = diagonal * field
        for direction in range(6):
            total = total - effective[direction] * neighbour(field, MOVES[direction])
        return total

    def shaped(field):
        return field.reshape(NSLAB, BS, LXB, BS, LYB, BS)
    face_sums = [jnp.take(shaped(effective[0]), BS - 1, axis=3).sum(axis=(1, 4)), jnp.take(shaped(effective[1]), 0, axis=3).sum(axis=(1, 4)), jnp.take(shaped(effective[2]), BS - 1, axis=5).sum(axis=(1, 3)), jnp.take(shaped(effective[3]), 0, axis=5).sum(axis=(1, 3)), jnp.take(shaped(effective[4]), BS - 1, axis=1).sum(axis=(2, 4)), jnp.take(shaped(effective[5]), 0, axis=1).sum(axis=(2, 4))]
    position_x = jnp.arange(LXB) % PATCH_X
    position_y = jnp.arange(LYB) % PATCH_Y
    inside = [(position_x < PATCH_X - 1).astype(jnp.float32)[None, :, None], (position_x > 0).astype(jnp.float32)[None, :, None], (position_y < PATCH_Y - 1).astype(jnp.float32)[None, None, :], (position_y > 0).astype(jnp.float32)[None, None, :]]
    coarse_diag = brick_sums(absorb)
    for direction in range(4):
        coarse_diag = coarse_diag + face_sums[direction] * inside[direction]
    coarse_diag = coarse_diag + face_sums[4] + face_sums[5]
    matrices = jax.vmap(build)(per_patch(coarse_diag), per_patch(face_sums[0] * inside[0]), per_patch(face_sums[2] * inside[2]), per_patch(face_sums[4]))
    factors = jnp.linalg.cholesky(matrices)

    def coarse(residual_field):
        terms = per_patch(brick_sums(residual_field))[:, :, None]
        middle = lax.linalg.triangular_solve(factors, terms, left_side=True, lower=True)
        result = lax.linalg.triangular_solve(factors, middle, left_side=True, lower=True, transpose_a=True)
        grid = from_patches(result[:, :, 0])
        return jnp.broadcast_to(grid[:, None, :, None, :, None], (NSLAB, BS, LXB, BS, LYB, BS)).reshape(cube_shape)

    def precondition(residual_field):
        smoothed = OMEGA * residual_field / diagonal
        for _ in range(SWEEPS - 1):
            smoothed = smoothed + OMEGA * (residual_field - operate(smoothed)) / diagonal
        return smoothed + coarse(residual_field)
    forcing = to_lattice(source, owners) * live_cells
    solution_field = jnp.zeros_like(forcing)
    residual = forcing
    search = precondition(residual)
    energy = jnp.sum(residual * search)
    for iteration in range(ITERS):
        mapped = operate(search)
        step_size = energy / jnp.sum(search * mapped)
        solution_field = solution_field + step_size * search
        residual = residual - step_size * mapped
        if iteration + 1 < ITERS:
            smoothed = precondition(residual)
            renewed = jnp.sum(residual * smoothed)
            search = smoothed + renewed / energy * search
            energy = renewed
    return (to_devices(solution_field, assignment), to_devices(residual, assignment))
```

```python
import functools

import jax
import jax.numpy as jnp
from jax import lax
from jax.experimental import pallas as pl
from jax.experimental.pallas import tpu as pltpu
from jax.sharding import PartitionSpec as P

BS = 32
CHUNKS = 16
OMEGA = 0.6
ITERS = 3
F32 = jnp.float32
FIELD = (CHUNKS, BS, 128)

XY_X1, XY_XP, XY_Y, XY_S = 0, 16, 32, 64
XY_ROWS = 72
XY_XD, XY_YC, XY_K = 72, 88, 120
XY_ROWS_FIRST = 128
Z_Y1, Z_Q, Z_Y, Z_X = 0, 32, 64, 96
Z_ROWS = 104
Z_D = 104
Z_ROWS_FIRST = 136
H_X1, H_XP, H_Y, H_Z1, H_ZQ, H_YZ, H_R = 0, 16, 32, 64, 96, 128, 160
H_ROWS = 168
C_XD, C_YC, C_ZD, C_K = 0, 16, 48, 80
C_ROWS = 88
E_XP, E_XM, E_YP, E_YM = 0, 16, 32, 64
E_ROWS = 96


def roll(block, shift):
    return pltpu.roll(block, shift % 128, axis=1)


def roll_row(row, shift):
    return pltpu.roll(jnp.broadcast_to(row, (8, 128)), shift % 128, axis=1)[0:1]


def lanes(rows=BS):
    return lax.broadcasted_iota(jnp.int32, (rows, 128), 1)


def rows_of(height=BS):
    return lax.broadcasted_iota(jnp.int32, (height, 128), 0)


def pack(chunks):
    height = chunks[0].shape[0]
    pair = (lanes(height) % BS) // 2
    total = jnp.zeros((height, 128), F32)
    for c in range(CHUNKS):
        moved = roll(chunks[c], 2 * c - 31) if height > 1 else roll_row(chunks[c], 2 * c - 31)
        total = jnp.where(pair == c, moved, total)
    return total


def stencil(field, effective, diagonal, x_halo, y_low, y_high, z_halo):
    lane = lanes()
    height = rows_of()
    depth = lane % BS
    zero = jnp.zeros((BS, 128), F32)
    back = [roll(f, -32) for f in field]
    forth = [roll(f, 32) for f in field]
    out = []
    for c in range(CHUNKS):
        f = field[c]
        x_row = zero if x_halo is None else x_halo[c : c + 1]
        total = diagonal(c) * f
        total -= effective(0, c) * jnp.where(height == BS - 1, x_row, pltpu.roll(f, BS - 1, axis=0))
        total -= effective(1, c) * jnp.where(height == 0, x_row, pltpu.roll(f, 1, axis=0))
        following = back[c + 1] if c < CHUNKS - 1 else (zero if y_high is None else y_high)
        previous = forth[c - 1] if c > 0 else (zero if y_low is None else y_low)
        total -= effective(2, c) * jnp.where(lane < 96, back[c], following)
        total -= effective(3, c) * jnp.where(lane >= 32, forth[c], previous)
        ends = zero if z_halo is None else roll(z_halo, 31 - 2 * c)
        total -= effective(4, c) * jnp.where(depth == BS - 1, ends, roll(f, -1))
        total -= effective(5, c) * jnp.where(depth == 0, ends, roll(f, 1))
        out.append(total)
    return out


def total_of(blocks):
    acc = blocks[0]
    for block in blocks[1:]:
        acc = acc + block
    return jnp.sum(jnp.sum(acc, axis=0, keepdims=True), axis=1, keepdims=True)


def facing(block, row):
    return jnp.where(row == 0, block[BS - 1 : BS], block[0:1])


def side_blocks(low_first, high_first, low_second, high_second):
    group = lanes() // 32
    return jnp.where(
        group == 0,
        low_first,
        jnp.where(
            group == 1,
            roll(high_first, 64),
            jnp.where(group == 2, roll(low_second, 64), high_second),
        ),
    )


def write_xy(xy_ref, row, y1, partial):
    for c in range(CHUNKS):
        xy_ref[XY_X1 + c : XY_X1 + c + 1] = facing(y1[c], row)
        xy_ref[XY_XP + c : XY_XP + c + 1] = facing(partial[c], row)
    last = CHUNKS - 1
    xy_ref[XY_Y : XY_Y + BS] = side_blocks(y1[0], y1[last], partial[0], partial[last])


def write_scalars(ref, start, values):
    for i, value in enumerate(values):
        ref[start + i : start + i + 1] = jnp.broadcast_to(value, (1, 128))
    for i in range(len(values), 8):
        ref[start + i : start + i + 1] = jnp.zeros((1, 128), F32)


def locate(bricks, place_ref, assignment_ref):
    across = bricks // 2
    place = place_ref[0]
    slab = place // bricks
    patch = assignment_ref[place % bricks]
    row = patch // across
    column = patch % across
    return slab, patch, row, column


def setup_kernel(
    slabs, bricks, place_ref, assignment_ref, occupancy_ref, source_ref, uptake_ref, conductance_ref,
    info_ref, effective_ref, diagonal_ref, relax_ref, residual_ref, partial_ref, edge_ref, xy_ref,
):
    across = bricks // 2
    slab, patch, row, column = locate(bricks, place_ref, assignment_ref)

    def holder(row_target, column_target):
        inside = (column_target >= 0) & (column_target < across)
        wanted = jnp.where(inside, row_target * across + column_target, patch)
        found = jnp.int32(0)
        for b in range(bricks):
            found = jnp.where(assignment_ref[b] == wanted, b, found)
        return found

    info_ref[0] = row
    info_ref[1] = slab
    info_ref[2] = holder(row, column)
    info_ref[3] = holder(1 - row, column)
    info_ref[4] = holder(row, column - 1)
    info_ref[5] = holder(row, column + 1)
    info_ref[6] = holder(1 - row, column - 1)
    info_ref[7] = holder(1 - row, column + 1)

    breadth = 2 * across

    def live_at(g, x, y):
        inside = (g >= 0) & (g < slabs) & (x >= 0) & (x < 2) & (y >= 0) & (y < breadth)
        index = (jnp.clip(g, 0, slabs - 1) * 2 + jnp.clip(x, 0, 1)) * breadth + jnp.clip(y, 0, breadth - 1)
        return jnp.where(inside, occupancy_ref[index], 0).astype(F32)

    lane = lanes()
    height = rows_of()
    depth = lane % BS
    absorbed = []
    low_ends = []
    high_ends = []
    first_y = None
    second_y = None
    y1 = []
    for s in range(2):
        y = column * 2 + s
        here = live_at(slab, row, y)
        around = [
            here * live_at(slab, row + 1, y),
            here * live_at(slab, row - 1, y),
            here * live_at(slab, row, y + 1),
            here * live_at(slab, row, y - 1),
            here * live_at(slab + 1, row, y),
            here * live_at(slab - 1, row, y),
        ]
        borders = [height == BS - 1, height == 0, lane >= 96, lane < 32, depth == BS - 1, depth == 0]
        for k in range(8):
            c = 8 * s + k
            part = pl.ds(128 * k, 128)
            taken = uptake_ref[s, :, part]
            absorbed.append(taken)
            diagonal = taken
            for d in range(6):
                bond = conductance_ref[d, s, :, part]
                if (d == 2 and k < 7) or (d == 3 and k > 0):
                    value = bond * here
                else:
                    value = bond * jnp.where(borders[d], around[d], here)
                effective_ref[d, c] = value
                diagonal = diagonal + value
                if d == 2 and c == 7:
                    first_y = jnp.where(borders[d], value, 0.0)
                if d == 3 and c == 8:
                    second_y = jnp.where(borders[d], value, 0.0)
                if d == 4:
                    high_ends.append(jnp.where(borders[d], value, 0.0))
                if d == 5:
                    low_ends.append(jnp.where(borders[d], value, 0.0))
            relax = OMEGA / diagonal
            diagonal_ref[c] = diagonal
            relax_ref[c] = relax
            forcing = source_ref[s, :, part] * here
            residual_ref[c] = forcing
            y1.append(relax * forcing)

    outcome = stencil(
        y1, lambda d, c: effective_ref[d, c], lambda c: diagonal_ref[c], None, None, None, None
    )
    partial = []
    for c in range(CHUNKS):
        value = y1[c] + relax_ref[c] * (residual_ref[c] - outcome[c])
        partial_ref[c] = value
        partial.append(value)
    write_xy(xy_ref, row, y1, partial)

    first_coupling = total_of([first_y])
    high_sums = [total_of(high_ends[8 * s : 8 * s + 8]) for s in range(2)]
    low_sums = [total_of(low_ends[8 * s : 8 * s + 8]) for s in range(2)]
    taken_sums = [total_of(absorbed[8 * s : 8 * s + 8]) for s in range(2)]
    residual_sums = [total_of([residual_ref[8 * s + k] for k in range(8)]) for s in range(2)]
    write_scalars(
        xy_ref,
        XY_S,
        [
            residual_sums[0],
            residual_sums[1],
            taken_sums[0] + first_coupling + high_sums[0] + low_sums[0],
            taken_sums[1] + total_of([second_y]) + high_sums[1] + low_sums[1],
            first_coupling,
            high_sums[0],
            high_sums[1],
        ],
    )

    last = CHUNKS - 1
    z_ends = [relax_ref[c] * (high_ends[c] + low_ends[c]) for c in range(CHUNKS)]
    for c in range(CHUNKS):
        xy_ref[XY_XD + c : XY_XD + c + 1] = facing(relax_ref[c], row)
        edge_ref[E_XP + c : E_XP + c + 1] = (relax_ref[c] * effective_ref[0, c])[BS - 1 : BS]
        edge_ref[E_XM + c : E_XM + c + 1] = (relax_ref[c] * effective_ref[1, c])[0:1]
    high_y = jnp.where(lane >= 96, relax_ref[last] * effective_ref[2, last], 0.0)
    low_y = jnp.where(lane < 32, relax_ref[0] * effective_ref[3, 0], 0.0)
    edge_ref[E_YP : E_YP + BS] = high_y
    edge_ref[E_YM : E_YM + BS] = low_y
    xy_ref[XY_YC : XY_YC + BS] = side_blocks(relax_ref[0], relax_ref[last], z_ends[0], z_ends[last])
    xy_ref[XY_K : XY_K + 1] = facing(low_y + high_y, row)
    xy_ref[XY_K + 1 : XY_K + 2] = pack([facing(z, row) for z in z_ends])
    toward_low = facing_terms(relax_ref, effective_ref, 0)
    toward_high = facing_terms(relax_ref, effective_ref, last)
    lane_row = lanes(1)
    xy_ref[XY_K + 2 : XY_K + 3] = jnp.where(lane_row < 32, toward_low, roll_row(toward_high, 64))
    xy_ref[XY_K + 3 : XY_K + 8] = jnp.zeros((5, 128), F32)


def facing_terms(relax_ref, effective_ref, c):
    upper = (relax_ref[c] * effective_ref[0, c])[BS - 1 : BS]
    lower = (relax_ref[c] * effective_ref[1, c])[0:1]
    return upper + lower


def swap_sides(from_low, from_high):
    rows = from_low.shape[0]
    if rows == 1:
        low, high = roll_row(from_low, -32), roll_row(from_high, 32)
    else:
        low, high = roll(from_low, -32), roll(from_high, 32)
    return jnp.where((lanes(rows) // 32) % 2 == 0, low, high)


def middle_kernel(
    first, bricks, info_ref, xy_ref, field_ref, relax_ref, partial_ref, edge_ref, z_ref, tile_ref
):
    lane = lanes()
    height = rows_of()
    x_holder = info_ref[3]
    x_halo = xy_ref[x_holder, XY_X1 : XY_X1 + CHUNKS]
    sides = swap_sides(
        xy_ref[info_ref[4], XY_Y : XY_Y + BS], xy_ref[info_ref[5], XY_Y : XY_Y + BS]
    )
    upper = edge_ref[E_XP : E_XP + CHUNKS] * x_halo
    lower = edge_ref[E_XM : E_XM + CHUNKS] * x_halo
    y1 = []
    whole = []
    for c in range(CHUNKS):
        y1.append(relax_ref[c] * field_ref[c])
        value = partial_ref[c]
        value = value + jnp.where(height == BS - 1, upper[c : c + 1], 0.0)
        value = value + jnp.where(height == 0, lower[c : c + 1], 0.0)
        if c == 0:
            value = value + jnp.where(lane < 32, edge_ref[E_YM : E_YM + BS] * sides, 0.0)
        if c == CHUNKS - 1:
            value = value + jnp.where(
                lane >= 96, edge_ref[E_YP : E_YP + BS] * roll(sides, 64), 0.0
            )
        whole.append(value)
    z_ref[Z_Y1 : Z_Y1 + BS] = pack(y1)
    z_ref[Z_Q : Z_Q + BS] = pack(whole)
    z_ref[Z_Y : Z_Y + BS] = sides
    x_ends = pack([x_halo[c : c + 1] for c in range(CHUNKS)])
    z_ref[Z_X : Z_X + 8] = jnp.broadcast_to(x_ends, (8, 128))
    if first:
        z_ref[Z_D : Z_D + BS] = pack([relax_ref[c] for c in range(CHUNKS)])
    lane_tile = lanes(8)
    mixed = jnp.zeros((8, 128), F32)
    for q in range(4):
        mixed = jnp.where(lane_tile == q, xy_ref[info_ref[2 + q], XY_S : XY_S + 8], mixed)
    if not first:
        summed = xy_ref[0, XY_S : XY_S + 8]
        for b in range(1, bricks):
            summed = summed + xy_ref[b, XY_S : XY_S + 8]
        mixed = jnp.where(rows_of(8) < 2, mixed, summed)
    tile_ref[...] = mixed


def search_scalars(tiles, scalars, iteration):
    energy = tiles[2:3, 0:1]
    curvature = tiles[3:4, 0:1]
    if iteration == 0:
        return energy, curvature, energy / curvature, None
    growth = energy / scalars[0:1, 0:1]
    curvature = curvature + growth * (2.0 * tiles[4:5, 0:1] + growth * scalars[1:2, 0:1])
    return energy, curvature, energy / curvature, growth


def sum_tiles(ref, count):
    total = ref[0:8]
    for g in range(1, count):
        total = total + ref[8 * g : 8 * g + 8]
    return total


def step_kernel(iteration, slabs, bricks, *refs):
    first = iteration == 0
    last = iteration == ITERS - 1
    refs = list(refs)
    take = lambda count: [refs.pop(0) for _ in range(count)]
    info_ref, xy_ref, above_ref, below_ref, tiles_ref = take(5)
    effective_ref, diagonal_ref, relax_ref, residual_ref = take(4)
    if not first:
        mapped_ref, halo_in, constant_ref, factor_ref, sums_in, scalars_in = take(6)
    if iteration > 1:
        search_in, search_halo_in, search_sums_in = take(3)
    smoothed_ref, mapped_out = take(2)
    if first:
        constant_ref, factor_ref, halo_ref, sums_ref = take(4)
    else:
        residual_out, search_ref, scalars_ref = take(3)
        if not last:
            halo_ref, sums_ref, search_halo_ref, search_sums_ref = take(4)
    xy_out = take(1)[0]
    if not last:
        partial_ref = take(1)[0]

    row = info_ref[0]
    slab = info_ref[1]
    lane = lanes()
    height = rows_of()
    depth = lane % BS
    lane_row = lanes(1)
    even = lane % 2 == 0
    even_row = lane_row % 2 == 0
    low_holder, high_holder = info_ref[4], info_ref[5]
    low_corner, high_corner = info_ref[6], info_ref[7]
    x_holder = info_ref[3]

    def merge(start):
        up = roll(above_ref[start : start + BS], 31)
        down = roll(below_ref[start : start + BS], -31)
        return jnp.where(even, up, down)

    x_sides = xy_ref[x_holder, XY_X1 : XY_X1 + 2 * CHUNKS]
    y_sides = swap_sides(
        xy_ref[low_holder, XY_Y : XY_Y + BS], xy_ref[high_holder, XY_Y : XY_Y + BS]
    )
    z_first = merge(Z_Y1)
    z_second = merge(Z_Q)
    y_up = roll(above_ref[Z_Y : Z_Y + BS], 31)
    y_down = roll(below_ref[Z_Y : Z_Y + BS], -31)
    y_ends = jnp.where(depth == BS - 1, y_up, jnp.where(depth == 0, y_down, 0.0))
    x_ends = jnp.where(
        even_row,
        roll_row(above_ref[Z_X : Z_X + 1], 31),
        roll_row(below_ref[Z_X : Z_X + 1], -31),
    )
    corner_y = jnp.where(
        lane_row < 32,
        roll_row(xy_ref[low_corner, XY_X1 + CHUNKS - 1 : XY_X1 + CHUNKS], 32),
        roll_row(xy_ref[high_corner, XY_X1 : XY_X1 + 1], -32),
    )
    low_row = jnp.where(
        row == 0,
        xy_ref[low_corner, XY_Y : XY_Y + 1],
        xy_ref[low_corner, XY_Y + BS - 1 : XY_Y + BS],
    )
    high_row = jnp.where(
        row == 0,
        xy_ref[high_corner, XY_Y : XY_Y + 1],
        xy_ref[high_corner, XY_Y + BS - 1 : XY_Y + BS],
    )
    corner_x = swap_sides(low_row, high_row)
    ends = jnp.concatenate([x_ends, corner_y, corner_x, jnp.zeros((5, 128), F32)], axis=0)
    halo = [x_sides, y_sides, z_first, z_second, y_ends, ends]
    starts = [H_X1, H_Y, H_Z1, H_ZQ, H_YZ, H_R]
    sums = tiles_ref[...]

    if first:
        residual = [residual_ref[c] for c in range(CHUNKS)]
        constant_ref[C_XD : C_XD + CHUNKS] = xy_ref[x_holder, XY_XD : XY_XD + CHUNKS]
        constant_ref[C_YC : C_YC + BS] = swap_sides(
            xy_ref[low_holder, XY_YC : XY_YC + BS], xy_ref[high_holder, XY_YC : XY_YC + BS]
        )
        constant_ref[C_ZD : C_ZD + BS] = merge(Z_D)
        constant_ref[C_K : C_K + 8] = jnp.concatenate(
            [
                xy_ref[x_holder, XY_K : XY_K + 2],
                swap_sides(
                    xy_ref[low_holder, XY_K + 2 : XY_K + 3],
                    xy_ref[high_holder, XY_K + 2 : XY_K + 3],
                ),
                jnp.zeros((5, 128), F32),
            ],
            axis=0,
        )
        for g in range(slabs):
            tile = sums[8 * g : 8 * g + 8]
            a, b, off = tile[2:3], tile[3:4], tile[4:5]
            t0, t1 = tile[5:6], tile[6:7]
            if g > 0:
                a = a - u0 * u0 * i00
                b = b - u1 * u1 * i11
                off = off + u0 * u1 * i01
            a = jnp.where(lane_row < 4, a, 1.0)
            b = jnp.where(lane_row < 4, b, 1.0)
            scale = 1.0 / (a * b - off * off)
            i00, i01, i11 = b * scale, off * scale, a * scale
            u0, u1 = t0, t1
            factor_ref[8 * g : 8 * g + 8] = jnp.concatenate(
                [i00, i01, i11, t0, t1, jnp.zeros((3, 128), F32)], axis=0
            )
    else:
        scalars = None if iteration == 1 else scalars_in[...]
        energy, curvature, step, growth = search_scalars(
            sum_tiles(tiles_ref, slabs), scalars, iteration - 1
        )
        step_row = jnp.broadcast_to(step, (1, 128))
        residual = []
        for c in range(CHUNKS):
            mapped = mapped_ref[c]
            if growth is not None:
                mapped = mapped + growth * search_in[c]
            search_ref[c] = mapped
            value = residual_ref[c] - step * mapped
            residual_out[c] = value
            residual.append(value)
        old_halo = halo
        halo = []
        for start, block in zip(starts, old_halo):
            span = slice(start, start + block.shape[0])
            if growth is not None:
                block = block + growth * search_halo_in[span]
            if not last:
                search_halo_ref[span] = block
            halo.append(halo_in[span] - step * block)
        if growth is not None:
            sums = sums + growth * search_sums_in[...]
        if not last:
            search_sums_ref[...] = sums
        sums = sums_in[...] - step * sums
        kept = [energy, curvature, step]
        if growth is not None:
            kept = [energy, curvature, scalars[2:3, 0:1], step, growth]
        write_scalars(scalars_ref, 0, kept)

    if not last:
        for start, block in zip(starts, halo):
            halo_ref[start : start + block.shape[0]] = block
        sums_ref[...] = sums
    x_sides, y_sides, z_first, z_second, y_ends, ends = halo

    forward = []
    for g in range(slabs):
        t0, t1 = sums[8 * g : 8 * g + 1], sums[8 * g + 1 : 8 * g + 2]
        if g > 0:
            t0 = t0 + w0 * v0
            t1 = t1 + w1 * v1
        factor = factor_ref[8 * g : 8 * g + 8]
        v0 = factor[0:1] * t0 + factor[1:2] * t1
        v1 = factor[1:2] * t0 + factor[2:3] * t1
        w0, w1 = factor[3:4], factor[4:5]
        forward.append((v0, v1))
    blank = jnp.zeros((1, 128), F32)
    below0, below1, here0, here1, above0, above1 = [blank] * 6
    for g in reversed(range(slabs)):
        v0, v1 = forward[g]
        if g < slabs - 1:
            factor = factor_ref[8 * g : 8 * g + 8]
            s0, s1 = factor[3:4] * n0, factor[4:5] * n1
            v0 = v0 + factor[0:1] * s0 + factor[1:2] * s1
            v1 = v1 + factor[1:2] * s0 + factor[2:3] * s1
        n0, n1 = v0, v1
        here0 = jnp.where(slab == g, n0, here0)
        here1 = jnp.where(slab == g, n1, here1)
        above0 = jnp.where(slab + 1 == g, n0, above0)
        above1 = jnp.where(slab + 1 == g, n1, above1)
        below0 = jnp.where(slab - 1 == g, n0, below0)
        below1 = jnp.where(slab - 1 == g, n1, below1)
    own = [here0[:, 0:1], here1[:, 0:1]]

    effective = lambda d, c: effective_ref[d, c]
    diagonal = lambda c: diagonal_ref[c]
    end = CHUNKS - 1

    y1 = [relax_ref[c] * residual[c] for c in range(CHUNKS)]
    outcome = stencil(
        y1, effective, diagonal, x_sides[:CHUNKS], y_sides, roll(y_sides, 64), z_first
    )
    smoothed = []
    for c in range(CHUNKS):
        value = y1[c] + relax_ref[c] * (residual[c] - outcome[c]) + own[c // 8]
        smoothed_ref[c] = value
        smoothed.append(value)
    keys = constant_ref[C_K : C_K + 8]
    crossing = jnp.concatenate(
        [
            effective(0, c)[BS - 1 : BS] * y1[c][BS - 1 : BS] + effective(1, c)[0:1] * y1[c][0:1]
            for c in range(CHUNKS)
        ],
        axis=0,
    )
    end_row = keys[1:2] * ends[0:1]
    corner_row = keys[0:1] * ends[1:2]
    depth_row = lane_row % BS
    additions = []
    for c in range(CHUNKS):
        value = jnp.where(
            (depth_row == BS - 1) | (depth_row == 0), roll_row(end_row, 31 - 2 * c), 0.0
        )
        if c == 0:
            value = value + jnp.where(lane_row < 32, corner_row, 0.0)
        if c == end:
            value = value + jnp.where(lane_row >= 96, corner_row, 0.0)
        value = value + (here0 if c < 8 else here1)[:, 1:2]
        additions.append(value)
    x_next = (
        x_sides[CHUNKS:]
        + constant_ref[C_XD : C_XD + CHUNKS] * crossing
        + jnp.concatenate(additions, axis=0)
    )
    y_constant = constant_ref[C_YC : C_YC + BS]
    y_crossing = jnp.where(
        lane < 32, effective(3, 0) * y1[0], roll(effective(2, end) * y1[end], 64)
    )
    x_side_row = jnp.where(row == 0, BS - 1, 0)
    y_next = (
        roll(y_sides, 64)
        + y_constant * y_crossing
        + roll(y_constant, 64) * y_ends
        + jnp.where(height == x_side_row, keys[2:3] * ends[2:3], 0.0)
        + jnp.where(lane < 32, here1[:, 2:3], here0[:, 3:4])
    )
    z_crossing = pack(
        [
            jnp.where(depth == BS - 1, effective(4, c), effective(5, c)) * y1[c]
            for c in range(CHUNKS)
        ]
    )
    z_coarse = jnp.where(
        even_row,
        jnp.where(depth_row < 16, above0[:, 0:1], above1[:, 0:1]),
        jnp.where(depth_row < 16, below0[:, 0:1], below1[:, 0:1]),
    )
    z_next = z_second + constant_ref[C_ZD : C_ZD + BS] * z_crossing + z_coarse
    mapped = stencil(smoothed, effective, diagonal, x_next, y_next, roll(y_next, 64), z_next)
    for c in range(CHUNKS):
        mapped_out[c] = mapped[c]

    values = [
        total_of(mapped[:8]),
        total_of(mapped[8:]),
        total_of([residual[c] * smoothed[c] for c in range(CHUNKS)]),
        total_of([mapped[c] * smoothed[c] for c in range(CHUNKS)]),
    ]
    if not first:
        values.append(total_of([search_ref[c] * smoothed[c] for c in range(CHUNKS)]))
    if last:
        write_scalars(xy_out, 0, values)
        return
    write_scalars(xy_out, XY_S, values)
    y1 = [relax_ref[c] * mapped[c] for c in range(CHUNKS)]
    outcome = stencil(y1, effective, diagonal, None, None, None, None)
    partial = []
    for c in range(CHUNKS):
        value = y1[c] + relax_ref[c] * (mapped[c] - outcome[c])
        partial_ref[c] = value
        partial.append(value)
    write_xy(xy_out, row, y1, partial)


def finish_kernel(
    count, tiles_ref, scalars_ref, residual_ref, mapped_ref, search_ref, first_ref, second_ref, third_ref,
    solution_ref, residual_out,
):
    scalars = scalars_ref[...]
    _, _, step, growth = search_scalars(sum_tiles(tiles_ref, count), scalars, ITERS - 1)
    first_step, second_step, second_growth = scalars[2:3, 0:1], scalars[3:4, 0:1], scalars[4:5, 0:1]
    third_weight = step
    second_weight = second_step + growth * step
    first_weight = first_step + second_growth * second_weight
    for c in range(CHUNKS):
        s, part = c // 8, pl.ds(128 * (c % 8), 128)
        solution_ref[s, :, part] = (
            first_weight * first_ref[c] + second_weight * second_ref[c] + third_weight * third_ref[c]
        )
        residual_out[s, :, part] = residual_ref[c] - step * (mapped_ref[c] + growth * search_ref[c])


def call(kernel, name, outs, operands, scalar_operands=0, scalar_outs=0):
    vmem = pl.BlockSpec(memory_space=pltpu.VMEM)
    smem = pl.BlockSpec(memory_space=pltpu.SMEM)
    return pl.pallas_call(
        kernel,
        out_shape=tuple(outs),
        in_specs=[smem] * scalar_operands + [vmem] * (len(operands) - scalar_operands),
        out_specs=tuple([smem] * scalar_outs + [vmem] * (len(outs) - scalar_outs)),
        compiler_params=pltpu.CompilerParams(vmem_limit_bytes=40 * 1024 * 1024),
        name=name,
    )(*operands)


def array(*shape):
    return jax.ShapeDtypeStruct(shape, F32)


def gather_bricks(message):
    return lax.all_gather(message, "brick", axis=0, tiled=False)


def gather_slabs(tile):
    return lax.all_gather(tile, "grp", axis=0, tiled=True)


def exchange_slabs(message):
    count = lax.axis_size("grp")
    upward = [(i, i + 1) for i in range(count - 1)]
    downward = [(i + 1, i) for i in range(count - 1)]
    return lax.ppermute(message, "grp", downward), lax.ppermute(message, "grp", upward)


def on_device(source, uptake, conductance, occupancy, assignment):
    slabs = lax.axis_size("grp")
    bricks = lax.axis_size("brick")
    place = (lax.axis_index("grp") * bricks + lax.axis_index("brick")).astype(jnp.int32).reshape(1)
    field = array(*FIELD)
    info, effective, diagonal, relax, residual, partial, edge, message = call(
        functools.partial(setup_kernel, slabs, bricks),
        "setup",
        [
            jax.ShapeDtypeStruct((8,), jnp.int32), array(6, *FIELD), field, field, field, field,
            array(E_ROWS, 128), array(XY_ROWS_FIRST, 128),
        ],
        [place, assignment, occupancy.reshape(-1), source[0, 0], uptake[0, 0], conductance[0, 0]],
        scalar_operands=3,
        scalar_outs=1,
    )
    mapped = residual
    directions = []
    state = {}
    for iteration in range(ITERS):
        first, last = iteration == 0, iteration == ITERS - 1
        gathered = gather_bricks(message)
        z_message, tile = call(
            functools.partial(middle_kernel, first, bricks),
            f"middle_{iteration}",
            [array(Z_ROWS_FIRST if first else Z_ROWS, 128), array(8, 128)],
            [info, gathered, mapped, relax, partial, edge],
            scalar_operands=1,
        )
        above, below = exchange_slabs(z_message)
        tiles = gather_slabs(tile)
        operands = [info, gathered, above, below, tiles, effective, diagonal, relax, residual]
        tall = array(8 * slabs, 128)
        outs = {"smoothed": field, "mapped": field}
        if not first:
            operands += [mapped] + [state[k] for k in ("halo", "constant", "factor", "sums", "scalars")]
        if iteration > 1:
            operands += [state[k] for k in ("search", "search_halo", "search_sums")]
        if first:
            outs |= {"constant": array(C_ROWS, 128), "factor": tall, "halo": array(H_ROWS, 128), "sums": tall}
        else:
            outs |= {"residual": field, "search": field, "scalars": array(8, 128)}
            if not last:
                outs |= {
                    "halo": array(H_ROWS, 128), "sums": tall,
                    "search_halo": array(H_ROWS, 128), "search_sums": tall,
                }
        outs["message"] = array(8 if last else XY_ROWS, 128)
        if not last:
            outs["partial"] = field
        results = call(
            functools.partial(step_kernel, iteration, slabs, bricks),
            f"step_{iteration}",
            list(outs.values()),
            operands,
            scalar_operands=1,
        )
        state |= dict(zip(outs, results))
        if first:
            state["scalars"] = jnp.zeros((8, 128), F32)
        mapped, message, partial = state["mapped"], state["message"], state.get("partial")
        residual = state.get("residual", residual)
        directions.append(state["smoothed"])
    tiles = gather_slabs(gather_bricks(message).reshape(bricks * 8, 128))
    brick_pair = array(2, BS, BS * BS)
    solution_field, residual = call(
        functools.partial(finish_kernel, slabs * bricks),
        "finish",
        [brick_pair, brick_pair],
        [tiles, state["scalars"], residual, mapped, state["search"]] + directions,
    )
    return solution_field[None, None], residual[None, None]


def solution(mesh):
    return jax.shard_map(
        on_device,
        mesh=mesh,
        in_specs=(
            P("grp", "brick", None, None, None),
            P("grp", "brick", None, None, None),
            P("grp", "brick", None, None, None, None),
            P(),
            P(),
        ),
        out_specs=(P("grp", "brick", None, None, None), P("grp", "brick", None, None, None)),
        check_vma=False,
    )
```

```python
import functools

import jax
import jax.numpy as jnp
from jax import lax
from jax.experimental import pallas as pl
from jax.experimental.pallas import tpu as pltpu
from jax.sharding import PartitionSpec as P

BS = 32
CHUNKS = 16
OMEGA = 0.6
ITERS = 3
F32 = jnp.float32
FIELD = (CHUNKS, BS, 128)

XY_X1, XY_XP, XY_Y, XY_S = 0, 16, 32, 64
XY_ROWS = 72
XY_XD, XY_YC, XY_K = 72, 88, 120
XY_ROWS_FIRST = 128
Z_Y1, Z_Q, Z_Y, Z_X = 0, 32, 64, 96
Z_ROWS = 104
Z_D = 104
Z_ROWS_FIRST = 136
H_X1, H_XP, H_Y, H_Z1, H_ZQ, H_YZ, H_R = 0, 16, 32, 64, 96, 128, 160
H_ROWS = 168
C_XD, C_YC, C_ZD, C_K = 0, 16, 48, 80
C_ROWS = 88
E_XP, E_XM, E_YP, E_YM = 0, 16, 32, 64
E_ROWS = 96


def roll(block, shift):
    return pltpu.roll(block, shift % 128, axis=1)


def roll_row(row, shift):
    return pltpu.roll(jnp.broadcast_to(row, (8, 128)), shift % 128, axis=1)[0:1]


def lanes(rows=BS):
    return lax.broadcasted_iota(jnp.int32, (rows, 128), 1)


def rows_of(height=BS):
    return lax.broadcasted_iota(jnp.int32, (height, 128), 0)


def pack(chunks):
    height = chunks[0].shape[0]
    pair = (lanes(height) % BS) // 2
    total = jnp.zeros((height, 128), F32)
    for c in range(CHUNKS):
        moved = roll(chunks[c], 2 * c - 31) if height > 1 else roll_row(chunks[c], 2 * c - 31)
        total = jnp.where(pair == c, moved, total)
    return total


def stencil(field, effective, diagonal, x_halo, y_low, y_high, z_halo):
    lane = lanes()
    height = rows_of()
    depth = lane % BS
    zero = jnp.zeros((BS, 128), F32)
    back = [roll(f, -32) for f in field]
    forth = [roll(f, 32) for f in field]
    out = []
    for c in range(CHUNKS):
        f = field[c]
        x_row = zero if x_halo is None else x_halo[c : c + 1]
        total = diagonal(c) * f
        total -= effective(0, c) * jnp.where(height == BS - 1, x_row, pltpu.roll(f, BS - 1, axis=0))
        total -= effective(1, c) * jnp.where(height == 0, x_row, pltpu.roll(f, 1, axis=0))
        following = back[c + 1] if c < CHUNKS - 1 else (zero if y_high is None else y_high)
        previous = forth[c - 1] if c > 0 else (zero if y_low is None else y_low)
        total -= effective(2, c) * jnp.where(lane < 96, back[c], following)
        total -= effective(3, c) * jnp.where(lane >= 32, forth[c], previous)
        ends = zero if z_halo is None else roll(z_halo, 31 - 2 * c)
        total -= effective(4, c) * jnp.where(depth == BS - 1, ends, roll(f, -1))
        total -= effective(5, c) * jnp.where(depth == 0, ends, roll(f, 1))
        out.append(total)
    return out


def total_of(blocks):
    acc = blocks[0]
    for block in blocks[1:]:
        acc = acc + block
    return jnp.sum(jnp.sum(acc, axis=0, keepdims=True), axis=1, keepdims=True)


def facing(block, row):
    return jnp.where(row == 0, block[BS - 1 : BS], block[0:1])


def side_blocks(low_first, high_first, low_second, high_second):
    group = lanes() // 32
    return jnp.where(
        group == 0,
        low_first,
        jnp.where(
            group == 1,
            roll(high_first, 64),
            jnp.where(group == 2, roll(low_second, 64), high_second),
        ),
    )


def write_xy(xy_ref, row, y1, partial):
    for c in range(CHUNKS):
        xy_ref[XY_X1 + c : XY_X1 + c + 1] = facing(y1[c], row)
        xy_ref[XY_XP + c : XY_XP + c + 1] = facing(partial[c], row)
    last = CHUNKS - 1
    xy_ref[XY_Y : XY_Y + BS] = side_blocks(y1[0], y1[last], partial[0], partial[last])


def write_scalars(ref, start, values):
    for i, value in enumerate(values):
        ref[start + i : start + i + 1] = jnp.broadcast_to(value, (1, 128))
    for i in range(len(values), 8):
        ref[start + i : start + i + 1] = jnp.zeros((1, 128), F32)


def locate(bricks, place_ref, assignment_ref):
    across = bricks // 2
    place = place_ref[0]
    slab = place // bricks
    patch = assignment_ref[place % bricks]
    row = patch // across
    column = patch % across
    return slab, patch, row, column


def setup_kernel(
    slabs, bricks, place_ref, assignment_ref, occupancy_ref, source_ref, uptake_ref, conductance_ref,
    info_ref, effective_ref, diagonal_ref, relax_ref, residual_ref, partial_ref, edge_ref, xy_ref,
):
    across = bricks // 2
    slab, patch, row, column = locate(bricks, place_ref, assignment_ref)

    def holder(row_target, column_target):
        inside = (column_target >= 0) & (column_target < across)
        wanted = jnp.where(inside, row_target * across + column_target, patch)
        found = jnp.int32(0)
        for b in range(bricks):
            found = jnp.where(assignment_ref[b] == wanted, b, found)
        return found

    info_ref[0] = row
    info_ref[1] = slab
    info_ref[2] = holder(row, column)
    info_ref[3] = holder(1 - row, column)
    info_ref[4] = holder(row, column - 1)
    info_ref[5] = holder(row, column + 1)
    info_ref[6] = holder(1 - row, column - 1)
    info_ref[7] = holder(1 - row, column + 1)

    breadth = 2 * across

    def live_at(g, x, y):
        inside = (g >= 0) & (g < slabs) & (x >= 0) & (x < 2) & (y >= 0) & (y < breadth)
        index = (jnp.clip(g, 0, slabs - 1) * 2 + jnp.clip(x, 0, 1)) * breadth + jnp.clip(y, 0, breadth - 1)
        return jnp.where(inside, occupancy_ref[index], 0).astype(F32)

    lane = lanes()
    height = rows_of()
    depth = lane % BS
    absorbed = []
    low_ends = []
    high_ends = []
    first_y = None
    second_y = None
    y1 = []
    for s in range(2):
        y = column * 2 + s
        here = live_at(slab, row, y)
        around = [
            here * live_at(slab, row + 1, y),
            here * live_at(slab, row - 1, y),
            here * live_at(slab, row, y + 1),
            here * live_at(slab, row, y - 1),
            here * live_at(slab + 1, row, y),
            here * live_at(slab - 1, row, y),
        ]
        borders = [height == BS - 1, height == 0, lane >= 96, lane < 32, depth == BS - 1, depth == 0]
        for k in range(8):
            c = 8 * s + k
            part = pl.ds(128 * k, 128)
            taken = uptake_ref[s, :, part]
            absorbed.append(taken)
            diagonal = taken
            for d in range(6):
                bond = conductance_ref[d, s, :, part]
                if (d == 2 and k < 7) or (d == 3 and k > 0):
                    value = bond * here
                else:
                    value = bond * jnp.where(borders[d], around[d], here)
                effective_ref[d, c] = value
                diagonal = diagonal + value
                if d == 2 and c == 7:
                    first_y = jnp.where(borders[d], value, 0.0)
                if d == 3 and c == 8:
                    second_y = jnp.where(borders[d], value, 0.0)
                if d == 4:
                    high_ends.append(jnp.where(borders[d], value, 0.0))
                if d == 5:
                    low_ends.append(jnp.where(borders[d], value, 0.0))
            relax = OMEGA / diagonal
            diagonal_ref[c] = diagonal
            relax_ref[c] = relax
            forcing = source_ref[s, :, part] * here
            residual_ref[c] = forcing
            y1.append(relax * forcing)

    outcome = stencil(
        y1, lambda d, c: effective_ref[d, c], lambda c: diagonal_ref[c], None, None, None, None
    )
    partial = []
    for c in range(CHUNKS):
        value = y1[c] + relax_ref[c] * (residual_ref[c] - outcome[c])
        partial_ref[c] = value
        partial.append(value)
    write_xy(xy_ref, row, y1, partial)

    first_coupling = total_of([first_y])
    high_sums = [total_of(high_ends[8 * s : 8 * s + 8]) for s in range(2)]
    low_sums = [total_of(low_ends[8 * s : 8 * s + 8]) for s in range(2)]
    taken_sums = [total_of(absorbed[8 * s : 8 * s + 8]) for s in range(2)]
    residual_sums = [total_of([residual_ref[8 * s + k] for k in range(8)]) for s in range(2)]
    write_scalars(
        xy_ref,
        XY_S,
        [
            residual_sums[0],
            residual_sums[1],
            taken_sums[0] + first_coupling + high_sums[0] + low_sums[0],
            taken_sums[1] + total_of([second_y]) + high_sums[1] + low_sums[1],
            first_coupling,
            high_sums[0],
            high_sums[1],
        ],
    )

    last = CHUNKS - 1
    z_ends = [relax_ref[c] * (high_ends[c] + low_ends[c]) for c in range(CHUNKS)]
    for c in range(CHUNKS):
        xy_ref[XY_XD + c : XY_XD + c + 1] = facing(relax_ref[c], row)
        edge_ref[E_XP + c : E_XP + c + 1] = (relax_ref[c] * effective_ref[0, c])[BS - 1 : BS]
        edge_ref[E_XM + c : E_XM + c + 1] = (relax_ref[c] * effective_ref[1, c])[0:1]
    high_y = jnp.where(lane >= 96, relax_ref[last] * effective_ref[2, last], 0.0)
    low_y = jnp.where(lane < 32, relax_ref[0] * effective_ref[3, 0], 0.0)
    edge_ref[E_YP : E_YP + BS] = high_y
    edge_ref[E_YM : E_YM + BS] = low_y
    xy_ref[XY_YC : XY_YC + BS] = side_blocks(relax_ref[0], relax_ref[last], z_ends[0], z_ends[last])
    xy_ref[XY_K : XY_K + 1] = facing(low_y + high_y, row)
    xy_ref[XY_K + 1 : XY_K + 2] = pack([facing(z, row) for z in z_ends])
    toward_low = facing_terms(relax_ref, effective_ref, 0)
    toward_high = facing_terms(relax_ref, effective_ref, last)
    lane_row = lanes(1)
    xy_ref[XY_K + 2 : XY_K + 3] = jnp.where(lane_row < 32, toward_low, roll_row(toward_high, 64))
    xy_ref[XY_K + 3 : XY_K + 8] = jnp.zeros((5, 128), F32)


def facing_terms(relax_ref, effective_ref, c):
    upper = (relax_ref[c] * effective_ref[0, c])[BS - 1 : BS]
    lower = (relax_ref[c] * effective_ref[1, c])[0:1]
    return upper + lower


def swap_sides(from_low, from_high):
    rows = from_low.shape[0]
    if rows == 1:
        low, high = roll_row(from_low, -32), roll_row(from_high, 32)
    else:
        low, high = roll(from_low, -32), roll(from_high, 32)
    return jnp.where((lanes(rows) // 32) % 2 == 0, low, high)


def middle_kernel(
    first, bricks, info_ref, xy_ref, field_ref, relax_ref, partial_ref, edge_ref, z_ref, tile_ref
):
    lane = lanes()
    height = rows_of()
    x_holder = info_ref[3]
    x_halo = xy_ref[x_holder, XY_X1 : XY_X1 + CHUNKS]
    sides = swap_sides(
        xy_ref[info_ref[4], XY_Y : XY_Y + BS], xy_ref[info_ref[5], XY_Y : XY_Y + BS]
    )
    upper = edge_ref[E_XP : E_XP + CHUNKS] * x_halo
    lower = edge_ref[E_XM : E_XM + CHUNKS] * x_halo
    y1 = []
    whole = []
    for c in range(CHUNKS):
        y1.append(relax_ref[c] * field_ref[c])
        value = partial_ref[c]
        value = value + jnp.where(height == BS - 1, upper[c : c + 1], 0.0)
        value = value + jnp.where(height == 0, lower[c : c + 1], 0.0)
        if c == 0:
            value = value + jnp.where(lane < 32, edge_ref[E_YM : E_YM + BS] * sides, 0.0)
        if c == CHUNKS - 1:
            value = value + jnp.where(
                lane >= 96, edge_ref[E_YP : E_YP + BS] * roll(sides, 64), 0.0
            )
        whole.append(value)
    z_ref[Z_Y1 : Z_Y1 + BS] = pack(y1)
    z_ref[Z_Q : Z_Q + BS] = pack(whole)
    z_ref[Z_Y : Z_Y + BS] = sides
    x_ends = pack([x_halo[c : c + 1] for c in range(CHUNKS)])
    z_ref[Z_X : Z_X + 8] = jnp.broadcast_to(x_ends, (8, 128))
    if first:
        z_ref[Z_D : Z_D + BS] = pack([relax_ref[c] for c in range(CHUNKS)])
    lane_tile = lanes(8)
    mixed = jnp.zeros((8, 128), F32)
    for q in range(4):
        mixed = jnp.where(lane_tile == q, xy_ref[info_ref[2 + q], XY_S : XY_S + 8], mixed)
    if not first:
        summed = xy_ref[0, XY_S : XY_S + 8]
        for b in range(1, bricks):
            summed = summed + xy_ref[b, XY_S : XY_S + 8]
        mixed = jnp.where(rows_of(8) < 2, mixed, summed)
    tile_ref[...] = mixed


def search_scalars(tiles, scalars, iteration):
    energy = tiles[2:3, 0:1]
    curvature = tiles[3:4, 0:1]
    if iteration == 0:
        return energy, curvature, energy / curvature, None
    growth = energy / scalars[0:1, 0:1]
    curvature = curvature + growth * (2.0 * tiles[4:5, 0:1] + growth * scalars[1:2, 0:1])
    return energy, curvature, energy / curvature, growth


def sum_tiles(ref, count):
    total = ref[0:8]
    for g in range(1, count):
        total = total + ref[8 * g : 8 * g + 8]
    return total


def step_kernel(iteration, slabs, bricks, *refs):
    first = iteration == 0
    last = iteration == ITERS - 1
    refs = list(refs)
    take = lambda count: [refs.pop(0) for _ in range(count)]
    info_ref, xy_ref, above_ref, below_ref, tiles_ref = take(5)
    effective_ref, diagonal_ref, relax_ref, residual_ref = take(4)
    if not first:
        mapped_ref, halo_in, constant_ref, factor_ref, sums_in, scalars_in = take(6)
    if iteration > 1:
        search_in, search_halo_in, search_sums_in = take(3)
    smoothed_ref, mapped_out = take(2)
    if first:
        constant_ref, factor_ref, halo_ref, sums_ref = take(4)
    else:
        residual_out, search_ref, scalars_ref = take(3)
        if not last:
            halo_ref, sums_ref, search_halo_ref, search_sums_ref = take(4)
    xy_out = take(1)[0]
    if not last:
        partial_ref = take(1)[0]

    row = info_ref[0]
    slab = info_ref[1]
    lane = lanes()
    height = rows_of()
    depth = lane % BS
    lane_row = lanes(1)
    even = lane % 2 == 0
    even_row = lane_row % 2 == 0
    low_holder, high_holder = info_ref[4], info_ref[5]
    low_corner, high_corner = info_ref[6], info_ref[7]
    x_holder = info_ref[3]

    def merge(start):
        up = roll(above_ref[start : start + BS], 31)
        down = roll(below_ref[start : start + BS], -31)
        return jnp.where(even, up, down)

    x_sides = xy_ref[x_holder, XY_X1 : XY_X1 + 2 * CHUNKS]
    y_sides = swap_sides(
        xy_ref[low_holder, XY_Y : XY_Y + BS], xy_ref[high_holder, XY_Y : XY_Y + BS]
    )
    z_first = merge(Z_Y1)
    z_second = merge(Z_Q)
    y_up = roll(above_ref[Z_Y : Z_Y + BS], 31)
    y_down = roll(below_ref[Z_Y : Z_Y + BS], -31)
    y_ends = jnp.where(depth == BS - 1, y_up, jnp.where(depth == 0, y_down, 0.0))
    x_ends = jnp.where(
        even_row,
        roll_row(above_ref[Z_X : Z_X + 1], 31),
        roll_row(below_ref[Z_X : Z_X + 1], -31),
    )
    corner_y = jnp.where(
        lane_row < 32,
        roll_row(xy_ref[low_corner, XY_X1 + CHUNKS - 1 : XY_X1 + CHUNKS], 32),
        roll_row(xy_ref[high_corner, XY_X1 : XY_X1 + 1], -32),
    )
    low_row = jnp.where(
        row == 0,
        xy_ref[low_corner, XY_Y : XY_Y + 1],
        xy_ref[low_corner, XY_Y + BS - 1 : XY_Y + BS],
    )
    high_row = jnp.where(
        row == 0,
        xy_ref[high_corner, XY_Y : XY_Y + 1],
        xy_ref[high_corner, XY_Y + BS - 1 : XY_Y + BS],
    )
    corner_x = swap_sides(low_row, high_row)
    ends = jnp.concatenate([x_ends, corner_y, corner_x, jnp.zeros((5, 128), F32)], axis=0)
    halo = [x_sides, y_sides, z_first, z_second, y_ends, ends]
    starts = [H_X1, H_Y, H_Z1, H_ZQ, H_YZ, H_R]
    sums = tiles_ref[...]

    if first:
        residual = [residual_ref[c] for c in range(CHUNKS)]
        constant_ref[C_XD : C_XD + CHUNKS] = xy_ref[x_holder, XY_XD : XY_XD + CHUNKS]
        constant_ref[C_YC : C_YC + BS] = swap_sides(
            xy_ref[low_holder, XY_YC : XY_YC + BS], xy_ref[high_holder, XY_YC : XY_YC + BS]
        )
        constant_ref[C_ZD : C_ZD + BS] = merge(Z_D)
        constant_ref[C_K : C_K + 8] = jnp.concatenate(
            [
                xy_ref[x_holder, XY_K : XY_K + 2],
                swap_sides(
                    xy_ref[low_holder, XY_K + 2 : XY_K + 3],
                    xy_ref[high_holder, XY_K + 2 : XY_K + 3],
                ),
                jnp.zeros((5, 128), F32),
            ],
            axis=0,
        )
        for g in range(slabs):
            tile = sums[8 * g : 8 * g + 8]
            a, b, off = tile[2:3], tile[3:4], tile[4:5]
            t0, t1 = tile[5:6], tile[6:7]
            if g > 0:
                a = a - u0 * u0 * i00
                b = b - u1 * u1 * i11
                off = off + u0 * u1 * i01
            a = jnp.where(lane_row < 4, a, 1.0)
            b = jnp.where(lane_row < 4, b, 1.0)
            scale = 1.0 / (a * b - off * off)
            i00, i01, i11 = b * scale, off * scale, a * scale
            u0, u1 = t0, t1
            factor_ref[8 * g : 8 * g + 8] = jnp.concatenate(
                [i00, i01, i11, t0, t1, jnp.zeros((3, 128), F32)], axis=0
            )
    else:
        scalars = None if iteration == 1 else scalars_in[...]
        energy, curvature, step, growth = search_scalars(
            sum_tiles(tiles_ref, slabs), scalars, iteration - 1
        )
        step_row = jnp.broadcast_to(step, (1, 128))
        residual = []
        for c in range(CHUNKS):
            mapped = mapped_ref[c]
            if growth is not None:
                mapped = mapped + growth * search_in[c]
            search_ref[c] = mapped
            value = residual_ref[c] - step * mapped
            residual_out[c] = value
            residual.append(value)
        old_halo = halo
        halo = []
        for start, block in zip(starts, old_halo):
            span = slice(start, start + block.shape[0])
            if growth is not None:
                block = block + growth * search_halo_in[span]
            if not last:
                search_halo_ref[span] = block
            halo.append(halo_in[span] - step * block)
        if growth is not None:
            sums = sums + growth * search_sums_in[...]
        if not last:
            search_sums_ref[...] = sums
        sums = sums_in[...] - step * sums
        kept = [energy, curvature, step]
        if growth is not None:
            kept = [energy, curvature, scalars[2:3, 0:1], step, growth]
        write_scalars(scalars_ref, 0, kept)

    if not last:
        for start, block in zip(starts, halo):
            halo_ref[start : start + block.shape[0]] = block
        sums_ref[...] = sums
    x_sides, y_sides, z_first, z_second, y_ends, ends = halo

    forward = []
    for g in range(slabs):
        t0, t1 = sums[8 * g : 8 * g + 1], sums[8 * g + 1 : 8 * g + 2]
        if g > 0:
            t0 = t0 + w0 * v0
            t1 = t1 + w1 * v1
        factor = factor_ref[8 * g : 8 * g + 8]
        v0 = factor[0:1] * t0 + factor[1:2] * t1
        v1 = factor[1:2] * t0 + factor[2:3] * t1
        w0, w1 = factor[3:4], factor[4:5]
        forward.append((v0, v1))
    blank = jnp.zeros((1, 128), F32)
    below0, below1, here0, here1, above0, above1 = [blank] * 6
    for g in reversed(range(slabs)):
        v0, v1 = forward[g]
        if g < slabs - 1:
            factor = factor_ref[8 * g : 8 * g + 8]
            s0, s1 = factor[3:4] * n0, factor[4:5] * n1
            v0 = v0 + factor[0:1] * s0 + factor[1:2] * s1
            v1 = v1 + factor[1:2] * s0 + factor[2:3] * s1
        n0, n1 = v0, v1
        here0 = jnp.where(slab == g, n0, here0)
        here1 = jnp.where(slab == g, n1, here1)
        above0 = jnp.where(slab + 1 == g, n0, above0)
        above1 = jnp.where(slab + 1 == g, n1, above1)
        below0 = jnp.where(slab - 1 == g, n0, below0)
        below1 = jnp.where(slab - 1 == g, n1, below1)
    own = [here0[:, 0:1], here1[:, 0:1]]

    effective = lambda d, c: effective_ref[d, c]
    diagonal = lambda c: diagonal_ref[c]
    end = CHUNKS - 1

    y1 = [relax_ref[c] * residual[c] for c in range(CHUNKS)]
    outcome = stencil(
        y1, effective, diagonal, x_sides[:CHUNKS], y_sides, roll(y_sides, 64), z_first
    )
    smoothed = []
    for c in range(CHUNKS):
        value = y1[c] + relax_ref[c] * (residual[c] - outcome[c]) + own[c // 8]
        smoothed_ref[c] = value
        smoothed.append(value)
    keys = constant_ref[C_K : C_K + 8]
    crossing = jnp.concatenate(
        [
            effective(0, c)[BS - 1 : BS] * y1[c][BS - 1 : BS] + effective(1, c)[0:1] * y1[c][0:1]
            for c in range(CHUNKS)
        ],
        axis=0,
    )
    end_row = keys[1:2] * ends[0:1]
    corner_row = keys[0:1] * ends[1:2]
    depth_row = lane_row % BS
    additions = []
    for c in range(CHUNKS):
        value = jnp.where(
            (depth_row == BS - 1) | (depth_row == 0), roll_row(end_row, 31 - 2 * c), 0.0
        )
        if c == 0:
            value = value + jnp.where(lane_row < 32, corner_row, 0.0)
        if c == end:
            value = value + jnp.where(lane_row >= 96, corner_row, 0.0)
        value = value + (here0 if c < 8 else here1)[:, 1:2]
        additions.append(value)
    x_next = (
        x_sides[CHUNKS:]
        + constant_ref[C_XD : C_XD + CHUNKS] * crossing
        + jnp.concatenate(additions, axis=0)
    )
    y_constant = constant_ref[C_YC : C_YC + BS]
    y_crossing = jnp.where(
        lane < 32, effective(3, 0) * y1[0], roll(effective(2, end) * y1[end], 64)
    )
    x_side_row = jnp.where(row == 0, BS - 1, 0)
    y_next = (
        roll(y_sides, 64)
        + y_constant * y_crossing
        + roll(y_constant, 64) * y_ends
        + jnp.where(height == x_side_row, keys[2:3] * ends[2:3], 0.0)
        + jnp.where(lane < 32, here1[:, 2:3], here0[:, 3:4])
    )
    z_crossing = pack(
        [
            jnp.where(depth == BS - 1, effective(4, c), effective(5, c)) * y1[c]
            for c in range(CHUNKS)
        ]
    )
    z_coarse = jnp.where(
        even_row,
        jnp.where(depth_row < 16, above0[:, 0:1], above1[:, 0:1]),
        jnp.where(depth_row < 16, below0[:, 0:1], below1[:, 0:1]),
    )
    z_next = z_second + constant_ref[C_ZD : C_ZD + BS] * z_crossing + z_coarse
    mapped = stencil(smoothed, effective, diagonal, x_next, y_next, roll(y_next, 64), z_next)
    for c in range(CHUNKS):
        mapped_out[c] = mapped[c]

    values = [
        total_of(mapped[:8]),
        total_of(mapped[8:]),
        total_of([residual[c] * smoothed[c] for c in range(CHUNKS)]),
        total_of([mapped[c] * smoothed[c] for c in range(CHUNKS)]),
    ]
    if not first:
        values.append(total_of([search_ref[c] * smoothed[c] for c in range(CHUNKS)]))
    if last:
        write_scalars(xy_out, 0, values)
        return
    write_scalars(xy_out, XY_S, values)
    y1 = [relax_ref[c] * mapped[c] for c in range(CHUNKS)]
    outcome = stencil(y1, effective, diagonal, None, None, None, None)
    partial = []
    for c in range(CHUNKS):
        value = y1[c] + relax_ref[c] * (mapped[c] - outcome[c])
        partial_ref[c] = value
        partial.append(value)
    write_xy(xy_out, row, y1, partial)


def finish_kernel(
    count, tiles_ref, scalars_ref, residual_ref, mapped_ref, search_ref, first_ref, second_ref, third_ref,
    solution_ref, residual_out,
):
    scalars = scalars_ref[...]
    _, _, step, growth = search_scalars(sum_tiles(tiles_ref, count), scalars, ITERS - 1)
    first_step, second_step, second_growth = scalars[2:3, 0:1], scalars[3:4, 0:1], scalars[4:5, 0:1]
    third_weight = step
    second_weight = second_step + growth * step
    first_weight = first_step + second_growth * second_weight
    for c in range(CHUNKS):
        s, part = c // 8, pl.ds(128 * (c % 8), 128)
        solution_ref[s, :, part] = (
            first_weight * first_ref[c] + second_weight * second_ref[c] + third_weight * third_ref[c]
        )
        residual_out[s, :, part] = residual_ref[c] - step * (mapped_ref[c] + growth * search_ref[c])


def call(kernel, name, outs, operands, scalar_operands=0, scalar_outs=0):
    vmem = pl.BlockSpec(memory_space=pltpu.VMEM)
    smem = pl.BlockSpec(memory_space=pltpu.SMEM)
    return pl.pallas_call(
        kernel,
        out_shape=tuple(outs),
        in_specs=[smem] * scalar_operands + [vmem] * (len(operands) - scalar_operands),
        out_specs=tuple([smem] * scalar_outs + [vmem] * (len(outs) - scalar_outs)),
        compiler_params=pltpu.CompilerParams(vmem_limit_bytes=40 * 1024 * 1024),
        name=name,
    )(*operands)


def array(*shape):
    return jax.ShapeDtypeStruct(shape, F32)


def gather_bricks(message):
    return lax.all_gather(message, "brick", axis=0, tiled=False)


def gather_slabs(tile):
    count = lax.axis_size("grp")
    inner = max(count // 4, 1)
    outer = count // inner
    near = [[i * inner + j for j in range(inner)] for i in range(outer)]
    far = [[i * inner + j for i in range(outer)] for j in range(inner)]
    pairs = lax.all_gather(tile, "grp", axis=0, tiled=True, axis_index_groups=near)
    return lax.all_gather(pairs, "grp", axis=0, tiled=True, axis_index_groups=far)


def exchange_slabs(message):
    count = lax.axis_size("grp")
    upward = [(i, i + 1) for i in range(count - 1)]
    downward = [(i + 1, i) for i in range(count - 1)]
    return lax.ppermute(message, "grp", downward), lax.ppermute(message, "grp", upward)


def on_device(source, uptake, conductance, occupancy, assignment):
    slabs = lax.axis_size("grp")
    bricks = lax.axis_size("brick")
    place = (lax.axis_index("grp") * bricks + lax.axis_index("brick")).astype(jnp.int32).reshape(1)
    field = array(*FIELD)
    info, effective, diagonal, relax, residual, partial, edge, message = call(
        functools.partial(setup_kernel, slabs, bricks),
        "setup",
        [
            jax.ShapeDtypeStruct((8,), jnp.int32), array(6, *FIELD), field, field, field, field,
            array(E_ROWS, 128), array(XY_ROWS_FIRST, 128),
        ],
        [place, assignment, occupancy.reshape(-1), source[0, 0], uptake[0, 0], conductance[0, 0]],
        scalar_operands=3,
        scalar_outs=1,
    )
    mapped = residual
    directions = []
    state = {}
    for iteration in range(ITERS):
        first, last = iteration == 0, iteration == ITERS - 1
        gathered = gather_bricks(message)
        z_message, tile = call(
            functools.partial(middle_kernel, first, bricks),
            f"middle_{iteration}",
            [array(Z_ROWS_FIRST if first else Z_ROWS, 128), array(8, 128)],
            [info, gathered, mapped, relax, partial, edge],
            scalar_operands=1,
        )
        above, below = exchange_slabs(z_message)
        tiles = gather_slabs(tile)
        operands = [info, gathered, above, below, tiles, effective, diagonal, relax, residual]
        tall = array(8 * slabs, 128)
        outs = {"smoothed": field, "mapped": field}
        if not first:
            operands += [mapped] + [state[k] for k in ("halo", "constant", "factor", "sums", "scalars")]
        if iteration > 1:
            operands += [state[k] for k in ("search", "search_halo", "search_sums")]
        if first:
            outs |= {"constant": array(C_ROWS, 128), "factor": tall, "halo": array(H_ROWS, 128), "sums": tall}
        else:
            outs |= {"residual": field, "search": field, "scalars": array(8, 128)}
            if not last:
                outs |= {
                    "halo": array(H_ROWS, 128), "sums": tall,
                    "search_halo": array(H_ROWS, 128), "search_sums": tall,
                }
        outs["message"] = array(8 if last else XY_ROWS, 128)
        if not last:
            outs["partial"] = field
        results = call(
            functools.partial(step_kernel, iteration, slabs, bricks),
            f"step_{iteration}",
            list(outs.values()),
            operands,
            scalar_operands=1,
        )
        state |= dict(zip(outs, results))
        if first:
            state["scalars"] = jnp.zeros((8, 128), F32)
        mapped, message, partial = state["mapped"], state["message"], state.get("partial")
        residual = state.get("residual", residual)
        directions.append(state["smoothed"])
    tiles = gather_slabs(gather_bricks(message).reshape(bricks * 8, 128))
    brick_pair = array(2, BS, BS * BS)
    solution_field, residual = call(
        functools.partial(finish_kernel, slabs * bricks),
        "finish",
        [brick_pair, brick_pair],
        [tiles, state["scalars"], residual, mapped, state["search"]] + directions,
    )
    return solution_field[None, None], residual[None, None]


def solution(mesh):
    return jax.shard_map(
        on_device,
        mesh=mesh,
        in_specs=(
            P("grp", "brick", None, None, None),
            P("grp", "brick", None, None, None),
            P("grp", "brick", None, None, None, None),
            P(),
            P(),
        ),
        out_specs=(P("grp", "brick", None, None, None), P("grp", "brick", None, None, None)),
        check_vma=False,
    )
```

```python
import functools

import jax
import jax.numpy as jnp
from jax import lax
from jax.experimental import pallas as pl
from jax.experimental.pallas import tpu as pltpu
from jax.sharding import PartitionSpec as P

BS = 32
CHUNKS = 16
OMEGA = 0.6
ITERS = 3
F32 = jnp.float32
FIELD = (CHUNKS, BS, 128)

XY_X1, XY_XP, XY_Y, XY_S = 0, 16, 32, 64
XY_ROWS = 72
XY_XD, XY_YC, XY_K = 72, 88, 120
XY_ROWS_FIRST = 128
Z_Y1, Z_Q, Z_Y, Z_X, Z_T = 0, 32, 64, 96, 104
Z_ROWS = 112
Z_D = 112
Z_ROWS_FIRST = 144
H_X1, H_XP, H_Y, H_Z1, H_ZQ, H_YZ, H_R = 0, 16, 32, 64, 96, 128, 160
H_ROWS = 168
C_XD, C_YC, C_ZD, C_K = 0, 16, 48, 80
C_ROWS = 88
E_XP, E_XM, E_YP, E_YM = 0, 16, 32, 64
E_ROWS = 96


def roll(block, shift):
    return pltpu.roll(block, shift % 128, axis=1)


def roll_row(row, shift):
    return pltpu.roll(jnp.broadcast_to(row, (8, 128)), shift % 128, axis=1)[0:1]


def lanes(rows=BS):
    return lax.broadcasted_iota(jnp.int32, (rows, 128), 1)


def rows_of(height=BS):
    return lax.broadcasted_iota(jnp.int32, (height, 128), 0)


def pack(chunks):
    height = chunks[0].shape[0]
    pair = (lanes(height) % BS) // 2
    total = jnp.zeros((height, 128), F32)
    for c in range(CHUNKS):
        moved = roll(chunks[c], 2 * c - 31) if height > 1 else roll_row(chunks[c], 2 * c - 31)
        total = jnp.where(pair == c, moved, total)
    return total


def stencil(field, effective, diagonal, x_halo, y_low, y_high, z_halo):
    lane = lanes()
    height = rows_of()
    depth = lane % BS
    zero = jnp.zeros((BS, 128), F32)
    back = [roll(f, -32) for f in field]
    forth = [roll(f, 32) for f in field]
    out = []
    for c in range(CHUNKS):
        f = field[c]
        x_row = zero if x_halo is None else x_halo[c : c + 1]
        total = diagonal(c) * f
        total -= effective(0, c) * jnp.where(height == BS - 1, x_row, pltpu.roll(f, BS - 1, axis=0))
        total -= effective(1, c) * jnp.where(height == 0, x_row, pltpu.roll(f, 1, axis=0))
        following = back[c + 1] if c < CHUNKS - 1 else (zero if y_high is None else y_high)
        previous = forth[c - 1] if c > 0 else (zero if y_low is None else y_low)
        total -= effective(2, c) * jnp.where(lane < 96, back[c], following)
        total -= effective(3, c) * jnp.where(lane >= 32, forth[c], previous)
        ends = zero if z_halo is None else roll(z_halo, 31 - 2 * c)
        total -= effective(4, c) * jnp.where(depth == BS - 1, ends, roll(f, -1))
        total -= effective(5, c) * jnp.where(depth == 0, ends, roll(f, 1))
        out.append(total)
    return out


def total_of(blocks):
    acc = blocks[0]
    for block in blocks[1:]:
        acc = acc + block
    return jnp.sum(jnp.sum(acc, axis=0, keepdims=True), axis=1, keepdims=True)


def facing(block, row):
    return jnp.where(row == 0, block[BS - 1 : BS], block[0:1])


def side_blocks(low_first, high_first, low_second, high_second):
    group = lanes() // 32
    return jnp.where(
        group == 0,
        low_first,
        jnp.where(
            group == 1,
            roll(high_first, 64),
            jnp.where(group == 2, roll(low_second, 64), high_second),
        ),
    )


def write_xy(xy_ref, row, y1, partial):
    for c in range(CHUNKS):
        xy_ref[XY_X1 + c : XY_X1 + c + 1] = facing(y1[c], row)
        xy_ref[XY_XP + c : XY_XP + c + 1] = facing(partial[c], row)
    last = CHUNKS - 1
    xy_ref[XY_Y : XY_Y + BS] = side_blocks(y1[0], y1[last], partial[0], partial[last])


def write_scalars(ref, start, values):
    for i, value in enumerate(values):
        ref[start + i : start + i + 1] = jnp.broadcast_to(value, (1, 128))
    for i in range(len(values), 8):
        ref[start + i : start + i + 1] = jnp.zeros((1, 128), F32)


def locate(bricks, place_ref, assignment_ref):
    across = bricks // 2
    place = place_ref[0]
    slab = place // bricks
    patch = assignment_ref[place % bricks]
    row = patch // across
    column = patch % across
    return slab, patch, row, column


def setup_kernel(
    slabs, bricks, place_ref, assignment_ref, occupancy_ref, source_ref, uptake_ref, conductance_ref,
    info_ref, effective_ref, diagonal_ref, relax_ref, residual_ref, partial_ref, edge_ref, xy_ref,
):
    across = bricks // 2
    slab, patch, row, column = locate(bricks, place_ref, assignment_ref)

    def holder(row_target, column_target):
        inside = (column_target >= 0) & (column_target < across)
        wanted = jnp.where(inside, row_target * across + column_target, patch)
        found = jnp.int32(0)
        for b in range(bricks):
            found = jnp.where(assignment_ref[b] == wanted, b, found)
        return found

    info_ref[0] = row
    info_ref[1] = slab
    info_ref[2] = holder(row, column)
    info_ref[3] = holder(1 - row, column)
    info_ref[4] = holder(row, column - 1)
    info_ref[5] = holder(row, column + 1)
    info_ref[6] = holder(1 - row, column - 1)
    info_ref[7] = holder(1 - row, column + 1)

    breadth = 2 * across

    def live_at(g, x, y):
        inside = (g >= 0) & (g < slabs) & (x >= 0) & (x < 2) & (y >= 0) & (y < breadth)
        index = (jnp.clip(g, 0, slabs - 1) * 2 + jnp.clip(x, 0, 1)) * breadth + jnp.clip(y, 0, breadth - 1)
        return jnp.where(inside, occupancy_ref[index], 0).astype(F32)

    lane = lanes()
    height = rows_of()
    depth = lane % BS
    absorbed = []
    low_ends = []
    high_ends = []
    first_y = None
    second_y = None
    y1 = []
    for s in range(2):
        y = column * 2 + s
        here = live_at(slab, row, y)
        around = [
            here * live_at(slab, row + 1, y),
            here * live_at(slab, row - 1, y),
            here * live_at(slab, row, y + 1),
            here * live_at(slab, row, y - 1),
            here * live_at(slab + 1, row, y),
            here * live_at(slab - 1, row, y),
        ]
        borders = [height == BS - 1, height == 0, lane >= 96, lane < 32, depth == BS - 1, depth == 0]
        for k in range(8):
            c = 8 * s + k
            part = pl.ds(128 * k, 128)
            taken = uptake_ref[s, :, part]
            absorbed.append(taken)
            diagonal = taken
            for d in range(6):
                bond = conductance_ref[d, s, :, part]
                if (d == 2 and k < 7) or (d == 3 and k > 0):
                    value = bond * here
                else:
                    value = bond * jnp.where(borders[d], around[d], here)
                effective_ref[d, c] = value
                diagonal = diagonal + value
                if d == 2 and c == 7:
                    first_y = jnp.where(borders[d], value, 0.0)
                if d == 3 and c == 8:
                    second_y = jnp.where(borders[d], value, 0.0)
                if d == 4:
                    high_ends.append(jnp.where(borders[d], value, 0.0))
                if d == 5:
                    low_ends.append(jnp.where(borders[d], value, 0.0))
            relax = OMEGA / diagonal
            diagonal_ref[c] = diagonal
            relax_ref[c] = relax
            forcing = source_ref[s, :, part] * here
            residual_ref[c] = forcing
            y1.append(relax * forcing)

    outcome = stencil(
        y1, lambda d, c: effective_ref[d, c], lambda c: diagonal_ref[c], None, None, None, None
    )
    partial = []
    for c in range(CHUNKS):
        value = y1[c] + relax_ref[c] * (residual_ref[c] - outcome[c])
        partial_ref[c] = value
        partial.append(value)
    write_xy(xy_ref, row, y1, partial)

    first_coupling = total_of([first_y])
    high_sums = [total_of(high_ends[8 * s : 8 * s + 8]) for s in range(2)]
    low_sums = [total_of(low_ends[8 * s : 8 * s + 8]) for s in range(2)]
    taken_sums = [total_of(absorbed[8 * s : 8 * s + 8]) for s in range(2)]
    residual_sums = [total_of([residual_ref[8 * s + k] for k in range(8)]) for s in range(2)]
    write_scalars(
        xy_ref,
        XY_S,
        [
            residual_sums[0],
            residual_sums[1],
            taken_sums[0] + first_coupling + high_sums[0] + low_sums[0],
            taken_sums[1] + total_of([second_y]) + high_sums[1] + low_sums[1],
            first_coupling,
            high_sums[0],
            high_sums[1],
        ],
    )

    last = CHUNKS - 1
    z_ends = [relax_ref[c] * (high_ends[c] + low_ends[c]) for c in range(CHUNKS)]
    for c in range(CHUNKS):
        xy_ref[XY_XD + c : XY_XD + c + 1] = facing(relax_ref[c], row)
        edge_ref[E_XP + c : E_XP + c + 1] = (relax_ref[c] * effective_ref[0, c])[BS - 1 : BS]
        edge_ref[E_XM + c : E_XM + c + 1] = (relax_ref[c] * effective_ref[1, c])[0:1]
    high_y = jnp.where(lane >= 96, relax_ref[last] * effective_ref[2, last], 0.0)
    low_y = jnp.where(lane < 32, relax_ref[0] * effective_ref[3, 0], 0.0)
    edge_ref[E_YP : E_YP + BS] = high_y
    edge_ref[E_YM : E_YM + BS] = low_y
    xy_ref[XY_YC : XY_YC + BS] = side_blocks(relax_ref[0], relax_ref[last], z_ends[0], z_ends[last])
    xy_ref[XY_K : XY_K + 1] = facing(low_y + high_y, row)
    xy_ref[XY_K + 1 : XY_K + 2] = pack([facing(z, row) for z in z_ends])
    toward_low = facing_terms(relax_ref, effective_ref, 0)
    toward_high = facing_terms(relax_ref, effective_ref, last)
    lane_row = lanes(1)
    xy_ref[XY_K + 2 : XY_K + 3] = jnp.where(lane_row < 32, toward_low, roll_row(toward_high, 64))
    xy_ref[XY_K + 3 : XY_K + 8] = jnp.zeros((5, 128), F32)


def facing_terms(relax_ref, effective_ref, c):
    upper = (relax_ref[c] * effective_ref[0, c])[BS - 1 : BS]
    lower = (relax_ref[c] * effective_ref[1, c])[0:1]
    return upper + lower


def swap_sides(from_low, from_high):
    rows = from_low.shape[0]
    if rows == 1:
        low, high = roll_row(from_low, -32), roll_row(from_high, 32)
    else:
        low, high = roll(from_low, -32), roll(from_high, 32)
    return jnp.where((lanes(rows) // 32) % 2 == 0, low, high)


def middle_kernel(
    first, bricks, info_ref, xy_ref, field_ref, relax_ref, partial_ref, edge_ref, z_ref, tile_ref
):
    lane = lanes()
    height = rows_of()
    x_holder = info_ref[3]
    x_halo = xy_ref[x_holder, XY_X1 : XY_X1 + CHUNKS]
    sides = swap_sides(
        xy_ref[info_ref[4], XY_Y : XY_Y + BS], xy_ref[info_ref[5], XY_Y : XY_Y + BS]
    )
    upper = edge_ref[E_XP : E_XP + CHUNKS] * x_halo
    lower = edge_ref[E_XM : E_XM + CHUNKS] * x_halo
    y1 = []
    whole = []
    for c in range(CHUNKS):
        y1.append(relax_ref[c] * field_ref[c])
        value = partial_ref[c]
        value = value + jnp.where(height == BS - 1, upper[c : c + 1], 0.0)
        value = value + jnp.where(height == 0, lower[c : c + 1], 0.0)
        if c == 0:
            value = value + jnp.where(lane < 32, edge_ref[E_YM : E_YM + BS] * sides, 0.0)
        if c == CHUNKS - 1:
            value = value + jnp.where(
                lane >= 96, edge_ref[E_YP : E_YP + BS] * roll(sides, 64), 0.0
            )
        whole.append(value)
    z_ref[Z_Y1 : Z_Y1 + BS] = pack(y1)
    z_ref[Z_Q : Z_Q + BS] = pack(whole)
    z_ref[Z_Y : Z_Y + BS] = sides
    x_ends = pack([x_halo[c : c + 1] for c in range(CHUNKS)])
    z_ref[Z_X : Z_X + 8] = jnp.broadcast_to(x_ends, (8, 128))
    if first:
        z_ref[Z_D : Z_D + BS] = pack([relax_ref[c] for c in range(CHUNKS)])
    lane_tile = lanes(8)
    mixed = jnp.zeros((8, 128), F32)
    for q in range(4):
        mixed = jnp.where(lane_tile == q, xy_ref[info_ref[2 + q], XY_S : XY_S + 8], mixed)
    if not first:
        summed = xy_ref[0, XY_S : XY_S + 8]
        for b in range(1, bricks):
            summed = summed + xy_ref[b, XY_S : XY_S + 8]
        mixed = jnp.where(rows_of(8) < 2, mixed, summed)
    z_ref[Z_T : Z_T + 8] = mixed
    tile_ref[...] = mixed


def search_scalars(tiles, scalars, iteration):
    energy = tiles[2:3, 0:1]
    curvature = tiles[3:4, 0:1]
    if iteration == 0:
        return energy, curvature, energy / curvature, None
    growth = energy / scalars[0:1, 0:1]
    curvature = curvature + growth * (2.0 * tiles[4:5, 0:1] + growth * scalars[1:2, 0:1])
    return energy, curvature, energy / curvature, growth


def sum_tiles(ref, count):
    total = ref[0:8]
    for g in range(1, count):
        total = total + ref[8 * g : 8 * g + 8]
    return total


def step_kernel(iteration, slabs, bricks, *refs):
    first = iteration == 0
    last = iteration == ITERS - 1
    refs = list(refs)
    take = lambda count: [refs.pop(0) for _ in range(count)]
    info_ref, xy_ref, above_ref, below_ref = take(4)
    shift_refs = take(slabs - 2)
    effective_ref, diagonal_ref, relax_ref, residual_ref = take(4)
    if not first:
        mapped_ref, halo_in, constant_ref, factor_ref, sums_in, scalars_in = take(6)
    if iteration > 1:
        search_in, search_halo_in, search_sums_in = take(3)
    smoothed_ref, mapped_out = take(2)
    if first:
        constant_ref, factor_ref, halo_ref, sums_ref = take(4)
    else:
        residual_out, search_ref, scalars_ref = take(3)
        if not last:
            halo_ref, sums_ref, search_halo_ref, search_sums_ref = take(4)
    xy_out = take(1)[0]
    if not last:
        partial_ref = take(1)[0]
    tiles_ref = take(1)[0]

    row = info_ref[0]
    slab = info_ref[1]
    for d in range(slabs):
        if d == 1:
            tile = below_ref[Z_T : Z_T + 8]
        elif d == slabs - 1:
            tile = above_ref[Z_T : Z_T + 8]
        else:
            tile = shift_refs[max(d - 1, 0)][...]
        start = pl.multiple_of(8 * lax.rem(slab - d + slabs, slabs), 8)
        tiles_ref[pl.ds(start, 8)] = tile
    lane = lanes()
    height = rows_of()
    depth = lane % BS
    lane_row = lanes(1)
    even = lane % 2 == 0
    even_row = lane_row % 2 == 0
    low_holder, high_holder = info_ref[4], info_ref[5]
    low_corner, high_corner = info_ref[6], info_ref[7]
    x_holder = info_ref[3]

    def merge(start):
        up = roll(above_ref[start : start + BS], 31)
        down = roll(below_ref[start : start + BS], -31)
        return jnp.where(even, up, down)

    x_sides = xy_ref[x_holder, XY_X1 : XY_X1 + 2 * CHUNKS]
    y_sides = swap_sides(
        xy_ref[low_holder, XY_Y : XY_Y + BS], xy_ref[high_holder, XY_Y : XY_Y + BS]
    )
    z_first = merge(Z_Y1)
    z_second = merge(Z_Q)
    y_up = roll(above_ref[Z_Y : Z_Y + BS], 31)
    y_down = roll(below_ref[Z_Y : Z_Y + BS], -31)
    y_ends = jnp.where(depth == BS - 1, y_up, jnp.where(depth == 0, y_down, 0.0))
    x_ends = jnp.where(
        even_row,
        roll_row(above_ref[Z_X : Z_X + 1], 31),
        roll_row(below_ref[Z_X : Z_X + 1], -31),
    )
    corner_y = jnp.where(
        lane_row < 32,
        roll_row(xy_ref[low_corner, XY_X1 + CHUNKS - 1 : XY_X1 + CHUNKS], 32),
        roll_row(xy_ref[high_corner, XY_X1 : XY_X1 + 1], -32),
    )
    low_row = jnp.where(
        row == 0,
        xy_ref[low_corner, XY_Y : XY_Y + 1],
        xy_ref[low_corner, XY_Y + BS - 1 : XY_Y + BS],
    )
    high_row = jnp.where(
        row == 0,
        xy_ref[high_corner, XY_Y : XY_Y + 1],
        xy_ref[high_corner, XY_Y + BS - 1 : XY_Y + BS],
    )
    corner_x = swap_sides(low_row, high_row)
    ends = jnp.concatenate([x_ends, corner_y, corner_x, jnp.zeros((5, 128), F32)], axis=0)
    halo = [x_sides, y_sides, z_first, z_second, y_ends, ends]
    starts = [H_X1, H_Y, H_Z1, H_ZQ, H_YZ, H_R]
    sums = tiles_ref[...]

    if first:
        residual = [residual_ref[c] for c in range(CHUNKS)]
        constant_ref[C_XD : C_XD + CHUNKS] = xy_ref[x_holder, XY_XD : XY_XD + CHUNKS]
        constant_ref[C_YC : C_YC + BS] = swap_sides(
            xy_ref[low_holder, XY_YC : XY_YC + BS], xy_ref[high_holder, XY_YC : XY_YC + BS]
        )
        constant_ref[C_ZD : C_ZD + BS] = merge(Z_D)
        constant_ref[C_K : C_K + 8] = jnp.concatenate(
            [
                xy_ref[x_holder, XY_K : XY_K + 2],
                swap_sides(
                    xy_ref[low_holder, XY_K + 2 : XY_K + 3],
                    xy_ref[high_holder, XY_K + 2 : XY_K + 3],
                ),
                jnp.zeros((5, 128), F32),
            ],
            axis=0,
        )
        for g in range(slabs):
            tile = sums[8 * g : 8 * g + 8]
            a, b, off = tile[2:3], tile[3:4], tile[4:5]
            t0, t1 = tile[5:6], tile[6:7]
            if g > 0:
                a = a - u0 * u0 * i00
                b = b - u1 * u1 * i11
                off = off + u0 * u1 * i01
            a = jnp.where(lane_row < 4, a, 1.0)
            b = jnp.where(lane_row < 4, b, 1.0)
            scale = 1.0 / (a * b - off * off)
            i00, i01, i11 = b * scale, off * scale, a * scale
            u0, u1 = t0, t1
            factor_ref[8 * g : 8 * g + 8] = jnp.concatenate(
                [i00, i01, i11, t0, t1, jnp.zeros((3, 128), F32)], axis=0
            )
    else:
        scalars = None if iteration == 1 else scalars_in[...]
        energy, curvature, step, growth = search_scalars(
            sum_tiles(tiles_ref, slabs), scalars, iteration - 1
        )
        step_row = jnp.broadcast_to(step, (1, 128))
        residual = []
        for c in range(CHUNKS):
            mapped = mapped_ref[c]
            if growth is not None:
                mapped = mapped + growth * search_in[c]
            search_ref[c] = mapped
            value = residual_ref[c] - step * mapped
            residual_out[c] = value
            residual.append(value)
        old_halo = halo
        halo = []
        for start, block in zip(starts, old_halo):
            span = slice(start, start + block.shape[0])
            if growth is not None:
                block = block + growth * search_halo_in[span]
            if not last:
                search_halo_ref[span] = block
            halo.append(halo_in[span] - step * block)
        if growth is not None:
            sums = sums + growth * search_sums_in[...]
        if not last:
            search_sums_ref[...] = sums
        sums = sums_in[...] - step * sums
        kept = [energy, curvature, step]
        if growth is not None:
            kept = [energy, curvature, scalars[2:3, 0:1], step, growth]
        write_scalars(scalars_ref, 0, kept)

    if not last:
        for start, block in zip(starts, halo):
            halo_ref[start : start + block.shape[0]] = block
        sums_ref[...] = sums
    x_sides, y_sides, z_first, z_second, y_ends, ends = halo

    forward = []
    for g in range(slabs):
        t0, t1 = sums[8 * g : 8 * g + 1], sums[8 * g + 1 : 8 * g + 2]
        if g > 0:
            t0 = t0 + w0 * v0
            t1 = t1 + w1 * v1
        factor = factor_ref[8 * g : 8 * g + 8]
        v0 = factor[0:1] * t0 + factor[1:2] * t1
        v1 = factor[1:2] * t0 + factor[2:3] * t1
        w0, w1 = factor[3:4], factor[4:5]
        forward.append((v0, v1))
    blank = jnp.zeros((1, 128), F32)
    below0, below1, here0, here1, above0, above1 = [blank] * 6
    for g in reversed(range(slabs)):
        v0, v1 = forward[g]
        if g < slabs - 1:
            factor = factor_ref[8 * g : 8 * g + 8]
            s0, s1 = factor[3:4] * n0, factor[4:5] * n1
            v0 = v0 + factor[0:1] * s0 + factor[1:2] * s1
            v1 = v1 + factor[1:2] * s0 + factor[2:3] * s1
        n0, n1 = v0, v1
        here0 = jnp.where(slab == g, n0, here0)
        here1 = jnp.where(slab == g, n1, here1)
        above0 = jnp.where(slab + 1 == g, n0, above0)
        above1 = jnp.where(slab + 1 == g, n1, above1)
        below0 = jnp.where(slab - 1 == g, n0, below0)
        below1 = jnp.where(slab - 1 == g, n1, below1)
    own = [here0[:, 0:1], here1[:, 0:1]]

    effective = lambda d, c: effective_ref[d, c]
    diagonal = lambda c: diagonal_ref[c]
    end = CHUNKS - 1

    y1 = [relax_ref[c] * residual[c] for c in range(CHUNKS)]
    outcome = stencil(
        y1, effective, diagonal, x_sides[:CHUNKS], y_sides, roll(y_sides, 64), z_first
    )
    smoothed = []
    for c in range(CHUNKS):
        value = y1[c] + relax_ref[c] * (residual[c] - outcome[c]) + own[c // 8]
        smoothed_ref[c] = value
        smoothed.append(value)
    keys = constant_ref[C_K : C_K + 8]
    crossing = jnp.concatenate(
        [
            effective(0, c)[BS - 1 : BS] * y1[c][BS - 1 : BS] + effective(1, c)[0:1] * y1[c][0:1]
            for c in range(CHUNKS)
        ],
        axis=0,
    )
    end_row = keys[1:2] * ends[0:1]
    corner_row = keys[0:1] * ends[1:2]
    depth_row = lane_row % BS
    additions = []
    for c in range(CHUNKS):
        value = jnp.where(
            (depth_row == BS - 1) | (depth_row == 0), roll_row(end_row, 31 - 2 * c), 0.0
        )
        if c == 0:
            value = value + jnp.where(lane_row < 32, corner_row, 0.0)
        if c == end:
            value = value + jnp.where(lane_row >= 96, corner_row, 0.0)
        value = value + (here0 if c < 8 else here1)[:, 1:2]
        additions.append(value)
    x_next = (
        x_sides[CHUNKS:]
        + constant_ref[C_XD : C_XD + CHUNKS] * crossing
        + jnp.concatenate(additions, axis=0)
    )
    y_constant = constant_ref[C_YC : C_YC + BS]
    y_crossing = jnp.where(
        lane < 32, effective(3, 0) * y1[0], roll(effective(2, end) * y1[end], 64)
    )
    x_side_row = jnp.where(row == 0, BS - 1, 0)
    y_next = (
        roll(y_sides, 64)
        + y_constant * y_crossing
        + roll(y_constant, 64) * y_ends
        + jnp.where(height == x_side_row, keys[2:3] * ends[2:3], 0.0)
        + jnp.where(lane < 32, here1[:, 2:3], here0[:, 3:4])
    )
    z_crossing = pack(
        [
            jnp.where(depth == BS - 1, effective(4, c), effective(5, c)) * y1[c]
            for c in range(CHUNKS)
        ]
    )
    z_coarse = jnp.where(
        even_row,
        jnp.where(depth_row < 16, above0[:, 0:1], above1[:, 0:1]),
        jnp.where(depth_row < 16, below0[:, 0:1], below1[:, 0:1]),
    )
    z_next = z_second + constant_ref[C_ZD : C_ZD + BS] * z_crossing + z_coarse
    mapped = stencil(smoothed, effective, diagonal, x_next, y_next, roll(y_next, 64), z_next)
    for c in range(CHUNKS):
        mapped_out[c] = mapped[c]

    values = [
        total_of(mapped[:8]),
        total_of(mapped[8:]),
        total_of([residual[c] * smoothed[c] for c in range(CHUNKS)]),
        total_of([mapped[c] * smoothed[c] for c in range(CHUNKS)]),
    ]
    if not first:
        values.append(total_of([search_ref[c] * smoothed[c] for c in range(CHUNKS)]))
    if last:
        write_scalars(xy_out, 0, values)
        return
    write_scalars(xy_out, XY_S, values)
    y1 = [relax_ref[c] * mapped[c] for c in range(CHUNKS)]
    outcome = stencil(y1, effective, diagonal, None, None, None, None)
    partial = []
    for c in range(CHUNKS):
        value = y1[c] + relax_ref[c] * (mapped[c] - outcome[c])
        partial_ref[c] = value
        partial.append(value)
    write_xy(xy_out, row, y1, partial)


def finish_kernel(slabs, bricks, *refs):
    tile_refs = refs[:slabs]
    scalars_ref, residual_ref, mapped_ref, search_ref, first_ref, second_ref, third_ref = refs[slabs:-2]
    solution_ref, residual_out = refs[-2:]
    scalars = scalars_ref[...]
    tiles = sum_tiles(tile_refs[0], bricks)
    for ref in tile_refs[1:]:
        tiles = tiles + sum_tiles(ref, bricks)
    _, _, step, growth = search_scalars(tiles, scalars, ITERS - 1)
    first_step, second_step, second_growth = scalars[2:3, 0:1], scalars[3:4, 0:1], scalars[4:5, 0:1]
    third_weight = step
    second_weight = second_step + growth * step
    first_weight = first_step + second_growth * second_weight
    for c in range(CHUNKS):
        s, part = c // 8, pl.ds(128 * (c % 8), 128)
        solution_ref[s, :, part] = (
            first_weight * first_ref[c] + second_weight * second_ref[c] + third_weight * third_ref[c]
        )
        residual_out[s, :, part] = residual_ref[c] - step * (mapped_ref[c] + growth * search_ref[c])


def call(kernel, name, outs, operands, scalar_operands=0, scalar_outs=0, scratch=()):
    vmem = pl.BlockSpec(memory_space=pltpu.VMEM)
    smem = pl.BlockSpec(memory_space=pltpu.SMEM)
    return pl.pallas_call(
        kernel,
        out_shape=tuple(outs),
        in_specs=[smem] * scalar_operands + [vmem] * (len(operands) - scalar_operands),
        out_specs=tuple([smem] * scalar_outs + [vmem] * (len(outs) - scalar_outs)),
        scratch_shapes=list(scratch),
        compiler_params=pltpu.CompilerParams(vmem_limit_bytes=40 * 1024 * 1024),
        name=name,
    )(*operands)


def array(*shape):
    return jax.ShapeDtypeStruct(shape, F32)


def gather_bricks(message):
    return lax.all_gather(message, "brick", axis=0, tiled=False)


def shifted(block, shift):
    count = lax.axis_size("grp")
    return lax.ppermute(block, "grp", [(i, (i + shift) % count) for i in range(count)])


def on_device(source, uptake, conductance, occupancy, assignment):
    slabs = lax.axis_size("grp")
    bricks = lax.axis_size("brick")
    place = (lax.axis_index("grp") * bricks + lax.axis_index("brick")).astype(jnp.int32).reshape(1)
    field = array(*FIELD)
    info, effective, diagonal, relax, residual, partial, edge, message = call(
        functools.partial(setup_kernel, slabs, bricks),
        "setup",
        [
            jax.ShapeDtypeStruct((8,), jnp.int32), array(6, *FIELD), field, field, field, field,
            array(E_ROWS, 128), array(XY_ROWS_FIRST, 128),
        ],
        [place, assignment, occupancy.reshape(-1), source[0, 0], uptake[0, 0], conductance[0, 0]],
        scalar_operands=3,
        scalar_outs=1,
    )
    mapped = residual
    directions = []
    state = {}
    for iteration in range(ITERS):
        first, last = iteration == 0, iteration == ITERS - 1
        gathered = gather_bricks(message)
        z_message, tile = call(
            functools.partial(middle_kernel, first, bricks),
            f"middle_{iteration}",
            [array(Z_ROWS_FIRST if first else Z_ROWS, 128), array(8, 128)],
            [info, gathered, mapped, relax, partial, edge],
            scalar_operands=1,
        )
        above, below = shifted(z_message, -1), shifted(z_message, 1)
        tiles = [tile] + [shifted(tile, d) for d in range(2, slabs - 1)]
        operands = [info, gathered, above, below] + tiles + [effective, diagonal, relax, residual]
        tall = array(8 * slabs, 128)
        outs = {"smoothed": field, "mapped": field}
        if not first:
            operands += [mapped] + [state[k] for k in ("halo", "constant", "factor", "sums", "scalars")]
        if iteration > 1:
            operands += [state[k] for k in ("search", "search_halo", "search_sums")]
        if first:
            outs |= {"constant": array(C_ROWS, 128), "factor": tall, "halo": array(H_ROWS, 128), "sums": tall}
        else:
            outs |= {"residual": field, "search": field, "scalars": array(8, 128)}
            if not last:
                outs |= {
                    "halo": array(H_ROWS, 128), "sums": tall,
                    "search_halo": array(H_ROWS, 128), "search_sums": tall,
                }
        outs["message"] = array(8 if last else XY_ROWS, 128)
        if not last:
            outs["partial"] = field
        results = call(
            functools.partial(step_kernel, iteration, slabs, bricks),
            f"step_{iteration}",
            list(outs.values()),
            operands,
            scalar_operands=1,
            scratch=[pltpu.VMEM((8 * slabs, 128), F32)],
        )
        state |= dict(zip(outs, results))
        if first:
            state["scalars"] = jnp.zeros((8, 128), F32)
        mapped, message, partial = state["mapped"], state["message"], state.get("partial")
        residual = state.get("residual", residual)
        directions.append(state["smoothed"])
    summed = gather_bricks(message).reshape(bricks * 8, 128)
    tiles = [summed] + [shifted(summed, d) for d in range(1, slabs)]
    brick_pair = array(2, BS, BS * BS)
    solution_field, residual = call(
        functools.partial(finish_kernel, slabs, bricks),
        "finish",
        [brick_pair, brick_pair],
        tiles + [state["scalars"], residual, mapped, state["search"]] + directions,
    )
    return solution_field[None, None], residual[None, None]


def solution(mesh):
    return jax.shard_map(
        on_device,
        mesh=mesh,
        in_specs=(
            P("grp", "brick", None, None, None),
            P("grp", "brick", None, None, None),
            P("grp", "brick", None, None, None, None),
            P(),
            P(),
        ),
        out_specs=(P("grp", "brick", None, None, None), P("grp", "brick", None, None, None)),
        check_vma=False,
    )
```

```python
import functools

import jax
import jax.numpy as jnp
from jax import lax
from jax.experimental import pallas as pl
from jax.experimental.pallas import tpu as pltpu
from jax.sharding import PartitionSpec as P

BS = 32
CHUNKS = 16
OMEGA = 0.6
ITERS = 3
F32 = jnp.float32
FIELD = (CHUNKS, BS, 128)

XY_X1, XY_XP, XY_Y, XY_S = 0, 16, 32, 64
XY_ROWS = 72
XY_XD, XY_YC, XY_K = 72, 88, 120
XY_ROWS_FIRST = 128
Z_Y1, Z_Q, Z_Y, Z_X = 0, 32, 64, 96
Z_ROWS = 104
Z_D = 104
Z_ROWS_FIRST = 136
H_X1, H_XP, H_Y, H_Z1, H_ZQ, H_YZ, H_R = 0, 16, 32, 64, 96, 128, 160
H_ROWS = 168
C_XD, C_YC, C_ZD, C_K = 0, 16, 48, 80
C_ROWS = 88
E_XP, E_XM, E_YP, E_YM = 0, 16, 32, 64
E_ROWS = 96


def roll(block, shift):
    return pltpu.roll(block, shift % 128, axis=1)


def roll_row(row, shift):
    return pltpu.roll(jnp.broadcast_to(row, (8, 128)), shift % 128, axis=1)[0:1]


def lanes(rows=BS):
    return lax.broadcasted_iota(jnp.int32, (rows, 128), 1)


def rows_of(height=BS):
    return lax.broadcasted_iota(jnp.int32, (height, 128), 0)


def pack(chunks):
    height = chunks[0].shape[0]
    pair = (lanes(height) % BS) // 2
    total = jnp.zeros((height, 128), F32)
    for c in range(CHUNKS):
        moved = roll(chunks[c], 2 * c - 31) if height > 1 else roll_row(chunks[c], 2 * c - 31)
        total = jnp.where(pair == c, moved, total)
    return total


def stencil(field, effective, diagonal, x_halo, y_low, y_high, z_halo):
    lane = lanes()
    height = rows_of()
    depth = lane % BS
    zero = jnp.zeros((BS, 128), F32)
    back = [roll(f, -32) for f in field]
    forth = [roll(f, 32) for f in field]
    out = []
    for c in range(CHUNKS):
        f = field[c]
        x_row = zero if x_halo is None else x_halo[c : c + 1]
        total = diagonal(c) * f
        total -= effective(0, c) * jnp.where(height == BS - 1, x_row, pltpu.roll(f, BS - 1, axis=0))
        total -= effective(1, c) * jnp.where(height == 0, x_row, pltpu.roll(f, 1, axis=0))
        following = back[c + 1] if c < CHUNKS - 1 else (zero if y_high is None else y_high)
        previous = forth[c - 1] if c > 0 else (zero if y_low is None else y_low)
        total -= effective(2, c) * jnp.where(lane < 96, back[c], following)
        total -= effective(3, c) * jnp.where(lane >= 32, forth[c], previous)
        ends = zero if z_halo is None else roll(z_halo, 31 - 2 * c)
        total -= effective(4, c) * jnp.where(depth == BS - 1, ends, roll(f, -1))
        total -= effective(5, c) * jnp.where(depth == 0, ends, roll(f, 1))
        out.append(total)
    return out


def total_of(blocks):
    acc = blocks[0]
    for block in blocks[1:]:
        acc = acc + block
    return jnp.sum(jnp.sum(acc, axis=0, keepdims=True), axis=1, keepdims=True)


def facing(block, row):
    return jnp.where(row == 0, block[BS - 1 : BS], block[0:1])


def side_blocks(low_first, high_first, low_second, high_second):
    group = lanes() // 32
    return jnp.where(
        group == 0,
        low_first,
        jnp.where(
            group == 1,
            roll(high_first, 64),
            jnp.where(group == 2, roll(low_second, 64), high_second),
        ),
    )


def write_xy(xy_ref, row, y1, partial):
    for c in range(CHUNKS):
        xy_ref[XY_X1 + c : XY_X1 + c + 1] = facing(y1[c], row)
        xy_ref[XY_XP + c : XY_XP + c + 1] = facing(partial[c], row)
    last = CHUNKS - 1
    xy_ref[XY_Y : XY_Y + BS] = side_blocks(y1[0], y1[last], partial[0], partial[last])


def write_scalars(ref, start, values):
    for i, value in enumerate(values):
        ref[start + i : start + i + 1] = jnp.broadcast_to(value, (1, 128))
    for i in range(len(values), 8):
        ref[start + i : start + i + 1] = jnp.zeros((1, 128), F32)


def locate(bricks, place_ref, assignment_ref):
    across = bricks // 2
    place = place_ref[0]
    slab = place // bricks
    patch = assignment_ref[place % bricks]
    row = patch // across
    column = patch % across
    return slab, patch, row, column


def setup_kernel(
    slabs, bricks, place_ref, assignment_ref, occupancy_ref, source_ref, uptake_ref, conductance_ref,
    info_ref, effective_ref, diagonal_ref, relax_ref, residual_ref, partial_ref, edge_ref, xy_ref,
):
    across = bricks // 2
    slab, patch, row, column = locate(bricks, place_ref, assignment_ref)

    def holder(row_target, column_target):
        inside = (column_target >= 0) & (column_target < across)
        wanted = jnp.where(inside, row_target * across + column_target, patch)
        found = jnp.int32(0)
        for b in range(bricks):
            found = jnp.where(assignment_ref[b] == wanted, b, found)
        return found

    info_ref[0] = row
    info_ref[1] = slab
    info_ref[2] = holder(row, column)
    info_ref[3] = holder(1 - row, column)
    info_ref[4] = holder(row, column - 1)
    info_ref[5] = holder(row, column + 1)
    info_ref[6] = holder(1 - row, column - 1)
    info_ref[7] = holder(1 - row, column + 1)

    breadth = 2 * across

    def live_at(g, x, y):
        inside = (g >= 0) & (g < slabs) & (x >= 0) & (x < 2) & (y >= 0) & (y < breadth)
        index = (jnp.clip(g, 0, slabs - 1) * 2 + jnp.clip(x, 0, 1)) * breadth + jnp.clip(y, 0, breadth - 1)
        return jnp.where(inside, occupancy_ref[index], 0).astype(F32)

    lane = lanes()
    height = rows_of()
    depth = lane % BS
    absorbed = []
    low_ends = []
    high_ends = []
    first_y = None
    second_y = None
    y1 = []
    for s in range(2):
        y = column * 2 + s
        here = live_at(slab, row, y)
        around = [
            here * live_at(slab, row + 1, y),
            here * live_at(slab, row - 1, y),
            here * live_at(slab, row, y + 1),
            here * live_at(slab, row, y - 1),
            here * live_at(slab + 1, row, y),
            here * live_at(slab - 1, row, y),
        ]
        borders = [height == BS - 1, height == 0, lane >= 96, lane < 32, depth == BS - 1, depth == 0]
        for k in range(8):
            c = 8 * s + k
            part = pl.ds(128 * k, 128)
            taken = uptake_ref[s, :, part]
            absorbed.append(taken)
            diagonal = taken
            for d in range(6):
                bond = conductance_ref[d, s, :, part]
                if (d == 2 and k < 7) or (d == 3 and k > 0):
                    value = bond * here
                else:
                    value = bond * jnp.where(borders[d], around[d], here)
                effective_ref[d, c] = value
                diagonal = diagonal + value
                if d == 2 and c == 7:
                    first_y = jnp.where(borders[d], value, 0.0)
                if d == 3 and c == 8:
                    second_y = jnp.where(borders[d], value, 0.0)
                if d == 4:
                    high_ends.append(jnp.where(borders[d], value, 0.0))
                if d == 5:
                    low_ends.append(jnp.where(borders[d], value, 0.0))
            relax = OMEGA / diagonal
            diagonal_ref[c] = diagonal
            relax_ref[c] = relax
            forcing = source_ref[s, :, part] * here
            residual_ref[c] = forcing
            y1.append(relax * forcing)

    outcome = stencil(
        y1, lambda d, c: effective_ref[d, c], lambda c: diagonal_ref[c], None, None, None, None
    )
    partial = []
    for c in range(CHUNKS):
        value = y1[c] + relax_ref[c] * (residual_ref[c] - outcome[c])
        partial_ref[c] = value
        partial.append(value)
    write_xy(xy_ref, row, y1, partial)

    first_coupling = total_of([first_y])
    high_sums = [total_of(high_ends[8 * s : 8 * s + 8]) for s in range(2)]
    low_sums = [total_of(low_ends[8 * s : 8 * s + 8]) for s in range(2)]
    taken_sums = [total_of(absorbed[8 * s : 8 * s + 8]) for s in range(2)]
    residual_sums = [total_of([residual_ref[8 * s + k] for k in range(8)]) for s in range(2)]
    write_scalars(
        xy_ref,
        XY_S,
        [
            residual_sums[0],
            residual_sums[1],
            taken_sums[0] + first_coupling + high_sums[0] + low_sums[0],
            taken_sums[1] + total_of([second_y]) + high_sums[1] + low_sums[1],
            first_coupling,
            high_sums[0],
            high_sums[1],
        ],
    )

    last = CHUNKS - 1
    z_ends = [relax_ref[c] * (high_ends[c] + low_ends[c]) for c in range(CHUNKS)]
    for c in range(CHUNKS):
        xy_ref[XY_XD + c : XY_XD + c + 1] = facing(relax_ref[c], row)
        edge_ref[E_XP + c : E_XP + c + 1] = (relax_ref[c] * effective_ref[0, c])[BS - 1 : BS]
        edge_ref[E_XM + c : E_XM + c + 1] = (relax_ref[c] * effective_ref[1, c])[0:1]
    high_y = jnp.where(lane >= 96, relax_ref[last] * effective_ref[2, last], 0.0)
    low_y = jnp.where(lane < 32, relax_ref[0] * effective_ref[3, 0], 0.0)
    edge_ref[E_YP : E_YP + BS] = high_y
    edge_ref[E_YM : E_YM + BS] = low_y
    xy_ref[XY_YC : XY_YC + BS] = side_blocks(relax_ref[0], relax_ref[last], z_ends[0], z_ends[last])
    xy_ref[XY_K : XY_K + 1] = facing(low_y + high_y, row)
    xy_ref[XY_K + 1 : XY_K + 2] = pack([facing(z, row) for z in z_ends])
    toward_low = facing_terms(relax_ref, effective_ref, 0)
    toward_high = facing_terms(relax_ref, effective_ref, last)
    lane_row = lanes(1)
    xy_ref[XY_K + 2 : XY_K + 3] = jnp.where(lane_row < 32, toward_low, roll_row(toward_high, 64))
    xy_ref[XY_K + 3 : XY_K + 8] = jnp.zeros((5, 128), F32)


def facing_terms(relax_ref, effective_ref, c):
    upper = (relax_ref[c] * effective_ref[0, c])[BS - 1 : BS]
    lower = (relax_ref[c] * effective_ref[1, c])[0:1]
    return upper + lower


def swap_sides(from_low, from_high):
    rows = from_low.shape[0]
    if rows == 1:
        low, high = roll_row(from_low, -32), roll_row(from_high, 32)
    else:
        low, high = roll(from_low, -32), roll(from_high, 32)
    return jnp.where((lanes(rows) // 32) % 2 == 0, low, high)


def middle_kernel(
    first, bricks, info_ref, xy_ref, field_ref, relax_ref, partial_ref, edge_ref, z_ref, tile_ref
):
    lane = lanes()
    height = rows_of()
    x_holder = info_ref[3]
    x_halo = xy_ref[x_holder, XY_X1 : XY_X1 + CHUNKS]
    sides = swap_sides(
        xy_ref[info_ref[4], XY_Y : XY_Y + BS], xy_ref[info_ref[5], XY_Y : XY_Y + BS]
    )
    upper = edge_ref[E_XP : E_XP + CHUNKS] * x_halo
    lower = edge_ref[E_XM : E_XM + CHUNKS] * x_halo
    y1 = []
    whole = []
    for c in range(CHUNKS):
        y1.append(relax_ref[c] * field_ref[c])
        value = partial_ref[c]
        value = value + jnp.where(height == BS - 1, upper[c : c + 1], 0.0)
        value = value + jnp.where(height == 0, lower[c : c + 1], 0.0)
        if c == 0:
            value = value + jnp.where(lane < 32, edge_ref[E_YM : E_YM + BS] * sides, 0.0)
        if c == CHUNKS - 1:
            value = value + jnp.where(
                lane >= 96, edge_ref[E_YP : E_YP + BS] * roll(sides, 64), 0.0
            )
        whole.append(value)
    z_ref[Z_Y1 : Z_Y1 + BS] = pack(y1)
    z_ref[Z_Q : Z_Q + BS] = pack(whole)
    z_ref[Z_Y : Z_Y + BS] = sides
    x_ends = pack([x_halo[c : c + 1] for c in range(CHUNKS)])
    z_ref[Z_X : Z_X + 8] = jnp.broadcast_to(x_ends, (8, 128))
    if first:
        z_ref[Z_D : Z_D + BS] = pack([relax_ref[c] for c in range(CHUNKS)])
    lane_tile = lanes(8)
    mixed = jnp.zeros((8, 128), F32)
    for q in range(4):
        mixed = jnp.where(lane_tile == q, xy_ref[info_ref[2 + q], XY_S : XY_S + 8], mixed)
    if not first:
        summed = xy_ref[0, XY_S : XY_S + 8]
        for b in range(1, bricks):
            summed = summed + xy_ref[b, XY_S : XY_S + 8]
        mixed = jnp.where(rows_of(8) < 2, mixed, summed)
    for g in range(tile_ref.shape[0] // 8):
        tile_ref[8 * g : 8 * g + 8] = mixed


def search_scalars(tiles, scalars, iteration):
    energy = tiles[2:3, 0:1]
    curvature = tiles[3:4, 0:1]
    if iteration == 0:
        return energy, curvature, energy / curvature, None
    growth = energy / scalars[0:1, 0:1]
    curvature = curvature + growth * (2.0 * tiles[4:5, 0:1] + growth * scalars[1:2, 0:1])
    return energy, curvature, energy / curvature, growth


def sum_tiles(ref, count):
    total = ref[0:8]
    for g in range(1, count):
        total = total + ref[8 * g : 8 * g + 8]
    return total


def step_kernel(iteration, slabs, bricks, *refs):
    first = iteration == 0
    last = iteration == ITERS - 1
    refs = list(refs)
    take = lambda count: [refs.pop(0) for _ in range(count)]
    info_ref, xy_ref, above_ref, below_ref, tiles_ref = take(5)
    effective_ref, diagonal_ref, relax_ref, residual_ref = take(4)
    if not first:
        mapped_ref, halo_in, constant_ref, factor_ref, sums_in, scalars_in = take(6)
    if iteration > 1:
        search_in, search_halo_in, search_sums_in = take(3)
    smoothed_ref, mapped_out = take(2)
    if first:
        constant_ref, factor_ref, halo_ref, sums_ref = take(4)
    else:
        residual_out, search_ref, scalars_ref = take(3)
        if not last:
            halo_ref, sums_ref, search_halo_ref, search_sums_ref = take(4)
    xy_out = take(1)[0]
    if not last:
        partial_ref = take(1)[0]

    row = info_ref[0]
    slab = info_ref[1]
    lane = lanes()
    height = rows_of()
    depth = lane % BS
    lane_row = lanes(1)
    even = lane % 2 == 0
    even_row = lane_row % 2 == 0
    low_holder, high_holder = info_ref[4], info_ref[5]
    low_corner, high_corner = info_ref[6], info_ref[7]
    x_holder = info_ref[3]

    def merge(start):
        up = roll(above_ref[start : start + BS], 31)
        down = roll(below_ref[start : start + BS], -31)
        return jnp.where(even, up, down)

    x_sides = xy_ref[x_holder, XY_X1 : XY_X1 + 2 * CHUNKS]
    y_sides = swap_sides(
        xy_ref[low_holder, XY_Y : XY_Y + BS], xy_ref[high_holder, XY_Y : XY_Y + BS]
    )
    z_first = merge(Z_Y1)
    z_second = merge(Z_Q)
    y_up = roll(above_ref[Z_Y : Z_Y + BS], 31)
    y_down = roll(below_ref[Z_Y : Z_Y + BS], -31)
    y_ends = jnp.where(depth == BS - 1, y_up, jnp.where(depth == 0, y_down, 0.0))
    x_ends = jnp.where(
        even_row,
        roll_row(above_ref[Z_X : Z_X + 1], 31),
        roll_row(below_ref[Z_X : Z_X + 1], -31),
    )
    corner_y = jnp.where(
        lane_row < 32,
        roll_row(xy_ref[low_corner, XY_X1 + CHUNKS - 1 : XY_X1 + CHUNKS], 32),
        roll_row(xy_ref[high_corner, XY_X1 : XY_X1 + 1], -32),
    )
    low_row = jnp.where(
        row == 0,
        xy_ref[low_corner, XY_Y : XY_Y + 1],
        xy_ref[low_corner, XY_Y + BS - 1 : XY_Y + BS],
    )
    high_row = jnp.where(
        row == 0,
        xy_ref[high_corner, XY_Y : XY_Y + 1],
        xy_ref[high_corner, XY_Y + BS - 1 : XY_Y + BS],
    )
    corner_x = swap_sides(low_row, high_row)
    ends = jnp.concatenate([x_ends, corner_y, corner_x, jnp.zeros((5, 128), F32)], axis=0)
    halo = [x_sides, y_sides, z_first, z_second, y_ends, ends]
    starts = [H_X1, H_Y, H_Z1, H_ZQ, H_YZ, H_R]
    sums = tiles_ref[...]

    if first:
        residual = [residual_ref[c] for c in range(CHUNKS)]
        constant_ref[C_XD : C_XD + CHUNKS] = xy_ref[x_holder, XY_XD : XY_XD + CHUNKS]
        constant_ref[C_YC : C_YC + BS] = swap_sides(
            xy_ref[low_holder, XY_YC : XY_YC + BS], xy_ref[high_holder, XY_YC : XY_YC + BS]
        )
        constant_ref[C_ZD : C_ZD + BS] = merge(Z_D)
        constant_ref[C_K : C_K + 8] = jnp.concatenate(
            [
                xy_ref[x_holder, XY_K : XY_K + 2],
                swap_sides(
                    xy_ref[low_holder, XY_K + 2 : XY_K + 3],
                    xy_ref[high_holder, XY_K + 2 : XY_K + 3],
                ),
                jnp.zeros((5, 128), F32),
            ],
            axis=0,
        )
        for g in range(slabs):
            tile = sums[8 * g : 8 * g + 8]
            a, b, off = tile[2:3], tile[3:4], tile[4:5]
            t0, t1 = tile[5:6], tile[6:7]
            if g > 0:
                a = a - u0 * u0 * i00
                b = b - u1 * u1 * i11
                off = off + u0 * u1 * i01
            a = jnp.where(lane_row < 4, a, 1.0)
            b = jnp.where(lane_row < 4, b, 1.0)
            scale = 1.0 / (a * b - off * off)
            i00, i01, i11 = b * scale, off * scale, a * scale
            u0, u1 = t0, t1
            factor_ref[8 * g : 8 * g + 8] = jnp.concatenate(
                [i00, i01, i11, t0, t1, jnp.zeros((3, 128), F32)], axis=0
            )
    else:
        scalars = None if iteration == 1 else scalars_in[...]
        energy, curvature, step, growth = search_scalars(
            sum_tiles(tiles_ref, slabs), scalars, iteration - 1
        )
        step_row = jnp.broadcast_to(step, (1, 128))
        residual = []
        for c in range(CHUNKS):
            mapped = mapped_ref[c]
            if growth is not None:
                mapped = mapped + growth * search_in[c]
            search_ref[c] = mapped
            value = residual_ref[c] - step * mapped
            residual_out[c] = value
            residual.append(value)
        old_halo = halo
        halo = []
        for start, block in zip(starts, old_halo):
            span = slice(start, start + block.shape[0])
            if growth is not None:
                block = block + growth * search_halo_in[span]
            if not last:
                search_halo_ref[span] = block
            halo.append(halo_in[span] - step * block)
        if growth is not None:
            sums = sums + growth * search_sums_in[...]
        if not last:
            search_sums_ref[...] = sums
        sums = sums_in[...] - step * sums
        kept = [energy, curvature, step]
        if growth is not None:
            kept = [energy, curvature, scalars[2:3, 0:1], step, growth]
        write_scalars(scalars_ref, 0, kept)

    if not last:
        for start, block in zip(starts, halo):
            halo_ref[start : start + block.shape[0]] = block
        sums_ref[...] = sums
    x_sides, y_sides, z_first, z_second, y_ends, ends = halo

    forward = []
    for g in range(slabs):
        t0, t1 = sums[8 * g : 8 * g + 1], sums[8 * g + 1 : 8 * g + 2]
        if g > 0:
            t0 = t0 + w0 * v0
            t1 = t1 + w1 * v1
        factor = factor_ref[8 * g : 8 * g + 8]
        v0 = factor[0:1] * t0 + factor[1:2] * t1
        v1 = factor[1:2] * t0 + factor[2:3] * t1
        w0, w1 = factor[3:4], factor[4:5]
        forward.append((v0, v1))
    blank = jnp.zeros((1, 128), F32)
    below0, below1, here0, here1, above0, above1 = [blank] * 6
    for g in reversed(range(slabs)):
        v0, v1 = forward[g]
        if g < slabs - 1:
            factor = factor_ref[8 * g : 8 * g + 8]
            s0, s1 = factor[3:4] * n0, factor[4:5] * n1
            v0 = v0 + factor[0:1] * s0 + factor[1:2] * s1
            v1 = v1 + factor[1:2] * s0 + factor[2:3] * s1
        n0, n1 = v0, v1
        here0 = jnp.where(slab == g, n0, here0)
        here1 = jnp.where(slab == g, n1, here1)
        above0 = jnp.where(slab + 1 == g, n0, above0)
        above1 = jnp.where(slab + 1 == g, n1, above1)
        below0 = jnp.where(slab - 1 == g, n0, below0)
        below1 = jnp.where(slab - 1 == g, n1, below1)
    own = [here0[:, 0:1], here1[:, 0:1]]

    effective = lambda d, c: effective_ref[d, c]
    diagonal = lambda c: diagonal_ref[c]
    end = CHUNKS - 1

    y1 = [relax_ref[c] * residual[c] for c in range(CHUNKS)]
    outcome = stencil(
        y1, effective, diagonal, x_sides[:CHUNKS], y_sides, roll(y_sides, 64), z_first
    )
    smoothed = []
    for c in range(CHUNKS):
        value = y1[c] + relax_ref[c] * (residual[c] - outcome[c]) + own[c // 8]
        smoothed_ref[c] = value
        smoothed.append(value)
    keys = constant_ref[C_K : C_K + 8]
    crossing = jnp.concatenate(
        [
            effective(0, c)[BS - 1 : BS] * y1[c][BS - 1 : BS] + effective(1, c)[0:1] * y1[c][0:1]
            for c in range(CHUNKS)
        ],
        axis=0,
    )
    end_row = keys[1:2] * ends[0:1]
    corner_row = keys[0:1] * ends[1:2]
    depth_row = lane_row % BS
    additions = []
    for c in range(CHUNKS):
        value = jnp.where(
            (depth_row == BS - 1) | (depth_row == 0), roll_row(end_row, 31 - 2 * c), 0.0
        )
        if c == 0:
            value = value + jnp.where(lane_row < 32, corner_row, 0.0)
        if c == end:
            value = value + jnp.where(lane_row >= 96, corner_row, 0.0)
        value = value + (here0 if c < 8 else here1)[:, 1:2]
        additions.append(value)
    x_next = (
        x_sides[CHUNKS:]
        + constant_ref[C_XD : C_XD + CHUNKS] * crossing
        + jnp.concatenate(additions, axis=0)
    )
    y_constant = constant_ref[C_YC : C_YC + BS]
    y_crossing = jnp.where(
        lane < 32, effective(3, 0) * y1[0], roll(effective(2, end) * y1[end], 64)
    )
    x_side_row = jnp.where(row == 0, BS - 1, 0)
    y_next = (
        roll(y_sides, 64)
        + y_constant * y_crossing
        + roll(y_constant, 64) * y_ends
        + jnp.where(height == x_side_row, keys[2:3] * ends[2:3], 0.0)
        + jnp.where(lane < 32, here1[:, 2:3], here0[:, 3:4])
    )
    z_crossing = pack(
        [
            jnp.where(depth == BS - 1, effective(4, c), effective(5, c)) * y1[c]
            for c in range(CHUNKS)
        ]
    )
    z_coarse = jnp.where(
        even_row,
        jnp.where(depth_row < 16, above0[:, 0:1], above1[:, 0:1]),
        jnp.where(depth_row < 16, below0[:, 0:1], below1[:, 0:1]),
    )
    z_next = z_second + constant_ref[C_ZD : C_ZD + BS] * z_crossing + z_coarse
    mapped = stencil(smoothed, effective, diagonal, x_next, y_next, roll(y_next, 64), z_next)
    for c in range(CHUNKS):
        mapped_out[c] = mapped[c]

    values = [
        total_of(mapped[:8]),
        total_of(mapped[8:]),
        total_of([residual[c] * smoothed[c] for c in range(CHUNKS)]),
        total_of([mapped[c] * smoothed[c] for c in range(CHUNKS)]),
    ]
    if not first:
        values.append(total_of([search_ref[c] * smoothed[c] for c in range(CHUNKS)]))
    if last:
        write_scalars(xy_out, 0, values)
        tile = xy_out[0:8]
        for k in range(1, slabs * bricks):
            xy_out[8 * k : 8 * k + 8] = tile
        return
    write_scalars(xy_out, XY_S, values)
    y1 = [relax_ref[c] * mapped[c] for c in range(CHUNKS)]
    outcome = stencil(y1, effective, diagonal, None, None, None, None)
    partial = []
    for c in range(CHUNKS):
        value = y1[c] + relax_ref[c] * (mapped[c] - outcome[c])
        partial_ref[c] = value
        partial.append(value)
    write_xy(xy_out, row, y1, partial)


def finish_kernel(
    tiles_ref, scalars_ref, residual_ref, mapped_ref, search_ref, first_ref, second_ref, third_ref,
    solution_ref, residual_out,
):
    scalars = scalars_ref[...]
    tiles = sum_tiles(tiles_ref, tiles_ref.shape[0] // 8)
    _, _, step, growth = search_scalars(tiles, scalars, ITERS - 1)
    first_step, second_step, second_growth = scalars[2:3, 0:1], scalars[3:4, 0:1], scalars[4:5, 0:1]
    third_weight = step
    second_weight = second_step + growth * step
    first_weight = first_step + second_growth * second_weight
    for c in range(CHUNKS):
        s, part = c // 8, pl.ds(128 * (c % 8), 128)
        solution_ref[s, :, part] = (
            first_weight * first_ref[c] + second_weight * second_ref[c] + third_weight * third_ref[c]
        )
        residual_out[s, :, part] = residual_ref[c] - step * (mapped_ref[c] + growth * search_ref[c])


def call(kernel, name, outs, operands, scalar_operands=0, scalar_outs=0):
    vmem = pl.BlockSpec(memory_space=pltpu.VMEM)
    smem = pl.BlockSpec(memory_space=pltpu.SMEM)
    return pl.pallas_call(
        kernel,
        out_shape=tuple(outs),
        in_specs=[smem] * scalar_operands + [vmem] * (len(operands) - scalar_operands),
        out_specs=tuple([smem] * scalar_outs + [vmem] * (len(outs) - scalar_outs)),
        compiler_params=pltpu.CompilerParams(vmem_limit_bytes=40 * 1024 * 1024),
        name=name,
    )(*operands)


def array(*shape):
    return jax.ShapeDtypeStruct(shape, F32)


def gather_bricks(message):
    return lax.all_gather(message, "brick", axis=0, tiled=False)


def to_all(copies, axes):
    return lax.all_to_all(copies, axes, 0, 0, tiled=True)


def exchange_slabs(message):
    count = lax.axis_size("grp")
    upward = [(i, i + 1) for i in range(count - 1)]
    downward = [(i + 1, i) for i in range(count - 1)]
    return lax.ppermute(message, "grp", downward), lax.ppermute(message, "grp", upward)


def on_device(source, uptake, conductance, occupancy, assignment):
    slabs = lax.axis_size("grp")
    bricks = lax.axis_size("brick")
    place = (lax.axis_index("grp") * bricks + lax.axis_index("brick")).astype(jnp.int32).reshape(1)
    field = array(*FIELD)
    info, effective, diagonal, relax, residual, partial, edge, message = call(
        functools.partial(setup_kernel, slabs, bricks),
        "setup",
        [
            jax.ShapeDtypeStruct((8,), jnp.int32), array(6, *FIELD), field, field, field, field,
            array(E_ROWS, 128), array(XY_ROWS_FIRST, 128),
        ],
        [place, assignment, occupancy.reshape(-1), source[0, 0], uptake[0, 0], conductance[0, 0]],
        scalar_operands=3,
        scalar_outs=1,
    )
    mapped = residual
    directions = []
    state = {}
    for iteration in range(ITERS):
        first, last = iteration == 0, iteration == ITERS - 1
        gathered = gather_bricks(message)
        z_message, tile = call(
            functools.partial(middle_kernel, first, bricks),
            f"middle_{iteration}",
            [array(Z_ROWS_FIRST if first else Z_ROWS, 128), array(8 * slabs, 128)],
            [info, gathered, mapped, relax, partial, edge],
            scalar_operands=1,
        )
        above, below = exchange_slabs(z_message)
        tiles = to_all(tile, "grp")
        operands = [info, gathered, above, below, tiles, effective, diagonal, relax, residual]
        tall = array(8 * slabs, 128)
        outs = {"smoothed": field, "mapped": field}
        if not first:
            operands += [mapped] + [state[k] for k in ("halo", "constant", "factor", "sums", "scalars")]
        if iteration > 1:
            operands += [state[k] for k in ("search", "search_halo", "search_sums")]
        if first:
            outs |= {"constant": array(C_ROWS, 128), "factor": tall, "halo": array(H_ROWS, 128), "sums": tall}
        else:
            outs |= {"residual": field, "search": field, "scalars": array(8, 128)}
            if not last:
                outs |= {
                    "halo": array(H_ROWS, 128), "sums": tall,
                    "search_halo": array(H_ROWS, 128), "search_sums": tall,
                }
        outs["message"] = array(8 * slabs * bricks if last else XY_ROWS, 128)
        if not last:
            outs["partial"] = field
        results = call(
            functools.partial(step_kernel, iteration, slabs, bricks),
            f"step_{iteration}",
            list(outs.values()),
            operands,
            scalar_operands=1,
        )
        state |= dict(zip(outs, results))
        if first:
            state["scalars"] = jnp.zeros((8, 128), F32)
        mapped, message, partial = state["mapped"], state["message"], state.get("partial")
        residual = state.get("residual", residual)
        directions.append(state["smoothed"])
    tiles = to_all(message, ("brick", "grp"))
    brick_pair = array(2, BS, BS * BS)
    solution_field, residual = call(
        finish_kernel,
        "finish",
        [brick_pair, brick_pair],
        [tiles, state["scalars"], residual, mapped, state["search"]] + directions,
    )
    return solution_field[None, None], residual[None, None]


def solution(mesh):
    return jax.shard_map(
        on_device,
        mesh=mesh,
        in_specs=(
            P("grp", "brick", None, None, None),
            P("grp", "brick", None, None, None),
            P("grp", "brick", None, None, None, None),
            P(),
            P(),
        ),
        out_specs=(P("grp", "brick", None, None, None), P("grp", "brick", None, None, None)),
        check_vma=False,
    )
```

```python
import functools

import jax
import jax.numpy as jnp
from jax import lax
from jax.experimental import pallas as pl
from jax.experimental.pallas import tpu as pltpu
from jax.sharding import PartitionSpec as P

BS = 32
CHUNKS = 16
OMEGA = 0.6
ITERS = 3
F32 = jnp.float32
FIELD = (CHUNKS, BS, 128)

XY_X1, XY_XP, XY_Y = 0, 16, 32
XY_ROWS = 64
XY_XD, XY_YC, XY_K = 64, 80, 112
XY_ROWS_FIRST = 120
Z_Y1, Z_P = 0, 32
Z_ROWS = 64
Z_D, Z_K, Z_X = 64, 96, 128
Z_ROWS_FIRST = 136
T_N, T_Y = 16, 64
H_X1, H_Y, H_Z1, H_ZP, H_E, H_R = 0, 32, 64, 96, 128, 160
H_ROWS = 168
C_XD, C_YC, C_ZD, C_ZK, C_K = 0, 16, 48, 80, 112
C_ROWS = 120


def roll(block, shift):
    return pltpu.roll(block, shift % 128, axis=1)


def roll_row(row, shift):
    return pltpu.roll(jnp.broadcast_to(row, (8, 128)), shift % 128, axis=1)[0:1]


def lanes(rows=BS):
    return lax.broadcasted_iota(jnp.int32, (rows, 128), 1)


def rows_of(height=BS):
    return lax.broadcasted_iota(jnp.int32, (height, 128), 0)


def pack(chunks):
    height = chunks[0].shape[0]
    pair = (lanes(height) % BS) // 2
    total = jnp.zeros((height, 128), F32)
    for c in range(CHUNKS):
        moved = roll(chunks[c], 2 * c - 31) if height > 1 else roll_row(chunks[c], 2 * c - 31)
        total = jnp.where(pair == c, moved, total)
    return total


def stencil(field, effective, diagonal, x_halo, y_low, y_high, z_halo):
    lane = lanes()
    height = rows_of()
    depth = lane % BS
    zero = jnp.zeros((BS, 128), F32)
    back = [roll(f, -32) for f in field]
    forth = [roll(f, 32) for f in field]
    out = []
    for c in range(CHUNKS):
        f = field[c]
        x_row = zero if x_halo is None else x_halo[c : c + 1]
        total = diagonal(c) * f
        total -= effective(0, c) * jnp.where(height == BS - 1, x_row, pltpu.roll(f, BS - 1, axis=0))
        total -= effective(1, c) * jnp.where(height == 0, x_row, pltpu.roll(f, 1, axis=0))
        following = back[c + 1] if c < CHUNKS - 1 else (zero if y_high is None else y_high)
        previous = forth[c - 1] if c > 0 else (zero if y_low is None else y_low)
        total -= effective(2, c) * jnp.where(lane < 96, back[c], following)
        total -= effective(3, c) * jnp.where(lane >= 32, forth[c], previous)
        ends = zero if z_halo is None else roll(z_halo, 31 - 2 * c)
        total -= effective(4, c) * jnp.where(depth == BS - 1, ends, roll(f, -1))
        total -= effective(5, c) * jnp.where(depth == 0, ends, roll(f, 1))
        out.append(total)
    return out


def total_of(blocks):
    acc = blocks[0]
    for block in blocks[1:]:
        acc = acc + block
    return jnp.sum(jnp.sum(acc, axis=0, keepdims=True), axis=1, keepdims=True)


def facing(block, row):
    return jnp.where(row == 0, block[BS - 1 : BS], block[0:1])


def side_blocks(low_first, high_first, low_second, high_second):
    group = lanes() // 32
    return jnp.where(
        group == 0,
        low_first,
        jnp.where(
            group == 1,
            roll(high_first, 64),
            jnp.where(group == 2, roll(low_second, 64), high_second),
        ),
    )


def write_xy(xy_ref, row, y1, partial):
    for c in range(CHUNKS):
        xy_ref[XY_X1 + c : XY_X1 + c + 1] = facing(y1[c], row)
        xy_ref[XY_XP + c : XY_XP + c + 1] = facing(partial[c], row)
    last = CHUNKS - 1
    xy_ref[XY_Y : XY_Y + BS] = side_blocks(y1[0], y1[last], partial[0], partial[last])


def write_scalars(ref, start, values):
    for i, value in enumerate(values):
        ref[start + i : start + i + 1] = jnp.broadcast_to(value, (1, 128))
    for i in range(len(values), 8):
        ref[start + i : start + i + 1] = jnp.zeros((1, 128), F32)


def tile_of(values, y1=None):
    lane = lanes(8)
    level = rows_of(8)
    tile = jnp.zeros((8, 128), F32)
    for i, value in enumerate(values):
        tile = jnp.where((level == i) & (lane >= T_N) & (lane < T_Y), value, tile)
    if y1 is None:
        return tile
    row, low, high = y1
    tile = jnp.where((level == 0) & (lane >= T_Y), row, tile)
    tile = jnp.where((level == 1) & (lane >= T_Y), roll_row(row, 64), tile)
    wide = lanes()
    edges = jnp.where(wide == 0, low, 0.0)
    edges = jnp.where(wide == 1, roll(low, -30), edges)
    edges = jnp.where(wide == 2, roll(high, -94), edges)
    edges = jnp.where(wide == 3, roll(high, -124), edges)
    for t in range(4):
        tile = tile + roll(edges[8 * t : 8 * t + 8], 4 * t)
    return tile


def write_copies(ref, tile):
    for k in range(ref.shape[0] // 8):
        ref[8 * k : 8 * k + 8] = tile


def edge_tile(y1, row, values):
    line = pack([facing(f, row) for f in y1])
    return tile_of(values, (line, y1[0], y1[CHUNKS - 1]))


def locate(bricks, place_ref, assignment_ref):
    across = bricks // 2
    place = place_ref[0]
    slab = place // bricks
    patch = assignment_ref[place % bricks]
    row = patch // across
    column = patch % across
    return slab, patch, row, column


def setup_kernel(
    slabs, bricks, place_ref, assignment_ref, occupancy_ref, source_ref, uptake_ref, conductance_ref,
    info_ref, effective_ref, diagonal_ref, relax_ref, residual_ref, xy_ref, z_ref, tile_ref,
):
    across = bricks // 2
    slab, patch, row, column = locate(bricks, place_ref, assignment_ref)

    def holder(row_target, column_target):
        inside = (column_target >= 0) & (column_target < across)
        wanted = jnp.where(inside, row_target * across + column_target, patch)
        found = jnp.int32(0)
        for b in range(bricks):
            found = jnp.where(assignment_ref[b] == wanted, b, found)
        return found

    info_ref[0] = row
    info_ref[1] = slab
    info_ref[2] = holder(row, column)
    info_ref[3] = holder(1 - row, column)
    info_ref[4] = holder(row, column - 1)
    info_ref[5] = holder(row, column + 1)
    info_ref[6] = holder(1 - row, column - 1)
    info_ref[7] = holder(1 - row, column + 1)

    breadth = 2 * across

    def live_at(g, x, y):
        inside = (g >= 0) & (g < slabs) & (x >= 0) & (x < 2) & (y >= 0) & (y < breadth)
        index = (jnp.clip(g, 0, slabs - 1) * 2 + jnp.clip(x, 0, 1)) * breadth + jnp.clip(y, 0, breadth - 1)
        return jnp.where(inside, occupancy_ref[index], 0).astype(F32)

    lane = lanes()
    height = rows_of()
    depth = lane % BS
    absorbed = []
    low_ends = []
    high_ends = []
    first_y = None
    second_y = None
    y1 = []
    for s in range(2):
        y = column * 2 + s
        here = live_at(slab, row, y)
        around = [
            here * live_at(slab, row + 1, y),
            here * live_at(slab, row - 1, y),
            here * live_at(slab, row, y + 1),
            here * live_at(slab, row, y - 1),
            here * live_at(slab + 1, row, y),
            here * live_at(slab - 1, row, y),
        ]
        borders = [height == BS - 1, height == 0, lane >= 96, lane < 32, depth == BS - 1, depth == 0]
        for k in range(8):
            c = 8 * s + k
            part = pl.ds(128 * k, 128)
            taken = uptake_ref[s, :, part]
            absorbed.append(taken)
            diagonal = taken
            for d in range(6):
                bond = conductance_ref[d, s, :, part]
                if (d == 2 and k < 7) or (d == 3 and k > 0):
                    value = bond * here
                else:
                    value = bond * jnp.where(borders[d], around[d], here)
                effective_ref[d, c] = value
                diagonal = diagonal + value
                if d == 2 and c == 7:
                    first_y = jnp.where(borders[d], value, 0.0)
                if d == 3 and c == 8:
                    second_y = jnp.where(borders[d], value, 0.0)
                if d == 4:
                    high_ends.append(jnp.where(borders[d], value, 0.0))
                if d == 5:
                    low_ends.append(jnp.where(borders[d], value, 0.0))
            relax = OMEGA / diagonal
            diagonal_ref[c] = diagonal
            relax_ref[c] = relax
            forcing = source_ref[s, :, part] * here
            residual_ref[c] = forcing
            y1.append(relax * forcing)

    outcome = stencil(
        y1, lambda d, c: effective_ref[d, c], lambda c: diagonal_ref[c], None, None, None, None
    )
    partial = []
    for c in range(CHUNKS):
        partial.append(y1[c] + relax_ref[c] * (residual_ref[c] - outcome[c]))
    write_xy(xy_ref, row, y1, partial)
    z_ref[Z_Y1 : Z_Y1 + BS] = pack(y1)
    z_ref[Z_P : Z_P + BS] = pack(partial)

    first_coupling = total_of([first_y])
    high_sums = [total_of(high_ends[8 * s : 8 * s + 8]) for s in range(2)]
    low_sums = [total_of(low_ends[8 * s : 8 * s + 8]) for s in range(2)]
    taken_sums = [total_of(absorbed[8 * s : 8 * s + 8]) for s in range(2)]
    residual_sums = [total_of([residual_ref[8 * s + k] for k in range(8)]) for s in range(2)]
    numbers = [
        residual_sums[0],
        residual_sums[1],
        taken_sums[0] + first_coupling + high_sums[0] + low_sums[0],
        taken_sums[1] + total_of([second_y]) + high_sums[1] + low_sums[1],
        first_coupling,
        high_sums[0],
        high_sums[1],
    ]
    write_copies(tile_ref, edge_tile(y1, row, numbers))

    last = CHUNKS - 1
    z_ends = [relax_ref[c] * (high_ends[c] + low_ends[c]) for c in range(CHUNKS)]
    for c in range(CHUNKS):
        xy_ref[XY_XD + c : XY_XD + c + 1] = facing(relax_ref[c], row)
    high_y = jnp.where(lane >= 96, relax_ref[last] * effective_ref[2, last], 0.0)
    low_y = jnp.where(lane < 32, relax_ref[0] * effective_ref[3, 0], 0.0)
    z_ref[Z_D : Z_D + BS] = pack([relax_ref[c] for c in range(CHUNKS)])
    z_ref[Z_K : Z_K + BS] = pack([low_y] + [jnp.zeros((BS, 128), F32)] * (CHUNKS - 2) + [high_y])
    x_row = pack([facing_terms(relax_ref, effective_ref, c) for c in range(CHUNKS)])
    z_ref[Z_X : Z_X + 8] = jnp.broadcast_to(x_row, (8, 128))
    xy_ref[XY_YC : XY_YC + BS] = side_blocks(relax_ref[0], relax_ref[last], z_ends[0], z_ends[last])
    xy_ref[XY_K : XY_K + 1] = facing(low_y + high_y, row)
    xy_ref[XY_K + 1 : XY_K + 2] = pack([facing(z, row) for z in z_ends])
    toward_low = facing_terms(relax_ref, effective_ref, 0)
    toward_high = facing_terms(relax_ref, effective_ref, last)
    lane_row = lanes(1)
    xy_ref[XY_K + 2 : XY_K + 3] = jnp.where(lane_row < 32, toward_low, roll_row(toward_high, 64))
    xy_ref[XY_K + 3 : XY_K + 8] = jnp.zeros((5, 128), F32)


def facing_terms(relax_ref, effective_ref, c):
    upper = (relax_ref[c] * effective_ref[0, c])[BS - 1 : BS]
    lower = (relax_ref[c] * effective_ref[1, c])[0:1]
    return upper + lower


def swap_sides(from_low, from_high):
    rows = from_low.shape[0]
    if rows == 1:
        low, high = roll_row(from_low, -32), roll_row(from_high, 32)
    else:
        low, high = roll(from_low, -32), roll(from_high, 32)
    return jnp.where((lanes(rows) // 32) % 2 == 0, low, high)


def search_scalars(tiles, scalars, iteration):
    energy = tiles[2:3, T_N : T_N + 1]
    curvature = tiles[3:4, T_N : T_N + 1]
    if iteration == 0:
        return energy, curvature, energy / curvature, None
    growth = energy / scalars[0:1, 0:1]
    curvature = curvature + growth * (2.0 * tiles[4:5, T_N : T_N + 1] + growth * scalars[1:2, 0:1])
    return energy, curvature, energy / curvature, growth


def sum_tiles(ref, count):
    total = ref[0:8]
    for g in range(1, count):
        total = total + ref[8 * g : 8 * g + 8]
    return total


def step_kernel(iteration, slabs, bricks, *refs):
    first = iteration == 0
    last = iteration == ITERS - 1
    refs = list(refs)
    take = lambda count: [refs.pop(0) for _ in range(count)]
    info_ref, xy_ref, above_ref, below_ref, tiles_ref = take(5)
    effective_ref, diagonal_ref, relax_ref, residual_ref = take(4)
    if not first:
        mapped_ref, halo_in, constant_ref, factor_ref, sums_in, scalars_in = take(6)
    if iteration > 1:
        search_in, search_halo_in, search_sums_in = take(3)
    smoothed_ref, mapped_out = take(2)
    if first:
        constant_ref, factor_ref, halo_ref, sums_ref = take(4)
    else:
        residual_out, search_ref, scalars_ref = take(3)
        if not last:
            halo_ref, sums_ref, search_halo_ref, search_sums_ref = take(4)
    tile_out = take(1)[0]
    if not last:
        xy_out, z_out = take(2)

    row = info_ref[0]
    slab = info_ref[1]
    lane = lanes()
    height = rows_of()
    depth = lane % BS
    lane_row = lanes(1)
    even = lane % 2 == 0
    even_row = lane_row % 2 == 0
    low_holder, high_holder = info_ref[4], info_ref[5]
    low_corner, high_corner = info_ref[6], info_ref[7]
    x_holder = info_ref[3]

    def merge(start):
        up = roll(above_ref[start : start + BS], 31)
        down = roll(below_ref[start : start + BS], -31)
        return jnp.where(even, up, down)

    x_sides = xy_ref[x_holder, XY_X1 : XY_X1 + 2 * CHUNKS]
    y_sides = swap_sides(
        xy_ref[low_holder, XY_Y : XY_Y + BS], xy_ref[high_holder, XY_Y : XY_Y + BS]
    )
    z_first = merge(Z_Y1)
    z_second = merge(Z_P)

    def tile_at(holder, g):
        return tiles_ref[pl.ds(pl.multiple_of((holder * slabs + g) * 8, 8), 8)]

    slab_above = jnp.minimum(slab + 1, slabs - 1)
    slab_below = jnp.maximum(slab - 1, 0)

    def edge_row(tile):
        return jnp.where(lane_row >= T_Y, tile[0:1], roll_row(tile[1:2], 64))

    x_ends = jnp.where(
        even_row,
        roll_row(edge_row(tile_at(x_holder, slab_above)), 31),
        roll_row(edge_row(tile_at(x_holder, slab_below)), -31),
    )
    kind = lanes(8) % 4
    mixed = jnp.where(
        kind == 0,
        roll(tile_at(low_holder, slab_above), -2),
        jnp.where(
            kind == 1,
            roll(tile_at(low_holder, slab_below), -2),
            jnp.where(
                kind == 2,
                roll(tile_at(high_holder, slab_above), 2),
                roll(tile_at(high_holder, slab_below), 2),
            ),
        ),
    )
    y_edges = jnp.where(
        lane < 4, jnp.concatenate([roll(mixed, -4 * t) for t in range(4)], axis=0), 0.0
    )
    corner_y = jnp.where(
        lane_row < 32,
        roll_row(xy_ref[low_corner, XY_X1 + CHUNKS - 1 : XY_X1 + CHUNKS], 32),
        roll_row(xy_ref[high_corner, XY_X1 : XY_X1 + 1], -32),
    )
    low_row = jnp.where(
        row == 0,
        xy_ref[low_corner, XY_Y : XY_Y + 1],
        xy_ref[low_corner, XY_Y + BS - 1 : XY_Y + BS],
    )
    high_row = jnp.where(
        row == 0,
        xy_ref[high_corner, XY_Y : XY_Y + 1],
        xy_ref[high_corner, XY_Y + BS - 1 : XY_Y + BS],
    )
    corner_x = swap_sides(low_row, high_row)
    ends = jnp.concatenate([x_ends, corner_y, corner_x, jnp.zeros((5, 128), F32)], axis=0)
    halo = [x_sides, y_sides, z_first, z_second, y_edges, ends]
    starts = [H_X1, H_Y, H_Z1, H_ZP, H_E, H_R]
    lane_tile = lanes(8)
    slab_tiles = []
    for g in range(slabs):
        tile = tile_at(info_ref[2], g)
        for q in range(1, 4):
            tile = jnp.where(lane_tile == T_N + q, tile_at(info_ref[2 + q], g), tile)
        slab_tiles.append(tile)
    sums = jnp.concatenate(slab_tiles, axis=0)

    if first:
        residual = [residual_ref[c] for c in range(CHUNKS)]
        constant_ref[C_XD : C_XD + CHUNKS] = xy_ref[x_holder, XY_XD : XY_XD + CHUNKS]
        constant_ref[C_YC : C_YC + BS] = swap_sides(
            xy_ref[low_holder, XY_YC : XY_YC + BS], xy_ref[high_holder, XY_YC : XY_YC + BS]
        )
        constant_ref[C_ZD : C_ZD + BS] = merge(Z_D)
        constant_ref[C_ZK : C_ZK + BS] = merge(Z_K)
        constant_ref[C_K : C_K + 8] = jnp.concatenate(
            [
                xy_ref[x_holder, XY_K : XY_K + 2],
                swap_sides(
                    xy_ref[low_holder, XY_K + 2 : XY_K + 3],
                    xy_ref[high_holder, XY_K + 2 : XY_K + 3],
                ),
                jnp.where(
                    even_row,
                    roll_row(above_ref[Z_X : Z_X + 1], 31),
                    roll_row(below_ref[Z_X : Z_X + 1], -31),
                ),
                jnp.zeros((4, 128), F32),
            ],
            axis=0,
        )
        for g in range(slabs):
            tile = sums[8 * g : 8 * g + 8]
            a, b, off = tile[2:3], tile[3:4], tile[4:5]
            t0, t1 = tile[5:6], tile[6:7]
            if g > 0:
                a = a - u0 * u0 * i00
                b = b - u1 * u1 * i11
                off = off + u0 * u1 * i01
            used = (lane_row >= T_N) & (lane_row < T_N + 4)
            a = jnp.where(used, a, 1.0)
            b = jnp.where(used, b, 1.0)
            off = jnp.where(used, off, 0.0)
            t0 = jnp.where(used, t0, 0.0)
            t1 = jnp.where(used, t1, 0.0)
            scale = 1.0 / (a * b - off * off)
            i00, i01, i11 = b * scale, off * scale, a * scale
            u0, u1 = t0, t1
            factor_ref[8 * g : 8 * g + 8] = jnp.concatenate(
                [i00, i01, i11, t0, t1, jnp.zeros((3, 128), F32)], axis=0
            )
    else:
        scalars = None if iteration == 1 else scalars_in[...]
        energy, curvature, step, growth = search_scalars(
            sum_tiles(tiles_ref, slabs * bricks), scalars, iteration - 1
        )
        step_row = jnp.broadcast_to(step, (1, 128))
        residual = []
        for c in range(CHUNKS):
            mapped = mapped_ref[c]
            if growth is not None:
                mapped = mapped + growth * search_in[c]
            search_ref[c] = mapped
            value = residual_ref[c] - step * mapped
            residual_out[c] = value
            residual.append(value)
        old_halo = halo
        halo = []
        for start, block in zip(starts, old_halo):
            span = slice(start, start + block.shape[0])
            if growth is not None:
                block = block + growth * search_halo_in[span]
            if not last:
                search_halo_ref[span] = block
            halo.append(halo_in[span] - step * block)
        if growth is not None:
            sums = sums + growth * search_sums_in[...]
        if not last:
            search_sums_ref[...] = sums
        sums = sums_in[...] - step * sums
        kept = [energy, curvature, step]
        if growth is not None:
            kept = [energy, curvature, scalars[2:3, 0:1], step, growth]
        write_scalars(scalars_ref, 0, kept)

    if not last:
        for start, block in zip(starts, halo):
            halo_ref[start : start + block.shape[0]] = block
        sums_ref[...] = sums
    x_sides, y_sides, z_first, z_second, y_edges, ends = halo

    forward = []
    for g in range(slabs):
        t0, t1 = sums[8 * g : 8 * g + 1], sums[8 * g + 1 : 8 * g + 2]
        if g > 0:
            t0 = t0 + w0 * v0
            t1 = t1 + w1 * v1
        factor = factor_ref[8 * g : 8 * g + 8]
        v0 = factor[0:1] * t0 + factor[1:2] * t1
        v1 = factor[1:2] * t0 + factor[2:3] * t1
        w0, w1 = factor[3:4], factor[4:5]
        forward.append((v0, v1))
    blank = jnp.zeros((1, 128), F32)
    below0, below1, here0, here1, above0, above1 = [blank] * 6
    for g in reversed(range(slabs)):
        v0, v1 = forward[g]
        if g < slabs - 1:
            factor = factor_ref[8 * g : 8 * g + 8]
            s0, s1 = factor[3:4] * n0, factor[4:5] * n1
            v0 = v0 + factor[0:1] * s0 + factor[1:2] * s1
            v1 = v1 + factor[1:2] * s0 + factor[2:3] * s1
        n0, n1 = v0, v1
        here0 = jnp.where(slab == g, n0, here0)
        here1 = jnp.where(slab == g, n1, here1)
        above0 = jnp.where(slab + 1 == g, n0, above0)
        above1 = jnp.where(slab + 1 == g, n1, above1)
        below0 = jnp.where(slab - 1 == g, n0, below0)
        below1 = jnp.where(slab - 1 == g, n1, below1)
    def coarse_of(row, q):
        return row[:, T_N + q : T_N + q + 1]

    own = [coarse_of(here0, 0), coarse_of(here1, 0)]

    effective = lambda d, c: effective_ref[d, c]
    diagonal = lambda c: diagonal_ref[c]
    end = CHUNKS - 1

    y1 = [relax_ref[c] * residual[c] for c in range(CHUNKS)]
    outcome = stencil(
        y1, effective, diagonal, x_sides[:CHUNKS], y_sides, roll(y_sides, 64), z_first
    )
    smoothed = []
    for c in range(CHUNKS):
        value = y1[c] + relax_ref[c] * (residual[c] - outcome[c]) + own[c // 8]
        smoothed_ref[c] = value
        smoothed.append(value)
    keys = constant_ref[C_K : C_K + 8]
    crossing = jnp.concatenate(
        [
            effective(0, c)[BS - 1 : BS] * y1[c][BS - 1 : BS] + effective(1, c)[0:1] * y1[c][0:1]
            for c in range(CHUNKS)
        ],
        axis=0,
    )
    end_row = keys[1:2] * ends[0:1]
    corner_row = keys[0:1] * ends[1:2]
    depth_row = lane_row % BS
    additions = []
    for c in range(CHUNKS):
        value = jnp.where(
            (depth_row == BS - 1) | (depth_row == 0), roll_row(end_row, 31 - 2 * c), 0.0
        )
        if c == 0:
            value = value + jnp.where(lane_row < 32, corner_row, 0.0)
        if c == end:
            value = value + jnp.where(lane_row >= 96, corner_row, 0.0)
        value = value + coarse_of(here0 if c < 8 else here1, 1)
        additions.append(value)
    x_next = (
        x_sides[CHUNKS:]
        + constant_ref[C_XD : C_XD + CHUNKS] * crossing
        + jnp.concatenate(additions, axis=0)
    )
    y_constant = constant_ref[C_YC : C_YC + BS]
    y_crossing = jnp.where(
        lane < 32, effective(3, 0) * y1[0], roll(effective(2, end) * y1[end], 64)
    )
    x_side_row = jnp.where(row == 0, BS - 1, 0)
    y_ends = jnp.where(lane == 0, roll(y_edges, -1), 0.0)
    y_ends = jnp.where(lane == 31, roll(y_edges, 31), y_ends)
    y_ends = jnp.where(lane == 32, roll(y_edges, 29), y_ends)
    y_ends = jnp.where(lane == 63, roll(y_edges, 61), y_ends)
    z_sides = jnp.where(lane == 0, y_edges, 0.0)
    z_sides = jnp.where(lane == 97, roll(y_edges, 96), z_sides)
    z_sides = jnp.where(lane == 126, roll(y_edges, 124), z_sides)
    z_sides = jnp.where(lane == 95, roll(y_edges, 92), z_sides)
    y_next = (
        roll(y_sides, 64)
        + y_constant * y_crossing
        + roll(y_constant, 64) * y_ends
        + jnp.where(height == x_side_row, keys[2:3] * ends[2:3], 0.0)
        + jnp.where(lane < 32, coarse_of(here1, 2), coarse_of(here0, 3))
    )
    z_crossing = pack(
        [
            jnp.where(depth == BS - 1, effective(4, c), effective(5, c)) * y1[c]
            for c in range(CHUNKS)
        ]
    )
    z_coarse = jnp.where(
        even_row,
        jnp.where(depth_row < 16, coarse_of(above0, 0), coarse_of(above1, 0)),
        jnp.where(depth_row < 16, coarse_of(below0, 0), coarse_of(below1, 0)),
    )
    z_next = (
        z_second
        + constant_ref[C_ZD : C_ZD + BS] * z_crossing
        + constant_ref[C_ZK : C_ZK + BS] * z_sides
        + jnp.where(height == x_side_row, keys[3:4] * ends[0:1], 0.0)
        + z_coarse
    )
    mapped = stencil(smoothed, effective, diagonal, x_next, y_next, roll(y_next, 64), z_next)
    for c in range(CHUNKS):
        mapped_out[c] = mapped[c]

    values = [
        total_of(mapped[:8]),
        total_of(mapped[8:]),
        total_of([residual[c] * smoothed[c] for c in range(CHUNKS)]),
        total_of([mapped[c] * smoothed[c] for c in range(CHUNKS)]),
    ]
    if not first:
        values.append(total_of([search_ref[c] * smoothed[c] for c in range(CHUNKS)]))
    if last:
        write_copies(tile_out, tile_of(values))
        return
    y1 = [relax_ref[c] * mapped[c] for c in range(CHUNKS)]
    write_copies(tile_out, edge_tile(y1, row, values))
    outcome = stencil(y1, effective, diagonal, None, None, None, None)
    partial = [y1[c] + relax_ref[c] * (mapped[c] - outcome[c]) for c in range(CHUNKS)]
    write_xy(xy_out, row, y1, partial)
    z_out[Z_Y1 : Z_Y1 + BS] = pack(y1)
    z_out[Z_P : Z_P + BS] = pack(partial)


def finish_kernel(
    tiles_ref, scalars_ref, residual_ref, mapped_ref, search_ref, first_ref, second_ref, third_ref,
    solution_ref, residual_out,
):
    scalars = scalars_ref[...]
    tiles = sum_tiles(tiles_ref, tiles_ref.shape[0] // 8)
    _, _, step, growth = search_scalars(tiles, scalars, ITERS - 1)
    first_step, second_step, second_growth = scalars[2:3, 0:1], scalars[3:4, 0:1], scalars[4:5, 0:1]
    third_weight = step
    second_weight = second_step + growth * step
    first_weight = first_step + second_growth * second_weight
    for c in range(CHUNKS):
        s, part = c // 8, pl.ds(128 * (c % 8), 128)
        solution_ref[s, :, part] = (
            first_weight * first_ref[c] + second_weight * second_ref[c] + third_weight * third_ref[c]
        )
        residual_out[s, :, part] = residual_ref[c] - step * (mapped_ref[c] + growth * search_ref[c])


def call(kernel, name, outs, operands, scalar_operands=0, scalar_outs=0):
    vmem = pl.BlockSpec(memory_space=pltpu.VMEM)
    smem = pl.BlockSpec(memory_space=pltpu.SMEM)
    return pl.pallas_call(
        kernel,
        out_shape=tuple(outs),
        in_specs=[smem] * scalar_operands + [vmem] * (len(operands) - scalar_operands),
        out_specs=tuple([smem] * scalar_outs + [vmem] * (len(outs) - scalar_outs)),
        compiler_params=pltpu.CompilerParams(vmem_limit_bytes=16 * 1024 * 1024),
        name=name,
    )(*operands)


def array(*shape):
    return jax.ShapeDtypeStruct(shape, F32)


def gather_bricks(message):
    return lax.all_gather(message, "brick", axis=0, tiled=False)


def to_all(copies, axes):
    return lax.all_to_all(copies, axes, 0, 0, tiled=True)


def exchange_slabs(message):
    count = lax.axis_size("grp")
    upward = [(i, i + 1) for i in range(count - 1)]
    downward = [(i + 1, i) for i in range(count - 1)]
    return lax.ppermute(message, "grp", downward), lax.ppermute(message, "grp", upward)


def on_device(source, uptake, conductance, occupancy, assignment):
    slabs = lax.axis_size("grp")
    bricks = lax.axis_size("brick")
    place = (lax.axis_index("grp") * bricks + lax.axis_index("brick")).astype(jnp.int32).reshape(1)
    field = array(*FIELD)
    copies = array(8 * slabs * bricks, 128)
    info, effective, diagonal, relax, residual, sides, ends, tile = call(
        functools.partial(setup_kernel, slabs, bricks),
        "setup",
        [
            jax.ShapeDtypeStruct((8,), jnp.int32), array(6, *FIELD), field, field, field,
            array(XY_ROWS_FIRST, 128), array(Z_ROWS_FIRST, 128), copies,
        ],
        [place, assignment, occupancy.reshape(-1), source[0, 0], uptake[0, 0], conductance[0, 0]],
        scalar_operands=3,
        scalar_outs=1,
    )
    mapped = residual
    directions = []
    state = {}
    for iteration in range(ITERS):
        first, last = iteration == 0, iteration == ITERS - 1
        tiles = to_all(tile, ("brick", "grp"))
        above, below = exchange_slabs(ends)
        gathered = gather_bricks(sides)
        operands = [info, gathered, above, below, tiles, effective, diagonal, relax, residual]
        tall = array(8 * slabs, 128)
        outs = {"smoothed": field, "mapped": field}
        if not first:
            operands += [mapped] + [state[k] for k in ("halo", "constant", "factor", "sums", "scalars")]
        if iteration > 1:
            operands += [state[k] for k in ("search", "search_halo", "search_sums")]
        if first:
            outs |= {"constant": array(C_ROWS, 128), "factor": tall, "halo": array(H_ROWS, 128), "sums": tall}
        else:
            outs |= {"residual": field, "search": field, "scalars": array(8, 128)}
            if not last:
                outs |= {
                    "halo": array(H_ROWS, 128), "sums": tall,
                    "search_halo": array(H_ROWS, 128), "search_sums": tall,
                }
        outs["tile"] = copies
        if not last:
            outs |= {"sides": array(XY_ROWS, 128), "ends": array(Z_ROWS, 128)}
        results = call(
            functools.partial(step_kernel, iteration, slabs, bricks),
            f"step_{iteration}",
            list(outs.values()),
            operands,
            scalar_operands=1,
        )
        state |= dict(zip(outs, results))
        if first:
            state["scalars"] = jnp.zeros((8, 128), F32)
        mapped, tile = state["mapped"], state["tile"]
        sides, ends = state.get("sides"), state.get("ends")
        residual = state.get("residual", residual)
        directions.append(state["smoothed"])
    tiles = to_all(tile, ("brick", "grp"))
    brick_pair = array(2, BS, BS * BS)
    solution_field, residual = call(
        finish_kernel,
        "finish",
        [brick_pair, brick_pair],
        [tiles, state["scalars"], residual, mapped, state["search"]] + directions,
    )
    return solution_field[None, None], residual[None, None]


def solution(mesh):
    return jax.shard_map(
        on_device,
        mesh=mesh,
        in_specs=(
            P("grp", "brick", None, None, None),
            P("grp", "brick", None, None, None),
            P("grp", "brick", None, None, None, None),
            P(),
            P(),
        ),
        out_specs=(P("grp", "brick", None, None, None), P("grp", "brick", None, None, None)),
        check_vma=False,
    )
```

```python
import functools

import jax
import jax.numpy as jnp
from jax import lax
from jax.experimental import pallas as pl
from jax.experimental.pallas import tpu as pltpu
from jax.sharding import PartitionSpec as P

BS = 32
CHUNKS = 16
OMEGA = 0.6
ITERS = 3
F32 = jnp.float32
FIELD = (CHUNKS, BS, 128)

XY_X1, XY_XP, XY_Y = 0, 16, 32
XY_ROWS = 64
XY_XD, XY_YC, XY_K = 64, 80, 112
XY_ROWS_FIRST = 120
Z_Y1, Z_P = 0, 32
Z_ROWS = 64
Z_D, Z_K, Z_X = 64, 96, 128
Z_ROWS_FIRST = 136
T_N, T_Y = 16, 64
H_X1, H_Y, H_Z1, H_ZP, H_E, H_R = 0, 32, 64, 96, 128, 160
H_ROWS = 168
C_XD, C_YC, C_ZD, C_ZK, C_K = 0, 16, 48, 80, 112
C_ROWS = 120
B_XP, B_XM, B_YP, B_YM, B_Z = 0, 16, 32, 64, 96
B_ROWS = 128


def roll(block, shift):
    return pltpu.roll(block, shift % 128, axis=1)


def roll_row(row, shift):
    return pltpu.roll(jnp.broadcast_to(row, (8, 128)), shift % 128, axis=1)[0:1]


def lanes(rows=BS):
    return lax.broadcasted_iota(jnp.int32, (rows, 128), 1)


def rows_of(height=BS):
    return lax.broadcasted_iota(jnp.int32, (height, 128), 0)


def pack(chunks):
    height = chunks[0].shape[0]
    pair = (lanes(height) % BS) // 2
    total = jnp.zeros((height, 128), F32)
    for c in range(CHUNKS):
        moved = roll(chunks[c], 2 * c - 31) if height > 1 else roll_row(chunks[c], 2 * c - 31)
        total = jnp.where(pair == c, moved, total)
    return total


def stencil(field, bonds, diagonal, outer=None):
    lane = lanes()
    height = rows_of()
    depth = lane % BS
    at_end = (depth == BS - 1) | (depth == 0)
    back = [roll(f, -32) for f in field]
    forth = [roll(bonds(1, c) * field[c], 32) for c in range(CHUNKS)]
    out = []
    for c in range(CHUNKS):
        f = field[c]
        total = diagonal(c) * f
        total -= bonds(0, c) * pltpu.roll(f, BS - 1, axis=0)
        total -= pltpu.roll(bonds(0, c) * f, 1, axis=0)
        following = back[c + 1] if c < CHUNKS - 1 else back[c]
        previous = forth[c - 1] if c > 0 else jnp.zeros((BS, 128), F32)
        total -= bonds(1, c) * jnp.where(lane < 96, back[c], following)
        total -= jnp.where(lane >= 32, forth[c], previous)
        total -= bonds(2, c) * roll(f, -1)
        total -= roll(bonds(2, c) * f, 1)
        if outer is not None:
            x_up, x_down, y_low, y_high, z_ends = outer
            total -= jnp.where(height == BS - 1, x_up[c : c + 1], 0.0)
            total -= jnp.where(height == 0, x_down[c : c + 1], 0.0)
            total -= jnp.where(at_end, roll(z_ends, 31 - 2 * c), 0.0)
            if c == 0:
                total -= jnp.where(lane < 32, y_low, 0.0)
            if c == CHUNKS - 1:
                total -= jnp.where(lane >= 96, y_high, 0.0)
        out.append(total)
    return out


def total_of(blocks):
    acc = blocks[0]
    for block in blocks[1:]:
        acc = acc + block
    return jnp.sum(jnp.sum(acc, axis=0, keepdims=True), axis=1, keepdims=True)


def facing(block, row):
    return jnp.where(row == 0, block[BS - 1 : BS], block[0:1])


def side_blocks(low_first, high_first, low_second, high_second):
    group = lanes() // 32
    return jnp.where(
        group == 0,
        low_first,
        jnp.where(
            group == 1,
            roll(high_first, 64),
            jnp.where(group == 2, roll(low_second, 64), high_second),
        ),
    )


def write_xy(xy_ref, row, y1, partial):
    for c in range(CHUNKS):
        xy_ref[XY_X1 + c : XY_X1 + c + 1] = facing(y1[c], row)
        xy_ref[XY_XP + c : XY_XP + c + 1] = facing(partial[c], row)
    last = CHUNKS - 1
    xy_ref[XY_Y : XY_Y + BS] = side_blocks(y1[0], y1[last], partial[0], partial[last])


def write_scalars(ref, start, values):
    for i, value in enumerate(values):
        ref[start + i : start + i + 1] = jnp.broadcast_to(value, (1, 128))
    for i in range(len(values), 8):
        ref[start + i : start + i + 1] = jnp.zeros((1, 128), F32)


def tile_of(values, y1=None):
    lane = lanes(8)
    level = rows_of(8)
    tile = jnp.zeros((8, 128), F32)
    for i, value in enumerate(values):
        tile = jnp.where((level == i) & (lane >= T_N) & (lane < T_Y), value, tile)
    if y1 is None:
        return tile
    row, low, high = y1
    tile = jnp.where((level == 0) & (lane >= T_Y), row, tile)
    tile = jnp.where((level == 1) & (lane >= T_Y), roll_row(row, 64), tile)
    wide = lanes()
    edges = jnp.where(wide == 0, low, 0.0)
    edges = jnp.where(wide == 1, roll(low, -30), edges)
    edges = jnp.where(wide == 2, roll(high, -94), edges)
    edges = jnp.where(wide == 3, roll(high, -124), edges)
    for t in range(4):
        tile = tile + roll(edges[8 * t : 8 * t + 8], 4 * t)
    return tile


def write_copies(ref, tile):
    for k in range(ref.shape[0] // 8):
        ref[8 * k : 8 * k + 8] = tile


def edge_tile(y1, row, values):
    line = pack([facing(f, row) for f in y1])
    return tile_of(values, (line, y1[0], y1[CHUNKS - 1]))


def locate(bricks, place_ref, assignment_ref):
    across = bricks // 2
    place = place_ref[0]
    slab = place // bricks
    patch = assignment_ref[place % bricks]
    row = patch // across
    column = patch % across
    return slab, patch, row, column


def setup_kernel(
    slabs, bricks, place_ref, assignment_hbm, occupancy_hbm, source_hbm, uptake_hbm, conductance_hbm,
    info_ref, bonds_ref, outer_ref, diagonal_ref, residual_ref, xy_ref, z_ref, tile_ref,
    assignment_ref, occupancy_ref, source_ref, uptake_ref, conductance_ref, relax_ref, y1_ref, arrived,
):
    pairs = [
        (assignment_hbm, assignment_ref),
        (occupancy_hbm, occupancy_ref),
        (source_hbm, source_ref),
        (uptake_hbm, uptake_ref),
        (conductance_hbm, conductance_ref),
    ]
    copies = [
        pltpu.make_async_copy(there, here, arrived.at[i]) for i, (there, here) in enumerate(pairs)
    ]
    for copy in copies:
        copy.start()
    for copy in copies:
        copy.wait()
    across = bricks // 2
    slab, patch, row, column = locate(bricks, place_ref, assignment_ref)

    def holder(row_target, column_target):
        inside = (column_target >= 0) & (column_target < across)
        wanted = jnp.where(inside, row_target * across + column_target, patch)
        found = jnp.int32(0)
        for b in range(bricks):
            found = jnp.where(assignment_ref[b] == wanted, b, found)
        return found

    info_ref[0] = row
    info_ref[1] = slab
    info_ref[2] = holder(row, column)
    info_ref[3] = holder(1 - row, column)
    info_ref[4] = holder(row, column - 1)
    info_ref[5] = holder(row, column + 1)
    info_ref[6] = holder(1 - row, column - 1)
    info_ref[7] = holder(1 - row, column + 1)

    breadth = 2 * across

    def live_at(g, x, y):
        inside = (g >= 0) & (g < slabs) & (x >= 0) & (x < 2) & (y >= 0) & (y < breadth)
        taken = occupancy_ref[jnp.clip(x, 0, 1), jnp.clip(y, 0, breadth - 1), jnp.clip(g, 0, slabs - 1)]
        return jnp.where(inside, taken, 0).astype(F32)

    lane = lanes()
    height = rows_of()
    depth = lane % BS
    absorbed = []
    low_ends = []
    high_ends = []
    first_y = None
    second_y = None
    for s in range(2):
        y = column * 2 + s
        here = live_at(slab, row, y)
        around = [
            here * live_at(slab, row + 1, y),
            here * live_at(slab, row - 1, y),
            here * live_at(slab, row, y + 1),
            here * live_at(slab, row, y - 1),
            here * live_at(slab + 1, row, y),
            here * live_at(slab - 1, row, y),
        ]
        borders = [height == BS - 1, height == 0, lane >= 96, lane < 32, depth == BS - 1, depth == 0]
        for k in range(8):
            c = 8 * s + k
            part = pl.ds(128 * k, 128)
            taken = uptake_ref[s, :, part]
            absorbed.append(taken)
            diagonal = taken
            values = []
            for d in range(6):
                bond = conductance_ref[d, s, :, part]
                if (d == 2 and k < 7) or (d == 3 and k > 0):
                    value = bond * here
                else:
                    value = bond * jnp.where(borders[d], around[d], here)
                values.append(value)
                diagonal = diagonal + value
            if c == 7:
                first_y = jnp.where(borders[2], values[2], 0.0)
            if c == 8:
                second_y = jnp.where(borders[3], values[3], 0.0)
            high_ends.append(jnp.where(borders[4], values[4], 0.0))
            low_ends.append(jnp.where(borders[5], values[5], 0.0))
            outer_ref[B_XP + c : B_XP + c + 1] = values[0][BS - 1 : BS]
            outer_ref[B_XM + c : B_XM + c + 1] = values[1][0:1]
            bonds_ref[0, c] = jnp.where(borders[0], 0.0, values[0])
            if c == CHUNKS - 1:
                outer_ref[B_YP : B_YP + BS] = jnp.where(borders[2], values[2], 0.0)
                bonds_ref[1, c] = jnp.where(borders[2], 0.0, values[2])
            else:
                bonds_ref[1, c] = values[2]
            if c == 0:
                outer_ref[B_YM : B_YM + BS] = jnp.where(borders[3], values[3], 0.0)
            bonds_ref[2, c] = jnp.where(borders[4], 0.0, values[4])
            relax = OMEGA / diagonal
            diagonal_ref[c] = diagonal
            relax_ref[c] = relax
            forcing = source_ref[s, :, part] * here
            residual_ref[c] = forcing
            y1_ref[c] = relax * forcing

    ends = [high_ends[c] + low_ends[c] for c in range(CHUNKS)]
    outer_ref[B_Z : B_Z + BS] = pack(ends)
    y1 = [y1_ref[c] for c in range(CHUNKS)]
    outcome = stencil(y1, lambda d, c: bonds_ref[d, c], lambda c: diagonal_ref[c])
    partial = [y1[c] + relax_ref[c] * (residual_ref[c] - outcome[c]) for c in range(CHUNKS)]
    write_xy(xy_ref, row, y1, partial)
    z_ref[Z_Y1 : Z_Y1 + BS] = pack(y1)
    z_ref[Z_P : Z_P + BS] = pack(partial)

    first_coupling = total_of([first_y])
    high_sums = [total_of(high_ends[8 * s : 8 * s + 8]) for s in range(2)]
    low_sums = [total_of(low_ends[8 * s : 8 * s + 8]) for s in range(2)]
    taken_sums = [total_of(absorbed[8 * s : 8 * s + 8]) for s in range(2)]
    residual_sums = [total_of([residual_ref[8 * s + k] for k in range(8)]) for s in range(2)]
    numbers = [
        residual_sums[0],
        residual_sums[1],
        taken_sums[0] + first_coupling + high_sums[0] + low_sums[0],
        taken_sums[1] + total_of([second_y]) + high_sums[1] + low_sums[1],
        first_coupling,
        high_sums[0],
        high_sums[1],
    ]
    write_copies(tile_ref, edge_tile(y1, row, numbers))

    last = CHUNKS - 1
    z_ends = [relax_ref[c] * ends[c] for c in range(CHUNKS)]
    for c in range(CHUNKS):
        xy_ref[XY_XD + c : XY_XD + c + 1] = facing(relax_ref[c], row)
    high_y = relax_ref[last] * outer_ref[B_YP : B_YP + BS]
    low_y = relax_ref[0] * outer_ref[B_YM : B_YM + BS]
    xy_ref[XY_YC : XY_YC + BS] = side_blocks(relax_ref[0], relax_ref[last], z_ends[0], z_ends[last])
    xy_ref[XY_K : XY_K + 1] = facing(low_y + high_y, row)
    xy_ref[XY_K + 1 : XY_K + 2] = pack([facing(z, row) for z in z_ends])
    toward = [
        relax_ref[c][BS - 1 : BS] * outer_ref[B_XP + c : B_XP + c + 1]
        + relax_ref[c][0:1] * outer_ref[B_XM + c : B_XM + c + 1]
        for c in range(CHUNKS)
    ]
    xy_ref[XY_K + 2 : XY_K + 3] = jnp.where(lanes(1) < 32, toward[0], roll_row(toward[last], 64))
    xy_ref[XY_K + 3 : XY_K + 8] = jnp.zeros((5, 128), F32)
    z_ref[Z_D : Z_D + BS] = pack([relax_ref[c] for c in range(CHUNKS)])
    z_ref[Z_K : Z_K + BS] = pack([low_y] + [jnp.zeros((BS, 128), F32)] * (CHUNKS - 2) + [high_y])
    z_ref[Z_X : Z_X + 8] = jnp.broadcast_to(pack(toward), (8, 128))


def swap_sides(from_low, from_high):
    rows = from_low.shape[0]
    if rows == 1:
        low, high = roll_row(from_low, -32), roll_row(from_high, 32)
    else:
        low, high = roll(from_low, -32), roll(from_high, 32)
    return jnp.where((lanes(rows) // 32) % 2 == 0, low, high)


def search_scalars(tiles, scalars, iteration):
    energy = tiles[2:3, T_N : T_N + 1]
    curvature = tiles[3:4, T_N : T_N + 1]
    if iteration == 0:
        return energy, curvature, energy / curvature, None
    growth = energy / scalars[0:1, 0:1]
    curvature = curvature + growth * (2.0 * tiles[4:5, T_N : T_N + 1] + growth * scalars[1:2, 0:1])
    return energy, curvature, energy / curvature, growth


def sum_tiles(ref, count):
    total = ref[0:8]
    for g in range(1, count):
        total = total + ref[8 * g : 8 * g + 8]
    return total


def step_kernel(iteration, slabs, bricks, *refs):
    first = iteration == 0
    last = iteration == ITERS - 1
    refs = list(refs)
    take = lambda count: [refs.pop(0) for _ in range(count)]
    info_ref, xy_ref, above_ref, below_ref, tiles_ref = take(5)
    bonds_ref, outer_ref, diagonal_ref, residual_ref = take(4)
    if not first:
        mapped_ref, halo_in, constant_ref, factor_ref, sums_in, scalars_in = take(6)
    if iteration > 1:
        search_in, search_halo_in, search_sums_in = take(3)
    smoothed_ref, mapped_out = take(2)
    if first:
        constant_ref, factor_ref, halo_ref, sums_ref = take(4)
    else:
        residual_out, search_ref, scalars_ref = take(3)
        if not last:
            halo_ref, sums_ref, search_halo_ref, search_sums_ref = take(4)
    tile_out = take(1)[0]
    if not last:
        xy_out, z_out = take(2)
    relax_ref = take(1)[0]
    for c in range(CHUNKS):
        relax_ref[c] = OMEGA / diagonal_ref[c]

    row = info_ref[0]
    slab = info_ref[1]
    lane = lanes()
    height = rows_of()
    depth = lane % BS
    lane_row = lanes(1)
    even = lane % 2 == 0
    even_row = lane_row % 2 == 0
    low_holder, high_holder = info_ref[4], info_ref[5]
    low_corner, high_corner = info_ref[6], info_ref[7]
    x_holder = info_ref[3]

    def merge(start):
        up = roll(above_ref[start : start + BS], 31)
        down = roll(below_ref[start : start + BS], -31)
        return jnp.where(even, up, down)

    x_sides = xy_ref[x_holder, XY_X1 : XY_X1 + 2 * CHUNKS]
    y_sides = swap_sides(
        xy_ref[low_holder, XY_Y : XY_Y + BS], xy_ref[high_holder, XY_Y : XY_Y + BS]
    )
    z_first = merge(Z_Y1)
    z_second = merge(Z_P)

    def tile_at(holder, g):
        return tiles_ref[pl.ds(pl.multiple_of((holder * slabs + g) * 8, 8), 8)]

    slab_above = jnp.minimum(slab + 1, slabs - 1)
    slab_below = jnp.maximum(slab - 1, 0)

    def edge_row(tile):
        return jnp.where(lane_row >= T_Y, tile[0:1], roll_row(tile[1:2], 64))

    x_ends = jnp.where(
        even_row,
        roll_row(edge_row(tile_at(x_holder, slab_above)), 31),
        roll_row(edge_row(tile_at(x_holder, slab_below)), -31),
    )
    kind = lanes(8) % 4
    mixed = jnp.where(
        kind == 0,
        roll(tile_at(low_holder, slab_above), -2),
        jnp.where(
            kind == 1,
            roll(tile_at(low_holder, slab_below), -2),
            jnp.where(
                kind == 2,
                roll(tile_at(high_holder, slab_above), 2),
                roll(tile_at(high_holder, slab_below), 2),
            ),
        ),
    )
    y_edges = jnp.where(
        lane < 4, jnp.concatenate([roll(mixed, -4 * t) for t in range(4)], axis=0), 0.0
    )
    corner_y = jnp.where(
        lane_row < 32,
        roll_row(xy_ref[low_corner, XY_X1 + CHUNKS - 1 : XY_X1 + CHUNKS], 32),
        roll_row(xy_ref[high_corner, XY_X1 : XY_X1 + 1], -32),
    )
    low_row = jnp.where(
        row == 0,
        xy_ref[low_corner, XY_Y : XY_Y + 1],
        xy_ref[low_corner, XY_Y + BS - 1 : XY_Y + BS],
    )
    high_row = jnp.where(
        row == 0,
        xy_ref[high_corner, XY_Y : XY_Y + 1],
        xy_ref[high_corner, XY_Y + BS - 1 : XY_Y + BS],
    )
    corner_x = swap_sides(low_row, high_row)
    ends = jnp.concatenate([x_ends, corner_y, corner_x, jnp.zeros((5, 128), F32)], axis=0)
    halo = [x_sides, y_sides, z_first, z_second, y_edges, ends]
    starts = [H_X1, H_Y, H_Z1, H_ZP, H_E, H_R]
    lane_tile = lanes(8)
    slab_tiles = []
    for g in range(slabs):
        tile = tile_at(info_ref[2], g)
        for q in range(1, 4):
            tile = jnp.where(lane_tile == T_N + q, tile_at(info_ref[2 + q], g), tile)
        slab_tiles.append(tile)
    sums = jnp.concatenate(slab_tiles, axis=0)

    if first:
        residual = [residual_ref[c] for c in range(CHUNKS)]
        constant_ref[C_XD : C_XD + CHUNKS] = xy_ref[x_holder, XY_XD : XY_XD + CHUNKS]
        constant_ref[C_YC : C_YC + BS] = swap_sides(
            xy_ref[low_holder, XY_YC : XY_YC + BS], xy_ref[high_holder, XY_YC : XY_YC + BS]
        )
        constant_ref[C_ZD : C_ZD + BS] = merge(Z_D)
        constant_ref[C_ZK : C_ZK + BS] = merge(Z_K)
        constant_ref[C_K : C_K + 8] = jnp.concatenate(
            [
                xy_ref[x_holder, XY_K : XY_K + 2],
                swap_sides(
                    xy_ref[low_holder, XY_K + 2 : XY_K + 3],
                    xy_ref[high_holder, XY_K + 2 : XY_K + 3],
                ),
                jnp.where(
                    even_row,
                    roll_row(above_ref[Z_X : Z_X + 1], 31),
                    roll_row(below_ref[Z_X : Z_X + 1], -31),
                ),
                jnp.zeros((4, 128), F32),
            ],
            axis=0,
        )
        for g in range(slabs):
            tile = sums[8 * g : 8 * g + 8]
            a, b, off = tile[2:3], tile[3:4], tile[4:5]
            t0, t1 = tile[5:6], tile[6:7]
            if g > 0:
                a = a - u0 * u0 * i00
                b = b - u1 * u1 * i11
                off = off + u0 * u1 * i01
            used = (lane_row >= T_N) & (lane_row < T_N + 4)
            a = jnp.where(used, a, 1.0)
            b = jnp.where(used, b, 1.0)
            off = jnp.where(used, off, 0.0)
            t0 = jnp.where(used, t0, 0.0)
            t1 = jnp.where(used, t1, 0.0)
            scale = 1.0 / (a * b - off * off)
            i00, i01, i11 = b * scale, off * scale, a * scale
            u0, u1 = t0, t1
            factor_ref[8 * g : 8 * g + 8] = jnp.concatenate(
                [i00, i01, i11, t0, t1, jnp.zeros((3, 128), F32)], axis=0
            )
    else:
        scalars = None if iteration == 1 else scalars_in[...]
        energy, curvature, step, growth = search_scalars(
            sum_tiles(tiles_ref, slabs * bricks), scalars, iteration - 1
        )
        step_row = jnp.broadcast_to(step, (1, 128))
        residual = []
        for c in range(CHUNKS):
            mapped = mapped_ref[c]
            if growth is not None:
                mapped = mapped + growth * search_in[c]
            search_ref[c] = mapped
            value = residual_ref[c] - step * mapped
            residual_out[c] = value
            residual.append(value)
        old_halo = halo
        halo = []
        for start, block in zip(starts, old_halo):
            span = slice(start, start + block.shape[0])
            if growth is not None:
                block = block + growth * search_halo_in[span]
            if not last:
                search_halo_ref[span] = block
            halo.append(halo_in[span] - step * block)
        if growth is not None:
            sums = sums + growth * search_sums_in[...]
        if not last:
            search_sums_ref[...] = sums
        sums = sums_in[...] - step * sums
        kept = [energy, curvature, step]
        if growth is not None:
            kept = [energy, curvature, scalars[2:3, 0:1], step, growth]
        write_scalars(scalars_ref, 0, kept)

    if not last:
        for start, block in zip(starts, halo):
            halo_ref[start : start + block.shape[0]] = block
        sums_ref[...] = sums
    x_sides, y_sides, z_first, z_second, y_edges, ends = halo

    forward = []
    for g in range(slabs):
        t0, t1 = sums[8 * g : 8 * g + 1], sums[8 * g + 1 : 8 * g + 2]
        if g > 0:
            t0 = t0 + w0 * v0
            t1 = t1 + w1 * v1
        factor = factor_ref[8 * g : 8 * g + 8]
        v0 = factor[0:1] * t0 + factor[1:2] * t1
        v1 = factor[1:2] * t0 + factor[2:3] * t1
        w0, w1 = factor[3:4], factor[4:5]
        forward.append((v0, v1))
    blank = jnp.zeros((1, 128), F32)
    below0, below1, here0, here1, above0, above1 = [blank] * 6
    for g in reversed(range(slabs)):
        v0, v1 = forward[g]
        if g < slabs - 1:
            factor = factor_ref[8 * g : 8 * g + 8]
            s0, s1 = factor[3:4] * n0, factor[4:5] * n1
            v0 = v0 + factor[0:1] * s0 + factor[1:2] * s1
            v1 = v1 + factor[1:2] * s0 + factor[2:3] * s1
        n0, n1 = v0, v1
        here0 = jnp.where(slab == g, n0, here0)
        here1 = jnp.where(slab == g, n1, here1)
        above0 = jnp.where(slab + 1 == g, n0, above0)
        above1 = jnp.where(slab + 1 == g, n1, above1)
        below0 = jnp.where(slab - 1 == g, n0, below0)
        below1 = jnp.where(slab - 1 == g, n1, below1)
    def coarse_of(row, q):
        return row[:, T_N + q : T_N + q + 1]

    own = [coarse_of(here0, 0), coarse_of(here1, 0)]

    bonds = lambda d, c: bonds_ref[d, c]
    diagonal = lambda c: diagonal_ref[c]
    end = CHUNKS - 1
    x_plus = outer_ref[B_XP : B_XP + CHUNKS]
    x_minus = outer_ref[B_XM : B_XM + CHUNKS]
    y_plus = outer_ref[B_YP : B_YP + BS]
    y_minus = outer_ref[B_YM : B_YM + BS]
    z_bonds = outer_ref[B_Z : B_Z + BS]

    def brought(x_rows, y_block, z_block):
        return (
            x_plus * x_rows,
            x_minus * x_rows,
            y_minus * y_block,
            y_plus * roll(y_block, 64),
            z_bonds * z_block,
        )

    y1 = [relax_ref[c] * residual[c] for c in range(CHUNKS)]
    outcome = stencil(y1, bonds, diagonal, brought(x_sides[:CHUNKS], y_sides, z_first))
    smoothed = []
    for c in range(CHUNKS):
        value = y1[c] + relax_ref[c] * (residual[c] - outcome[c]) + own[c // 8]
        smoothed_ref[c] = value
        smoothed.append(value)
    keys = constant_ref[C_K : C_K + 8]
    crossing = x_plus * jnp.concatenate([f[BS - 1 : BS] for f in y1], axis=0)
    crossing += x_minus * jnp.concatenate([f[0:1] for f in y1], axis=0)
    end_row = keys[1:2] * ends[0:1]
    corner_row = keys[0:1] * ends[1:2]
    depth_row = lane_row % BS
    additions = []
    for c in range(CHUNKS):
        value = jnp.where(
            (depth_row == BS - 1) | (depth_row == 0), roll_row(end_row, 31 - 2 * c), 0.0
        )
        if c == 0:
            value = value + jnp.where(lane_row < 32, corner_row, 0.0)
        if c == end:
            value = value + jnp.where(lane_row >= 96, corner_row, 0.0)
        value = value + coarse_of(here0 if c < 8 else here1, 1)
        additions.append(value)
    x_next = (
        x_sides[CHUNKS:]
        + constant_ref[C_XD : C_XD + CHUNKS] * crossing
        + jnp.concatenate(additions, axis=0)
    )
    y_constant = constant_ref[C_YC : C_YC + BS]
    y_crossing = jnp.where(lane < 32, y_minus * y1[0], roll(y_plus * y1[end], 64))
    x_side_row = jnp.where(row == 0, BS - 1, 0)
    y_ends = jnp.where(lane == 0, roll(y_edges, -1), 0.0)
    y_ends = jnp.where(lane == 31, roll(y_edges, 31), y_ends)
    y_ends = jnp.where(lane == 32, roll(y_edges, 29), y_ends)
    y_ends = jnp.where(lane == 63, roll(y_edges, 61), y_ends)
    z_sides = jnp.where(lane == 0, y_edges, 0.0)
    z_sides = jnp.where(lane == 97, roll(y_edges, 96), z_sides)
    z_sides = jnp.where(lane == 126, roll(y_edges, 124), z_sides)
    z_sides = jnp.where(lane == 95, roll(y_edges, 92), z_sides)
    y_next = (
        roll(y_sides, 64)
        + y_constant * y_crossing
        + roll(y_constant, 64) * y_ends
        + jnp.where(height == x_side_row, keys[2:3] * ends[2:3], 0.0)
        + jnp.where(lane < 32, coarse_of(here1, 2), coarse_of(here0, 3))
    )
    z_crossing = z_bonds * pack(y1)
    z_coarse = jnp.where(
        even_row,
        jnp.where(depth_row < 16, coarse_of(above0, 0), coarse_of(above1, 0)),
        jnp.where(depth_row < 16, coarse_of(below0, 0), coarse_of(below1, 0)),
    )
    z_next = (
        z_second
        + constant_ref[C_ZD : C_ZD + BS] * z_crossing
        + constant_ref[C_ZK : C_ZK + BS] * z_sides
        + jnp.where(height == x_side_row, keys[3:4] * ends[0:1], 0.0)
        + z_coarse
    )
    mapped = stencil(smoothed, bonds, diagonal, brought(x_next, y_next, z_next))
    for c in range(CHUNKS):
        mapped_out[c] = mapped[c]

    values = [
        total_of(mapped[:8]),
        total_of(mapped[8:]),
        total_of([residual[c] * smoothed[c] for c in range(CHUNKS)]),
        total_of([mapped[c] * smoothed[c] for c in range(CHUNKS)]),
    ]
    if not first:
        values.append(total_of([search_ref[c] * smoothed[c] for c in range(CHUNKS)]))
    if last:
        write_copies(tile_out, tile_of(values))
        return
    y1 = [relax_ref[c] * mapped[c] for c in range(CHUNKS)]
    write_copies(tile_out, edge_tile(y1, row, values))
    outcome = stencil(y1, bonds, diagonal)
    partial = [y1[c] + relax_ref[c] * (mapped[c] - outcome[c]) for c in range(CHUNKS)]
    write_xy(xy_out, row, y1, partial)
    z_out[Z_Y1 : Z_Y1 + BS] = pack(y1)
    z_out[Z_P : Z_P + BS] = pack(partial)


def finish_kernel(
    tiles_ref, scalars_ref, residual_ref, mapped_ref, search_ref, first_ref, second_ref, third_ref,
    solution_ref, residual_out,
):
    scalars = scalars_ref[...]
    tiles = sum_tiles(tiles_ref, tiles_ref.shape[0] // 8)
    _, _, step, growth = search_scalars(tiles, scalars, ITERS - 1)
    first_step, second_step, second_growth = scalars[2:3, 0:1], scalars[3:4, 0:1], scalars[4:5, 0:1]
    third_weight = step
    second_weight = second_step + growth * step
    first_weight = first_step + second_growth * second_weight
    for c in range(CHUNKS):
        s, part = c // 8, pl.ds(128 * (c % 8), 128)
        solution_ref[s, :, part] = (
            first_weight * first_ref[c] + second_weight * second_ref[c] + third_weight * third_ref[c]
        )
        residual_out[s, :, part] = residual_ref[c] - step * (mapped_ref[c] + growth * search_ref[c])


def call(kernel, name, outs, in_spaces, out_spaces, operands, scratch=()):
    spec = lambda space: pl.BlockSpec(memory_space=space)
    in_spaces = list(in_spaces) + [pltpu.VMEM] * (len(operands) - len(in_spaces))
    out_spaces = list(out_spaces) + [pltpu.VMEM] * (len(outs) - len(out_spaces))
    return pl.pallas_call(
        kernel,
        out_shape=tuple(outs),
        in_specs=[spec(space) for space in in_spaces],
        out_specs=tuple(spec(space) for space in out_spaces),
        scratch_shapes=list(scratch),
        compiler_params=pltpu.CompilerParams(vmem_limit_bytes=16 * 1024 * 1024),
        name=name,
    )(*operands)


def array(*shape):
    return jax.ShapeDtypeStruct(shape, F32)


def gather_bricks(message):
    return lax.all_gather(message, "brick", axis=0, tiled=False)


def to_all(copies, axes):
    return lax.all_to_all(copies, axes, 0, 0, tiled=True)


def exchange_slabs(message):
    count = lax.axis_size("grp")
    upward = [(i, i + 1) for i in range(count - 1)]
    downward = [(i + 1, i) for i in range(count - 1)]
    return lax.ppermute(message, "grp", downward), lax.ppermute(message, "grp", upward)


def on_device(source, uptake, conductance, occupancy, assignment):
    slabs = lax.axis_size("grp")
    bricks = lax.axis_size("brick")
    place = (lax.axis_index("grp") * bricks + lax.axis_index("brick")).astype(jnp.int32).reshape(1)
    field = array(*FIELD)
    copies = array(8 * slabs * bricks, 128)
    info, bonds, outer, diagonal, residual, sides, ends, tile = call(
        functools.partial(setup_kernel, slabs, bricks),
        "setup",
        [
            jax.ShapeDtypeStruct((8,), jnp.int32), array(3, *FIELD), array(B_ROWS, 128), field, field,
            array(XY_ROWS_FIRST, 128), array(Z_ROWS_FIRST, 128), copies,
        ],
        [pltpu.SMEM] + [pl.ANY] * 5,
        [pltpu.SMEM],
        [
            place, assignment, jnp.transpose(occupancy, (1, 2, 0)),
            source[0, 0], uptake[0, 0], conductance[0, 0],
        ],
        [
            pltpu.SMEM((bricks,), jnp.int32), pltpu.SMEM((2, bricks, slabs), jnp.int32),
            pltpu.VMEM((2, BS, BS * BS), F32), pltpu.VMEM((2, BS, BS * BS), F32),
            pltpu.VMEM((6, 2, BS, BS * BS), F32), pltpu.VMEM(FIELD, F32), pltpu.VMEM(FIELD, F32),
            pltpu.SemaphoreType.DMA((5,)),
        ],
    )
    mapped = residual
    directions = []
    state = {}
    for iteration in range(ITERS):
        first, last = iteration == 0, iteration == ITERS - 1
        tiles = to_all(tile, ("brick", "grp"))
        above, below = exchange_slabs(ends)
        gathered = gather_bricks(sides)
        operands = [info, gathered, above, below, tiles, bonds, outer, diagonal, residual]
        tall = array(8 * slabs, 128)
        outs = {"smoothed": field, "mapped": field}
        if not first:
            operands += [mapped] + [state[k] for k in ("halo", "constant", "factor", "sums", "scalars")]
        if iteration > 1:
            operands += [state[k] for k in ("search", "search_halo", "search_sums")]
        if first:
            outs |= {"constant": array(C_ROWS, 128), "factor": tall, "halo": array(H_ROWS, 128), "sums": tall}
        else:
            outs |= {"residual": field, "search": field, "scalars": array(8, 128)}
            if not last:
                outs |= {
                    "halo": array(H_ROWS, 128), "sums": tall,
                    "search_halo": array(H_ROWS, 128), "search_sums": tall,
                }
        outs["tile"] = copies
        if not last:
            outs |= {"sides": array(XY_ROWS, 128), "ends": array(Z_ROWS, 128)}
        results = call(
            functools.partial(step_kernel, iteration, slabs, bricks),
            f"step_{iteration}",
            list(outs.values()),
            [pltpu.SMEM],
            [],
            operands,
            [pltpu.VMEM(FIELD, F32)],
        )
        state |= dict(zip(outs, results))
        if first:
            state["scalars"] = jnp.zeros((8, 128), F32)
        mapped, tile = state["mapped"], state["tile"]
        sides, ends = state.get("sides"), state.get("ends")
        residual = state.get("residual", residual)
        directions.append(state["smoothed"])
    tiles = to_all(tile, ("brick", "grp"))
    brick_pair = array(2, BS, BS * BS)
    solution_field, residual = call(
        finish_kernel,
        "finish",
        [brick_pair, brick_pair],
        [],
        [],
        [tiles, state["scalars"], residual, mapped, state["search"]] + directions,
    )
    return solution_field[None, None], residual[None, None]


def solution(mesh):
    return jax.shard_map(
        on_device,
        mesh=mesh,
        in_specs=(
            P("grp", "brick", None, None, None),
            P("grp", "brick", None, None, None),
            P("grp", "brick", None, None, None, None),
            P(),
            P(),
        ),
        out_specs=(P("grp", "brick", None, None, None), P("grp", "brick", None, None, None)),
        check_vma=False,
    )
```

```python
import functools

import jax
import jax.numpy as jnp
from jax import lax
from jax.experimental import pallas as pl
from jax.experimental.pallas import tpu as pltpu
from jax.sharding import PartitionSpec as P

BS = 32
CHUNKS = 16
OMEGA = 0.6
ITERS = 3
F32 = jnp.float32
FIELD = (CHUNKS, BS, 128)

XY_X1, XY_XP, XY_Y = 0, 16, 32
XY_ROWS = 64
XY_XD, XY_YC, XY_K = 64, 80, 112
XY_ROWS_FIRST = 120
Z_Y1, Z_P = 0, 32
Z_ROWS = 64
Z_D, Z_K, Z_X = 64, 96, 128
Z_ROWS_FIRST = 136
T_N, T_Y = 16, 64
H_X1, H_Y, H_Z1, H_ZP, H_E, H_R, H_S = 0, 32, 64, 96, 128, 160, 168
C_XD, C_YC, C_ZD, C_ZK, C_K, C_F = 0, 16, 48, 80, 112, 120
B_XP, B_XM, B_YP, B_YM, B_Z = 0, 16, 32, 64, 96
B_ROWS = 128


def roll(block, shift):
    return pltpu.roll(block, shift % 128, axis=1)


def roll_row(row, shift):
    return pltpu.roll(jnp.broadcast_to(row, (8, 128)), shift % 128, axis=1)[0:1]


def lanes(rows=BS):
    return lax.broadcasted_iota(jnp.int32, (rows, 128), 1)


def rows_of(height=BS):
    return lax.broadcasted_iota(jnp.int32, (height, 128), 0)


def pack(chunks):
    height = chunks[0].shape[0]
    pair = (lanes(height) % BS) // 2
    total = jnp.zeros((height, 128), F32)
    for c in range(CHUNKS):
        moved = roll(chunks[c], 2 * c - 31) if height > 1 else roll_row(chunks[c], 2 * c - 31)
        total = jnp.where(pair == c, moved, total)
    return total


def stencil(field, bonds, diagonal, outer=None):
    lane = lanes()
    height = rows_of()
    depth = lane % BS
    at_end = (depth == BS - 1) | (depth == 0)
    back = [roll(f, -32) for f in field]
    forth = [roll(bonds(1, c) * field[c], 32) for c in range(CHUNKS)]
    out = []
    for c in range(CHUNKS):
        f = field[c]
        total = diagonal(c) * f
        total -= bonds(0, c) * pltpu.roll(f, BS - 1, axis=0)
        total -= pltpu.roll(bonds(0, c) * f, 1, axis=0)
        following = back[c + 1] if c < CHUNKS - 1 else back[c]
        previous = forth[c - 1] if c > 0 else jnp.zeros((BS, 128), F32)
        total -= bonds(1, c) * jnp.where(lane < 96, back[c], following)
        total -= jnp.where(lane >= 32, forth[c], previous)
        total -= bonds(2, c) * roll(f, -1)
        total -= roll(bonds(2, c) * f, 1)
        if outer is not None:
            x_up, x_down, y_low, y_high, z_ends = outer
            total -= jnp.where(height == BS - 1, x_up[c : c + 1], 0.0)
            total -= jnp.where(height == 0, x_down[c : c + 1], 0.0)
            total -= jnp.where(at_end, roll(z_ends, 31 - 2 * c), 0.0)
            if c == 0:
                total -= jnp.where(lane < 32, y_low, 0.0)
            if c == CHUNKS - 1:
                total -= jnp.where(lane >= 96, y_high, 0.0)
        out.append(total)
    return out


def total_of(blocks):
    acc = blocks[0]
    for block in blocks[1:]:
        acc = acc + block
    return jnp.sum(jnp.sum(acc, axis=0, keepdims=True), axis=1, keepdims=True)


def facing(block, row):
    return jnp.where(row == 0, block[BS - 1 : BS], block[0:1])


def side_blocks(low_first, high_first, low_second, high_second):
    group = lanes() // 32
    return jnp.where(
        group == 0,
        low_first,
        jnp.where(
            group == 1,
            roll(high_first, 64),
            jnp.where(group == 2, roll(low_second, 64), high_second),
        ),
    )


def write_xy(xy_ref, row, y1, partial):
    for c in range(CHUNKS):
        xy_ref[XY_X1 + c : XY_X1 + c + 1] = facing(y1[c], row)
        xy_ref[XY_XP + c : XY_XP + c + 1] = facing(partial[c], row)
    last = CHUNKS - 1
    xy_ref[XY_Y : XY_Y + BS] = side_blocks(y1[0], y1[last], partial[0], partial[last])


def write_scalars(ref, start, values):
    for i, value in enumerate(values):
        ref[start + i : start + i + 1] = jnp.broadcast_to(value, (1, 128))
    for i in range(len(values), 8):
        ref[start + i : start + i + 1] = jnp.zeros((1, 128), F32)


def tile_of(values, y1=None):
    lane = lanes(8)
    level = rows_of(8)
    tile = jnp.zeros((8, 128), F32)
    for i, value in enumerate(values):
        tile = jnp.where((level == i) & (lane >= T_N) & (lane < T_Y), value, tile)
    if y1 is None:
        return tile
    row, low, high = y1
    tile = jnp.where((level == 0) & (lane >= T_Y), row, tile)
    tile = jnp.where((level == 1) & (lane >= T_Y), roll_row(row, 64), tile)
    wide = lanes()
    edges = jnp.where(wide == 0, low, 0.0)
    edges = jnp.where(wide == 1, roll(low, -30), edges)
    edges = jnp.where(wide == 2, roll(high, -94), edges)
    edges = jnp.where(wide == 3, roll(high, -124), edges)
    for t in range(4):
        tile = tile + roll(edges[8 * t : 8 * t + 8], 4 * t)
    return tile


def repeat_message(ref, rows):
    for k in range(1, ref.shape[0] // rows):
        ref[k * rows : (k + 1) * rows] = ref[0:rows]


def write_copies(ref, tile):
    for k in range(ref.shape[0] // 8):
        ref[8 * k : 8 * k + 8] = tile


def edge_tile(y1, row, values):
    line = pack([facing(f, row) for f in y1])
    return tile_of(values, (line, y1[0], y1[CHUNKS - 1]))


def locate(bricks, place_ref, assignment_ref):
    across = bricks // 2
    place = place_ref[0]
    slab = place // bricks
    patch = assignment_ref[place % bricks]
    row = patch // across
    column = patch % across
    return slab, patch, row, column


def setup_kernel(
    slabs, bricks, place_ref, assignment_hbm, occupancy_hbm, source_hbm, uptake_hbm, conductance_hbm,
    info_ref, bonds_ref, outer_ref, diagonal_ref, residual_ref, xy_ref, z_ref, tile_ref,
    assignment_ref, occupancy_ref, source_ref, uptake_ref, conductance_ref, relax_ref, y1_ref, arrived,
):
    pairs = [
        (assignment_hbm, assignment_ref),
        (occupancy_hbm, occupancy_ref),
        (source_hbm, source_ref),
        (uptake_hbm, uptake_ref),
        (conductance_hbm, conductance_ref),
    ]
    copies = [
        pltpu.make_async_copy(there, here, arrived.at[i]) for i, (there, here) in enumerate(pairs)
    ]
    for copy in copies:
        copy.start()
    for copy in copies:
        copy.wait()
    across = bricks // 2
    slab, patch, row, column = locate(bricks, place_ref, assignment_ref)

    def holder(row_target, column_target):
        inside = (column_target >= 0) & (column_target < across)
        wanted = jnp.where(inside, row_target * across + column_target, patch)
        found = jnp.int32(0)
        for b in range(bricks):
            found = jnp.where(assignment_ref[b] == wanted, b, found)
        return found

    info_ref[0] = row
    info_ref[1] = slab
    info_ref[2] = holder(row, column)
    info_ref[3] = holder(1 - row, column)
    info_ref[4] = holder(row, column - 1)
    info_ref[5] = holder(row, column + 1)
    info_ref[6] = holder(1 - row, column - 1)
    info_ref[7] = holder(1 - row, column + 1)

    breadth = 2 * across

    def live_at(g, x, y):
        inside = (g >= 0) & (g < slabs) & (x >= 0) & (x < 2) & (y >= 0) & (y < breadth)
        taken = occupancy_ref[jnp.clip(x, 0, 1), jnp.clip(y, 0, breadth - 1), jnp.clip(g, 0, slabs - 1)]
        return jnp.where(inside, taken, 0).astype(F32)

    lane = lanes()
    height = rows_of()
    depth = lane % BS
    absorbed = []
    low_ends = []
    high_ends = []
    first_y = None
    second_y = None
    for s in range(2):
        y = column * 2 + s
        here = live_at(slab, row, y)
        around = [
            here * live_at(slab, row + 1, y),
            here * live_at(slab, row - 1, y),
            here * live_at(slab, row, y + 1),
            here * live_at(slab, row, y - 1),
            here * live_at(slab + 1, row, y),
            here * live_at(slab - 1, row, y),
        ]
        borders = [height == BS - 1, height == 0, lane >= 96, lane < 32, depth == BS - 1, depth == 0]
        for k in range(8):
            c = 8 * s + k
            part = pl.ds(128 * k, 128)
            taken = uptake_ref[s, :, part]
            absorbed.append(taken)
            diagonal = taken
            values = []
            for d in range(6):
                bond = conductance_ref[d, s, :, part]
                if (d == 2 and k < 7) or (d == 3 and k > 0):
                    value = bond * here
                else:
                    value = bond * jnp.where(borders[d], around[d], here)
                values.append(value)
                diagonal = diagonal + value
            if c == 7:
                first_y = jnp.where(borders[2], values[2], 0.0)
            if c == 8:
                second_y = jnp.where(borders[3], values[3], 0.0)
            high_ends.append(jnp.where(borders[4], values[4], 0.0))
            low_ends.append(jnp.where(borders[5], values[5], 0.0))
            outer_ref[B_XP + c : B_XP + c + 1] = values[0][BS - 1 : BS]
            outer_ref[B_XM + c : B_XM + c + 1] = values[1][0:1]
            bonds_ref[0, c] = jnp.where(borders[0], 0.0, values[0])
            if c == CHUNKS - 1:
                outer_ref[B_YP : B_YP + BS] = jnp.where(borders[2], values[2], 0.0)
                bonds_ref[1, c] = jnp.where(borders[2], 0.0, values[2])
            else:
                bonds_ref[1, c] = values[2]
            if c == 0:
                outer_ref[B_YM : B_YM + BS] = jnp.where(borders[3], values[3], 0.0)
            bonds_ref[2, c] = jnp.where(borders[4], 0.0, values[4])
            relax = OMEGA / diagonal
            diagonal_ref[c] = diagonal
            relax_ref[c] = relax
            forcing = source_ref[s, :, part] * here
            residual_ref[c] = forcing
            y1_ref[c] = relax * forcing

    ends = [high_ends[c] + low_ends[c] for c in range(CHUNKS)]
    outer_ref[B_Z : B_Z + BS] = pack(ends)
    y1 = [y1_ref[c] for c in range(CHUNKS)]
    outcome = stencil(y1, lambda d, c: bonds_ref[d, c], lambda c: diagonal_ref[c])
    partial = [y1[c] + relax_ref[c] * (residual_ref[c] - outcome[c]) for c in range(CHUNKS)]
    write_xy(xy_ref, row, y1, partial)
    z_ref[Z_Y1 : Z_Y1 + BS] = pack(y1)
    z_ref[Z_P : Z_P + BS] = pack(partial)

    first_coupling = total_of([first_y])
    high_sums = [total_of(high_ends[8 * s : 8 * s + 8]) for s in range(2)]
    low_sums = [total_of(low_ends[8 * s : 8 * s + 8]) for s in range(2)]
    taken_sums = [total_of(absorbed[8 * s : 8 * s + 8]) for s in range(2)]
    residual_sums = [total_of([residual_ref[8 * s + k] for k in range(8)]) for s in range(2)]
    numbers = [
        residual_sums[0],
        residual_sums[1],
        taken_sums[0] + first_coupling + high_sums[0] + low_sums[0],
        taken_sums[1] + total_of([second_y]) + high_sums[1] + low_sums[1],
        first_coupling,
        high_sums[0],
        high_sums[1],
    ]
    write_copies(tile_ref, edge_tile(y1, row, numbers))

    last = CHUNKS - 1
    z_ends = [relax_ref[c] * ends[c] for c in range(CHUNKS)]
    for c in range(CHUNKS):
        xy_ref[XY_XD + c : XY_XD + c + 1] = facing(relax_ref[c], row)
    high_y = relax_ref[last] * outer_ref[B_YP : B_YP + BS]
    low_y = relax_ref[0] * outer_ref[B_YM : B_YM + BS]
    xy_ref[XY_YC : XY_YC + BS] = side_blocks(relax_ref[0], relax_ref[last], z_ends[0], z_ends[last])
    xy_ref[XY_K : XY_K + 1] = facing(low_y + high_y, row)
    xy_ref[XY_K + 1 : XY_K + 2] = pack([facing(z, row) for z in z_ends])
    toward = [
        relax_ref[c][BS - 1 : BS] * outer_ref[B_XP + c : B_XP + c + 1]
        + relax_ref[c][0:1] * outer_ref[B_XM + c : B_XM + c + 1]
        for c in range(CHUNKS)
    ]
    xy_ref[XY_K + 2 : XY_K + 3] = jnp.where(lanes(1) < 32, toward[0], roll_row(toward[last], 64))
    xy_ref[XY_K + 3 : XY_K + 8] = jnp.zeros((5, 128), F32)
    z_ref[Z_D : Z_D + BS] = pack([relax_ref[c] for c in range(CHUNKS)])
    z_ref[Z_K : Z_K + BS] = pack([low_y] + [jnp.zeros((BS, 128), F32)] * (CHUNKS - 2) + [high_y])
    z_ref[Z_X : Z_X + 8] = jnp.broadcast_to(pack(toward), (8, 128))
    repeat_message(xy_ref, XY_ROWS_FIRST)


def swap_sides(from_low, from_high):
    rows = from_low.shape[0]
    if rows == 1:
        low, high = roll_row(from_low, -32), roll_row(from_high, 32)
    else:
        low, high = roll(from_low, -32), roll(from_high, 32)
    return jnp.where((lanes(rows) // 32) % 2 == 0, low, high)


def search_scalars(tiles, scalars, iteration):
    energy = tiles[2:3, T_N : T_N + 1]
    curvature = tiles[3:4, T_N : T_N + 1]
    if iteration == 0:
        return energy, curvature, energy / curvature, None
    growth = energy / scalars[0:1, 0:1]
    curvature = curvature + growth * (2.0 * tiles[4:5, T_N : T_N + 1] + growth * scalars[1:2, 0:1])
    return energy, curvature, energy / curvature, growth


def sum_tiles(ref, count):
    total = ref[0:8]
    for g in range(1, count):
        total = total + ref[8 * g : 8 * g + 8]
    return total


def step_kernel(iteration, slabs, bricks, *refs):
    first = iteration == 0
    last = iteration == ITERS - 1
    refs = list(refs)
    take = lambda count: [refs.pop(0) for _ in range(count)]
    info_ref, xy_ref, above_ref, below_ref, tiles_ref = take(5)
    bonds_ref, outer_ref, diagonal_ref, residual_ref = take(4)
    if not first:
        mapped_ref, halo_in, constant_ref, scalars_in = take(4)
    if iteration > 1:
        search_in, search_halo_in = take(2)
    smoothed_hbm, mapped_out = take(2)
    if first:
        constant_ref, halo_ref = take(2)
    else:
        residual_out, search_ref, scalars_ref = take(3)
        if not last:
            halo_ref, search_halo_ref = take(2)
    tile_out = take(1)[0]
    if not last:
        xy_out, z_out = take(2)
    relax_ref, smoothed_ref, written = take(3)
    for c in range(CHUNKS):
        relax_ref[c] = OMEGA / diagonal_ref[c]

    row = info_ref[0]
    slab = info_ref[1]
    lane = lanes()
    height = rows_of()
    depth = lane % BS
    lane_row = lanes(1)
    even = lane % 2 == 0
    even_row = lane_row % 2 == 0
    low_holder, high_holder = info_ref[4], info_ref[5]
    low_corner, high_corner = info_ref[6], info_ref[7]
    x_holder = info_ref[3]

    def merge(start):
        up = roll(above_ref[start : start + BS], 31)
        down = roll(below_ref[start : start + BS], -31)
        return jnp.where(even, up, down)

    x_sides = xy_ref[x_holder, XY_X1 : XY_X1 + 2 * CHUNKS]
    y_sides = swap_sides(
        xy_ref[low_holder, XY_Y : XY_Y + BS], xy_ref[high_holder, XY_Y : XY_Y + BS]
    )
    z_first = merge(Z_Y1)
    z_second = merge(Z_P)

    def tile_at(holder, g):
        return tiles_ref[pl.ds(pl.multiple_of((holder * slabs + g) * 8, 8), 8)]

    slab_above = jnp.minimum(slab + 1, slabs - 1)
    slab_below = jnp.maximum(slab - 1, 0)

    def edge_row(tile):
        return jnp.where(lane_row >= T_Y, tile[0:1], roll_row(tile[1:2], 64))

    x_ends = jnp.where(
        even_row,
        roll_row(edge_row(tile_at(x_holder, slab_above)), 31),
        roll_row(edge_row(tile_at(x_holder, slab_below)), -31),
    )
    kind = lanes(8) % 4
    mixed = jnp.where(
        kind == 0,
        roll(tile_at(low_holder, slab_above), -2),
        jnp.where(
            kind == 1,
            roll(tile_at(low_holder, slab_below), -2),
            jnp.where(
                kind == 2,
                roll(tile_at(high_holder, slab_above), 2),
                roll(tile_at(high_holder, slab_below), 2),
            ),
        ),
    )
    y_edges = jnp.where(
        lane < 4, jnp.concatenate([roll(mixed, -4 * t) for t in range(4)], axis=0), 0.0
    )
    corner_y = jnp.where(
        lane_row < 32,
        roll_row(xy_ref[low_corner, XY_X1 + CHUNKS - 1 : XY_X1 + CHUNKS], 32),
        roll_row(xy_ref[high_corner, XY_X1 : XY_X1 + 1], -32),
    )
    low_row = jnp.where(
        row == 0,
        xy_ref[low_corner, XY_Y : XY_Y + 1],
        xy_ref[low_corner, XY_Y + BS - 1 : XY_Y + BS],
    )
    high_row = jnp.where(
        row == 0,
        xy_ref[high_corner, XY_Y : XY_Y + 1],
        xy_ref[high_corner, XY_Y + BS - 1 : XY_Y + BS],
    )
    corner_x = swap_sides(low_row, high_row)
    ends = jnp.concatenate([x_ends, corner_y, corner_x, jnp.zeros((5, 128), F32)], axis=0)
    lane_tile = lanes(8)
    slab_tiles = []
    for g in range(slabs):
        tile = tile_at(info_ref[2], g)
        for q in range(1, 4):
            tile = jnp.where(lane_tile == T_N + q, tile_at(info_ref[2 + q], g), tile)
        slab_tiles.append(tile)
    sums = jnp.concatenate(slab_tiles, axis=0)
    halo = [x_sides, y_sides, z_first, z_second, y_edges, ends, sums]
    starts = [H_X1, H_Y, H_Z1, H_ZP, H_E, H_R, H_S]

    if first:
        residual = [residual_ref[c] for c in range(CHUNKS)]
        constant_ref[C_XD : C_XD + CHUNKS] = xy_ref[x_holder, XY_XD : XY_XD + CHUNKS]
        constant_ref[C_YC : C_YC + BS] = swap_sides(
            xy_ref[low_holder, XY_YC : XY_YC + BS], xy_ref[high_holder, XY_YC : XY_YC + BS]
        )
        constant_ref[C_ZD : C_ZD + BS] = merge(Z_D)
        constant_ref[C_ZK : C_ZK + BS] = merge(Z_K)
        constant_ref[C_K : C_K + 8] = jnp.concatenate(
            [
                xy_ref[x_holder, XY_K : XY_K + 2],
                swap_sides(
                    xy_ref[low_holder, XY_K + 2 : XY_K + 3],
                    xy_ref[high_holder, XY_K + 2 : XY_K + 3],
                ),
                jnp.where(
                    even_row,
                    roll_row(above_ref[Z_X : Z_X + 1], 31),
                    roll_row(below_ref[Z_X : Z_X + 1], -31),
                ),
                jnp.zeros((4, 128), F32),
            ],
            axis=0,
        )
        for g in range(slabs):
            tile = sums[8 * g : 8 * g + 8]
            a, b, off = tile[2:3], tile[3:4], tile[4:5]
            t0, t1 = tile[5:6], tile[6:7]
            if g > 0:
                a = a - u0 * u0 * i00
                b = b - u1 * u1 * i11
                off = off + u0 * u1 * i01
            used = (lane_row >= T_N) & (lane_row < T_N + 4)
            a = jnp.where(used, a, 1.0)
            b = jnp.where(used, b, 1.0)
            off = jnp.where(used, off, 0.0)
            t0 = jnp.where(used, t0, 0.0)
            t1 = jnp.where(used, t1, 0.0)
            scale = 1.0 / (a * b - off * off)
            i00, i01, i11 = b * scale, off * scale, a * scale
            u0, u1 = t0, t1
            constant_ref[C_F + 8 * g : C_F + 8 * g + 8] = jnp.concatenate(
                [i00, i01, i11, t0, t1, jnp.zeros((3, 128), F32)], axis=0
            )
    else:
        scalars = None if iteration == 1 else scalars_in[...]
        energy, curvature, step, growth = search_scalars(
            sum_tiles(tiles_ref, slabs * bricks), scalars, iteration - 1
        )
        step_row = jnp.broadcast_to(step, (1, 128))
        residual = []
        for c in range(CHUNKS):
            mapped = mapped_ref[c]
            if growth is not None:
                mapped = mapped + growth * search_in[c]
            search_ref[c] = mapped
            value = residual_ref[c] - step * mapped
            residual_out[c] = value
            residual.append(value)
        old_halo = halo
        halo = []
        for start, block in zip(starts, old_halo):
            span = slice(start, start + block.shape[0])
            if growth is not None:
                block = block + growth * search_halo_in[span]
            if not last:
                search_halo_ref[span] = block
            halo.append(halo_in[span] - step * block)
        kept = [energy, curvature, step]
        if growth is not None:
            kept = [energy, curvature, scalars[2:3, 0:1], step, growth]
        write_scalars(scalars_ref, 0, kept)

    if not last:
        for start, block in zip(starts, halo):
            halo_ref[start : start + block.shape[0]] = block
    x_sides, y_sides, z_first, z_second, y_edges, ends, sums = halo

    forward = []
    for g in range(slabs):
        t0, t1 = sums[8 * g : 8 * g + 1], sums[8 * g + 1 : 8 * g + 2]
        if g > 0:
            t0 = t0 + w0 * v0
            t1 = t1 + w1 * v1
        factor = constant_ref[C_F + 8 * g : C_F + 8 * g + 8]
        v0 = factor[0:1] * t0 + factor[1:2] * t1
        v1 = factor[1:2] * t0 + factor[2:3] * t1
        w0, w1 = factor[3:4], factor[4:5]
        forward.append((v0, v1))
    blank = jnp.zeros((1, 128), F32)
    below0, below1, here0, here1, above0, above1 = [blank] * 6
    for g in reversed(range(slabs)):
        v0, v1 = forward[g]
        if g < slabs - 1:
            factor = constant_ref[C_F + 8 * g : C_F + 8 * g + 8]
            s0, s1 = factor[3:4] * n0, factor[4:5] * n1
            v0 = v0 + factor[0:1] * s0 + factor[1:2] * s1
            v1 = v1 + factor[1:2] * s0 + factor[2:3] * s1
        n0, n1 = v0, v1
        here0 = jnp.where(slab == g, n0, here0)
        here1 = jnp.where(slab == g, n1, here1)
        above0 = jnp.where(slab + 1 == g, n0, above0)
        above1 = jnp.where(slab + 1 == g, n1, above1)
        below0 = jnp.where(slab - 1 == g, n0, below0)
        below1 = jnp.where(slab - 1 == g, n1, below1)
    def coarse_of(row, q):
        return row[:, T_N + q : T_N + q + 1]

    own = [coarse_of(here0, 0), coarse_of(here1, 0)]

    bonds = lambda d, c: bonds_ref[d, c]
    diagonal = lambda c: diagonal_ref[c]
    end = CHUNKS - 1
    x_plus = outer_ref[B_XP : B_XP + CHUNKS]
    x_minus = outer_ref[B_XM : B_XM + CHUNKS]
    y_plus = outer_ref[B_YP : B_YP + BS]
    y_minus = outer_ref[B_YM : B_YM + BS]
    z_bonds = outer_ref[B_Z : B_Z + BS]

    def brought(x_rows, y_block, z_block):
        return (
            x_plus * x_rows,
            x_minus * x_rows,
            y_minus * y_block,
            y_plus * roll(y_block, 64),
            z_bonds * z_block,
        )

    y1 = [relax_ref[c] * residual[c] for c in range(CHUNKS)]
    outcome = stencil(y1, bonds, diagonal, brought(x_sides[:CHUNKS], y_sides, z_first))
    smoothed = []
    for c in range(CHUNKS):
        value = y1[c] + relax_ref[c] * (residual[c] - outcome[c]) + own[c // 8]
        smoothed_ref[c] = value
        smoothed.append(value)
    writing = pltpu.make_async_copy(smoothed_ref, smoothed_hbm, written)
    writing.start()
    keys = constant_ref[C_K : C_K + 8]
    crossing = x_plus * jnp.concatenate([f[BS - 1 : BS] for f in y1], axis=0)
    crossing += x_minus * jnp.concatenate([f[0:1] for f in y1], axis=0)
    end_row = keys[1:2] * ends[0:1]
    corner_row = keys[0:1] * ends[1:2]
    depth_row = lane_row % BS
    additions = []
    for c in range(CHUNKS):
        value = jnp.where(
            (depth_row == BS - 1) | (depth_row == 0), roll_row(end_row, 31 - 2 * c), 0.0
        )
        if c == 0:
            value = value + jnp.where(lane_row < 32, corner_row, 0.0)
        if c == end:
            value = value + jnp.where(lane_row >= 96, corner_row, 0.0)
        value = value + coarse_of(here0 if c < 8 else here1, 1)
        additions.append(value)
    x_next = (
        x_sides[CHUNKS:]
        + constant_ref[C_XD : C_XD + CHUNKS] * crossing
        + jnp.concatenate(additions, axis=0)
    )
    y_constant = constant_ref[C_YC : C_YC + BS]
    y_crossing = jnp.where(lane < 32, y_minus * y1[0], roll(y_plus * y1[end], 64))
    x_side_row = jnp.where(row == 0, BS - 1, 0)
    y_ends = jnp.where(lane == 0, roll(y_edges, -1), 0.0)
    y_ends = jnp.where(lane == 31, roll(y_edges, 31), y_ends)
    y_ends = jnp.where(lane == 32, roll(y_edges, 29), y_ends)
    y_ends = jnp.where(lane == 63, roll(y_edges, 61), y_ends)
    z_sides = jnp.where(lane == 0, y_edges, 0.0)
    z_sides = jnp.where(lane == 97, roll(y_edges, 96), z_sides)
    z_sides = jnp.where(lane == 126, roll(y_edges, 124), z_sides)
    z_sides = jnp.where(lane == 95, roll(y_edges, 92), z_sides)
    y_next = (
        roll(y_sides, 64)
        + y_constant * y_crossing
        + roll(y_constant, 64) * y_ends
        + jnp.where(height == x_side_row, keys[2:3] * ends[2:3], 0.0)
        + jnp.where(lane < 32, coarse_of(here1, 2), coarse_of(here0, 3))
    )
    z_crossing = z_bonds * pack(y1)
    z_coarse = jnp.where(
        even_row,
        jnp.where(depth_row < 16, coarse_of(above0, 0), coarse_of(above1, 0)),
        jnp.where(depth_row < 16, coarse_of(below0, 0), coarse_of(below1, 0)),
    )
    z_next = (
        z_second
        + constant_ref[C_ZD : C_ZD + BS] * z_crossing
        + constant_ref[C_ZK : C_ZK + BS] * z_sides
        + jnp.where(height == x_side_row, keys[3:4] * ends[0:1], 0.0)
        + z_coarse
    )
    mapped = stencil(smoothed, bonds, diagonal, brought(x_next, y_next, z_next))
    for c in range(CHUNKS):
        mapped_out[c] = mapped[c]

    values = [
        total_of(mapped[:8]),
        total_of(mapped[8:]),
        total_of([residual[c] * smoothed[c] for c in range(CHUNKS)]),
        total_of([mapped[c] * smoothed[c] for c in range(CHUNKS)]),
    ]
    if not first:
        values.append(total_of([search_ref[c] * smoothed[c] for c in range(CHUNKS)]))
    if last:
        write_copies(tile_out, tile_of(values))
        writing.wait()
        return
    y1 = [relax_ref[c] * mapped[c] for c in range(CHUNKS)]
    write_copies(tile_out, edge_tile(y1, row, values))
    outcome = stencil(y1, bonds, diagonal)
    partial = [y1[c] + relax_ref[c] * (mapped[c] - outcome[c]) for c in range(CHUNKS)]
    write_xy(xy_out, row, y1, partial)
    z_out[Z_Y1 : Z_Y1 + BS] = pack(y1)
    z_out[Z_P : Z_P + BS] = pack(partial)
    repeat_message(xy_out, XY_ROWS)
    writing.wait()


def finish_kernel(
    tiles_ref, scalars_ref, residual_ref, mapped_ref, search_ref, first_ref, second_ref, third_ref,
    solution_ref, residual_out,
):
    scalars = scalars_ref[...]
    tiles = sum_tiles(tiles_ref, tiles_ref.shape[0] // 8)
    _, _, step, growth = search_scalars(tiles, scalars, ITERS - 1)
    first_step, second_step, second_growth = scalars[2:3, 0:1], scalars[3:4, 0:1], scalars[4:5, 0:1]
    third_weight = step
    second_weight = second_step + growth * step
    first_weight = first_step + second_growth * second_weight
    for c in range(CHUNKS):
        s, part = c // 8, pl.ds(128 * (c % 8), 128)
        solution_ref[s, :, part] = (
            first_weight * first_ref[c] + second_weight * second_ref[c] + third_weight * third_ref[c]
        )
        residual_out[s, :, part] = residual_ref[c] - step * (mapped_ref[c] + growth * search_ref[c])


def call(kernel, name, outs, in_spaces, out_spaces, operands, scratch=()):
    spec = lambda space: pl.BlockSpec(memory_space=space)
    in_spaces = list(in_spaces) + [pltpu.VMEM] * (len(operands) - len(in_spaces))
    out_spaces = list(out_spaces) + [pltpu.VMEM] * (len(outs) - len(out_spaces))
    return pl.pallas_call(
        kernel,
        out_shape=tuple(outs),
        in_specs=[spec(space) for space in in_spaces],
        out_specs=tuple(spec(space) for space in out_spaces),
        scratch_shapes=list(scratch),
        compiler_params=pltpu.CompilerParams(vmem_limit_bytes=16 * 1024 * 1024),
        name=name,
    )(*operands)


def array(*shape):
    return jax.ShapeDtypeStruct(shape, F32)


def to_all(copies, axes):
    return lax.all_to_all(copies, axes, 0, 0, tiled=True)


def exchange_slabs(message):
    count = lax.axis_size("grp")
    upward = [(i, i + 1) for i in range(count - 1)]
    downward = [(i + 1, i) for i in range(count - 1)]
    return lax.ppermute(message, "grp", downward), lax.ppermute(message, "grp", upward)


def on_device(source, uptake, conductance, occupancy, assignment):
    slabs = lax.axis_size("grp")
    bricks = lax.axis_size("brick")
    place = (lax.axis_index("grp") * bricks + lax.axis_index("brick")).astype(jnp.int32).reshape(1)
    field = array(*FIELD)
    copies = array(8 * slabs * bricks, 128)
    info, bonds, outer, diagonal, residual, sides, ends, tile = call(
        functools.partial(setup_kernel, slabs, bricks),
        "setup",
        [
            jax.ShapeDtypeStruct((8,), jnp.int32), array(3, *FIELD), array(B_ROWS, 128), field, field,
            array(bricks * XY_ROWS_FIRST, 128), array(Z_ROWS_FIRST, 128), copies,
        ],
        [pltpu.SMEM] + [pltpu.HBM] * 5,
        [pltpu.SMEM],
        [
            place, assignment, jnp.transpose(occupancy, (1, 2, 0)),
            source[0, 0], uptake[0, 0], conductance[0, 0],
        ],
        [
            pltpu.SMEM((bricks,), jnp.int32), pltpu.SMEM((2, bricks, slabs), jnp.int32),
            pltpu.VMEM((2, BS, BS * BS), F32), pltpu.VMEM((2, BS, BS * BS), F32),
            pltpu.VMEM((6, 2, BS, BS * BS), F32), pltpu.VMEM(FIELD, F32), pltpu.VMEM(FIELD, F32),
            pltpu.SemaphoreType.DMA((5,)),
        ],
    )
    mapped = residual
    directions = []
    state = {}
    for iteration in range(ITERS):
        first, last = iteration == 0, iteration == ITERS - 1
        tiles = to_all(tile, ("brick", "grp"))
        above, below = exchange_slabs(ends)
        gathered = to_all(sides, "brick").reshape(bricks, -1, 128)
        operands = [info, gathered, above, below, tiles, bonds, outer, diagonal, residual]
        tall = array(H_S + 8 * slabs, 128)
        outs = {"smoothed": field, "mapped": field}
        if not first:
            operands += [mapped] + [state[k] for k in ("halo", "constant", "scalars")]
        if iteration > 1:
            operands += [state[k] for k in ("search", "search_halo")]
        if first:
            outs |= {"constant": array(C_F + 8 * slabs, 128), "halo": tall}
        else:
            outs |= {"residual": field, "search": field, "scalars": array(8, 128)}
            if not last:
                outs |= {"halo": tall, "search_halo": tall}
        outs["tile"] = copies
        if not last:
            outs |= {"sides": array(bricks * XY_ROWS, 128), "ends": array(Z_ROWS, 128)}
        results = call(
            functools.partial(step_kernel, iteration, slabs, bricks),
            f"step_{iteration}",
            list(outs.values()),
            [pltpu.SMEM],
            [pltpu.HBM],
            operands,
            [pltpu.VMEM(FIELD, F32), pltpu.VMEM(FIELD, F32), pltpu.SemaphoreType.DMA],
        )
        state |= dict(zip(outs, results))
        if first:
            state["scalars"] = jnp.zeros((8, 128), F32)
        mapped, tile = state["mapped"], state["tile"]
        sides, ends = state.get("sides"), state.get("ends")
        residual = state.get("residual", residual)
        directions.append(state["smoothed"])
    tiles = to_all(tile, ("brick", "grp"))
    brick_pair = array(2, BS, BS * BS)
    solution_field, residual = call(
        finish_kernel,
        "finish",
        [brick_pair, brick_pair],
        [],
        [],
        [tiles, state["scalars"], residual, mapped, state["search"]] + directions,
    )
    return solution_field[None, None], residual[None, None]


def solution(mesh):
    return jax.shard_map(
        on_device,
        mesh=mesh,
        in_specs=(
            P("grp", "brick", None, None, None),
            P("grp", "brick", None, None, None),
            P("grp", "brick", None, None, None, None),
            P(),
            P(),
        ),
        out_specs=(P("grp", "brick", None, None, None), P("grp", "brick", None, None, None)),
        check_vma=False,
    )
```

```python
import functools

import jax
import jax.numpy as jnp
from jax import lax
from jax.experimental import pallas as pl
from jax.experimental.pallas import tpu as pltpu
from jax.sharding import PartitionSpec as P

BS = 32
CHUNKS = 16
OMEGA = 0.6
ITERS = 3
F32 = jnp.float32
FIELD = (CHUNKS, BS, 128)

XY_X1, XY_XP, XY_Y = 0, 16, 32
XY_ROWS = 64
XY_XD, XY_YC, XY_K = 64, 80, 112
XY_ROWS_FIRST = 120
Z_Y1, Z_P = 0, 32
Z_ROWS = 64
Z_D, Z_K, Z_X = 64, 96, 128
Z_ROWS_FIRST = 136
T_N, T_Y = 16, 64
H_X1, H_Y, H_Z1, H_ZP, H_E, H_R, H_S = 0, 32, 64, 96, 128, 160, 168
C_XD, C_YC, C_ZD, C_ZK, C_K, C_F = 0, 16, 48, 80, 112, 120
B_XP, B_XM, B_YP, B_YM, B_Z = 0, 16, 32, 64, 96
B_ROWS = 128


def roll(block, shift):
    return pltpu.roll(block, shift % 128, axis=1)


def roll_row(row, shift):
    return pltpu.roll(jnp.broadcast_to(row, (8, 128)), shift % 128, axis=1)[0:1]


def lanes(rows=BS):
    return lax.broadcasted_iota(jnp.int32, (rows, 128), 1)


def rows_of(height=BS):
    return lax.broadcasted_iota(jnp.int32, (height, 128), 0)


def pack(chunks):
    height = chunks[0].shape[0]
    pair = (lanes(height) % BS) // 2
    total = jnp.zeros((height, 128), F32)
    for c in range(CHUNKS):
        moved = roll(chunks[c], 2 * c - 31) if height > 1 else roll_row(chunks[c], 2 * c - 31)
        total = jnp.where(pair == c, moved, total)
    return total


def stencil(field, bonds, diagonal, outer=None):
    lane = lanes()
    height = rows_of()
    depth = lane % BS
    at_end = (depth == BS - 1) | (depth == 0)
    back = [roll(f, -32) for f in field]
    forth = [roll(bonds(1, c) * field[c], 32) for c in range(CHUNKS)]
    out = []
    for c in range(CHUNKS):
        f = field[c]
        total = diagonal(c) * f
        total -= bonds(0, c) * pltpu.roll(f, BS - 1, axis=0)
        total -= pltpu.roll(bonds(0, c) * f, 1, axis=0)
        following = back[c + 1] if c < CHUNKS - 1 else back[c]
        previous = forth[c - 1] if c > 0 else jnp.zeros((BS, 128), F32)
        total -= bonds(1, c) * jnp.where(lane < 96, back[c], following)
        total -= jnp.where(lane >= 32, forth[c], previous)
        total -= bonds(2, c) * roll(f, -1)
        total -= roll(bonds(2, c) * f, 1)
        if outer is not None:
            x_up, x_down, y_low, y_high, z_ends = outer
            total -= jnp.where(height == BS - 1, x_up[c : c + 1], 0.0)
            total -= jnp.where(height == 0, x_down[c : c + 1], 0.0)
            total -= jnp.where(at_end, roll(z_ends, 31 - 2 * c), 0.0)
            if c == 0:
                total -= jnp.where(lane < 32, y_low, 0.0)
            if c == CHUNKS - 1:
                total -= jnp.where(lane >= 96, y_high, 0.0)
        out.append(total)
    return out


def total_of(blocks):
    acc = blocks[0]
    for block in blocks[1:]:
        acc = acc + block
    return jnp.sum(jnp.sum(acc, axis=0, keepdims=True), axis=1, keepdims=True)


def facing(block, row):
    return jnp.where(row == 0, block[BS - 1 : BS], block[0:1])


def side_blocks(low_first, high_first, low_second, high_second):
    group = lanes() // 32
    return jnp.where(
        group == 0,
        low_first,
        jnp.where(
            group == 1,
            roll(high_first, 64),
            jnp.where(group == 2, roll(low_second, 64), high_second),
        ),
    )


def write_xy(xy_ref, row, y1, partial):
    for c in range(CHUNKS):
        xy_ref[XY_X1 + c : XY_X1 + c + 1] = facing(y1[c], row)
        xy_ref[XY_XP + c : XY_XP + c + 1] = facing(partial[c], row)
    last = CHUNKS - 1
    xy_ref[XY_Y : XY_Y + BS] = side_blocks(y1[0], y1[last], partial[0], partial[last])


def write_scalars(ref, start, values):
    for i, value in enumerate(values):
        ref[start + i : start + i + 1] = jnp.broadcast_to(value, (1, 128))
    for i in range(len(values), 8):
        ref[start + i : start + i + 1] = jnp.zeros((1, 128), F32)


def tile_of(values, y1=None):
    lane = lanes(8)
    level = rows_of(8)
    tile = jnp.zeros((8, 128), F32)
    for i, value in enumerate(values):
        tile = jnp.where((level == i) & (lane >= T_N) & (lane < T_Y), value, tile)
    if y1 is None:
        return tile
    row, low, high = y1
    tile = jnp.where((level == 0) & (lane >= T_Y), row, tile)
    tile = jnp.where((level == 1) & (lane >= T_Y), roll_row(row, 64), tile)
    wide = lanes()
    edges = jnp.where(wide == 0, low, 0.0)
    edges = jnp.where(wide == 1, roll(low, -30), edges)
    edges = jnp.where(wide == 2, roll(high, -94), edges)
    edges = jnp.where(wide == 3, roll(high, -124), edges)
    for t in range(4):
        tile = tile + roll(edges[8 * t : 8 * t + 8], 4 * t)
    return tile


def write_copies(ref, tile):
    for k in range(ref.shape[0] // 8):
        ref[8 * k : 8 * k + 8] = tile


def edge_tile(y1, row, values):
    line = pack([facing(f, row) for f in y1])
    return tile_of(values, (line, y1[0], y1[CHUNKS - 1]))


def locate(bricks, place_ref, assignment_ref):
    across = bricks // 2
    place = place_ref[0]
    slab = place // bricks
    patch = assignment_ref[place % bricks]
    row = patch // across
    column = patch % across
    return slab, patch, row, column


def setup_kernel(
    slabs, bricks, place_ref, assignment_ref, occupancy_ref, source_ref, uptake_ref, conductance_ref,
    info_ref, bonds_ref, outer_ref, diagonal_ref, residual_ref, xy_ref, z_ref, tile_ref,
    relax_ref, y1_ref,
):
    across = bricks // 2
    slab, patch, row, column = locate(bricks, place_ref, assignment_ref)

    def holder(row_target, column_target):
        inside = (column_target >= 0) & (column_target < across)
        wanted = jnp.where(inside, row_target * across + column_target, patch)
        found = jnp.int32(0)
        for b in range(bricks):
            found = jnp.where(assignment_ref[b] == wanted, b, found)
        return found

    info_ref[0] = row
    info_ref[1] = slab
    info_ref[2] = holder(row, column)
    info_ref[3] = holder(1 - row, column)
    info_ref[4] = holder(row, column - 1)
    info_ref[5] = holder(row, column + 1)
    info_ref[6] = holder(1 - row, column - 1)
    info_ref[7] = holder(1 - row, column + 1)

    breadth = 2 * across

    def live_at(g, x, y):
        inside = (g >= 0) & (g < slabs) & (x >= 0) & (x < 2) & (y >= 0) & (y < breadth)
        taken = occupancy_ref[jnp.clip(x, 0, 1), jnp.clip(y, 0, breadth - 1), jnp.clip(g, 0, slabs - 1)]
        return jnp.where(inside, taken, 0).astype(F32)

    lane = lanes()
    height = rows_of()
    depth = lane % BS
    absorbed = []
    low_ends = []
    high_ends = []
    first_y = None
    second_y = None
    for s in range(2):
        y = column * 2 + s
        here = live_at(slab, row, y)
        around = [
            here * live_at(slab, row + 1, y),
            here * live_at(slab, row - 1, y),
            here * live_at(slab, row, y + 1),
            here * live_at(slab, row, y - 1),
            here * live_at(slab + 1, row, y),
            here * live_at(slab - 1, row, y),
        ]
        borders = [height == BS - 1, height == 0, lane >= 96, lane < 32, depth == BS - 1, depth == 0]
        for k in range(8):
            c = 8 * s + k
            part = pl.ds(128 * k, 128)
            taken = uptake_ref[s, :, part]
            absorbed.append(taken)
            diagonal = taken
            values = []
            for d in range(6):
                bond = conductance_ref[d, s, :, part]
                if (d == 2 and k < 7) or (d == 3 and k > 0):
                    value = bond * here
                else:
                    value = bond * jnp.where(borders[d], around[d], here)
                values.append(value)
                diagonal = diagonal + value
            if c == 7:
                first_y = jnp.where(borders[2], values[2], 0.0)
            if c == 8:
                second_y = jnp.where(borders[3], values[3], 0.0)
            high_ends.append(jnp.where(borders[4], values[4], 0.0))
            low_ends.append(jnp.where(borders[5], values[5], 0.0))
            outer_ref[B_XP + c : B_XP + c + 1] = values[0][BS - 1 : BS]
            outer_ref[B_XM + c : B_XM + c + 1] = values[1][0:1]
            bonds_ref[0, c] = jnp.where(borders[0], 0.0, values[0])
            if c == CHUNKS - 1:
                outer_ref[B_YP : B_YP + BS] = jnp.where(borders[2], values[2], 0.0)
                bonds_ref[1, c] = jnp.where(borders[2], 0.0, values[2])
            else:
                bonds_ref[1, c] = values[2]
            if c == 0:
                outer_ref[B_YM : B_YM + BS] = jnp.where(borders[3], values[3], 0.0)
            bonds_ref[2, c] = jnp.where(borders[4], 0.0, values[4])
            relax = OMEGA / diagonal
            diagonal_ref[c] = diagonal
            relax_ref[c] = relax
            forcing = source_ref[s, :, part] * here
            residual_ref[c] = forcing
            y1_ref[c] = relax * forcing

    ends = [high_ends[c] + low_ends[c] for c in range(CHUNKS)]
    outer_ref[B_Z : B_Z + BS] = pack(ends)
    y1 = [y1_ref[c] for c in range(CHUNKS)]
    outcome = stencil(y1, lambda d, c: bonds_ref[d, c], lambda c: diagonal_ref[c])
    partial = [y1[c] + relax_ref[c] * (residual_ref[c] - outcome[c]) for c in range(CHUNKS)]
    write_xy(xy_ref, row, y1, partial)
    z_ref[Z_Y1 : Z_Y1 + BS] = pack(y1)
    z_ref[Z_P : Z_P + BS] = pack(partial)

    first_coupling = total_of([first_y])
    high_sums = [total_of(high_ends[8 * s : 8 * s + 8]) for s in range(2)]
    low_sums = [total_of(low_ends[8 * s : 8 * s + 8]) for s in range(2)]
    taken_sums = [total_of(absorbed[8 * s : 8 * s + 8]) for s in range(2)]
    residual_sums = [total_of([residual_ref[8 * s + k] for k in range(8)]) for s in range(2)]
    numbers = [
        residual_sums[0],
        residual_sums[1],
        taken_sums[0] + first_coupling + high_sums[0] + low_sums[0],
        taken_sums[1] + total_of([second_y]) + high_sums[1] + low_sums[1],
        first_coupling,
        high_sums[0],
        high_sums[1],
    ]
    write_copies(tile_ref, edge_tile(y1, row, numbers))

    last = CHUNKS - 1
    z_ends = [relax_ref[c] * ends[c] for c in range(CHUNKS)]
    for c in range(CHUNKS):
        xy_ref[XY_XD + c : XY_XD + c + 1] = facing(relax_ref[c], row)
    high_y = relax_ref[last] * outer_ref[B_YP : B_YP + BS]
    low_y = relax_ref[0] * outer_ref[B_YM : B_YM + BS]
    xy_ref[XY_YC : XY_YC + BS] = side_blocks(relax_ref[0], relax_ref[last], z_ends[0], z_ends[last])
    xy_ref[XY_K : XY_K + 1] = facing(low_y + high_y, row)
    xy_ref[XY_K + 1 : XY_K + 2] = pack([facing(z, row) for z in z_ends])
    toward = [
        relax_ref[c][BS - 1 : BS] * outer_ref[B_XP + c : B_XP + c + 1]
        + relax_ref[c][0:1] * outer_ref[B_XM + c : B_XM + c + 1]
        for c in range(CHUNKS)
    ]
    xy_ref[XY_K + 2 : XY_K + 3] = jnp.where(lanes(1) < 32, toward[0], roll_row(toward[last], 64))
    xy_ref[XY_K + 3 : XY_K + 8] = jnp.zeros((5, 128), F32)
    z_ref[Z_D : Z_D + BS] = pack([relax_ref[c] for c in range(CHUNKS)])
    z_ref[Z_K : Z_K + BS] = pack([low_y] + [jnp.zeros((BS, 128), F32)] * (CHUNKS - 2) + [high_y])
    z_ref[Z_X : Z_X + 8] = jnp.broadcast_to(pack(toward), (8, 128))


def swap_sides(from_low, from_high):
    rows = from_low.shape[0]
    if rows == 1:
        low, high = roll_row(from_low, -32), roll_row(from_high, 32)
    else:
        low, high = roll(from_low, -32), roll(from_high, 32)
    return jnp.where((lanes(rows) // 32) % 2 == 0, low, high)


def search_scalars(tiles, scalars, iteration):
    energy = tiles[2:3, T_N : T_N + 1]
    curvature = tiles[3:4, T_N : T_N + 1]
    if iteration == 0:
        return energy, curvature, energy / curvature, None
    growth = energy / scalars[0:1, 0:1]
    curvature = curvature + growth * (2.0 * tiles[4:5, T_N : T_N + 1] + growth * scalars[1:2, 0:1])
    return energy, curvature, energy / curvature, growth


def sum_tiles(ref, count):
    total = ref[0:8]
    for g in range(1, count):
        total = total + ref[8 * g : 8 * g + 8]
    return total


def step_kernel(iteration, slabs, bricks, *refs):
    first = iteration == 0
    last = iteration == ITERS - 1
    refs = list(refs)
    take = lambda count: [refs.pop(0) for _ in range(count)]
    info_ref, xy_ref, above_ref, below_ref, tiles_ref = take(5)
    bonds_ref, outer_ref, diagonal_ref, residual_ref = take(4)
    if not first:
        mapped_ref, halo_in, constant_ref, scalars_in = take(4)
    if iteration > 1:
        search_in, search_halo_in = take(2)
    smoothed_hbm, mapped_out = take(2)
    if first:
        constant_ref, halo_ref = take(2)
    else:
        residual_out, search_ref, scalars_ref = take(3)
        if not last:
            halo_ref, search_halo_ref = take(2)
    tile_out = take(1)[0]
    if not last:
        xy_out, z_out = take(2)
    relax_ref, smoothed_ref, written = take(3)
    for c in range(CHUNKS):
        relax_ref[c] = OMEGA / diagonal_ref[c]

    row = info_ref[0]
    slab = info_ref[1]
    lane = lanes()
    height = rows_of()
    depth = lane % BS
    lane_row = lanes(1)
    even = lane % 2 == 0
    even_row = lane_row % 2 == 0
    low_holder, high_holder = info_ref[4], info_ref[5]
    low_corner, high_corner = info_ref[6], info_ref[7]
    x_holder = info_ref[3]

    def merge(start):
        up = roll(above_ref[start : start + BS], 31)
        down = roll(below_ref[start : start + BS], -31)
        return jnp.where(even, up, down)

    x_sides = xy_ref[x_holder, XY_X1 : XY_X1 + 2 * CHUNKS]
    y_sides = swap_sides(
        xy_ref[low_holder, XY_Y : XY_Y + BS], xy_ref[high_holder, XY_Y : XY_Y + BS]
    )
    z_first = merge(Z_Y1)
    z_second = merge(Z_P)

    def tile_at(holder, g):
        return tiles_ref[pl.ds(pl.multiple_of((holder * slabs + g) * 8, 8), 8)]

    slab_above = jnp.minimum(slab + 1, slabs - 1)
    slab_below = jnp.maximum(slab - 1, 0)

    def edge_row(tile):
        return jnp.where(lane_row >= T_Y, tile[0:1], roll_row(tile[1:2], 64))

    x_ends = jnp.where(
        even_row,
        roll_row(edge_row(tile_at(x_holder, slab_above)), 31),
        roll_row(edge_row(tile_at(x_holder, slab_below)), -31),
    )
    kind = lanes(8) % 4
    mixed = jnp.where(
        kind == 0,
        roll(tile_at(low_holder, slab_above), -2),
        jnp.where(
            kind == 1,
            roll(tile_at(low_holder, slab_below), -2),
            jnp.where(
                kind == 2,
                roll(tile_at(high_holder, slab_above), 2),
                roll(tile_at(high_holder, slab_below), 2),
            ),
        ),
    )
    y_edges = jnp.where(
        lane < 4, jnp.concatenate([roll(mixed, -4 * t) for t in range(4)], axis=0), 0.0
    )
    corner_y = jnp.where(
        lane_row < 32,
        roll_row(xy_ref[low_corner, XY_X1 + CHUNKS - 1 : XY_X1 + CHUNKS], 32),
        roll_row(xy_ref[high_corner, XY_X1 : XY_X1 + 1], -32),
    )
    low_row = jnp.where(
        row == 0,
        xy_ref[low_corner, XY_Y : XY_Y + 1],
        xy_ref[low_corner, XY_Y + BS - 1 : XY_Y + BS],
    )
    high_row = jnp.where(
        row == 0,
        xy_ref[high_corner, XY_Y : XY_Y + 1],
        xy_ref[high_corner, XY_Y + BS - 1 : XY_Y + BS],
    )
    corner_x = swap_sides(low_row, high_row)
    ends = jnp.concatenate([x_ends, corner_y, corner_x, jnp.zeros((5, 128), F32)], axis=0)
    lane_tile = lanes(8)
    slab_tiles = []
    for g in range(slabs):
        tile = tile_at(info_ref[2], g)
        for q in range(1, 4):
            tile = jnp.where(lane_tile == T_N + q, tile_at(info_ref[2 + q], g), tile)
        slab_tiles.append(tile)
    sums = jnp.concatenate(slab_tiles, axis=0)
    halo = [x_sides, y_sides, z_first, z_second, y_edges, ends, sums]
    starts = [H_X1, H_Y, H_Z1, H_ZP, H_E, H_R, H_S]

    if first:
        residual = [residual_ref[c] for c in range(CHUNKS)]
        constant_ref[C_XD : C_XD + CHUNKS] = xy_ref[x_holder, XY_XD : XY_XD + CHUNKS]
        constant_ref[C_YC : C_YC + BS] = swap_sides(
            xy_ref[low_holder, XY_YC : XY_YC + BS], xy_ref[high_holder, XY_YC : XY_YC + BS]
        )
        constant_ref[C_ZD : C_ZD + BS] = merge(Z_D)
        constant_ref[C_ZK : C_ZK + BS] = merge(Z_K)
        constant_ref[C_K : C_K + 8] = jnp.concatenate(
            [
                xy_ref[x_holder, XY_K : XY_K + 2],
                swap_sides(
                    xy_ref[low_holder, XY_K + 2 : XY_K + 3],
                    xy_ref[high_holder, XY_K + 2 : XY_K + 3],
                ),
                jnp.where(
                    even_row,
                    roll_row(above_ref[Z_X : Z_X + 1], 31),
                    roll_row(below_ref[Z_X : Z_X + 1], -31),
                ),
                jnp.zeros((4, 128), F32),
            ],
            axis=0,
        )
        for g in range(slabs):
            tile = sums[8 * g : 8 * g + 8]
            a, b, off = tile[2:3], tile[3:4], tile[4:5]
            t0, t1 = tile[5:6], tile[6:7]
            if g > 0:
                a = a - u0 * u0 * i00
                b = b - u1 * u1 * i11
                off = off + u0 * u1 * i01
            used = (lane_row >= T_N) & (lane_row < T_N + 4)
            a = jnp.where(used, a, 1.0)
            b = jnp.where(used, b, 1.0)
            off = jnp.where(used, off, 0.0)
            t0 = jnp.where(used, t0, 0.0)
            t1 = jnp.where(used, t1, 0.0)
            scale = 1.0 / (a * b - off * off)
            i00, i01, i11 = b * scale, off * scale, a * scale
            u0, u1 = t0, t1
            constant_ref[C_F + 8 * g : C_F + 8 * g + 8] = jnp.concatenate(
                [i00, i01, i11, t0, t1, jnp.zeros((3, 128), F32)], axis=0
            )
    else:
        scalars = None if iteration == 1 else scalars_in[...]
        energy, curvature, step, growth = search_scalars(
            sum_tiles(tiles_ref, slabs * bricks), scalars, iteration - 1
        )
        step_row = jnp.broadcast_to(step, (1, 128))
        residual = []
        for c in range(CHUNKS):
            mapped = mapped_ref[c]
            if growth is not None:
                mapped = mapped + growth * search_in[c]
            search_ref[c] = mapped
            value = residual_ref[c] - step * mapped
            residual_out[c] = value
            residual.append(value)
        old_halo = halo
        halo = []
        for start, block in zip(starts, old_halo):
            span = slice(start, start + block.shape[0])
            if growth is not None:
                block = block + growth * search_halo_in[span]
            if not last:
                search_halo_ref[span] = block
            halo.append(halo_in[span] - step * block)
        kept = [energy, curvature, step]
        if growth is not None:
            kept = [energy, curvature, scalars[2:3, 0:1], step, growth]
        write_scalars(scalars_ref, 0, kept)

    if not last:
        for start, block in zip(starts, halo):
            halo_ref[start : start + block.shape[0]] = block
    x_sides, y_sides, z_first, z_second, y_edges, ends, sums = halo

    forward = []
    for g in range(slabs):
        t0, t1 = sums[8 * g : 8 * g + 1], sums[8 * g + 1 : 8 * g + 2]
        if g > 0:
            t0 = t0 + w0 * v0
            t1 = t1 + w1 * v1
        factor = constant_ref[C_F + 8 * g : C_F + 8 * g + 8]
        v0 = factor[0:1] * t0 + factor[1:2] * t1
        v1 = factor[1:2] * t0 + factor[2:3] * t1
        w0, w1 = factor[3:4], factor[4:5]
        forward.append((v0, v1))
    blank = jnp.zeros((1, 128), F32)
    below0, below1, here0, here1, above0, above1 = [blank] * 6
    for g in reversed(range(slabs)):
        v0, v1 = forward[g]
        if g < slabs - 1:
            factor = constant_ref[C_F + 8 * g : C_F + 8 * g + 8]
            s0, s1 = factor[3:4] * n0, factor[4:5] * n1
            v0 = v0 + factor[0:1] * s0 + factor[1:2] * s1
            v1 = v1 + factor[1:2] * s0 + factor[2:3] * s1
        n0, n1 = v0, v1
        here0 = jnp.where(slab == g, n0, here0)
        here1 = jnp.where(slab == g, n1, here1)
        above0 = jnp.where(slab + 1 == g, n0, above0)
        above1 = jnp.where(slab + 1 == g, n1, above1)
        below0 = jnp.where(slab - 1 == g, n0, below0)
        below1 = jnp.where(slab - 1 == g, n1, below1)
    def coarse_of(row, q):
        return row[:, T_N + q : T_N + q + 1]

    own = [coarse_of(here0, 0), coarse_of(here1, 0)]

    bonds = lambda d, c: bonds_ref[d, c]
    diagonal = lambda c: diagonal_ref[c]
    end = CHUNKS - 1
    x_plus = outer_ref[B_XP : B_XP + CHUNKS]
    x_minus = outer_ref[B_XM : B_XM + CHUNKS]
    y_plus = outer_ref[B_YP : B_YP + BS]
    y_minus = outer_ref[B_YM : B_YM + BS]
    z_bonds = outer_ref[B_Z : B_Z + BS]

    def brought(x_rows, y_block, z_block):
        return (
            x_plus * x_rows,
            x_minus * x_rows,
            y_minus * y_block,
            y_plus * roll(y_block, 64),
            z_bonds * z_block,
        )

    y1 = [relax_ref[c] * residual[c] for c in range(CHUNKS)]
    outcome = stencil(y1, bonds, diagonal, brought(x_sides[:CHUNKS], y_sides, z_first))
    smoothed = []
    for c in range(CHUNKS):
        value = y1[c] + relax_ref[c] * (residual[c] - outcome[c]) + own[c // 8]
        smoothed_ref[c] = value
        smoothed.append(value)
    writing = pltpu.make_async_copy(smoothed_ref, smoothed_hbm, written)
    writing.start()
    keys = constant_ref[C_K : C_K + 8]
    crossing = x_plus * jnp.concatenate([f[BS - 1 : BS] for f in y1], axis=0)
    crossing += x_minus * jnp.concatenate([f[0:1] for f in y1], axis=0)
    end_row = keys[1:2] * ends[0:1]
    corner_row = keys[0:1] * ends[1:2]
    depth_row = lane_row % BS
    additions = []
    for c in range(CHUNKS):
        value = jnp.where(
            (depth_row == BS - 1) | (depth_row == 0), roll_row(end_row, 31 - 2 * c), 0.0
        )
        if c == 0:
            value = value + jnp.where(lane_row < 32, corner_row, 0.0)
        if c == end:
            value = value + jnp.where(lane_row >= 96, corner_row, 0.0)
        value = value + coarse_of(here0 if c < 8 else here1, 1)
        additions.append(value)
    x_next = (
        x_sides[CHUNKS:]
        + constant_ref[C_XD : C_XD + CHUNKS] * crossing
        + jnp.concatenate(additions, axis=0)
    )
    y_constant = constant_ref[C_YC : C_YC + BS]
    y_crossing = jnp.where(lane < 32, y_minus * y1[0], roll(y_plus * y1[end], 64))
    x_side_row = jnp.where(row == 0, BS - 1, 0)
    y_ends = jnp.where(lane == 0, roll(y_edges, -1), 0.0)
    y_ends = jnp.where(lane == 31, roll(y_edges, 31), y_ends)
    y_ends = jnp.where(lane == 32, roll(y_edges, 29), y_ends)
    y_ends = jnp.where(lane == 63, roll(y_edges, 61), y_ends)
    z_sides = jnp.where(lane == 0, y_edges, 0.0)
    z_sides = jnp.where(lane == 97, roll(y_edges, 96), z_sides)
    z_sides = jnp.where(lane == 126, roll(y_edges, 124), z_sides)
    z_sides = jnp.where(lane == 95, roll(y_edges, 92), z_sides)
    y_next = (
        roll(y_sides, 64)
        + y_constant * y_crossing
        + roll(y_constant, 64) * y_ends
        + jnp.where(height == x_side_row, keys[2:3] * ends[2:3], 0.0)
        + jnp.where(lane < 32, coarse_of(here1, 2), coarse_of(here0, 3))
    )
    z_crossing = z_bonds * pack(y1)
    z_coarse = jnp.where(
        even_row,
        jnp.where(depth_row < 16, coarse_of(above0, 0), coarse_of(above1, 0)),
        jnp.where(depth_row < 16, coarse_of(below0, 0), coarse_of(below1, 0)),
    )
    z_next = (
        z_second
        + constant_ref[C_ZD : C_ZD + BS] * z_crossing
        + constant_ref[C_ZK : C_ZK + BS] * z_sides
        + jnp.where(height == x_side_row, keys[3:4] * ends[0:1], 0.0)
        + z_coarse
    )
    mapped = stencil(smoothed, bonds, diagonal, brought(x_next, y_next, z_next))
    for c in range(CHUNKS):
        mapped_out[c] = mapped[c]

    values = [
        total_of(mapped[:8]),
        total_of(mapped[8:]),
        total_of([residual[c] * smoothed[c] for c in range(CHUNKS)]),
        total_of([mapped[c] * smoothed[c] for c in range(CHUNKS)]),
    ]
    if not first:
        values.append(total_of([search_ref[c] * smoothed[c] for c in range(CHUNKS)]))
    if last:
        write_copies(tile_out, tile_of(values))
        writing.wait()
        return
    y1 = [relax_ref[c] * mapped[c] for c in range(CHUNKS)]
    write_copies(tile_out, edge_tile(y1, row, values))
    outcome = stencil(y1, bonds, diagonal)
    partial = [y1[c] + relax_ref[c] * (mapped[c] - outcome[c]) for c in range(CHUNKS)]
    write_xy(xy_out, row, y1, partial)
    z_out[Z_Y1 : Z_Y1 + BS] = pack(y1)
    z_out[Z_P : Z_P + BS] = pack(partial)
    writing.wait()


def finish_kernel(
    tiles_ref, scalars_ref, residual_ref, mapped_ref, search_ref, first_ref, second_ref, third_ref,
    solution_ref, residual_out,
):
    scalars = scalars_ref[...]
    tiles = sum_tiles(tiles_ref, tiles_ref.shape[0] // 8)
    _, _, step, growth = search_scalars(tiles, scalars, ITERS - 1)
    first_step, second_step, second_growth = scalars[2:3, 0:1], scalars[3:4, 0:1], scalars[4:5, 0:1]
    third_weight = step
    second_weight = second_step + growth * step
    first_weight = first_step + second_growth * second_weight
    for c in range(CHUNKS):
        s, part = c // 8, pl.ds(128 * (c % 8), 128)
        solution_ref[s, :, part] = (
            first_weight * first_ref[c] + second_weight * second_ref[c] + third_weight * third_ref[c]
        )
        residual_out[s, :, part] = residual_ref[c] - step * (mapped_ref[c] + growth * search_ref[c])


def call(kernel, name, outs, in_spaces, out_spaces, operands, scratch=()):
    spec = lambda space: pl.BlockSpec(memory_space=space)
    in_spaces = list(in_spaces) + [pltpu.VMEM] * (len(operands) - len(in_spaces))
    out_spaces = list(out_spaces) + [pltpu.VMEM] * (len(outs) - len(out_spaces))
    return pl.pallas_call(
        kernel,
        out_shape=tuple(outs),
        in_specs=[spec(space) for space in in_spaces],
        out_specs=tuple(spec(space) for space in out_spaces),
        scratch_shapes=list(scratch),
        compiler_params=pltpu.CompilerParams(vmem_limit_bytes=16 * 1024 * 1024),
        name=name,
    )(*operands)


def array(*shape):
    return jax.ShapeDtypeStruct(shape, F32)


def to_all(copies, axes):
    return lax.all_to_all(copies, axes, 0, 0, tiled=True)


def exchange_slabs(message):
    count = lax.axis_size("grp")
    upward = [(i, i + 1) for i in range(count - 1)]
    downward = [(i + 1, i) for i in range(count - 1)]
    return lax.ppermute(message, "grp", downward), lax.ppermute(message, "grp", upward)


def on_device(source, uptake, conductance, occupancy, assignment):
    slabs = lax.axis_size("grp")
    bricks = lax.axis_size("brick")
    place = (lax.axis_index("grp") * bricks + lax.axis_index("brick")).astype(jnp.int32).reshape(1)
    field = array(*FIELD)
    copies = array(8 * slabs * bricks, 128)
    info, bonds, outer, diagonal, residual, sides, ends, tile = call(
        functools.partial(setup_kernel, slabs, bricks),
        "setup",
        [
            jax.ShapeDtypeStruct((8,), jnp.int32), array(3, *FIELD), array(B_ROWS, 128), field, field,
            array(XY_ROWS_FIRST, 128), array(Z_ROWS_FIRST, 128), copies,
        ],
        [pltpu.SMEM] * 3,
        [pltpu.SMEM],
        [
            place, assignment, jnp.transpose(occupancy, (1, 2, 0)),
            source[0, 0], uptake[0, 0], conductance[0, 0],
        ],
        [
            pltpu.VMEM(FIELD, F32), pltpu.VMEM(FIELD, F32),
        ],
    )
    mapped = residual
    directions = []
    state = {}
    for iteration in range(ITERS):
        first, last = iteration == 0, iteration == ITERS - 1
        tiles = to_all(tile, ("brick", "grp"))
        above, below = exchange_slabs(ends)
        gathered = lax.all_gather(sides, "brick", axis=0, tiled=False)
        operands = [info, gathered, above, below, tiles, bonds, outer, diagonal, residual]
        tall = array(H_S + 8 * slabs, 128)
        outs = {"smoothed": field, "mapped": field}
        if not first:
            operands += [mapped] + [state[k] for k in ("halo", "constant", "scalars")]
        if iteration > 1:
            operands += [state[k] for k in ("search", "search_halo")]
        if first:
            outs |= {"constant": array(C_F + 8 * slabs, 128), "halo": tall}
        else:
            outs |= {"residual": field, "search": field, "scalars": array(8, 128)}
            if not last:
                outs |= {"halo": tall, "search_halo": tall}
        outs["tile"] = copies
        if not last:
            outs |= {"sides": array(XY_ROWS, 128), "ends": array(Z_ROWS, 128)}
        results = call(
            functools.partial(step_kernel, iteration, slabs, bricks),
            f"step_{iteration}",
            list(outs.values()),
            [pltpu.SMEM],
            [pltpu.HBM],
            operands,
            [pltpu.VMEM(FIELD, F32), pltpu.VMEM(FIELD, F32), pltpu.SemaphoreType.DMA],
        )
        state |= dict(zip(outs, results))
        if first:
            state["scalars"] = jnp.zeros((8, 128), F32)
        mapped, tile = state["mapped"], state["tile"]
        sides, ends = state.get("sides"), state.get("ends")
        residual = state.get("residual", residual)
        directions.append(state["smoothed"])
    tiles = to_all(tile, ("brick", "grp"))
    brick_pair = array(2, BS, BS * BS)
    solution_field, residual = call(
        finish_kernel,
        "finish",
        [brick_pair, brick_pair],
        [],
        [],
        [tiles, state["scalars"], residual, mapped, state["search"]] + directions,
    )
    return solution_field[None, None], residual[None, None]


def solution(mesh):
    return jax.shard_map(
        on_device,
        mesh=mesh,
        in_specs=(
            P("grp", "brick", None, None, None),
            P("grp", "brick", None, None, None),
            P("grp", "brick", None, None, None, None),
            P(),
            P(),
        ),
        out_specs=(P("grp", "brick", None, None, None), P("grp", "brick", None, None, None)),
        check_vma=False,
    )
```

```python
import functools

import jax
import jax.numpy as jnp
from jax import lax
from jax.experimental import pallas as pl
from jax.experimental.pallas import tpu as pltpu
from jax.sharding import PartitionSpec as P

BS = 32
CHUNKS = 16
OMEGA = 0.6
ITERS = 3
F32 = jnp.float32
FIELD = (CHUNKS, BS, 128)

XY_X1, XY_XP, XY_Y = 0, 16, 32
XY_ROWS = 64
XY_XD, XY_YC, XY_K = 64, 80, 112
XY_ROWS_FIRST = 120
Z_Y1, Z_P = 0, 32
Z_ROWS = 64
Z_D, Z_K, Z_X = 64, 96, 128
Z_ROWS_FIRST = 136
T_N, T_Y = 16, 64
H_X1, H_Y, H_Z1, H_ZP, H_E, H_R, H_S = 0, 32, 64, 96, 128, 160, 168
C_XD, C_YC, C_ZD, C_ZK, C_K, C_F = 0, 16, 48, 80, 112, 120
B_XP, B_XM, B_YP, B_YM, B_Z = 0, 16, 32, 64, 96
B_ROWS = 128


def roll(block, shift):
    return pltpu.roll(block, shift % 128, axis=1)


def roll_row(row, shift):
    return pltpu.roll(jnp.broadcast_to(row, (8, 128)), shift % 128, axis=1)[0:1]


def lanes(rows=BS):
    return lax.broadcasted_iota(jnp.int32, (rows, 128), 1)


def rows_of(height=BS):
    return lax.broadcasted_iota(jnp.int32, (height, 128), 0)


def pack(chunks):
    height = chunks[0].shape[0]
    pair = (lanes(height) % BS) // 2
    total = jnp.zeros((height, 128), F32)
    for c in range(CHUNKS):
        moved = roll(chunks[c], 2 * c - 31) if height > 1 else roll_row(chunks[c], 2 * c - 31)
        total = jnp.where(pair == c, moved, total)
    return total


def stencil(field, bonds, diagonal, outer=None):
    lane = lanes()
    height = rows_of()
    depth = lane % BS
    at_end = (depth == BS - 1) | (depth == 0)
    back = [roll(f, -32) for f in field]
    forth = [roll(bonds(1, c) * field[c], 32) for c in range(CHUNKS)]
    out = []
    for c in range(CHUNKS):
        f = field[c]
        total = diagonal(c) * f
        total -= bonds(0, c) * pltpu.roll(f, BS - 1, axis=0)
        total -= pltpu.roll(bonds(0, c) * f, 1, axis=0)
        following = back[c + 1] if c < CHUNKS - 1 else back[c]
        previous = forth[c - 1] if c > 0 else jnp.zeros((BS, 128), F32)
        total -= bonds(1, c) * jnp.where(lane < 96, back[c], following)
        total -= jnp.where(lane >= 32, forth[c], previous)
        total -= bonds(2, c) * roll(f, -1)
        total -= roll(bonds(2, c) * f, 1)
        if outer is not None:
            x_up, x_down, y_low, y_high, z_ends = outer
            total -= jnp.where(height == BS - 1, x_up[c : c + 1], 0.0)
            total -= jnp.where(height == 0, x_down[c : c + 1], 0.0)
            total -= jnp.where(at_end, roll(z_ends, 31 - 2 * c), 0.0)
            if c == 0:
                total -= jnp.where(lane < 32, y_low, 0.0)
            if c == CHUNKS - 1:
                total -= jnp.where(lane >= 96, y_high, 0.0)
        out.append(total)
    return out


def total_of(blocks):
    acc = blocks[0]
    for block in blocks[1:]:
        acc = acc + block
    return jnp.sum(jnp.sum(acc, axis=0, keepdims=True), axis=1, keepdims=True)


def facing(block, row):
    return jnp.where(row == 0, block[BS - 1 : BS], block[0:1])


def side_blocks(low_first, high_first, low_second, high_second):
    group = lanes() // 32
    return jnp.where(
        group == 0,
        low_first,
        jnp.where(
            group == 1,
            roll(high_first, 64),
            jnp.where(group == 2, roll(low_second, 64), high_second),
        ),
    )


def write_xy(xy_ref, row, y1, partial):
    for c in range(CHUNKS):
        xy_ref[XY_X1 + c : XY_X1 + c + 1] = facing(y1[c], row)
        xy_ref[XY_XP + c : XY_XP + c + 1] = facing(partial[c], row)
    last = CHUNKS - 1
    xy_ref[XY_Y : XY_Y + BS] = side_blocks(y1[0], y1[last], partial[0], partial[last])


def write_scalars(ref, start, values):
    for i, value in enumerate(values):
        ref[start + i : start + i + 1] = jnp.broadcast_to(value, (1, 128))
    for i in range(len(values), 8):
        ref[start + i : start + i + 1] = jnp.zeros((1, 128), F32)


def tile_of(values, y1=None):
    lane = lanes(8)
    level = rows_of(8)
    tile = jnp.zeros((8, 128), F32)
    for i, value in enumerate(values):
        tile = jnp.where((level == i) & (lane >= T_N) & (lane < T_Y), value, tile)
    if y1 is None:
        return tile
    row, low, high = y1
    tile = jnp.where((level == 0) & (lane >= T_Y), row, tile)
    tile = jnp.where((level == 1) & (lane >= T_Y), roll_row(row, 64), tile)
    wide = lanes()
    edges = jnp.where(wide == 0, low, 0.0)
    edges = jnp.where(wide == 1, roll(low, -30), edges)
    edges = jnp.where(wide == 2, roll(high, -94), edges)
    edges = jnp.where(wide == 3, roll(high, -124), edges)
    for t in range(4):
        tile = tile + roll(edges[8 * t : 8 * t + 8], 4 * t)
    return tile


def write_copies(ref, tile):
    for k in range(ref.shape[0] // 8):
        ref[8 * k : 8 * k + 8] = tile


def edge_tile(y1, row, values):
    line = pack([facing(f, row) for f in y1])
    return tile_of(values, (line, y1[0], y1[CHUNKS - 1]))


def locate(bricks, place_ref, assignment_ref):
    across = bricks // 2
    place = place_ref[0]
    slab = place // bricks
    patch = assignment_ref[place % bricks]
    row = patch // across
    column = patch % across
    return slab, patch, row, column


def setup_kernel(
    slabs, bricks, place_ref, assignment_ref, occupancy_ref, source_ref, uptake_ref, conductance_ref,
    info_ref, bonds_ref, outer_ref, diagonal_ref, residual_ref, xy_ref, z_ref, tile_ref,
    relax_ref, y1_ref,
):
    across = bricks // 2
    slab, patch, row, column = locate(bricks, place_ref, assignment_ref)

    def holder(row_target, column_target):
        inside = (column_target >= 0) & (column_target < across)
        wanted = jnp.where(inside, row_target * across + column_target, patch)
        found = jnp.int32(0)
        for b in range(bricks):
            found = jnp.where(assignment_ref[b] == wanted, b, found)
        return found

    info_ref[0] = row
    info_ref[1] = slab
    info_ref[2] = holder(row, column)
    info_ref[3] = holder(1 - row, column)
    info_ref[4] = holder(row, column - 1)
    info_ref[5] = holder(row, column + 1)
    info_ref[6] = holder(1 - row, column - 1)
    info_ref[7] = holder(1 - row, column + 1)

    breadth = 2 * across

    def live_at(g, x, y):
        inside = (g >= 0) & (g < slabs) & (x >= 0) & (x < 2) & (y >= 0) & (y < breadth)
        taken = occupancy_ref[jnp.clip(x, 0, 1), jnp.clip(y, 0, breadth - 1), jnp.clip(g, 0, slabs - 1)]
        return jnp.where(inside, taken, 0).astype(F32)

    lane = lanes()
    height = rows_of()
    depth = lane % BS
    absorbed = []
    low_ends = []
    high_ends = []
    first_y = None
    second_y = None
    for s in range(2):
        y = column * 2 + s
        here = live_at(slab, row, y)
        around = [
            here * live_at(slab, row + 1, y),
            here * live_at(slab, row - 1, y),
            here * live_at(slab, row, y + 1),
            here * live_at(slab, row, y - 1),
            here * live_at(slab + 1, row, y),
            here * live_at(slab - 1, row, y),
        ]
        borders = [height == BS - 1, height == 0, lane >= 96, lane < 32, depth == BS - 1, depth == 0]
        for k in range(8):
            c = 8 * s + k
            part = pl.ds(128 * k, 128)
            taken = uptake_ref[s, :, part]
            absorbed.append(taken)
            diagonal = taken
            values = []
            for d in range(6):
                bond = conductance_ref[d, s, :, part]
                if (d == 2 and k < 7) or (d == 3 and k > 0):
                    value = bond * here
                else:
                    value = bond * jnp.where(borders[d], around[d], here)
                values.append(value)
                diagonal = diagonal + value
            if c == 7:
                first_y = jnp.where(borders[2], values[2], 0.0)
            if c == 8:
                second_y = jnp.where(borders[3], values[3], 0.0)
            high_ends.append(jnp.where(borders[4], values[4], 0.0))
            low_ends.append(jnp.where(borders[5], values[5], 0.0))
            outer_ref[B_XP + c : B_XP + c + 1] = values[0][BS - 1 : BS]
            outer_ref[B_XM + c : B_XM + c + 1] = values[1][0:1]
            bonds_ref[0, c] = jnp.where(borders[0], 0.0, values[0])
            if c == CHUNKS - 1:
                outer_ref[B_YP : B_YP + BS] = jnp.where(borders[2], values[2], 0.0)
                bonds_ref[1, c] = jnp.where(borders[2], 0.0, values[2])
            else:
                bonds_ref[1, c] = values[2]
            if c == 0:
                outer_ref[B_YM : B_YM + BS] = jnp.where(borders[3], values[3], 0.0)
            bonds_ref[2, c] = jnp.where(borders[4], 0.0, values[4])
            relax = OMEGA / diagonal
            diagonal_ref[c] = diagonal
            relax_ref[c] = relax
            forcing = source_ref[s, :, part] * here
            residual_ref[c] = forcing
            y1_ref[c] = relax * forcing

    ends = [high_ends[c] + low_ends[c] for c in range(CHUNKS)]
    outer_ref[B_Z : B_Z + BS] = pack(ends)
    y1 = [y1_ref[c] for c in range(CHUNKS)]
    outcome = stencil(y1, lambda d, c: bonds_ref[d, c], lambda c: diagonal_ref[c])
    partial = [y1[c] + relax_ref[c] * (residual_ref[c] - outcome[c]) for c in range(CHUNKS)]
    write_xy(xy_ref, row, y1, partial)
    z_ref[Z_Y1 : Z_Y1 + BS] = pack(y1)
    z_ref[Z_P : Z_P + BS] = pack(partial)

    first_coupling = total_of([first_y])
    high_sums = [total_of(high_ends[8 * s : 8 * s + 8]) for s in range(2)]
    low_sums = [total_of(low_ends[8 * s : 8 * s + 8]) for s in range(2)]
    taken_sums = [total_of(absorbed[8 * s : 8 * s + 8]) for s in range(2)]
    residual_sums = [total_of([residual_ref[8 * s + k] for k in range(8)]) for s in range(2)]
    numbers = [
        residual_sums[0],
        residual_sums[1],
        taken_sums[0] + first_coupling + high_sums[0] + low_sums[0],
        taken_sums[1] + total_of([second_y]) + high_sums[1] + low_sums[1],
        first_coupling,
        high_sums[0],
        high_sums[1],
    ]
    write_copies(tile_ref, edge_tile(y1, row, numbers))

    last = CHUNKS - 1
    z_ends = [relax_ref[c] * ends[c] for c in range(CHUNKS)]
    for c in range(CHUNKS):
        xy_ref[XY_XD + c : XY_XD + c + 1] = facing(relax_ref[c], row)
    high_y = relax_ref[last] * outer_ref[B_YP : B_YP + BS]
    low_y = relax_ref[0] * outer_ref[B_YM : B_YM + BS]
    xy_ref[XY_YC : XY_YC + BS] = side_blocks(relax_ref[0], relax_ref[last], z_ends[0], z_ends[last])
    xy_ref[XY_K : XY_K + 1] = facing(low_y + high_y, row)
    xy_ref[XY_K + 1 : XY_K + 2] = pack([facing(z, row) for z in z_ends])
    toward = [
        relax_ref[c][BS - 1 : BS] * outer_ref[B_XP + c : B_XP + c + 1]
        + relax_ref[c][0:1] * outer_ref[B_XM + c : B_XM + c + 1]
        for c in range(CHUNKS)
    ]
    xy_ref[XY_K + 2 : XY_K + 3] = jnp.where(lanes(1) < 32, toward[0], roll_row(toward[last], 64))
    xy_ref[XY_K + 3 : XY_K + 8] = jnp.zeros((5, 128), F32)
    z_ref[Z_D : Z_D + BS] = pack([relax_ref[c] for c in range(CHUNKS)])
    z_ref[Z_K : Z_K + BS] = pack([low_y] + [jnp.zeros((BS, 128), F32)] * (CHUNKS - 2) + [high_y])
    z_ref[Z_X : Z_X + 8] = jnp.broadcast_to(pack(toward), (8, 128))


def swap_sides(from_low, from_high):
    rows = from_low.shape[0]
    if rows == 1:
        low, high = roll_row(from_low, -32), roll_row(from_high, 32)
    else:
        low, high = roll(from_low, -32), roll(from_high, 32)
    return jnp.where((lanes(rows) // 32) % 2 == 0, low, high)


def search_scalars(sums, scalars, iteration):
    energy = sums[0]
    curvature = sums[1]
    if iteration == 0:
        return energy, curvature, energy / curvature, None
    growth = energy / scalars[0:1, 0:1]
    curvature = curvature + growth * (2.0 * sums[2] + growth * scalars[1:2, 0:1])
    return energy, curvature, energy / curvature, growth


def sum_tiles(ref, count):
    total = ref[0:8]
    for g in range(1, count):
        total = total + ref[8 * g : 8 * g + 8]
    return total


def step_kernel(iteration, slabs, bricks, *refs):
    first = iteration == 0
    last = iteration == ITERS - 1
    refs = list(refs)
    take = lambda count: [refs.pop(0) for _ in range(count)]
    info_ref, xy_ref, above_ref, below_ref, tiles_ref = take(5)
    bonds_ref, outer_ref, diagonal_ref, residual_ref = take(4)
    if not first:
        mapped_ref, halo_in, constant_ref, scalars_in = take(4)
    if iteration > 1:
        search_in, search_halo_in = take(2)
    smoothed_hbm, mapped_out = take(2)
    if first:
        constant_ref, halo_ref = take(2)
    else:
        residual_out, search_ref, scalars_ref = take(3)
        if not last:
            halo_ref, search_halo_ref = take(2)
    tile_out = take(1)[0]
    if not last:
        xy_out, z_out = take(2)
    relax_ref, smoothed_ref, written = take(3)
    if not last:
        tile_ref, sent = take(2)
    for c in range(CHUNKS):
        relax_ref[c] = OMEGA / diagonal_ref[c]

    row = info_ref[0]
    slab = info_ref[1]
    lane = lanes()
    height = rows_of()
    depth = lane % BS
    lane_row = lanes(1)
    even = lane % 2 == 0
    even_row = lane_row % 2 == 0
    low_holder, high_holder = info_ref[4], info_ref[5]
    low_corner, high_corner = info_ref[6], info_ref[7]
    x_holder = info_ref[3]

    def merge(start):
        up = roll(above_ref[start : start + BS], 31)
        down = roll(below_ref[start : start + BS], -31)
        return jnp.where(even, up, down)

    x_sides = xy_ref[x_holder, XY_X1 : XY_X1 + 2 * CHUNKS]
    y_sides = swap_sides(
        xy_ref[low_holder, XY_Y : XY_Y + BS], xy_ref[high_holder, XY_Y : XY_Y + BS]
    )
    z_first = merge(Z_Y1)
    z_second = merge(Z_P)

    def tile_at(holder, g):
        return tiles_ref[pl.ds(pl.multiple_of((holder * slabs + g) * 8, 8), 8)]

    slab_above = jnp.minimum(slab + 1, slabs - 1)
    slab_below = jnp.maximum(slab - 1, 0)

    def edge_row(tile):
        return jnp.where(lane_row >= T_Y, tile[0:1], roll_row(tile[1:2], 64))

    x_ends = jnp.where(
        even_row,
        roll_row(edge_row(tile_at(x_holder, slab_above)), 31),
        roll_row(edge_row(tile_at(x_holder, slab_below)), -31),
    )
    kind = lanes(8) % 4
    mixed = jnp.where(
        kind == 0,
        roll(tile_at(low_holder, slab_above), -2),
        jnp.where(
            kind == 1,
            roll(tile_at(low_holder, slab_below), -2),
            jnp.where(
                kind == 2,
                roll(tile_at(high_holder, slab_above), 2),
                roll(tile_at(high_holder, slab_below), 2),
            ),
        ),
    )
    y_edges = jnp.where(
        lane < 4, jnp.concatenate([roll(mixed, -4 * t) for t in range(4)], axis=0), 0.0
    )
    corner_y = jnp.where(
        lane_row < 32,
        roll_row(xy_ref[low_corner, XY_X1 + CHUNKS - 1 : XY_X1 + CHUNKS], 32),
        roll_row(xy_ref[high_corner, XY_X1 : XY_X1 + 1], -32),
    )
    low_row = jnp.where(
        row == 0,
        xy_ref[low_corner, XY_Y : XY_Y + 1],
        xy_ref[low_corner, XY_Y + BS - 1 : XY_Y + BS],
    )
    high_row = jnp.where(
        row == 0,
        xy_ref[high_corner, XY_Y : XY_Y + 1],
        xy_ref[high_corner, XY_Y + BS - 1 : XY_Y + BS],
    )
    corner_x = swap_sides(low_row, high_row)
    ends = jnp.concatenate([x_ends, corner_y, corner_x, jnp.zeros((5, 128), F32)], axis=0)
    lane_tile = lanes(8)
    slab_tiles = []
    for g in range(slabs):
        tile = tile_at(info_ref[2], g)
        for q in range(1, 4):
            tile = jnp.where(lane_tile == T_N + q, tile_at(info_ref[2 + q], g), tile)
        slab_tiles.append(tile)
    sums = jnp.concatenate(slab_tiles, axis=0)
    halo = [x_sides, y_sides, z_first, z_second, y_edges, ends, sums]
    starts = [H_X1, H_Y, H_Z1, H_ZP, H_E, H_R, H_S]

    if first:
        residual = [residual_ref[c] for c in range(CHUNKS)]
        constant_ref[C_XD : C_XD + CHUNKS] = xy_ref[x_holder, XY_XD : XY_XD + CHUNKS]
        constant_ref[C_YC : C_YC + BS] = swap_sides(
            xy_ref[low_holder, XY_YC : XY_YC + BS], xy_ref[high_holder, XY_YC : XY_YC + BS]
        )
        constant_ref[C_ZD : C_ZD + BS] = merge(Z_D)
        constant_ref[C_ZK : C_ZK + BS] = merge(Z_K)
        constant_ref[C_K : C_K + 8] = jnp.concatenate(
            [
                xy_ref[x_holder, XY_K : XY_K + 2],
                swap_sides(
                    xy_ref[low_holder, XY_K + 2 : XY_K + 3],
                    xy_ref[high_holder, XY_K + 2 : XY_K + 3],
                ),
                jnp.where(
                    even_row,
                    roll_row(above_ref[Z_X : Z_X + 1], 31),
                    roll_row(below_ref[Z_X : Z_X + 1], -31),
                ),
                jnp.zeros((4, 128), F32),
            ],
            axis=0,
        )
        for g in range(slabs):
            tile = sums[8 * g : 8 * g + 8]
            a, b, off = tile[2:3], tile[3:4], tile[4:5]
            t0, t1 = tile[5:6], tile[6:7]
            if g > 0:
                a = a - u0 * u0 * i00
                b = b - u1 * u1 * i11
                off = off + u0 * u1 * i01
            used = (lane_row >= T_N) & (lane_row < T_N + 4)
            a = jnp.where(used, a, 1.0)
            b = jnp.where(used, b, 1.0)
            off = jnp.where(used, off, 0.0)
            t0 = jnp.where(used, t0, 0.0)
            t1 = jnp.where(used, t1, 0.0)
            scale = 1.0 / (a * b - off * off)
            i00, i01, i11 = b * scale, off * scale, a * scale
            u0, u1 = t0, t1
            constant_ref[C_F + 8 * g : C_F + 8 * g + 8] = jnp.concatenate(
                [i00, i01, i11, t0, t1, jnp.zeros((3, 128), F32)], axis=0
            )
    else:
        scalars = None if iteration == 1 else scalars_in[...]
        tile = sum_tiles(tiles_ref, slabs * bricks)
        energy, curvature, step, growth = search_scalars(
            [tile[i : i + 1, T_N : T_N + 1] for i in range(2, 5)], scalars, iteration - 1
        )
        step_row = jnp.broadcast_to(step, (1, 128))
        residual = []
        for c in range(CHUNKS):
            mapped = mapped_ref[c]
            if growth is not None:
                mapped = mapped + growth * search_in[c]
            search_ref[c] = mapped
            value = residual_ref[c] - step * mapped
            residual_out[c] = value
            residual.append(value)
        old_halo = halo
        halo = []
        for start, block in zip(starts, old_halo):
            span = slice(start, start + block.shape[0])
            if growth is not None:
                block = block + growth * search_halo_in[span]
            if not last:
                search_halo_ref[span] = block
            halo.append(halo_in[span] - step * block)
        kept = [energy, curvature, step]
        if growth is not None:
            kept = [energy, curvature, scalars[2:3, 0:1], step, growth]
        write_scalars(scalars_ref, 0, kept)

    if not last:
        for start, block in zip(starts, halo):
            halo_ref[start : start + block.shape[0]] = block
    x_sides, y_sides, z_first, z_second, y_edges, ends, sums = halo

    forward = []
    for g in range(slabs):
        t0, t1 = sums[8 * g : 8 * g + 1], sums[8 * g + 1 : 8 * g + 2]
        if g > 0:
            t0 = t0 + w0 * v0
            t1 = t1 + w1 * v1
        factor = constant_ref[C_F + 8 * g : C_F + 8 * g + 8]
        v0 = factor[0:1] * t0 + factor[1:2] * t1
        v1 = factor[1:2] * t0 + factor[2:3] * t1
        w0, w1 = factor[3:4], factor[4:5]
        forward.append((v0, v1))
    blank = jnp.zeros((1, 128), F32)
    below0, below1, here0, here1, above0, above1 = [blank] * 6
    for g in reversed(range(slabs)):
        v0, v1 = forward[g]
        if g < slabs - 1:
            factor = constant_ref[C_F + 8 * g : C_F + 8 * g + 8]
            s0, s1 = factor[3:4] * n0, factor[4:5] * n1
            v0 = v0 + factor[0:1] * s0 + factor[1:2] * s1
            v1 = v1 + factor[1:2] * s0 + factor[2:3] * s1
        n0, n1 = v0, v1
        here0 = jnp.where(slab == g, n0, here0)
        here1 = jnp.where(slab == g, n1, here1)
        above0 = jnp.where(slab + 1 == g, n0, above0)
        above1 = jnp.where(slab + 1 == g, n1, above1)
        below0 = jnp.where(slab - 1 == g, n0, below0)
        below1 = jnp.where(slab - 1 == g, n1, below1)
    def coarse_of(row, q):
        return row[:, T_N + q : T_N + q + 1]

    own = [coarse_of(here0, 0), coarse_of(here1, 0)]

    bonds = lambda d, c: bonds_ref[d, c]
    diagonal = lambda c: diagonal_ref[c]
    end = CHUNKS - 1
    x_plus = outer_ref[B_XP : B_XP + CHUNKS]
    x_minus = outer_ref[B_XM : B_XM + CHUNKS]
    y_plus = outer_ref[B_YP : B_YP + BS]
    y_minus = outer_ref[B_YM : B_YM + BS]
    z_bonds = outer_ref[B_Z : B_Z + BS]

    def brought(x_rows, y_block, z_block):
        return (
            x_plus * x_rows,
            x_minus * x_rows,
            y_minus * y_block,
            y_plus * roll(y_block, 64),
            z_bonds * z_block,
        )

    y1 = [relax_ref[c] * residual[c] for c in range(CHUNKS)]
    outcome = stencil(y1, bonds, diagonal, brought(x_sides[:CHUNKS], y_sides, z_first))
    smoothed = []
    for c in range(CHUNKS):
        value = y1[c] + relax_ref[c] * (residual[c] - outcome[c]) + own[c // 8]
        if last:
            smoothed_ref[c] = value
        else:
            smoothed_ref[c // 8, :, 128 * (c % 8) : 128 * (c % 8 + 1)] = value
        smoothed.append(value)
    writing = pltpu.make_async_copy(smoothed_ref, smoothed_hbm, written)
    writing.start()
    keys = constant_ref[C_K : C_K + 8]
    crossing = x_plus * jnp.concatenate([f[BS - 1 : BS] for f in y1], axis=0)
    crossing += x_minus * jnp.concatenate([f[0:1] for f in y1], axis=0)
    end_row = keys[1:2] * ends[0:1]
    corner_row = keys[0:1] * ends[1:2]
    depth_row = lane_row % BS
    additions = []
    for c in range(CHUNKS):
        value = jnp.where(
            (depth_row == BS - 1) | (depth_row == 0), roll_row(end_row, 31 - 2 * c), 0.0
        )
        if c == 0:
            value = value + jnp.where(lane_row < 32, corner_row, 0.0)
        if c == end:
            value = value + jnp.where(lane_row >= 96, corner_row, 0.0)
        value = value + coarse_of(here0 if c < 8 else here1, 1)
        additions.append(value)
    x_next = (
        x_sides[CHUNKS:]
        + constant_ref[C_XD : C_XD + CHUNKS] * crossing
        + jnp.concatenate(additions, axis=0)
    )
    y_constant = constant_ref[C_YC : C_YC + BS]
    y_crossing = jnp.where(lane < 32, y_minus * y1[0], roll(y_plus * y1[end], 64))
    x_side_row = jnp.where(row == 0, BS - 1, 0)
    y_ends = jnp.where(lane == 0, roll(y_edges, -1), 0.0)
    y_ends = jnp.where(lane == 31, roll(y_edges, 31), y_ends)
    y_ends = jnp.where(lane == 32, roll(y_edges, 29), y_ends)
    y_ends = jnp.where(lane == 63, roll(y_edges, 61), y_ends)
    z_sides = jnp.where(lane == 0, y_edges, 0.0)
    z_sides = jnp.where(lane == 97, roll(y_edges, 96), z_sides)
    z_sides = jnp.where(lane == 126, roll(y_edges, 124), z_sides)
    z_sides = jnp.where(lane == 95, roll(y_edges, 92), z_sides)
    y_next = (
        roll(y_sides, 64)
        + y_constant * y_crossing
        + roll(y_constant, 64) * y_ends
        + jnp.where(height == x_side_row, keys[2:3] * ends[2:3], 0.0)
        + jnp.where(lane < 32, coarse_of(here1, 2), coarse_of(here0, 3))
    )
    z_crossing = z_bonds * pack(y1)
    z_coarse = jnp.where(
        even_row,
        jnp.where(depth_row < 16, coarse_of(above0, 0), coarse_of(above1, 0)),
        jnp.where(depth_row < 16, coarse_of(below0, 0), coarse_of(below1, 0)),
    )
    z_next = (
        z_second
        + constant_ref[C_ZD : C_ZD + BS] * z_crossing
        + constant_ref[C_ZK : C_ZK + BS] * z_sides
        + jnp.where(height == x_side_row, keys[3:4] * ends[0:1], 0.0)
        + z_coarse
    )
    mapped = stencil(smoothed, bonds, diagonal, brought(x_next, y_next, z_next))
    for c in range(CHUNKS):
        mapped_out[c] = mapped[c]

    values = [
        total_of(mapped[:8]),
        total_of(mapped[8:]),
        total_of([residual[c] * smoothed[c] for c in range(CHUNKS)]),
        total_of([mapped[c] * smoothed[c] for c in range(CHUNKS)]),
    ]
    if not first:
        values.append(total_of([search_ref[c] * smoothed[c] for c in range(CHUNKS)]))
    if last:
        level = lane_row // 16
        line = jnp.zeros((1, 128), F32)
        for i in range(2, 5):
            line = jnp.where(level == i, values[i], line)
        for k in range(tile_out.shape[0]):
            tile_out[k] = line
        writing.wait()
        return
    y1 = [relax_ref[c] * mapped[c] for c in range(CHUNKS)]
    write_copies(tile_ref, edge_tile(y1, row, values))
    sending = pltpu.make_async_copy(tile_ref, tile_out, sent)
    sending.start()
    outcome = stencil(y1, bonds, diagonal)
    partial = [y1[c] + relax_ref[c] * (mapped[c] - outcome[c]) for c in range(CHUNKS)]
    write_xy(xy_out, row, y1, partial)
    z_out[Z_Y1 : Z_Y1 + BS] = pack(y1)
    z_out[Z_P : Z_P + BS] = pack(partial)
    writing.wait()
    sending.wait()


def finish_kernel(
    tiles_ref, scalars_ref, residual_ref, mapped_ref, search_ref, third_ref, first_hbm, second_hbm,
    solution_hbm, residual_hbm, first_ref, second_ref, arrived,
):
    copies = [
        pltpu.make_async_copy(first_hbm, first_ref, arrived.at[0]),
        pltpu.make_async_copy(second_hbm, second_ref, arrived.at[1]),
    ]
    for copy in copies:
        copy.start()
    scalars = scalars_ref[...]
    line = tiles_ref[0]
    for k in range(1, tiles_ref.shape[0]):
        line = line + tiles_ref[k]
    _, _, step, growth = search_scalars(
        [line[:, 16 * i : 16 * i + 1] for i in range(2, 5)], scalars, ITERS - 1
    )
    first_step, second_step, second_growth = scalars[2:3, 0:1], scalars[3:4, 0:1], scalars[4:5, 0:1]
    second_weight = second_step + growth * step
    first_weight = first_step + second_growth * second_weight
    for copy in copies:
        copy.wait()
    for c in range(CHUNKS):
        s, part = c // 8, slice(128 * (c % 8), 128 * (c % 8 + 1))
        total = first_weight * first_ref[s, :, part] + second_weight * second_ref[s, :, part]
        first_ref[s, :, part] = total + step * third_ref[c]
        second_ref[s, :, part] = residual_ref[c] - step * (mapped_ref[c] + growth * search_ref[c])
    copies = [
        pltpu.make_async_copy(first_ref, solution_hbm, arrived.at[0]),
        pltpu.make_async_copy(second_ref, residual_hbm, arrived.at[1]),
    ]
    for copy in copies:
        copy.start()
    for copy in copies:
        copy.wait()


def call(kernel, name, outs, in_spaces, out_spaces, operands, scratch=(), aliases=None):
    spec = lambda space: pl.BlockSpec(memory_space=space)
    in_spaces = list(in_spaces) + [pltpu.VMEM] * (len(operands) - len(in_spaces))
    out_spaces = list(out_spaces) + [pltpu.VMEM] * (len(outs) - len(out_spaces))
    return pl.pallas_call(
        kernel,
        out_shape=tuple(outs),
        in_specs=[spec(space) for space in in_spaces],
        out_specs=tuple(spec(space) for space in out_spaces),
        scratch_shapes=list(scratch),
        input_output_aliases=aliases or {},
        compiler_params=pltpu.CompilerParams(vmem_limit_bytes=16 * 1024 * 1024),
        name=name,
    )(*operands)


def array(*shape):
    return jax.ShapeDtypeStruct(shape, F32)


def to_all(copies, axes):
    return lax.all_to_all(copies, axes, 0, 0, tiled=True)


def exchange_slabs(message):
    count = lax.axis_size("grp")
    upward = [(i, i + 1) for i in range(count - 1)]
    downward = [(i + 1, i) for i in range(count - 1)]
    return lax.ppermute(message, "grp", downward), lax.ppermute(message, "grp", upward)


def on_device(source, uptake, conductance, occupancy, assignment):
    slabs = lax.axis_size("grp")
    bricks = lax.axis_size("brick")
    place = (lax.axis_index("grp") * bricks + lax.axis_index("brick")).astype(jnp.int32).reshape(1)
    field = array(*FIELD)
    brick_pair = array(2, BS, BS * BS)
    copies = array(8 * slabs * bricks, 128)
    info, bonds, outer, diagonal, residual, sides, ends, tile = call(
        functools.partial(setup_kernel, slabs, bricks),
        "setup",
        [
            jax.ShapeDtypeStruct((8,), jnp.int32), array(3, *FIELD), array(B_ROWS, 128), field, field,
            array(XY_ROWS_FIRST, 128), array(Z_ROWS_FIRST, 128), copies,
        ],
        [pltpu.SMEM] * 3,
        [pltpu.SMEM],
        [
            place, assignment, jnp.transpose(occupancy, (1, 2, 0)),
            source[0, 0], uptake[0, 0], conductance[0, 0],
        ],
        [
            pltpu.VMEM(FIELD, F32), pltpu.VMEM(FIELD, F32),
        ],
    )
    mapped = residual
    directions = []
    state = {}
    for iteration in range(ITERS):
        first, last = iteration == 0, iteration == ITERS - 1
        tiles = to_all(tile, ("brick", "grp"))
        above, below = exchange_slabs(ends)
        gathered = lax.all_gather(sides, "brick", axis=0, tiled=False)
        operands = [info, gathered, above, below, tiles, bonds, outer, diagonal, residual]
        tall = array(H_S + 8 * slabs, 128)
        outs = {"smoothed": field if last else brick_pair, "mapped": field}
        if not first:
            operands += [mapped] + [state[k] for k in ("halo", "constant", "scalars")]
        if iteration > 1:
            operands += [state[k] for k in ("search", "search_halo")]
        if first:
            outs |= {"constant": array(C_F + 8 * slabs, 128), "halo": tall}
        else:
            outs |= {"residual": field, "search": field, "scalars": array(8, 128)}
            if not last:
                outs |= {"halo": tall, "search_halo": tall}
        outs["tile"] = array(slabs * bricks, 1, 128) if last else copies
        if not last:
            outs |= {"sides": array(XY_ROWS, 128), "ends": array(Z_ROWS, 128)}
        moved = ("smoothed",) if last else ("smoothed", "tile")
        results = call(
            functools.partial(step_kernel, iteration, slabs, bricks),
            f"step_{iteration}",
            list(outs.values()),
            [pltpu.SMEM],
            [pl.ANY if name in moved else pltpu.VMEM for name in outs],
            operands,
            [
                pltpu.VMEM(FIELD, F32),
                pltpu.VMEM(FIELD if last else (2, BS, BS * BS), F32),
                pltpu.SemaphoreType.DMA,
            ]
            + ([] if last else [pltpu.VMEM(copies.shape, F32), pltpu.SemaphoreType.DMA]),
        )
        state |= dict(zip(outs, results))
        if first:
            state["scalars"] = jnp.zeros((8, 128), F32)
        mapped, tile = state["mapped"], state["tile"]
        sides, ends = state.get("sides"), state.get("ends")
        residual = state.get("residual", residual)
        directions.append(state["smoothed"])
    tiles = to_all(tile, ("brick", "grp"))
    solution_field, residual = call(
        finish_kernel,
        "finish",
        [brick_pair, brick_pair],
        [pltpu.VMEM] * 6 + [pl.ANY] * 2,
        [pl.ANY] * 2,
        [tiles, state["scalars"], residual, mapped, state["search"], directions[2]] + directions[:2],
        [
            pltpu.VMEM(brick_pair.shape, F32), pltpu.VMEM(brick_pair.shape, F32),
            pltpu.SemaphoreType.DMA((2,)),
        ],
        {6: 0, 7: 1},
    )
    return solution_field[None, None], residual[None, None]


def solution(mesh):
    return jax.shard_map(
        on_device,
        mesh=mesh,
        in_specs=(
            P("grp", "brick", None, None, None),
            P("grp", "brick", None, None, None),
            P("grp", "brick", None, None, None, None),
            P(),
            P(),
        ),
        out_specs=(P("grp", "brick", None, None, None), P("grp", "brick", None, None, None)),
        check_vma=False,
    )
```

```python
import functools

import jax
import jax.numpy as jnp
from jax import lax
from jax.experimental import pallas as pl
from jax.experimental.pallas import tpu as pltpu
from jax.sharding import PartitionSpec as P

BS = 32
CHUNKS = 16
OMEGA = 0.6
ITERS = 3
F32 = jnp.float32
FIELD = (CHUNKS, BS, 128)

XY_X1, XY_XP, XY_Y = 0, 16, 32
XY_ROWS = 64
XY_XD, XY_YC, XY_K = 64, 80, 112
XY_ROWS_FIRST = 120
Z_Y1, Z_P = 0, 32
Z_ROWS = 64
Z_D, Z_K, Z_X = 64, 96, 128
Z_ROWS_FIRST = 136
T_N, T_Y = 16, 64
H_X1, H_Y, H_Z1, H_ZP, H_E, H_R, H_S = 0, 32, 64, 96, 128, 160, 168
C_XD, C_YC, C_ZD, C_ZK, C_K, C_F = 0, 16, 48, 80, 112, 120
B_XP, B_XM, B_YP, B_YM, B_Z = 0, 16, 32, 64, 96
B_ROWS = 128


def roll(block, shift):
    return pltpu.roll(block, shift % 128, axis=1)


def roll_row(row, shift):
    return pltpu.roll(jnp.broadcast_to(row, (8, 128)), shift % 128, axis=1)[0:1]


def lanes(rows=BS):
    return lax.broadcasted_iota(jnp.int32, (rows, 128), 1)


def rows_of(height=BS):
    return lax.broadcasted_iota(jnp.int32, (height, 128), 0)


def pack(chunks):
    height = chunks[0].shape[0]
    pair = (lanes(height) % BS) // 2
    total = jnp.zeros((height, 128), F32)
    for c in range(CHUNKS):
        moved = roll(chunks[c], 2 * c - 31) if height > 1 else roll_row(chunks[c], 2 * c - 31)
        total = jnp.where(pair == c, moved, total)
    return total


def stencil(field, bonds, diagonal, outer=None):
    lane = lanes()
    height = rows_of()
    depth = lane % BS
    at_end = (depth == BS - 1) | (depth == 0)
    back = [roll(f, -32) for f in field]
    forth = [roll(bonds(1, c) * field[c], 32) for c in range(CHUNKS)]
    out = []
    for c in range(CHUNKS):
        f = field[c]
        total = diagonal(c) * f
        total -= bonds(0, c) * pltpu.roll(f, BS - 1, axis=0)
        total -= pltpu.roll(bonds(0, c) * f, 1, axis=0)
        following = back[c + 1] if c < CHUNKS - 1 else back[c]
        previous = forth[c - 1] if c > 0 else jnp.zeros((BS, 128), F32)
        total -= bonds(1, c) * jnp.where(lane < 96, back[c], following)
        total -= jnp.where(lane >= 32, forth[c], previous)
        total -= bonds(2, c) * roll(f, -1)
        total -= roll(bonds(2, c) * f, 1)
        if outer is not None:
            x_up, x_down, y_low, y_high, z_ends = outer
            total -= jnp.where(height == BS - 1, x_up[c : c + 1], 0.0)
            total -= jnp.where(height == 0, x_down[c : c + 1], 0.0)
            total -= jnp.where(at_end, roll(z_ends, 31 - 2 * c), 0.0)
            if c == 0:
                total -= jnp.where(lane < 32, y_low, 0.0)
            if c == CHUNKS - 1:
                total -= jnp.where(lane >= 96, y_high, 0.0)
        out.append(total)
    return out


def total_of(blocks):
    acc = blocks[0]
    for block in blocks[1:]:
        acc = acc + block
    return jnp.sum(jnp.sum(acc, axis=0, keepdims=True), axis=1, keepdims=True)


def facing(block, row):
    return jnp.where(row == 0, block[BS - 1 : BS], block[0:1])


def side_blocks(low_first, high_first, low_second, high_second):
    group = lanes() // 32
    return jnp.where(
        group == 0,
        low_first,
        jnp.where(
            group == 1,
            roll(high_first, 64),
            jnp.where(group == 2, roll(low_second, 64), high_second),
        ),
    )


def write_xy(xy_ref, row, y1, partial):
    for c in range(CHUNKS):
        xy_ref[XY_X1 + c : XY_X1 + c + 1] = facing(y1[c], row)
        xy_ref[XY_XP + c : XY_XP + c + 1] = facing(partial[c], row)
    last = CHUNKS - 1
    xy_ref[XY_Y : XY_Y + BS] = side_blocks(y1[0], y1[last], partial[0], partial[last])


def write_scalars(ref, start, values):
    for i, value in enumerate(values):
        ref[start + i : start + i + 1] = jnp.broadcast_to(value, (1, 128))
    for i in range(len(values), 8):
        ref[start + i : start + i + 1] = jnp.zeros((1, 128), F32)


def tile_of(values, y1=None):
    lane = lanes(8)
    level = rows_of(8)
    tile = jnp.zeros((8, 128), F32)
    for i, value in enumerate(values):
        tile = jnp.where((level == i) & (lane >= T_N) & (lane < T_Y), value, tile)
    if y1 is None:
        return tile
    row, low, high = y1
    tile = jnp.where((level == 0) & (lane >= T_Y), row, tile)
    tile = jnp.where((level == 1) & (lane >= T_Y), roll_row(row, 64), tile)
    wide = lanes()
    edges = jnp.where(wide == 0, low, 0.0)
    edges = jnp.where(wide == 1, roll(low, -30), edges)
    edges = jnp.where(wide == 2, roll(high, -94), edges)
    edges = jnp.where(wide == 3, roll(high, -124), edges)
    for t in range(4):
        tile = tile + roll(edges[8 * t : 8 * t + 8], 4 * t)
    return tile


def write_copies(ref, tile):
    for k in range(ref.shape[0] // 8):
        ref[8 * k : 8 * k + 8] = tile


def edge_tile(y1, row, values):
    line = pack([facing(f, row) for f in y1])
    return tile_of(values, (line, y1[0], y1[CHUNKS - 1]))


def locate(bricks, place_ref, assignment_ref):
    across = bricks // 2
    place = place_ref[0]
    slab = place // bricks
    patch = assignment_ref[place % bricks]
    row = patch // across
    column = patch % across
    return slab, patch, row, column


def setup_kernel(
    slabs, bricks, place_ref, assignment_ref, occupancy_ref, source_ref, uptake_ref, conductance_ref,
    info_ref, bonds_ref, outer_ref, diagonal_ref, residual_ref, xy_ref, z_ref, tile_ref,
    relax_ref, y1_ref,
):
    across = bricks // 2
    slab, patch, row, column = locate(bricks, place_ref, assignment_ref)

    def holder(row_target, column_target):
        inside = (column_target >= 0) & (column_target < across)
        wanted = jnp.where(inside, row_target * across + column_target, patch)
        found = jnp.int32(0)
        for b in range(bricks):
            found = jnp.where(assignment_ref[b] == wanted, b, found)
        return found

    info_ref[0] = row
    info_ref[1] = slab
    info_ref[2] = holder(row, column)
    info_ref[3] = holder(1 - row, column)
    info_ref[4] = holder(row, column - 1)
    info_ref[5] = holder(row, column + 1)
    info_ref[6] = holder(1 - row, column - 1)
    info_ref[7] = holder(1 - row, column + 1)

    breadth = 2 * across

    def live_at(g, x, y):
        inside = (g >= 0) & (g < slabs) & (x >= 0) & (x < 2) & (y >= 0) & (y < breadth)
        taken = occupancy_ref[jnp.clip(x, 0, 1), jnp.clip(y, 0, breadth - 1), jnp.clip(g, 0, slabs - 1)]
        return jnp.where(inside, taken, 0).astype(F32)

    lane = lanes()
    height = rows_of()
    depth = lane % BS
    absorbed = []
    low_ends = []
    high_ends = []
    first_y = None
    second_y = None
    for s in range(2):
        y = column * 2 + s
        here = live_at(slab, row, y)
        around = [
            here * live_at(slab, row + 1, y),
            here * live_at(slab, row - 1, y),
            here * live_at(slab, row, y + 1),
            here * live_at(slab, row, y - 1),
            here * live_at(slab + 1, row, y),
            here * live_at(slab - 1, row, y),
        ]
        borders = [height == BS - 1, height == 0, lane >= 96, lane < 32, depth == BS - 1, depth == 0]
        for k in range(8):
            c = 8 * s + k
            part = pl.ds(128 * k, 128)
            taken = uptake_ref[s, :, part]
            absorbed.append(taken)
            diagonal = taken
            values = []
            for d in range(6):
                bond = conductance_ref[d, s, :, part]
                if (d == 2 and k < 7) or (d == 3 and k > 0):
                    value = bond * here
                else:
                    value = bond * jnp.where(borders[d], around[d], here)
                values.append(value)
                diagonal = diagonal + value
            if c == 7:
                first_y = jnp.where(borders[2], values[2], 0.0)
            if c == 8:
                second_y = jnp.where(borders[3], values[3], 0.0)
            high_ends.append(jnp.where(borders[4], values[4], 0.0))
            low_ends.append(jnp.where(borders[5], values[5], 0.0))
            outer_ref[B_XP + c : B_XP + c + 1] = values[0][BS - 1 : BS]
            outer_ref[B_XM + c : B_XM + c + 1] = values[1][0:1]
            bonds_ref[0, c] = jnp.where(borders[0], 0.0, values[0])
            if c == CHUNKS - 1:
                outer_ref[B_YP : B_YP + BS] = jnp.where(borders[2], values[2], 0.0)
                bonds_ref[1, c] = jnp.where(borders[2], 0.0, values[2])
            else:
                bonds_ref[1, c] = values[2]
            if c == 0:
                outer_ref[B_YM : B_YM + BS] = jnp.where(borders[3], values[3], 0.0)
            bonds_ref[2, c] = jnp.where(borders[4], 0.0, values[4])
            relax = OMEGA / diagonal
            diagonal_ref[c] = diagonal
            relax_ref[c] = relax
            forcing = source_ref[s, :, part] * here
            residual_ref[c] = forcing
            y1_ref[c] = relax * forcing

    ends = [high_ends[c] + low_ends[c] for c in range(CHUNKS)]
    outer_ref[B_Z : B_Z + BS] = pack(ends)
    y1 = [y1_ref[c] for c in range(CHUNKS)]
    outcome = stencil(y1, lambda d, c: bonds_ref[d, c], lambda c: diagonal_ref[c])
    partial = [y1[c] + relax_ref[c] * (residual_ref[c] - outcome[c]) for c in range(CHUNKS)]
    write_xy(xy_ref, row, y1, partial)
    z_ref[Z_Y1 : Z_Y1 + BS] = pack(y1)
    z_ref[Z_P : Z_P + BS] = pack(partial)

    first_coupling = total_of([first_y])
    high_sums = [total_of(high_ends[8 * s : 8 * s + 8]) for s in range(2)]
    low_sums = [total_of(low_ends[8 * s : 8 * s + 8]) for s in range(2)]
    taken_sums = [total_of(absorbed[8 * s : 8 * s + 8]) for s in range(2)]
    residual_sums = [total_of([residual_ref[8 * s + k] for k in range(8)]) for s in range(2)]
    numbers = [
        residual_sums[0],
        residual_sums[1],
        taken_sums[0] + first_coupling + high_sums[0] + low_sums[0],
        taken_sums[1] + total_of([second_y]) + high_sums[1] + low_sums[1],
        first_coupling,
        high_sums[0],
        high_sums[1],
    ]
    write_copies(tile_ref, edge_tile(y1, row, numbers))

    last = CHUNKS - 1
    z_ends = [relax_ref[c] * ends[c] for c in range(CHUNKS)]
    for c in range(CHUNKS):
        xy_ref[XY_XD + c : XY_XD + c + 1] = facing(relax_ref[c], row)
    high_y = relax_ref[last] * outer_ref[B_YP : B_YP + BS]
    low_y = relax_ref[0] * outer_ref[B_YM : B_YM + BS]
    xy_ref[XY_YC : XY_YC + BS] = side_blocks(relax_ref[0], relax_ref[last], z_ends[0], z_ends[last])
    xy_ref[XY_K : XY_K + 1] = facing(low_y + high_y, row)
    xy_ref[XY_K + 1 : XY_K + 2] = pack([facing(z, row) for z in z_ends])
    toward = [
        relax_ref[c][BS - 1 : BS] * outer_ref[B_XP + c : B_XP + c + 1]
        + relax_ref[c][0:1] * outer_ref[B_XM + c : B_XM + c + 1]
        for c in range(CHUNKS)
    ]
    xy_ref[XY_K + 2 : XY_K + 3] = jnp.where(lanes(1) < 32, toward[0], roll_row(toward[last], 64))
    xy_ref[XY_K + 3 : XY_K + 8] = jnp.zeros((5, 128), F32)
    z_ref[Z_D : Z_D + BS] = pack([relax_ref[c] for c in range(CHUNKS)])
    z_ref[Z_K : Z_K + BS] = pack([low_y] + [jnp.zeros((BS, 128), F32)] * (CHUNKS - 2) + [high_y])
    z_ref[Z_X : Z_X + 8] = jnp.broadcast_to(pack(toward), (8, 128))


def swap_sides(from_low, from_high):
    rows = from_low.shape[0]
    if rows == 1:
        low, high = roll_row(from_low, -32), roll_row(from_high, 32)
    else:
        low, high = roll(from_low, -32), roll(from_high, 32)
    return jnp.where((lanes(rows) // 32) % 2 == 0, low, high)


def search_scalars(sums, scalars, iteration):
    energy = sums[0]
    curvature = sums[1]
    if iteration == 0:
        return energy, curvature, energy / curvature, None
    growth = energy / scalars[0:1, 0:1]
    curvature = curvature + growth * (2.0 * sums[2] + growth * scalars[1:2, 0:1])
    return energy, curvature, energy / curvature, growth


def sum_tiles(ref, count):
    total = ref[0:8]
    for g in range(1, count):
        total = total + ref[8 * g : 8 * g + 8]
    return total


def step_kernel(iteration, slabs, bricks, *refs):
    first = iteration == 0
    last = iteration == ITERS - 1
    refs = list(refs)
    take = lambda count: [refs.pop(0) for _ in range(count)]
    info_ref, xy_ref, above_ref, below_ref, tiles_ref = take(5)
    bonds_ref, outer_ref, diagonal_ref, residual_ref = take(4)
    if not first:
        mapped_ref, halo_in, constant_ref, scalars_in = take(4)
    if iteration > 1:
        search_in, search_halo_in = take(2)
    if last:
        zero_hbm, one_hbm = take(2)
        advance_ref, direction_ref, smoothed_ref, mapped_out = take(4)
    else:
        smoothed_hbm, mapped_out = take(2)
    if first:
        constant_ref, halo_ref = take(2)
    else:
        residual_out, search_ref, scalars_ref = take(3)
        if not last:
            halo_ref, search_halo_ref = take(2)
    tile_out = take(1)[0]
    if not last:
        xy_out, z_out = take(2)
    relax_ref = take(1)[0]
    if last:
        zero_ref, one_ref, arrived = take(3)
        reading = [
            pltpu.make_async_copy(zero_hbm, zero_ref, arrived.at[0]),
            pltpu.make_async_copy(one_hbm, one_ref, arrived.at[1]),
        ]
        for copy in reading:
            copy.start()
    else:
        smoothed_ref, written, tile_ref, sent = take(4)
    for c in range(CHUNKS):
        relax_ref[c] = OMEGA / diagonal_ref[c]

    row = info_ref[0]
    slab = info_ref[1]
    lane = lanes()
    height = rows_of()
    depth = lane % BS
    lane_row = lanes(1)
    even = lane % 2 == 0
    even_row = lane_row % 2 == 0
    low_holder, high_holder = info_ref[4], info_ref[5]
    low_corner, high_corner = info_ref[6], info_ref[7]
    x_holder = info_ref[3]

    def merge(start):
        up = roll(above_ref[start : start + BS], 31)
        down = roll(below_ref[start : start + BS], -31)
        return jnp.where(even, up, down)

    x_sides = xy_ref[x_holder, XY_X1 : XY_X1 + 2 * CHUNKS]
    y_sides = swap_sides(
        xy_ref[low_holder, XY_Y : XY_Y + BS], xy_ref[high_holder, XY_Y : XY_Y + BS]
    )
    z_first = merge(Z_Y1)
    z_second = merge(Z_P)

    def tile_at(holder, g):
        return tiles_ref[pl.ds(pl.multiple_of((holder * slabs + g) * 8, 8), 8)]

    slab_above = jnp.minimum(slab + 1, slabs - 1)
    slab_below = jnp.maximum(slab - 1, 0)

    def edge_row(tile):
        return jnp.where(lane_row >= T_Y, tile[0:1], roll_row(tile[1:2], 64))

    x_ends = jnp.where(
        even_row,
        roll_row(edge_row(tile_at(x_holder, slab_above)), 31),
        roll_row(edge_row(tile_at(x_holder, slab_below)), -31),
    )
    kind = lanes(8) % 4
    mixed = jnp.where(
        kind == 0,
        roll(tile_at(low_holder, slab_above), -2),
        jnp.where(
            kind == 1,
            roll(tile_at(low_holder, slab_below), -2),
            jnp.where(
                kind == 2,
                roll(tile_at(high_holder, slab_above), 2),
                roll(tile_at(high_holder, slab_below), 2),
            ),
        ),
    )
    y_edges = jnp.where(
        lane < 4, jnp.concatenate([roll(mixed, -4 * t) for t in range(4)], axis=0), 0.0
    )
    corner_y = jnp.where(
        lane_row < 32,
        roll_row(xy_ref[low_corner, XY_X1 + CHUNKS - 1 : XY_X1 + CHUNKS], 32),
        roll_row(xy_ref[high_corner, XY_X1 : XY_X1 + 1], -32),
    )
    low_row = jnp.where(
        row == 0,
        xy_ref[low_corner, XY_Y : XY_Y + 1],
        xy_ref[low_corner, XY_Y + BS - 1 : XY_Y + BS],
    )
    high_row = jnp.where(
        row == 0,
        xy_ref[high_corner, XY_Y : XY_Y + 1],
        xy_ref[high_corner, XY_Y + BS - 1 : XY_Y + BS],
    )
    corner_x = swap_sides(low_row, high_row)
    ends = jnp.concatenate([x_ends, corner_y, corner_x, jnp.zeros((5, 128), F32)], axis=0)
    lane_tile = lanes(8)
    slab_tiles = []
    for g in range(slabs):
        tile = tile_at(info_ref[2], g)
        for q in range(1, 4):
            tile = jnp.where(lane_tile == T_N + q, tile_at(info_ref[2 + q], g), tile)
        slab_tiles.append(tile)
    sums = jnp.concatenate(slab_tiles, axis=0)
    halo = [x_sides, y_sides, z_first, z_second, y_edges, ends, sums]
    starts = [H_X1, H_Y, H_Z1, H_ZP, H_E, H_R, H_S]

    if first:
        residual = [residual_ref[c] for c in range(CHUNKS)]
        constant_ref[C_XD : C_XD + CHUNKS] = xy_ref[x_holder, XY_XD : XY_XD + CHUNKS]
        constant_ref[C_YC : C_YC + BS] = swap_sides(
            xy_ref[low_holder, XY_YC : XY_YC + BS], xy_ref[high_holder, XY_YC : XY_YC + BS]
        )
        constant_ref[C_ZD : C_ZD + BS] = merge(Z_D)
        constant_ref[C_ZK : C_ZK + BS] = merge(Z_K)
        constant_ref[C_K : C_K + 8] = jnp.concatenate(
            [
                xy_ref[x_holder, XY_K : XY_K + 2],
                swap_sides(
                    xy_ref[low_holder, XY_K + 2 : XY_K + 3],
                    xy_ref[high_holder, XY_K + 2 : XY_K + 3],
                ),
                jnp.where(
                    even_row,
                    roll_row(above_ref[Z_X : Z_X + 1], 31),
                    roll_row(below_ref[Z_X : Z_X + 1], -31),
                ),
                jnp.zeros((4, 128), F32),
            ],
            axis=0,
        )
        for g in range(slabs):
            tile = sums[8 * g : 8 * g + 8]
            a, b, off = tile[2:3], tile[3:4], tile[4:5]
            t0, t1 = tile[5:6], tile[6:7]
            if g > 0:
                a = a - u0 * u0 * i00
                b = b - u1 * u1 * i11
                off = off + u0 * u1 * i01
            used = (lane_row >= T_N) & (lane_row < T_N + 4)
            a = jnp.where(used, a, 1.0)
            b = jnp.where(used, b, 1.0)
            off = jnp.where(used, off, 0.0)
            t0 = jnp.where(used, t0, 0.0)
            t1 = jnp.where(used, t1, 0.0)
            scale = 1.0 / (a * b - off * off)
            i00, i01, i11 = b * scale, off * scale, a * scale
            u0, u1 = t0, t1
            constant_ref[C_F + 8 * g : C_F + 8 * g + 8] = jnp.concatenate(
                [i00, i01, i11, t0, t1, jnp.zeros((3, 128), F32)], axis=0
            )
    else:
        scalars = None if iteration == 1 else scalars_in[...]
        tile = sum_tiles(tiles_ref, slabs * bricks)
        energy, curvature, step, growth = search_scalars(
            [tile[i : i + 1, T_N : T_N + 1] for i in range(2, 5)], scalars, iteration - 1
        )
        step_row = jnp.broadcast_to(step, (1, 128))
        residual = []
        for c in range(CHUNKS):
            mapped = mapped_ref[c]
            if growth is not None:
                mapped = mapped + growth * search_in[c]
            search_ref[c] = mapped
            value = residual_ref[c] - step * mapped
            residual_out[c] = value
            residual.append(value)
        old_halo = halo
        halo = []
        for start, block in zip(starts, old_halo):
            span = slice(start, start + block.shape[0])
            if growth is not None:
                block = block + growth * search_halo_in[span]
            if not last:
                search_halo_ref[span] = block
            halo.append(halo_in[span] - step * block)
        kept = [energy, curvature, step]
        if growth is not None:
            kept = [energy, curvature, scalars[2:3, 0:1], step, growth]
        write_scalars(scalars_ref, 0, kept)

    if not last:
        for start, block in zip(starts, halo):
            halo_ref[start : start + block.shape[0]] = block
    x_sides, y_sides, z_first, z_second, y_edges, ends, sums = halo

    forward = []
    for g in range(slabs):
        t0, t1 = sums[8 * g : 8 * g + 1], sums[8 * g + 1 : 8 * g + 2]
        if g > 0:
            t0 = t0 + w0 * v0
            t1 = t1 + w1 * v1
        factor = constant_ref[C_F + 8 * g : C_F + 8 * g + 8]
        v0 = factor[0:1] * t0 + factor[1:2] * t1
        v1 = factor[1:2] * t0 + factor[2:3] * t1
        w0, w1 = factor[3:4], factor[4:5]
        forward.append((v0, v1))
    blank = jnp.zeros((1, 128), F32)
    below0, below1, here0, here1, above0, above1 = [blank] * 6
    for g in reversed(range(slabs)):
        v0, v1 = forward[g]
        if g < slabs - 1:
            factor = constant_ref[C_F + 8 * g : C_F + 8 * g + 8]
            s0, s1 = factor[3:4] * n0, factor[4:5] * n1
            v0 = v0 + factor[0:1] * s0 + factor[1:2] * s1
            v1 = v1 + factor[1:2] * s0 + factor[2:3] * s1
        n0, n1 = v0, v1
        here0 = jnp.where(slab == g, n0, here0)
        here1 = jnp.where(slab == g, n1, here1)
        above0 = jnp.where(slab + 1 == g, n0, above0)
        above1 = jnp.where(slab + 1 == g, n1, above1)
        below0 = jnp.where(slab - 1 == g, n0, below0)
        below1 = jnp.where(slab - 1 == g, n1, below1)
    def coarse_of(row, q):
        return row[:, T_N + q : T_N + q + 1]

    own = [coarse_of(here0, 0), coarse_of(here1, 0)]

    bonds = lambda d, c: bonds_ref[d, c]
    diagonal = lambda c: diagonal_ref[c]
    end = CHUNKS - 1
    x_plus = outer_ref[B_XP : B_XP + CHUNKS]
    x_minus = outer_ref[B_XM : B_XM + CHUNKS]
    y_plus = outer_ref[B_YP : B_YP + BS]
    y_minus = outer_ref[B_YM : B_YM + BS]
    z_bonds = outer_ref[B_Z : B_Z + BS]

    def brought(x_rows, y_block, z_block):
        return (
            x_plus * x_rows,
            x_minus * x_rows,
            y_minus * y_block,
            y_plus * roll(y_block, 64),
            z_bonds * z_block,
        )

    y1 = [relax_ref[c] * residual[c] for c in range(CHUNKS)]
    outcome = stencil(y1, bonds, diagonal, brought(x_sides[:CHUNKS], y_sides, z_first))
    smoothed = []
    for c in range(CHUNKS):
        value = y1[c] + relax_ref[c] * (residual[c] - outcome[c]) + own[c // 8]
        if last:
            smoothed_ref[c] = value
        else:
            smoothed_ref[c // 8, :, 128 * (c % 8) : 128 * (c % 8 + 1)] = value
        smoothed.append(value)
    if not last:
        writing = pltpu.make_async_copy(smoothed_ref, smoothed_hbm, written)
        writing.start()
    keys = constant_ref[C_K : C_K + 8]
    crossing = x_plus * jnp.concatenate([f[BS - 1 : BS] for f in y1], axis=0)
    crossing += x_minus * jnp.concatenate([f[0:1] for f in y1], axis=0)
    end_row = keys[1:2] * ends[0:1]
    corner_row = keys[0:1] * ends[1:2]
    depth_row = lane_row % BS
    additions = []
    for c in range(CHUNKS):
        value = jnp.where(
            (depth_row == BS - 1) | (depth_row == 0), roll_row(end_row, 31 - 2 * c), 0.0
        )
        if c == 0:
            value = value + jnp.where(lane_row < 32, corner_row, 0.0)
        if c == end:
            value = value + jnp.where(lane_row >= 96, corner_row, 0.0)
        value = value + coarse_of(here0 if c < 8 else here1, 1)
        additions.append(value)
    x_next = (
        x_sides[CHUNKS:]
        + constant_ref[C_XD : C_XD + CHUNKS] * crossing
        + jnp.concatenate(additions, axis=0)
    )
    y_constant = constant_ref[C_YC : C_YC + BS]
    y_crossing = jnp.where(lane < 32, y_minus * y1[0], roll(y_plus * y1[end], 64))
    x_side_row = jnp.where(row == 0, BS - 1, 0)
    y_ends = jnp.where(lane == 0, roll(y_edges, -1), 0.0)
    y_ends = jnp.where(lane == 31, roll(y_edges, 31), y_ends)
    y_ends = jnp.where(lane == 32, roll(y_edges, 29), y_ends)
    y_ends = jnp.where(lane == 63, roll(y_edges, 61), y_ends)
    z_sides = jnp.where(lane == 0, y_edges, 0.0)
    z_sides = jnp.where(lane == 97, roll(y_edges, 96), z_sides)
    z_sides = jnp.where(lane == 126, roll(y_edges, 124), z_sides)
    z_sides = jnp.where(lane == 95, roll(y_edges, 92), z_sides)
    y_next = (
        roll(y_sides, 64)
        + y_constant * y_crossing
        + roll(y_constant, 64) * y_ends
        + jnp.where(height == x_side_row, keys[2:3] * ends[2:3], 0.0)
        + jnp.where(lane < 32, coarse_of(here1, 2), coarse_of(here0, 3))
    )
    z_crossing = z_bonds * pack(y1)
    z_coarse = jnp.where(
        even_row,
        jnp.where(depth_row < 16, coarse_of(above0, 0), coarse_of(above1, 0)),
        jnp.where(depth_row < 16, coarse_of(below0, 0), coarse_of(below1, 0)),
    )
    z_next = (
        z_second
        + constant_ref[C_ZD : C_ZD + BS] * z_crossing
        + constant_ref[C_ZK : C_ZK + BS] * z_sides
        + jnp.where(height == x_side_row, keys[3:4] * ends[0:1], 0.0)
        + z_coarse
    )
    mapped = stencil(smoothed, bonds, diagonal, brought(x_next, y_next, z_next))
    for c in range(CHUNKS):
        mapped_out[c] = mapped[c]

    values = [
        total_of(mapped[:8]),
        total_of(mapped[8:]),
        total_of([residual[c] * smoothed[c] for c in range(CHUNKS)]),
        total_of([mapped[c] * smoothed[c] for c in range(CHUNKS)]),
    ]
    if not first:
        values.append(total_of([search_ref[c] * smoothed[c] for c in range(CHUNKS)]))
    if last:
        level = lane_row // 16
        line = jnp.zeros((1, 128), F32)
        for i in range(2, 5):
            line = jnp.where(level == i, values[i], line)
        for k in range(tile_out.shape[0]):
            tile_out[k] = line
        for copy in reading:
            copy.wait()
        first_step = scalars_in[2:3, 0:1]
        for c in range(CHUNKS):
            s, part = c // 8, slice(128 * (c % 8), 128 * (c % 8 + 1))
            direction = one_ref[s, :, part] + growth * zero_ref[s, :, part]
            direction_ref[c] = direction
            advance_ref[c] = first_step * zero_ref[s, :, part] + step * direction
        return
    y1 = [relax_ref[c] * mapped[c] for c in range(CHUNKS)]
    write_copies(tile_ref, edge_tile(y1, row, values))
    sending = pltpu.make_async_copy(tile_ref, tile_out, sent)
    sending.start()
    outcome = stencil(y1, bonds, diagonal)
    partial = [y1[c] + relax_ref[c] * (mapped[c] - outcome[c]) for c in range(CHUNKS)]
    write_xy(xy_out, row, y1, partial)
    z_out[Z_Y1 : Z_Y1 + BS] = pack(y1)
    z_out[Z_P : Z_P + BS] = pack(partial)
    writing.wait()
    sending.wait()


def finish_kernel(
    tiles_ref, scalars_ref, residual_ref, mapped_ref, search_ref, smoothed_ref, advance_ref, direction_ref,
    first_hbm, second_hbm, solution_hbm, residual_hbm, solution_ref, change_ref, sent,
):
    scalars = scalars_ref[...]
    line = tiles_ref[0]
    for k in range(1, tiles_ref.shape[0]):
        line = line + tiles_ref[k]
    _, _, step, growth = search_scalars(
        [line[:, 16 * i : 16 * i + 1] for i in range(2, 5)], scalars, ITERS - 1
    )
    for c in range(CHUNKS):
        s, part = c // 8, slice(128 * (c % 8), 128 * (c % 8 + 1))
        solution_ref[s, :, part] = advance_ref[c] + step * (smoothed_ref[c] + growth * direction_ref[c])
    copies = [
        pltpu.make_async_copy(solution_ref, solution_hbm, sent.at[0]),
        pltpu.make_async_copy(change_ref, residual_hbm, sent.at[1]),
    ]
    copies[0].start()
    for c in range(CHUNKS):
        s, part = c // 8, slice(128 * (c % 8), 128 * (c % 8 + 1))
        change_ref[s, :, part] = residual_ref[c] - step * (mapped_ref[c] + growth * search_ref[c])
    copies[1].start()
    for copy in copies:
        copy.wait()


def call(kernel, name, outs, in_spaces, out_spaces, operands, scratch=(), aliases=None):
    spec = lambda space: pl.BlockSpec(memory_space=space)
    in_spaces = list(in_spaces) + [pltpu.VMEM] * (len(operands) - len(in_spaces))
    out_spaces = list(out_spaces) + [pltpu.VMEM] * (len(outs) - len(out_spaces))
    return pl.pallas_call(
        kernel,
        out_shape=tuple(outs),
        in_specs=[spec(space) for space in in_spaces],
        out_specs=tuple(spec(space) for space in out_spaces),
        scratch_shapes=list(scratch),
        input_output_aliases=aliases or {},
        compiler_params=pltpu.CompilerParams(vmem_limit_bytes=16 * 1024 * 1024),
        name=name,
    )(*operands)


def array(*shape):
    return jax.ShapeDtypeStruct(shape, F32)


def to_all(copies, axes):
    return lax.all_to_all(copies, axes, 0, 0, tiled=True)


def exchange_slabs(message):
    count = lax.axis_size("grp")
    upward = [(i, i + 1) for i in range(count - 1)]
    downward = [(i + 1, i) for i in range(count - 1)]
    return lax.ppermute(message, "grp", downward), lax.ppermute(message, "grp", upward)


def on_device(source, uptake, conductance, occupancy, assignment):
    slabs = lax.axis_size("grp")
    bricks = lax.axis_size("brick")
    place = (lax.axis_index("grp") * bricks + lax.axis_index("brick")).astype(jnp.int32).reshape(1)
    field = array(*FIELD)
    brick_pair = array(2, BS, BS * BS)
    copies = array(8 * slabs * bricks, 128)
    info, bonds, outer, diagonal, residual, sides, ends, tile = call(
        functools.partial(setup_kernel, slabs, bricks),
        "setup",
        [
            jax.ShapeDtypeStruct((8,), jnp.int32), array(3, *FIELD), array(B_ROWS, 128), field, field,
            array(XY_ROWS_FIRST, 128), array(Z_ROWS_FIRST, 128), copies,
        ],
        [pltpu.SMEM] * 3,
        [pltpu.SMEM],
        [
            place, assignment, jnp.transpose(occupancy, (1, 2, 0)),
            source[0, 0], uptake[0, 0], conductance[0, 0],
        ],
        [
            pltpu.VMEM(FIELD, F32), pltpu.VMEM(FIELD, F32),
        ],
    )
    mapped = residual
    directions = []
    state = {}
    for iteration in range(ITERS):
        first, last = iteration == 0, iteration == ITERS - 1
        tiles = to_all(tile, ("brick", "grp"))
        above, below = exchange_slabs(ends)
        gathered = lax.all_gather(sides, "brick", axis=0, tiled=False)
        operands = [info, gathered, above, below, tiles, bonds, outer, diagonal, residual]
        tall = array(H_S + 8 * slabs, 128)
        if last:
            outs = {"advance": field, "direction": field, "smoothed": field, "mapped": field}
        else:
            outs = {"smoothed": brick_pair, "mapped": field}
        if not first:
            operands += [mapped] + [state[k] for k in ("halo", "constant", "scalars")]
        if iteration > 1:
            operands += [state[k] for k in ("search", "search_halo")]
        in_spaces = [pltpu.SMEM]
        if last:
            in_spaces += [pltpu.VMEM] * (len(operands) - 1) + [pl.ANY] * 2
            operands += directions
        if first:
            outs |= {"constant": array(C_F + 8 * slabs, 128), "halo": tall}
        else:
            outs |= {"residual": field, "search": field, "scalars": array(8, 128)}
            if not last:
                outs |= {"halo": tall, "search_halo": tall}
        outs["tile"] = array(slabs * bricks, 1, 128) if last else copies
        if not last:
            outs |= {"sides": array(XY_ROWS, 128), "ends": array(Z_ROWS, 128)}
        moved = () if last else ("smoothed", "tile")
        pair = pltpu.VMEM(brick_pair.shape, F32)
        results = call(
            functools.partial(step_kernel, iteration, slabs, bricks),
            f"step_{iteration}",
            list(outs.values()),
            in_spaces,
            [pl.ANY if name in moved else pltpu.VMEM for name in outs],
            operands,
            [pltpu.VMEM(FIELD, F32)]
            + (
                [pair, pair, pltpu.SemaphoreType.DMA((2,))]
                if last
                else [
                    pair, pltpu.SemaphoreType.DMA,
                    pltpu.VMEM(copies.shape, F32), pltpu.SemaphoreType.DMA,
                ]
            ),
        )
        state |= dict(zip(outs, results))
        if first:
            state["scalars"] = jnp.zeros((8, 128), F32)
        mapped, tile = state["mapped"], state["tile"]
        sides, ends = state.get("sides"), state.get("ends")
        residual = state.get("residual", residual)
        directions.append(state["smoothed"])
    tiles = to_all(tile, ("brick", "grp"))
    solution_field, residual = call(
        finish_kernel,
        "finish",
        [brick_pair, brick_pair],
        [pltpu.VMEM] * 8 + [pl.ANY] * 2,
        [pl.ANY] * 2,
        [
            tiles, state["scalars"], residual, mapped, state["search"], directions[2],
            state["advance"], state["direction"],
        ]
        + directions[:2],
        [
            pltpu.VMEM(brick_pair.shape, F32), pltpu.VMEM(brick_pair.shape, F32),
            pltpu.SemaphoreType.DMA((2,)),
        ],
        {8: 0, 9: 1},
    )
    return solution_field[None, None], residual[None, None]


def solution(mesh):
    return jax.shard_map(
        on_device,
        mesh=mesh,
        in_specs=(
            P("grp", "brick", None, None, None),
            P("grp", "brick", None, None, None),
            P("grp", "brick", None, None, None, None),
            P(),
            P(),
        ),
        out_specs=(P("grp", "brick", None, None, None), P("grp", "brick", None, None, None)),
        check_vma=False,
    )
```

```python
import functools

import jax
import jax.numpy as jnp
from jax import lax
from jax.experimental import pallas as pl
from jax.experimental.pallas import tpu as pltpu
from jax.sharding import PartitionSpec as P

BS = 32
CHUNKS = 16
OMEGA = 0.6
ITERS = 3
F32 = jnp.float32
FIELD = (CHUNKS, BS, 128)

XY_X1, XY_XP, XY_Y = 0, 16, 32
XY_ROWS = 64
XY_XD, XY_YC, XY_K = 64, 80, 112
XY_ROWS_FIRST = 120
Z_Y1, Z_P = 0, 32
Z_ROWS = 64
Z_D, Z_K, Z_X = 64, 96, 128
Z_ROWS_FIRST = 136
T_N, T_Y = 16, 64
H_X1, H_Y, H_Z1, H_ZP, H_E, H_R, H_S = 0, 32, 64, 96, 128, 160, 168
C_XD, C_YC, C_ZD, C_ZK, C_K, C_F = 0, 16, 48, 80, 112, 120
B_XP, B_XM, B_YP, B_YM, B_Z = 0, 16, 32, 64, 96
B_ROWS = 128


def roll(block, shift):
    return pltpu.roll(block, shift % 128, axis=1)


def roll_row(row, shift):
    return pltpu.roll(jnp.broadcast_to(row, (8, 128)), shift % 128, axis=1)[0:1]


def lanes(rows=BS):
    return lax.broadcasted_iota(jnp.int32, (rows, 128), 1)


def rows_of(height=BS):
    return lax.broadcasted_iota(jnp.int32, (height, 128), 0)


def pack(chunks):
    height = chunks[0].shape[0]
    pair = (lanes(height) % BS) // 2
    total = jnp.zeros((height, 128), F32)
    for c in range(CHUNKS):
        moved = roll(chunks[c], 2 * c - 31) if height > 1 else roll_row(chunks[c], 2 * c - 31)
        total = jnp.where(pair == c, moved, total)
    return total


def stencil(field, bonds, diagonal, outer=None):
    lane = lanes()
    height = rows_of()
    depth = lane % BS
    at_end = (depth == BS - 1) | (depth == 0)
    back = [roll(f, -32) for f in field]
    forth = [roll(bonds(1, c) * field[c], 32) for c in range(CHUNKS)]
    out = []
    for c in range(CHUNKS):
        f = field[c]
        total = diagonal(c) * f
        total -= bonds(0, c) * pltpu.roll(f, BS - 1, axis=0)
        total -= pltpu.roll(bonds(0, c) * f, 1, axis=0)
        following = back[c + 1] if c < CHUNKS - 1 else back[c]
        previous = forth[c - 1] if c > 0 else jnp.zeros((BS, 128), F32)
        total -= bonds(1, c) * jnp.where(lane < 96, back[c], following)
        total -= jnp.where(lane >= 32, forth[c], previous)
        total -= bonds(2, c) * roll(f, -1)
        total -= roll(bonds(2, c) * f, 1)
        if outer is not None:
            x_up, x_down, y_low, y_high, z_ends = outer
            total -= jnp.where(height == BS - 1, x_up[c : c + 1], 0.0)
            total -= jnp.where(height == 0, x_down[c : c + 1], 0.0)
            total -= jnp.where(at_end, roll(z_ends, 31 - 2 * c), 0.0)
            if c == 0:
                total -= jnp.where(lane < 32, y_low, 0.0)
            if c == CHUNKS - 1:
                total -= jnp.where(lane >= 96, y_high, 0.0)
        out.append(total)
    return out


def total_of(blocks):
    acc = blocks[0]
    for block in blocks[1:]:
        acc = acc + block
    return jnp.sum(jnp.sum(acc, axis=0, keepdims=True), axis=1, keepdims=True)


def facing(block, row):
    return jnp.where(row == 0, block[BS - 1 : BS], block[0:1])


def side_blocks(low_first, high_first, low_second, high_second):
    group = lanes() // 32
    return jnp.where(
        group == 0,
        low_first,
        jnp.where(
            group == 1,
            roll(high_first, 64),
            jnp.where(group == 2, roll(low_second, 64), high_second),
        ),
    )


def write_xy(xy_ref, row, y1, partial):
    for c in range(CHUNKS):
        xy_ref[XY_X1 + c : XY_X1 + c + 1] = facing(y1[c], row)
        xy_ref[XY_XP + c : XY_XP + c + 1] = facing(partial[c], row)
    last = CHUNKS - 1
    xy_ref[XY_Y : XY_Y + BS] = side_blocks(y1[0], y1[last], partial[0], partial[last])


def write_scalars(ref, start, values):
    for i, value in enumerate(values):
        ref[start + i : start + i + 1] = jnp.broadcast_to(value, (1, 128))
    for i in range(len(values), 8):
        ref[start + i : start + i + 1] = jnp.zeros((1, 128), F32)


def tile_of(values, y1=None):
    lane = lanes(8)
    level = rows_of(8)
    tile = jnp.zeros((8, 128), F32)
    for i, value in enumerate(values):
        tile = jnp.where((level == i) & (lane >= T_N) & (lane < T_Y), value, tile)
    if y1 is None:
        return tile
    row, low, high = y1
    tile = jnp.where((level == 0) & (lane >= T_Y), row, tile)
    tile = jnp.where((level == 1) & (lane >= T_Y), roll_row(row, 64), tile)
    wide = lanes()
    edges = jnp.where(wide == 0, low, 0.0)
    edges = jnp.where(wide == 1, roll(low, -30), edges)
    edges = jnp.where(wide == 2, roll(high, -94), edges)
    edges = jnp.where(wide == 3, roll(high, -124), edges)
    for t in range(4):
        tile = tile + roll(edges[8 * t : 8 * t + 8], 4 * t)
    return tile


def write_copies(ref, tile):
    for k in range(ref.shape[0] // 8):
        ref[8 * k : 8 * k + 8] = tile


def edge_tile(y1, row, values):
    line = pack([facing(f, row) for f in y1])
    return tile_of(values, (line, y1[0], y1[CHUNKS - 1]))


def locate(bricks, place_ref, assignment_ref):
    across = bricks // 2
    place = place_ref[0]
    slab = place // bricks
    patch = assignment_ref[place % bricks]
    row = patch // across
    column = patch % across
    return slab, patch, row, column


def setup_kernel(
    slabs, bricks, place_ref, assignment_ref, occupancy_ref, source_ref, uptake_ref, conductance_ref,
    info_ref, bonds_ref, outer_ref, diagonal_ref, residual_ref, xy_ref, z_ref, tile_ref,
    relax_ref, y1_ref,
):
    across = bricks // 2
    slab, patch, row, column = locate(bricks, place_ref, assignment_ref)

    def holder(row_target, column_target):
        inside = (column_target >= 0) & (column_target < across)
        wanted = jnp.where(inside, row_target * across + column_target, patch)
        found = jnp.int32(0)
        for b in range(bricks):
            found = jnp.where(assignment_ref[b] == wanted, b, found)
        return found

    info_ref[0] = row
    info_ref[1] = slab
    info_ref[2] = holder(row, column)
    info_ref[3] = holder(1 - row, column)
    info_ref[4] = holder(row, column - 1)
    info_ref[5] = holder(row, column + 1)
    info_ref[6] = holder(1 - row, column - 1)
    info_ref[7] = holder(1 - row, column + 1)

    breadth = 2 * across

    def live_at(g, x, y):
        inside = (g >= 0) & (g < slabs) & (x >= 0) & (x < 2) & (y >= 0) & (y < breadth)
        taken = occupancy_ref[jnp.clip(x, 0, 1), jnp.clip(y, 0, breadth - 1), jnp.clip(g, 0, slabs - 1)]
        return jnp.where(inside, taken, 0).astype(F32)

    lane = lanes()
    height = rows_of()
    depth = lane % BS
    absorbed = []
    low_ends = []
    high_ends = []
    first_y = None
    second_y = None
    for s in range(2):
        y = column * 2 + s
        here = live_at(slab, row, y)
        around = [
            here * live_at(slab, row + 1, y),
            here * live_at(slab, row - 1, y),
            here * live_at(slab, row, y + 1),
            here * live_at(slab, row, y - 1),
            here * live_at(slab + 1, row, y),
            here * live_at(slab - 1, row, y),
        ]
        borders = [height == BS - 1, height == 0, lane >= 96, lane < 32, depth == BS - 1, depth == 0]
        for k in range(8):
            c = 8 * s + k
            part = pl.ds(128 * k, 128)
            taken = uptake_ref[s, :, part]
            absorbed.append(taken)
            diagonal = taken
            values = []
            for d in range(6):
                bond = conductance_ref[d, s, :, part]
                if (d == 2 and k < 7) or (d == 3 and k > 0):
                    value = bond * here
                else:
                    value = bond * jnp.where(borders[d], around[d], here)
                values.append(value)
                diagonal = diagonal + value
            if c == 7:
                first_y = jnp.where(borders[2], values[2], 0.0)
            if c == 8:
                second_y = jnp.where(borders[3], values[3], 0.0)
            high_ends.append(jnp.where(borders[4], values[4], 0.0))
            low_ends.append(jnp.where(borders[5], values[5], 0.0))
            outer_ref[B_XP + c : B_XP + c + 1] = values[0][BS - 1 : BS]
            outer_ref[B_XM + c : B_XM + c + 1] = values[1][0:1]
            bonds_ref[0, c] = jnp.where(borders[0], 0.0, values[0])
            if c == CHUNKS - 1:
                outer_ref[B_YP : B_YP + BS] = jnp.where(borders[2], values[2], 0.0)
                bonds_ref[1, c] = jnp.where(borders[2], 0.0, values[2])
            else:
                bonds_ref[1, c] = values[2]
            if c == 0:
                outer_ref[B_YM : B_YM + BS] = jnp.where(borders[3], values[3], 0.0)
            bonds_ref[2, c] = jnp.where(borders[4], 0.0, values[4])
            relax = OMEGA / diagonal
            diagonal_ref[c] = diagonal
            relax_ref[c] = relax
            forcing = source_ref[s, :, part] * here
            residual_ref[c] = forcing
            y1_ref[c] = relax * forcing

    ends = [high_ends[c] + low_ends[c] for c in range(CHUNKS)]
    outer_ref[B_Z : B_Z + BS] = pack(ends)
    y1 = [y1_ref[c] for c in range(CHUNKS)]
    outcome = stencil(y1, lambda d, c: bonds_ref[d, c], lambda c: diagonal_ref[c])
    partial = [y1[c] + relax_ref[c] * (residual_ref[c] - outcome[c]) for c in range(CHUNKS)]
    write_xy(xy_ref, row, y1, partial)
    z_ref[Z_Y1 : Z_Y1 + BS] = pack(y1)
    z_ref[Z_P : Z_P + BS] = pack(partial)

    first_coupling = total_of([first_y])
    high_sums = [total_of(high_ends[8 * s : 8 * s + 8]) for s in range(2)]
    low_sums = [total_of(low_ends[8 * s : 8 * s + 8]) for s in range(2)]
    taken_sums = [total_of(absorbed[8 * s : 8 * s + 8]) for s in range(2)]
    residual_sums = [total_of([residual_ref[8 * s + k] for k in range(8)]) for s in range(2)]
    numbers = [
        residual_sums[0],
        residual_sums[1],
        taken_sums[0] + first_coupling + high_sums[0] + low_sums[0],
        taken_sums[1] + total_of([second_y]) + high_sums[1] + low_sums[1],
        first_coupling,
        high_sums[0],
        high_sums[1],
    ]
    write_copies(tile_ref, edge_tile(y1, row, numbers))

    last = CHUNKS - 1
    z_ends = [relax_ref[c] * ends[c] for c in range(CHUNKS)]
    for c in range(CHUNKS):
        xy_ref[XY_XD + c : XY_XD + c + 1] = facing(relax_ref[c], row)
    high_y = relax_ref[last] * outer_ref[B_YP : B_YP + BS]
    low_y = relax_ref[0] * outer_ref[B_YM : B_YM + BS]
    xy_ref[XY_YC : XY_YC + BS] = side_blocks(relax_ref[0], relax_ref[last], z_ends[0], z_ends[last])
    xy_ref[XY_K : XY_K + 1] = facing(low_y + high_y, row)
    xy_ref[XY_K + 1 : XY_K + 2] = pack([facing(z, row) for z in z_ends])
    toward = [
        relax_ref[c][BS - 1 : BS] * outer_ref[B_XP + c : B_XP + c + 1]
        + relax_ref[c][0:1] * outer_ref[B_XM + c : B_XM + c + 1]
        for c in range(CHUNKS)
    ]
    xy_ref[XY_K + 2 : XY_K + 3] = jnp.where(lanes(1) < 32, toward[0], roll_row(toward[last], 64))
    xy_ref[XY_K + 3 : XY_K + 8] = jnp.zeros((5, 128), F32)
    z_ref[Z_D : Z_D + BS] = pack([relax_ref[c] for c in range(CHUNKS)])
    z_ref[Z_K : Z_K + BS] = pack([low_y] + [jnp.zeros((BS, 128), F32)] * (CHUNKS - 2) + [high_y])
    z_ref[Z_X : Z_X + 8] = jnp.broadcast_to(pack(toward), (8, 128))


def swap_sides(from_low, from_high):
    rows = from_low.shape[0]
    if rows == 1:
        low, high = roll_row(from_low, -32), roll_row(from_high, 32)
    else:
        low, high = roll(from_low, -32), roll(from_high, 32)
    return jnp.where((lanes(rows) // 32) % 2 == 0, low, high)


def search_scalars(sums, scalars, iteration):
    energy = sums[0]
    curvature = sums[1]
    if iteration == 0:
        return energy, curvature, energy / curvature, None
    growth = energy / scalars[0:1, 0:1]
    curvature = curvature + growth * (2.0 * sums[2] + growth * scalars[1:2, 0:1])
    return energy, curvature, energy / curvature, growth


def sum_tiles(ref, count):
    total = ref[0:8]
    for g in range(1, count):
        total = total + ref[8 * g : 8 * g + 8]
    return total


def step_kernel(iteration, slabs, bricks, *refs):
    first = iteration == 0
    last = iteration == ITERS - 1
    refs = list(refs)
    take = lambda count: [refs.pop(0) for _ in range(count)]
    info_ref, xy_ref, above_ref, below_ref, tiles_ref = take(5)
    bonds_ref, outer_ref, diagonal_ref, residual_ref = take(4)
    if not first:
        mapped_ref, halo_in, constant_ref, scalars_in = take(4)
    if iteration > 1:
        search_in, search_halo_in = take(2)
    if last:
        zero_hbm, one_hbm = take(2)
        advance_ref, direction_ref, smoothed_ref, mapped_out = take(4)
    else:
        smoothed_hbm, mapped_out = take(2)
    if first:
        constant_ref, halo_ref = take(2)
    else:
        residual_out, search_ref, scalars_ref = take(3)
        if not last:
            halo_ref, search_halo_ref = take(2)
    tile_out = take(1)[0]
    if last:
        take(2)
    else:
        xy_out, z_out = take(2)
    relax_ref = take(1)[0]
    if last:
        zero_ref, one_ref, arrived = take(3)
        reading = [
            pltpu.make_async_copy(zero_hbm, zero_ref, arrived.at[0]),
            pltpu.make_async_copy(one_hbm, one_ref, arrived.at[1]),
        ]
        for copy in reading:
            copy.start()
    else:
        smoothed_ref, written, tile_ref, sent = take(4)
    for c in range(CHUNKS):
        relax_ref[c] = OMEGA / diagonal_ref[c]

    row = info_ref[0]
    slab = info_ref[1]
    lane = lanes()
    height = rows_of()
    depth = lane % BS
    lane_row = lanes(1)
    even = lane % 2 == 0
    even_row = lane_row % 2 == 0
    low_holder, high_holder = info_ref[4], info_ref[5]
    low_corner, high_corner = info_ref[6], info_ref[7]
    x_holder = info_ref[3]

    def merge(start):
        up = roll(above_ref[start : start + BS], 31)
        down = roll(below_ref[start : start + BS], -31)
        return jnp.where(even, up, down)

    x_sides = xy_ref[x_holder, XY_X1 : XY_X1 + 2 * CHUNKS]
    y_sides = swap_sides(
        xy_ref[low_holder, XY_Y : XY_Y + BS], xy_ref[high_holder, XY_Y : XY_Y + BS]
    )
    z_first = merge(Z_Y1)
    z_second = merge(Z_P)

    def tile_at(holder, g):
        return tiles_ref[pl.ds(pl.multiple_of((holder * slabs + g) * 8, 8), 8)]

    slab_above = jnp.minimum(slab + 1, slabs - 1)
    slab_below = jnp.maximum(slab - 1, 0)

    def edge_row(tile):
        return jnp.where(lane_row >= T_Y, tile[0:1], roll_row(tile[1:2], 64))

    x_ends = jnp.where(
        even_row,
        roll_row(edge_row(tile_at(x_holder, slab_above)), 31),
        roll_row(edge_row(tile_at(x_holder, slab_below)), -31),
    )
    kind = lanes(8) % 4
    mixed = jnp.where(
        kind == 0,
        roll(tile_at(low_holder, slab_above), -2),
        jnp.where(
            kind == 1,
            roll(tile_at(low_holder, slab_below), -2),
            jnp.where(
                kind == 2,
                roll(tile_at(high_holder, slab_above), 2),
                roll(tile_at(high_holder, slab_below), 2),
            ),
        ),
    )
    y_edges = jnp.where(
        lane < 4, jnp.concatenate([roll(mixed, -4 * t) for t in range(4)], axis=0), 0.0
    )
    corner_y = jnp.where(
        lane_row < 32,
        roll_row(xy_ref[low_corner, XY_X1 + CHUNKS - 1 : XY_X1 + CHUNKS], 32),
        roll_row(xy_ref[high_corner, XY_X1 : XY_X1 + 1], -32),
    )
    low_row = jnp.where(
        row == 0,
        xy_ref[low_corner, XY_Y : XY_Y + 1],
        xy_ref[low_corner, XY_Y + BS - 1 : XY_Y + BS],
    )
    high_row = jnp.where(
        row == 0,
        xy_ref[high_corner, XY_Y : XY_Y + 1],
        xy_ref[high_corner, XY_Y + BS - 1 : XY_Y + BS],
    )
    corner_x = swap_sides(low_row, high_row)
    ends = jnp.concatenate([x_ends, corner_y, corner_x, jnp.zeros((5, 128), F32)], axis=0)
    lane_tile = lanes(8)
    slab_tiles = []
    for g in range(slabs):
        tile = tile_at(info_ref[2], g)
        for q in range(1, 4):
            tile = jnp.where(lane_tile == T_N + q, tile_at(info_ref[2 + q], g), tile)
        slab_tiles.append(tile)
    sums = jnp.concatenate(slab_tiles, axis=0)
    halo = [x_sides, y_sides, z_first, z_second, y_edges, ends, sums]
    starts = [H_X1, H_Y, H_Z1, H_ZP, H_E, H_R, H_S]

    if first:
        residual = [residual_ref[c] for c in range(CHUNKS)]
        constant_ref[C_XD : C_XD + CHUNKS] = xy_ref[x_holder, XY_XD : XY_XD + CHUNKS]
        constant_ref[C_YC : C_YC + BS] = swap_sides(
            xy_ref[low_holder, XY_YC : XY_YC + BS], xy_ref[high_holder, XY_YC : XY_YC + BS]
        )
        constant_ref[C_ZD : C_ZD + BS] = merge(Z_D)
        constant_ref[C_ZK : C_ZK + BS] = merge(Z_K)
        constant_ref[C_K : C_K + 8] = jnp.concatenate(
            [
                xy_ref[x_holder, XY_K : XY_K + 2],
                swap_sides(
                    xy_ref[low_holder, XY_K + 2 : XY_K + 3],
                    xy_ref[high_holder, XY_K + 2 : XY_K + 3],
                ),
                jnp.where(
                    even_row,
                    roll_row(above_ref[Z_X : Z_X + 1], 31),
                    roll_row(below_ref[Z_X : Z_X + 1], -31),
                ),
                jnp.zeros((4, 128), F32),
            ],
            axis=0,
        )
        for g in range(slabs):
            tile = sums[8 * g : 8 * g + 8]
            a, b, off = tile[2:3], tile[3:4], tile[4:5]
            t0, t1 = tile[5:6], tile[6:7]
            if g > 0:
                a = a - u0 * u0 * i00
                b = b - u1 * u1 * i11
                off = off + u0 * u1 * i01
            used = (lane_row >= T_N) & (lane_row < T_N + 4)
            a = jnp.where(used, a, 1.0)
            b = jnp.where(used, b, 1.0)
            off = jnp.where(used, off, 0.0)
            t0 = jnp.where(used, t0, 0.0)
            t1 = jnp.where(used, t1, 0.0)
            scale = 1.0 / (a * b - off * off)
            i00, i01, i11 = b * scale, off * scale, a * scale
            u0, u1 = t0, t1
            constant_ref[C_F + 8 * g : C_F + 8 * g + 8] = jnp.concatenate(
                [i00, i01, i11, t0, t1, jnp.zeros((3, 128), F32)], axis=0
            )
    else:
        scalars = None if iteration == 1 else scalars_in[...]
        tile = sum_tiles(tiles_ref, slabs * bricks)
        energy, curvature, step, growth = search_scalars(
            [tile[i : i + 1, T_N : T_N + 1] for i in range(2, 5)], scalars, iteration - 1
        )
        step_row = jnp.broadcast_to(step, (1, 128))
        residual = []
        for c in range(CHUNKS):
            mapped = mapped_ref[c]
            if growth is not None:
                mapped = mapped + growth * search_in[c]
            search_ref[c] = mapped
            value = residual_ref[c] - step * mapped
            residual_out[c] = value
            residual.append(value)
        old_halo = halo
        halo = []
        for start, block in zip(starts, old_halo):
            span = slice(start, start + block.shape[0])
            if growth is not None:
                block = block + growth * search_halo_in[span]
            if not last:
                search_halo_ref[span] = block
            halo.append(halo_in[span] - step * block)
        kept = [energy, curvature, step]
        if growth is not None:
            kept = [energy, curvature, scalars[2:3, 0:1], step, growth]
        write_scalars(scalars_ref, 0, kept)

    if not last:
        for start, block in zip(starts, halo):
            halo_ref[start : start + block.shape[0]] = block
    x_sides, y_sides, z_first, z_second, y_edges, ends, sums = halo

    forward = []
    for g in range(slabs):
        t0, t1 = sums[8 * g : 8 * g + 1], sums[8 * g + 1 : 8 * g + 2]
        if g > 0:
            t0 = t0 + w0 * v0
            t1 = t1 + w1 * v1
        factor = constant_ref[C_F + 8 * g : C_F + 8 * g + 8]
        v0 = factor[0:1] * t0 + factor[1:2] * t1
        v1 = factor[1:2] * t0 + factor[2:3] * t1
        w0, w1 = factor[3:4], factor[4:5]
        forward.append((v0, v1))
    blank = jnp.zeros((1, 128), F32)
    below0, below1, here0, here1, above0, above1 = [blank] * 6
    for g in reversed(range(slabs)):
        v0, v1 = forward[g]
        if g < slabs - 1:
            factor = constant_ref[C_F + 8 * g : C_F + 8 * g + 8]
            s0, s1 = factor[3:4] * n0, factor[4:5] * n1
            v0 = v0 + factor[0:1] * s0 + factor[1:2] * s1
            v1 = v1 + factor[1:2] * s0 + factor[2:3] * s1
        n0, n1 = v0, v1
        here0 = jnp.where(slab == g, n0, here0)
        here1 = jnp.where(slab == g, n1, here1)
        above0 = jnp.where(slab + 1 == g, n0, above0)
        above1 = jnp.where(slab + 1 == g, n1, above1)
        below0 = jnp.where(slab - 1 == g, n0, below0)
        below1 = jnp.where(slab - 1 == g, n1, below1)
    def coarse_of(row, q):
        return row[:, T_N + q : T_N + q + 1]

    own = [coarse_of(here0, 0), coarse_of(here1, 0)]

    bonds = lambda d, c: bonds_ref[d, c]
    diagonal = lambda c: diagonal_ref[c]
    end = CHUNKS - 1
    x_plus = outer_ref[B_XP : B_XP + CHUNKS]
    x_minus = outer_ref[B_XM : B_XM + CHUNKS]
    y_plus = outer_ref[B_YP : B_YP + BS]
    y_minus = outer_ref[B_YM : B_YM + BS]
    z_bonds = outer_ref[B_Z : B_Z + BS]

    def brought(x_rows, y_block, z_block):
        return (
            x_plus * x_rows,
            x_minus * x_rows,
            y_minus * y_block,
            y_plus * roll(y_block, 64),
            z_bonds * z_block,
        )

    y1 = [relax_ref[c] * residual[c] for c in range(CHUNKS)]
    outcome = stencil(y1, bonds, diagonal, brought(x_sides[:CHUNKS], y_sides, z_first))
    smoothed = []
    for c in range(CHUNKS):
        value = y1[c] + relax_ref[c] * (residual[c] - outcome[c]) + own[c // 8]
        if last:
            smoothed_ref[c] = value
        else:
            smoothed_ref[c // 8, :, 128 * (c % 8) : 128 * (c % 8 + 1)] = value
        smoothed.append(value)
    if not last:
        writing = pltpu.make_async_copy(smoothed_ref, smoothed_hbm, written)
        writing.start()
    keys = constant_ref[C_K : C_K + 8]
    crossing = x_plus * jnp.concatenate([f[BS - 1 : BS] for f in y1], axis=0)
    crossing += x_minus * jnp.concatenate([f[0:1] for f in y1], axis=0)
    end_row = keys[1:2] * ends[0:1]
    corner_row = keys[0:1] * ends[1:2]
    depth_row = lane_row % BS
    additions = []
    for c in range(CHUNKS):
        value = jnp.where(
            (depth_row == BS - 1) | (depth_row == 0), roll_row(end_row, 31 - 2 * c), 0.0
        )
        if c == 0:
            value = value + jnp.where(lane_row < 32, corner_row, 0.0)
        if c == end:
            value = value + jnp.where(lane_row >= 96, corner_row, 0.0)
        value = value + coarse_of(here0 if c < 8 else here1, 1)
        additions.append(value)
    x_next = (
        x_sides[CHUNKS:]
        + constant_ref[C_XD : C_XD + CHUNKS] * crossing
        + jnp.concatenate(additions, axis=0)
    )
    y_constant = constant_ref[C_YC : C_YC + BS]
    y_crossing = jnp.where(lane < 32, y_minus * y1[0], roll(y_plus * y1[end], 64))
    x_side_row = jnp.where(row == 0, BS - 1, 0)
    y_ends = jnp.where(lane == 0, roll(y_edges, -1), 0.0)
    y_ends = jnp.where(lane == 31, roll(y_edges, 31), y_ends)
    y_ends = jnp.where(lane == 32, roll(y_edges, 29), y_ends)
    y_ends = jnp.where(lane == 63, roll(y_edges, 61), y_ends)
    z_sides = jnp.where(lane == 0, y_edges, 0.0)
    z_sides = jnp.where(lane == 97, roll(y_edges, 96), z_sides)
    z_sides = jnp.where(lane == 126, roll(y_edges, 124), z_sides)
    z_sides = jnp.where(lane == 95, roll(y_edges, 92), z_sides)
    y_next = (
        roll(y_sides, 64)
        + y_constant * y_crossing
        + roll(y_constant, 64) * y_ends
        + jnp.where(height == x_side_row, keys[2:3] * ends[2:3], 0.0)
        + jnp.where(lane < 32, coarse_of(here1, 2), coarse_of(here0, 3))
    )
    z_crossing = z_bonds * pack(y1)
    z_coarse = jnp.where(
        even_row,
        jnp.where(depth_row < 16, coarse_of(above0, 0), coarse_of(above1, 0)),
        jnp.where(depth_row < 16, coarse_of(below0, 0), coarse_of(below1, 0)),
    )
    z_next = (
        z_second
        + constant_ref[C_ZD : C_ZD + BS] * z_crossing
        + constant_ref[C_ZK : C_ZK + BS] * z_sides
        + jnp.where(height == x_side_row, keys[3:4] * ends[0:1], 0.0)
        + z_coarse
    )
    mapped = stencil(smoothed, bonds, diagonal, brought(x_next, y_next, z_next))
    for c in range(CHUNKS):
        mapped_out[c] = mapped[c]

    values = [
        total_of(mapped[:8]),
        total_of(mapped[8:]),
        total_of([residual[c] * smoothed[c] for c in range(CHUNKS)]),
        total_of([mapped[c] * smoothed[c] for c in range(CHUNKS)]),
    ]
    if not first:
        values.append(total_of([search_ref[c] * smoothed[c] for c in range(CHUNKS)]))
    if last:
        level = lane_row // 16
        line = jnp.zeros((1, 128), F32)
        for i in range(2, 5):
            line = jnp.where(level == i, values[i], line)
        for k in range(tile_out.shape[0]):
            tile_out[k] = line
        for copy in reading:
            copy.wait()
        first_step = scalars_in[2:3, 0:1]
        for c in range(CHUNKS):
            s, part = c // 8, slice(128 * (c % 8), 128 * (c % 8 + 1))
            direction = one_ref[s, :, part] + growth * zero_ref[s, :, part]
            direction_ref[c] = direction
            advance_ref[c] = first_step * zero_ref[s, :, part] + step * direction
        return
    y1 = [relax_ref[c] * mapped[c] for c in range(CHUNKS)]
    write_copies(tile_ref, edge_tile(y1, row, values))
    sending = pltpu.make_async_copy(tile_ref, tile_out, sent)
    sending.start()
    outcome = stencil(y1, bonds, diagonal)
    partial = [y1[c] + relax_ref[c] * (mapped[c] - outcome[c]) for c in range(CHUNKS)]
    write_xy(xy_out, row, y1, partial)
    z_out[Z_Y1 : Z_Y1 + BS] = pack(y1)
    z_out[Z_P : Z_P + BS] = pack(partial)
    writing.wait()
    sending.wait()


def finish_kernel(
    tiles_ref, scalars_ref, residual_ref, mapped_ref, search_ref, smoothed_ref, advance_ref, direction_ref,
    first_hbm, second_hbm, solution_hbm, residual_hbm, solution_ref, change_ref, sent,
):
    scalars = scalars_ref[...]
    line = tiles_ref[0]
    for k in range(1, tiles_ref.shape[0]):
        line = line + tiles_ref[k]
    _, _, step, growth = search_scalars(
        [line[:, 16 * i : 16 * i + 1] for i in range(2, 5)], scalars, ITERS - 1
    )
    for c in range(CHUNKS):
        s, part = c // 8, slice(128 * (c % 8), 128 * (c % 8 + 1))
        solution_ref[s, :, part] = advance_ref[c] + step * (smoothed_ref[c] + growth * direction_ref[c])
    copies = [
        pltpu.make_async_copy(solution_ref, solution_hbm, sent.at[0]),
        pltpu.make_async_copy(change_ref, residual_hbm, sent.at[1]),
    ]
    copies[0].start()
    for c in range(CHUNKS):
        s, part = c // 8, slice(128 * (c % 8), 128 * (c % 8 + 1))
        change_ref[s, :, part] = residual_ref[c] - step * (mapped_ref[c] + growth * search_ref[c])
    copies[1].start()
    for copy in copies:
        copy.wait()


def call(kernel, name, outs, in_spaces, out_spaces, operands, scratch=(), aliases=None):
    spec = lambda space: pl.BlockSpec(memory_space=space)
    in_spaces = list(in_spaces) + [pltpu.VMEM] * (len(operands) - len(in_spaces))
    out_spaces = list(out_spaces) + [pltpu.VMEM] * (len(outs) - len(out_spaces))
    return pl.pallas_call(
        kernel,
        out_shape=tuple(outs),
        in_specs=[spec(space) for space in in_spaces],
        out_specs=tuple(spec(space) for space in out_spaces),
        scratch_shapes=list(scratch),
        input_output_aliases=aliases or {},
        compiler_params=pltpu.CompilerParams(vmem_limit_bytes=16 * 1024 * 1024),
        name=name,
    )(*operands)


def array(*shape):
    return jax.ShapeDtypeStruct(shape, F32)


def to_all(copies, axes):
    return lax.all_to_all(copies, axes, 0, 0, tiled=True)


def exchange_slabs(message):
    count = lax.axis_size("grp")
    upward = [(i, i + 1) for i in range(count - 1)]
    downward = [(i + 1, i) for i in range(count - 1)]
    return lax.ppermute(message, "grp", downward), lax.ppermute(message, "grp", upward)


def on_device(source, uptake, conductance, occupancy, assignment):
    slabs = lax.axis_size("grp")
    bricks = lax.axis_size("brick")
    place = (lax.axis_index("grp") * bricks + lax.axis_index("brick")).astype(jnp.int32).reshape(1)
    field = array(*FIELD)
    brick_pair = array(2, BS, BS * BS)
    copies = array(8 * slabs * bricks, 128)
    info, bonds, outer, diagonal, residual, sides, ends, tile = call(
        functools.partial(setup_kernel, slabs, bricks),
        "setup",
        [
            jax.ShapeDtypeStruct((8,), jnp.int32), array(3, *FIELD), array(B_ROWS, 128), field, field,
            array(XY_ROWS_FIRST, 128), array(Z_ROWS_FIRST, 128), copies,
        ],
        [pltpu.SMEM] * 3,
        [pltpu.SMEM],
        [
            place, assignment, jnp.transpose(occupancy, (1, 2, 0)),
            source[0, 0], uptake[0, 0], conductance[0, 0],
        ],
        [
            pltpu.VMEM(FIELD, F32), pltpu.VMEM(FIELD, F32),
        ],
    )
    mapped = residual
    directions = []
    state = {}
    for iteration in range(ITERS):
        first, last = iteration == 0, iteration == ITERS - 1
        tiles = to_all(tile, ("brick", "grp"))
        above, below = exchange_slabs(ends)
        gathered = lax.all_gather(sides, "brick", axis=0, tiled=False)
        operands = [info, gathered, above, below, tiles, bonds, outer, diagonal, residual]
        tall = array(H_S + 8 * slabs, 128)
        if last:
            outs = {"advance": field, "direction": field, "smoothed": field, "mapped": field}
        else:
            outs = {"smoothed": brick_pair, "mapped": field}
        if not first:
            operands += [mapped] + [state[k] for k in ("halo", "constant", "scalars")]
        if iteration > 1:
            operands += [state[k] for k in ("search", "search_halo")]
        in_spaces = [pltpu.SMEM]
        if last:
            in_spaces += [pltpu.VMEM] * (len(operands) - 1) + [pl.ANY] * 2
            operands += directions
            count = len(operands)
        if first:
            outs |= {"constant": array(C_F + 8 * slabs, 128), "halo": tall}
        else:
            outs |= {"residual": field, "search": field, "scalars": array(8, 128)}
            if not last:
                outs |= {"halo": tall, "search_halo": tall}
        outs["tile"] = array(slabs * bricks, 1, 128) if last else copies
        if last:
            outs |= {"zero": brick_pair, "one": brick_pair}
            aliases = {count - 2: len(outs) - 2, count - 1: len(outs) - 1}
        else:
            outs |= {"sides": array(XY_ROWS, 128), "ends": array(Z_ROWS, 128)}
            aliases = {}
        moved = ("zero", "one") if last else ("smoothed", "tile")
        pair = pltpu.VMEM(brick_pair.shape, F32)
        results = call(
            functools.partial(step_kernel, iteration, slabs, bricks),
            f"step_{iteration}",
            list(outs.values()),
            in_spaces,
            [pl.ANY if name in moved else pltpu.VMEM for name in outs],
            operands,
            [pltpu.VMEM(FIELD, F32)]
            + (
                [pair, pair, pltpu.SemaphoreType.DMA((2,))]
                if last
                else [
                    pair, pltpu.SemaphoreType.DMA,
                    pltpu.VMEM(copies.shape, F32), pltpu.SemaphoreType.DMA,
                ]
            ),
            aliases,
        )
        state |= dict(zip(outs, results))
        if first:
            state["scalars"] = jnp.zeros((8, 128), F32)
        mapped, tile = state["mapped"], state["tile"]
        sides, ends = state.get("sides"), state.get("ends")
        residual = state.get("residual", residual)
        directions.append(state["smoothed"])
    tiles = to_all(tile, ("brick", "grp"))
    solution_field, residual = call(
        finish_kernel,
        "finish",
        [brick_pair, brick_pair],
        [pltpu.VMEM] * 8 + [pl.ANY] * 2,
        [pl.ANY] * 2,
        [
            tiles, state["scalars"], residual, mapped, state["search"], directions[2],
            state["advance"], state["direction"], state["zero"], state["one"],
        ],
        [
            pltpu.VMEM(brick_pair.shape, F32), pltpu.VMEM(brick_pair.shape, F32),
            pltpu.SemaphoreType.DMA((2,)),
        ],
        {8: 0, 9: 1},
    )
    return solution_field[None, None], residual[None, None]


def solution(mesh):
    return jax.shard_map(
        on_device,
        mesh=mesh,
        in_specs=(
            P("grp", "brick", None, None, None),
            P("grp", "brick", None, None, None),
            P("grp", "brick", None, None, None, None),
            P(),
            P(),
        ),
        out_specs=(P("grp", "brick", None, None, None), P("grp", "brick", None, None, None)),
        check_vma=False,
    )
```

```python
import functools

import jax
import jax.numpy as jnp
from jax import lax
from jax.experimental import pallas as pl
from jax.experimental.pallas import tpu as pltpu
from jax.sharding import PartitionSpec as P

BS = 32
CHUNKS = 16
OMEGA = 0.6
ITERS = 3
F32 = jnp.float32
FIELD = (CHUNKS, BS, 128)

XY_X1, XY_XP, XY_Y = 0, 16, 32
XY_ROWS = 64
XY_XD, XY_YC, XY_K = 64, 80, 112
XY_ROWS_FIRST = 120
Z_Y1, Z_P = 0, 32
Z_ROWS = 64
Z_D, Z_K, Z_X = 64, 96, 128
Z_ROWS_FIRST = 136
T_N, T_Y = 16, 64
H_X1, H_Y, H_Z1, H_ZP, H_E, H_R, H_S = 0, 32, 64, 96, 128, 160, 168
C_XD, C_YC, C_ZD, C_ZK, C_K, C_F = 0, 16, 48, 80, 112, 120
B_XP, B_XM, B_YP, B_YM, B_Z = 0, 16, 32, 64, 96
B_ROWS = 128


def roll(block, shift):
    return pltpu.roll(block, shift % 128, axis=1)


def roll_row(row, shift):
    return pltpu.roll(jnp.broadcast_to(row, (8, 128)), shift % 128, axis=1)[0:1]


def lanes(rows=BS):
    return lax.broadcasted_iota(jnp.int32, (rows, 128), 1)


def rows_of(height=BS):
    return lax.broadcasted_iota(jnp.int32, (height, 128), 0)


def pack(chunks):
    height = chunks[0].shape[0]
    pair = (lanes(height) % BS) // 2
    total = jnp.zeros((height, 128), F32)
    for c in range(CHUNKS):
        moved = roll(chunks[c], 2 * c - 31) if height > 1 else roll_row(chunks[c], 2 * c - 31)
        total = jnp.where(pair == c, moved, total)
    return total


def stencil(field, bonds, diagonal, outer=None):
    lane = lanes()
    height = rows_of()
    depth = lane % BS
    at_end = (depth == BS - 1) | (depth == 0)
    back = [roll(f, -32) for f in field]
    forth = [roll(bonds(1, c) * field[c], 32) for c in range(CHUNKS)]
    out = []
    for c in range(CHUNKS):
        f = field[c]
        total = diagonal(c) * f
        total -= bonds(0, c) * pltpu.roll(f, BS - 1, axis=0)
        total -= pltpu.roll(bonds(0, c) * f, 1, axis=0)
        following = back[c + 1] if c < CHUNKS - 1 else back[c]
        previous = forth[c - 1] if c > 0 else jnp.zeros((BS, 128), F32)
        total -= bonds(1, c) * jnp.where(lane < 96, back[c], following)
        total -= jnp.where(lane >= 32, forth[c], previous)
        total -= bonds(2, c) * roll(f, -1)
        total -= roll(bonds(2, c) * f, 1)
        if outer is not None:
            x_up, x_down, y_low, y_high, z_ends = outer
            total -= jnp.where(height == BS - 1, x_up[c : c + 1], 0.0)
            total -= jnp.where(height == 0, x_down[c : c + 1], 0.0)
            total -= jnp.where(at_end, roll(z_ends, 31 - 2 * c), 0.0)
            if c == 0:
                total -= jnp.where(lane < 32, y_low, 0.0)
            if c == CHUNKS - 1:
                total -= jnp.where(lane >= 96, y_high, 0.0)
        out.append(total)
    return out


def total_of(blocks):
    acc = blocks[0]
    for block in blocks[1:]:
        acc = acc + block
    return jnp.sum(jnp.sum(acc, axis=0, keepdims=True), axis=1, keepdims=True)


def facing(block, row):
    return jnp.where(row == 0, block[BS - 1 : BS], block[0:1])


def side_blocks(low_first, high_first, low_second, high_second):
    group = lanes() // 32
    return jnp.where(
        group == 0,
        low_first,
        jnp.where(
            group == 1,
            roll(high_first, 64),
            jnp.where(group == 2, roll(low_second, 64), high_second),
        ),
    )


def write_xy(xy_ref, row, y1, partial):
    for c in range(CHUNKS):
        xy_ref[XY_X1 + c : XY_X1 + c + 1] = facing(y1[c], row)
        xy_ref[XY_XP + c : XY_XP + c + 1] = facing(partial[c], row)
    last = CHUNKS - 1
    xy_ref[XY_Y : XY_Y + BS] = side_blocks(y1[0], y1[last], partial[0], partial[last])


def write_scalars(ref, start, values):
    for i, value in enumerate(values):
        ref[start + i : start + i + 1] = jnp.broadcast_to(value, (1, 128))
    for i in range(len(values), 8):
        ref[start + i : start + i + 1] = jnp.zeros((1, 128), F32)


def tile_of(values, y1=None):
    lane = lanes(8)
    level = rows_of(8)
    tile = jnp.zeros((8, 128), F32)
    for i, value in enumerate(values):
        tile = jnp.where((level == i) & (lane >= T_N) & (lane < T_Y), value, tile)
    if y1 is None:
        return tile
    row, low, high = y1
    tile = jnp.where((level == 0) & (lane >= T_Y), row, tile)
    tile = jnp.where((level == 1) & (lane >= T_Y), roll_row(row, 64), tile)
    wide = lanes()
    edges = jnp.where(wide == 0, low, 0.0)
    edges = jnp.where(wide == 1, roll(low, -30), edges)
    edges = jnp.where(wide == 2, roll(high, -94), edges)
    edges = jnp.where(wide == 3, roll(high, -124), edges)
    for t in range(4):
        tile = tile + roll(edges[8 * t : 8 * t + 8], 4 * t)
    return tile


def write_copies(ref, tile):
    for k in range(ref.shape[0] // 8):
        ref[8 * k : 8 * k + 8] = tile


def edge_tile(y1, row, values):
    line = pack([facing(f, row) for f in y1])
    return tile_of(values, (line, y1[0], y1[CHUNKS - 1]))


def locate(bricks, place_ref, assignment_ref):
    across = bricks // 2
    place = place_ref[0]
    slab = place // bricks
    patch = assignment_ref[place % bricks]
    row = patch // across
    column = patch % across
    return slab, patch, row, column


def setup_kernel(
    slabs, bricks, place_ref, assignment_ref, occupancy_ref, source_ref, uptake_ref, conductance_ref,
    info_ref, bonds_ref, outer_ref, diagonal_ref, residual_ref, xy_ref, z_ref, tile_ref,
    relax_ref, y1_ref,
):
    across = bricks // 2
    slab, patch, row, column = locate(bricks, place_ref, assignment_ref)

    def holder(row_target, column_target):
        inside = (column_target >= 0) & (column_target < across)
        wanted = jnp.where(inside, row_target * across + column_target, patch)
        found = jnp.int32(0)
        for b in range(bricks):
            found = jnp.where(assignment_ref[b] == wanted, b, found)
        return found

    info_ref[0] = row
    info_ref[1] = slab
    info_ref[2] = holder(row, column)
    info_ref[3] = holder(1 - row, column)
    info_ref[4] = holder(row, column - 1)
    info_ref[5] = holder(row, column + 1)
    info_ref[6] = holder(1 - row, column - 1)
    info_ref[7] = holder(1 - row, column + 1)

    breadth = 2 * across

    def live_at(g, x, y):
        inside = (g >= 0) & (g < slabs) & (x >= 0) & (x < 2) & (y >= 0) & (y < breadth)
        taken = occupancy_ref[jnp.clip(x, 0, 1), jnp.clip(y, 0, breadth - 1), jnp.clip(g, 0, slabs - 1)]
        return jnp.where(inside, taken, 0).astype(F32)

    lane = lanes()
    height = rows_of()
    depth = lane % BS
    absorbed = []
    low_ends = []
    high_ends = []
    first_y = None
    second_y = None
    for s in range(2):
        y = column * 2 + s
        here = live_at(slab, row, y)
        around = [
            here * live_at(slab, row + 1, y),
            here * live_at(slab, row - 1, y),
            here * live_at(slab, row, y + 1),
            here * live_at(slab, row, y - 1),
            here * live_at(slab + 1, row, y),
            here * live_at(slab - 1, row, y),
        ]
        borders = [height == BS - 1, height == 0, lane >= 96, lane < 32, depth == BS - 1, depth == 0]
        for k in range(8):
            c = 8 * s + k
            part = pl.ds(128 * k, 128)
            taken = uptake_ref[s, :, part]
            absorbed.append(taken)
            diagonal = taken
            values = []
            for d in range(6):
                bond = conductance_ref[d, s, :, part]
                if (d == 2 and k < 7) or (d == 3 and k > 0):
                    value = bond * here
                else:
                    value = bond * jnp.where(borders[d], around[d], here)
                values.append(value)
                diagonal = diagonal + value
            if c == 7:
                first_y = jnp.where(borders[2], values[2], 0.0)
            if c == 8:
                second_y = jnp.where(borders[3], values[3], 0.0)
            high_ends.append(jnp.where(borders[4], values[4], 0.0))
            low_ends.append(jnp.where(borders[5], values[5], 0.0))
            outer_ref[B_XP + c : B_XP + c + 1] = values[0][BS - 1 : BS]
            outer_ref[B_XM + c : B_XM + c + 1] = values[1][0:1]
            bonds_ref[0, c] = jnp.where(borders[0], 0.0, values[0])
            if c == CHUNKS - 1:
                outer_ref[B_YP : B_YP + BS] = jnp.where(borders[2], values[2], 0.0)
                bonds_ref[1, c] = jnp.where(borders[2], 0.0, values[2])
            else:
                bonds_ref[1, c] = values[2]
            if c == 0:
                outer_ref[B_YM : B_YM + BS] = jnp.where(borders[3], values[3], 0.0)
            bonds_ref[2, c] = jnp.where(borders[4], 0.0, values[4])
            relax = OMEGA / diagonal
            diagonal_ref[c] = diagonal
            relax_ref[c] = relax
            forcing = source_ref[s, :, part] * here
            residual_ref[c] = forcing
            y1_ref[c] = relax * forcing

    ends = [high_ends[c] + low_ends[c] for c in range(CHUNKS)]
    outer_ref[B_Z : B_Z + BS] = pack(ends)
    y1 = [y1_ref[c] for c in range(CHUNKS)]
    outcome = stencil(y1, lambda d, c: bonds_ref[d, c], lambda c: diagonal_ref[c])
    partial = [y1[c] + relax_ref[c] * (residual_ref[c] - outcome[c]) for c in range(CHUNKS)]
    write_xy(xy_ref, row, y1, partial)
    z_ref[Z_Y1 : Z_Y1 + BS] = pack(y1)
    z_ref[Z_P : Z_P + BS] = pack(partial)

    first_coupling = total_of([first_y])
    high_sums = [total_of(high_ends[8 * s : 8 * s + 8]) for s in range(2)]
    low_sums = [total_of(low_ends[8 * s : 8 * s + 8]) for s in range(2)]
    taken_sums = [total_of(absorbed[8 * s : 8 * s + 8]) for s in range(2)]
    residual_sums = [total_of([residual_ref[8 * s + k] for k in range(8)]) for s in range(2)]
    numbers = [
        residual_sums[0],
        residual_sums[1],
        taken_sums[0] + first_coupling + high_sums[0] + low_sums[0],
        taken_sums[1] + total_of([second_y]) + high_sums[1] + low_sums[1],
        first_coupling,
        high_sums[0],
        high_sums[1],
    ]
    write_copies(tile_ref, edge_tile(y1, row, numbers))

    last = CHUNKS - 1
    z_ends = [relax_ref[c] * ends[c] for c in range(CHUNKS)]
    for c in range(CHUNKS):
        xy_ref[XY_XD + c : XY_XD + c + 1] = facing(relax_ref[c], row)
    high_y = relax_ref[last] * outer_ref[B_YP : B_YP + BS]
    low_y = relax_ref[0] * outer_ref[B_YM : B_YM + BS]
    xy_ref[XY_YC : XY_YC + BS] = side_blocks(relax_ref[0], relax_ref[last], z_ends[0], z_ends[last])
    xy_ref[XY_K : XY_K + 1] = facing(low_y + high_y, row)
    xy_ref[XY_K + 1 : XY_K + 2] = pack([facing(z, row) for z in z_ends])
    toward = [
        relax_ref[c][BS - 1 : BS] * outer_ref[B_XP + c : B_XP + c + 1]
        + relax_ref[c][0:1] * outer_ref[B_XM + c : B_XM + c + 1]
        for c in range(CHUNKS)
    ]
    xy_ref[XY_K + 2 : XY_K + 3] = jnp.where(lanes(1) < 32, toward[0], roll_row(toward[last], 64))
    xy_ref[XY_K + 3 : XY_K + 8] = jnp.zeros((5, 128), F32)
    z_ref[Z_D : Z_D + BS] = pack([relax_ref[c] for c in range(CHUNKS)])
    z_ref[Z_K : Z_K + BS] = pack([low_y] + [jnp.zeros((BS, 128), F32)] * (CHUNKS - 2) + [high_y])
    z_ref[Z_X : Z_X + 8] = jnp.broadcast_to(pack(toward), (8, 128))


def swap_sides(from_low, from_high):
    rows = from_low.shape[0]
    if rows == 1:
        low, high = roll_row(from_low, -32), roll_row(from_high, 32)
    else:
        low, high = roll(from_low, -32), roll(from_high, 32)
    return jnp.where((lanes(rows) // 32) % 2 == 0, low, high)


def search_scalars(sums, scalars, iteration):
    energy = sums[0]
    curvature = sums[1]
    if iteration == 0:
        return energy, curvature, energy / curvature, None
    growth = energy / scalars[0:1, 0:1]
    curvature = curvature + growth * (2.0 * sums[2] + growth * scalars[1:2, 0:1])
    return energy, curvature, energy / curvature, growth


def sum_tiles(ref, count):
    total = ref[0:8]
    for g in range(1, count):
        total = total + ref[8 * g : 8 * g + 8]
    return total


def step_kernel(iteration, slabs, bricks, *refs):
    first = iteration == 0
    last = iteration == ITERS - 1
    refs = list(refs)
    take = lambda count: [refs.pop(0) for _ in range(count)]
    info_ref, xy_ref, above_ref, below_ref, tiles_ref = take(5)
    bonds_ref, outer_ref, diagonal_ref, residual_ref = take(4)
    if not first:
        mapped_ref, halo_in, constant_ref, scalars_in = take(4)
    if iteration > 1:
        search_in, search_halo_in = take(2)
    smoothed_hbm, mapped_out = take(2)
    if first:
        constant_ref, halo_ref = take(2)
    else:
        residual_out, search_ref, scalars_ref = take(3)
        if not last:
            halo_ref, search_halo_ref = take(2)
    tile_out = take(1)[0]
    if not last:
        xy_out, z_out = take(2)
    relax_ref, smoothed_ref, written = take(3)
    if not last:
        tile_ref, sent = take(2)
    for c in range(CHUNKS):
        relax_ref[c] = OMEGA / diagonal_ref[c]

    row = info_ref[0]
    slab = info_ref[1]
    lane = lanes()
    height = rows_of()
    depth = lane % BS
    lane_row = lanes(1)
    even = lane % 2 == 0
    even_row = lane_row % 2 == 0
    low_holder, high_holder = info_ref[4], info_ref[5]
    low_corner, high_corner = info_ref[6], info_ref[7]
    x_holder = info_ref[3]

    def merge(start):
        up = roll(above_ref[start : start + BS], 31)
        down = roll(below_ref[start : start + BS], -31)
        return jnp.where(even, up, down)

    x_sides = xy_ref[x_holder, XY_X1 : XY_X1 + 2 * CHUNKS]
    y_sides = swap_sides(
        xy_ref[low_holder, XY_Y : XY_Y + BS], xy_ref[high_holder, XY_Y : XY_Y + BS]
    )
    z_first = merge(Z_Y1)
    z_second = merge(Z_P)

    def tile_at(holder, g):
        return tiles_ref[pl.ds(pl.multiple_of((holder * slabs + g) * 8, 8), 8)]

    slab_above = jnp.minimum(slab + 1, slabs - 1)
    slab_below = jnp.maximum(slab - 1, 0)

    def edge_row(tile):
        return jnp.where(lane_row >= T_Y, tile[0:1], roll_row(tile[1:2], 64))

    x_ends = jnp.where(
        even_row,
        roll_row(edge_row(tile_at(x_holder, slab_above)), 31),
        roll_row(edge_row(tile_at(x_holder, slab_below)), -31),
    )
    kind = lanes(8) % 4
    mixed = jnp.where(
        kind == 0,
        roll(tile_at(low_holder, slab_above), -2),
        jnp.where(
            kind == 1,
            roll(tile_at(low_holder, slab_below), -2),
            jnp.where(
                kind == 2,
                roll(tile_at(high_holder, slab_above), 2),
                roll(tile_at(high_holder, slab_below), 2),
            ),
        ),
    )
    y_edges = jnp.where(
        lane < 4, jnp.concatenate([roll(mixed, -4 * t) for t in range(4)], axis=0), 0.0
    )
    corner_y = jnp.where(
        lane_row < 32,
        roll_row(xy_ref[low_corner, XY_X1 + CHUNKS - 1 : XY_X1 + CHUNKS], 32),
        roll_row(xy_ref[high_corner, XY_X1 : XY_X1 + 1], -32),
    )
    low_row = jnp.where(
        row == 0,
        xy_ref[low_corner, XY_Y : XY_Y + 1],
        xy_ref[low_corner, XY_Y + BS - 1 : XY_Y + BS],
    )
    high_row = jnp.where(
        row == 0,
        xy_ref[high_corner, XY_Y : XY_Y + 1],
        xy_ref[high_corner, XY_Y + BS - 1 : XY_Y + BS],
    )
    corner_x = swap_sides(low_row, high_row)
    ends = jnp.concatenate([x_ends, corner_y, corner_x, jnp.zeros((5, 128), F32)], axis=0)
    lane_tile = lanes(8)
    slab_tiles = []
    for g in range(slabs):
        tile = tile_at(info_ref[2], g)
        for q in range(1, 4):
            tile = jnp.where(lane_tile == T_N + q, tile_at(info_ref[2 + q], g), tile)
        slab_tiles.append(tile)
    sums = jnp.concatenate(slab_tiles, axis=0)
    halo = [x_sides, y_sides, z_first, z_second, y_edges, ends, sums]
    starts = [H_X1, H_Y, H_Z1, H_ZP, H_E, H_R, H_S]

    if first:
        residual = [residual_ref[c] for c in range(CHUNKS)]
        constant_ref[C_XD : C_XD + CHUNKS] = xy_ref[x_holder, XY_XD : XY_XD + CHUNKS]
        constant_ref[C_YC : C_YC + BS] = swap_sides(
            xy_ref[low_holder, XY_YC : XY_YC + BS], xy_ref[high_holder, XY_YC : XY_YC + BS]
        )
        constant_ref[C_ZD : C_ZD + BS] = merge(Z_D)
        constant_ref[C_ZK : C_ZK + BS] = merge(Z_K)
        constant_ref[C_K : C_K + 8] = jnp.concatenate(
            [
                xy_ref[x_holder, XY_K : XY_K + 2],
                swap_sides(
                    xy_ref[low_holder, XY_K + 2 : XY_K + 3],
                    xy_ref[high_holder, XY_K + 2 : XY_K + 3],
                ),
                jnp.where(
                    even_row,
                    roll_row(above_ref[Z_X : Z_X + 1], 31),
                    roll_row(below_ref[Z_X : Z_X + 1], -31),
                ),
                jnp.zeros((4, 128), F32),
            ],
            axis=0,
        )
        for g in range(slabs):
            tile = sums[8 * g : 8 * g + 8]
            a, b, off = tile[2:3], tile[3:4], tile[4:5]
            t0, t1 = tile[5:6], tile[6:7]
            if g > 0:
                a = a - u0 * u0 * i00
                b = b - u1 * u1 * i11
                off = off + u0 * u1 * i01
            used = (lane_row >= T_N) & (lane_row < T_N + 4)
            a = jnp.where(used, a, 1.0)
            b = jnp.where(used, b, 1.0)
            off = jnp.where(used, off, 0.0)
            t0 = jnp.where(used, t0, 0.0)
            t1 = jnp.where(used, t1, 0.0)
            scale = 1.0 / (a * b - off * off)
            i00, i01, i11 = b * scale, off * scale, a * scale
            u0, u1 = t0, t1
            constant_ref[C_F + 8 * g : C_F + 8 * g + 8] = jnp.concatenate(
                [i00, i01, i11, t0, t1, jnp.zeros((3, 128), F32)], axis=0
            )
    else:
        scalars = None if iteration == 1 else scalars_in[...]
        tile = sum_tiles(tiles_ref, slabs * bricks)
        energy, curvature, step, growth = search_scalars(
            [tile[i : i + 1, T_N : T_N + 1] for i in range(2, 5)], scalars, iteration - 1
        )
        step_row = jnp.broadcast_to(step, (1, 128))
        residual = []
        for c in range(CHUNKS):
            mapped = mapped_ref[c]
            if growth is not None:
                mapped = mapped + growth * search_in[c]
            search_ref[c] = mapped
            value = residual_ref[c] - step * mapped
            residual_out[c] = value
            residual.append(value)
        old_halo = halo
        halo = []
        for start, block in zip(starts, old_halo):
            span = slice(start, start + block.shape[0])
            if growth is not None:
                block = block + growth * search_halo_in[span]
            if not last:
                search_halo_ref[span] = block
            halo.append(halo_in[span] - step * block)
        kept = [energy, curvature, step]
        if growth is not None:
            kept = [energy, curvature, scalars[2:3, 0:1], step, growth]
        write_scalars(scalars_ref, 0, kept)

    if not last:
        for start, block in zip(starts, halo):
            halo_ref[start : start + block.shape[0]] = block
    x_sides, y_sides, z_first, z_second, y_edges, ends, sums = halo

    forward = []
    for g in range(slabs):
        t0, t1 = sums[8 * g : 8 * g + 1], sums[8 * g + 1 : 8 * g + 2]
        if g > 0:
            t0 = t0 + w0 * v0
            t1 = t1 + w1 * v1
        factor = constant_ref[C_F + 8 * g : C_F + 8 * g + 8]
        v0 = factor[0:1] * t0 + factor[1:2] * t1
        v1 = factor[1:2] * t0 + factor[2:3] * t1
        w0, w1 = factor[3:4], factor[4:5]
        forward.append((v0, v1))
    blank = jnp.zeros((1, 128), F32)
    below0, below1, here0, here1, above0, above1 = [blank] * 6
    for g in reversed(range(slabs)):
        v0, v1 = forward[g]
        if g < slabs - 1:
            factor = constant_ref[C_F + 8 * g : C_F + 8 * g + 8]
            s0, s1 = factor[3:4] * n0, factor[4:5] * n1
            v0 = v0 + factor[0:1] * s0 + factor[1:2] * s1
            v1 = v1 + factor[1:2] * s0 + factor[2:3] * s1
        n0, n1 = v0, v1
        here0 = jnp.where(slab == g, n0, here0)
        here1 = jnp.where(slab == g, n1, here1)
        above0 = jnp.where(slab + 1 == g, n0, above0)
        above1 = jnp.where(slab + 1 == g, n1, above1)
        below0 = jnp.where(slab - 1 == g, n0, below0)
        below1 = jnp.where(slab - 1 == g, n1, below1)
    def coarse_of(row, q):
        return row[:, T_N + q : T_N + q + 1]

    own = [coarse_of(here0, 0), coarse_of(here1, 0)]

    bonds = lambda d, c: bonds_ref[d, c]
    diagonal = lambda c: diagonal_ref[c]
    end = CHUNKS - 1
    x_plus = outer_ref[B_XP : B_XP + CHUNKS]
    x_minus = outer_ref[B_XM : B_XM + CHUNKS]
    y_plus = outer_ref[B_YP : B_YP + BS]
    y_minus = outer_ref[B_YM : B_YM + BS]
    z_bonds = outer_ref[B_Z : B_Z + BS]

    def brought(x_rows, y_block, z_block):
        return (
            x_plus * x_rows,
            x_minus * x_rows,
            y_minus * y_block,
            y_plus * roll(y_block, 64),
            z_bonds * z_block,
        )

    y1 = [relax_ref[c] * residual[c] for c in range(CHUNKS)]
    outcome = stencil(y1, bonds, diagonal, brought(x_sides[:CHUNKS], y_sides, z_first))
    smoothed = []
    for c in range(CHUNKS):
        value = y1[c] + relax_ref[c] * (residual[c] - outcome[c]) + own[c // 8]
        if last:
            smoothed_ref[c] = value
        else:
            smoothed_ref[c // 8, :, 128 * (c % 8) : 128 * (c % 8 + 1)] = value
        smoothed.append(value)
    writing = pltpu.make_async_copy(smoothed_ref, smoothed_hbm, written)
    writing.start()
    keys = constant_ref[C_K : C_K + 8]
    crossing = x_plus * jnp.concatenate([f[BS - 1 : BS] for f in y1], axis=0)
    crossing += x_minus * jnp.concatenate([f[0:1] for f in y1], axis=0)
    end_row = keys[1:2] * ends[0:1]
    corner_row = keys[0:1] * ends[1:2]
    depth_row = lane_row % BS
    additions = []
    for c in range(CHUNKS):
        value = jnp.where(
            (depth_row == BS - 1) | (depth_row == 0), roll_row(end_row, 31 - 2 * c), 0.0
        )
        if c == 0:
            value = value + jnp.where(lane_row < 32, corner_row, 0.0)
        if c == end:
            value = value + jnp.where(lane_row >= 96, corner_row, 0.0)
        value = value + coarse_of(here0 if c < 8 else here1, 1)
        additions.append(value)
    x_next = (
        x_sides[CHUNKS:]
        + constant_ref[C_XD : C_XD + CHUNKS] * crossing
        + jnp.concatenate(additions, axis=0)
    )
    y_constant = constant_ref[C_YC : C_YC + BS]
    y_crossing = jnp.where(lane < 32, y_minus * y1[0], roll(y_plus * y1[end], 64))
    x_side_row = jnp.where(row == 0, BS - 1, 0)
    y_ends = jnp.where(lane == 0, roll(y_edges, -1), 0.0)
    y_ends = jnp.where(lane == 31, roll(y_edges, 31), y_ends)
    y_ends = jnp.where(lane == 32, roll(y_edges, 29), y_ends)
    y_ends = jnp.where(lane == 63, roll(y_edges, 61), y_ends)
    z_sides = jnp.where(lane == 0, y_edges, 0.0)
    z_sides = jnp.where(lane == 97, roll(y_edges, 96), z_sides)
    z_sides = jnp.where(lane == 126, roll(y_edges, 124), z_sides)
    z_sides = jnp.where(lane == 95, roll(y_edges, 92), z_sides)
    y_next = (
        roll(y_sides, 64)
        + y_constant * y_crossing
        + roll(y_constant, 64) * y_ends
        + jnp.where(height == x_side_row, keys[2:3] * ends[2:3], 0.0)
        + jnp.where(lane < 32, coarse_of(here1, 2), coarse_of(here0, 3))
    )
    z_crossing = z_bonds * pack(y1)
    z_coarse = jnp.where(
        even_row,
        jnp.where(depth_row < 16, coarse_of(above0, 0), coarse_of(above1, 0)),
        jnp.where(depth_row < 16, coarse_of(below0, 0), coarse_of(below1, 0)),
    )
    z_next = (
        z_second
        + constant_ref[C_ZD : C_ZD + BS] * z_crossing
        + constant_ref[C_ZK : C_ZK + BS] * z_sides
        + jnp.where(height == x_side_row, keys[3:4] * ends[0:1], 0.0)
        + z_coarse
    )
    mapped = stencil(smoothed, bonds, diagonal, brought(x_next, y_next, z_next))
    for c in range(CHUNKS):
        mapped_out[c] = mapped[c]

    values = [
        total_of(mapped[:8]),
        total_of(mapped[8:]),
        total_of([residual[c] * smoothed[c] for c in range(CHUNKS)]),
        total_of([mapped[c] * smoothed[c] for c in range(CHUNKS)]),
    ]
    if not first:
        values.append(total_of([search_ref[c] * smoothed[c] for c in range(CHUNKS)]))
    if last:
        level = lane_row // 16
        line = jnp.zeros((1, 128), F32)
        for i in range(2, 5):
            line = jnp.where(level == i, values[i], line)
        for k in range(tile_out.shape[0]):
            tile_out[k] = line
        writing.wait()
        return
    y1 = [relax_ref[c] * mapped[c] for c in range(CHUNKS)]
    write_copies(tile_ref, edge_tile(y1, row, values))
    sending = pltpu.make_async_copy(tile_ref, tile_out, sent)
    sending.start()
    outcome = stencil(y1, bonds, diagonal)
    partial = [y1[c] + relax_ref[c] * (mapped[c] - outcome[c]) for c in range(CHUNKS)]
    write_xy(xy_out, row, y1, partial)
    z_out[Z_Y1 : Z_Y1 + BS] = pack(y1)
    z_out[Z_P : Z_P + BS] = pack(partial)
    writing.wait()
    sending.wait()


def finish_kernel(
    tiles_ref, scalars_ref, residual_ref, mapped_ref, search_ref, third_ref, first_hbm, second_hbm,
    solution_hbm, residual_hbm, first_ref, second_ref, change_ref, arrived,
):
    copies = [
        pltpu.make_async_copy(first_hbm, first_ref, arrived.at[0]),
        pltpu.make_async_copy(second_hbm, second_ref, arrived.at[1]),
    ]
    for copy in copies:
        copy.start()
    scalars = scalars_ref[...]
    line = tiles_ref[0]
    for k in range(1, tiles_ref.shape[0]):
        line = line + tiles_ref[k]
    _, _, step, growth = search_scalars(
        [line[:, 16 * i : 16 * i + 1] for i in range(2, 5)], scalars, ITERS - 1
    )
    first_step, second_step, second_growth = scalars[2:3, 0:1], scalars[3:4, 0:1], scalars[4:5, 0:1]
    second_weight = second_step + growth * step
    first_weight = first_step + second_growth * second_weight
    for c in range(CHUNKS):
        s, part = c // 8, slice(128 * (c % 8), 128 * (c % 8 + 1))
        change_ref[s, :, part] = residual_ref[c] - step * (mapped_ref[c] + growth * search_ref[c])
    for copy in copies:
        copy.wait()
    copies = [
        pltpu.make_async_copy(change_ref, residual_hbm, arrived.at[1]),
        pltpu.make_async_copy(first_ref, solution_hbm, arrived.at[0]),
    ]
    copies[0].start()
    for c in range(CHUNKS):
        s, part = c // 8, slice(128 * (c % 8), 128 * (c % 8 + 1))
        total = first_weight * first_ref[s, :, part] + second_weight * second_ref[s, :, part]
        first_ref[s, :, part] = total + step * third_ref[c]
    copies[1].start()
    for copy in copies:
        copy.wait()


def call(kernel, name, outs, in_spaces, out_spaces, operands, scratch=(), aliases=None):
    spec = lambda space: pl.BlockSpec(memory_space=space)
    in_spaces = list(in_spaces) + [pltpu.VMEM] * (len(operands) - len(in_spaces))
    out_spaces = list(out_spaces) + [pltpu.VMEM] * (len(outs) - len(out_spaces))
    return pl.pallas_call(
        kernel,
        out_shape=tuple(outs),
        in_specs=[spec(space) for space in in_spaces],
        out_specs=tuple(spec(space) for space in out_spaces),
        scratch_shapes=list(scratch),
        input_output_aliases=aliases or {},
        compiler_params=pltpu.CompilerParams(vmem_limit_bytes=16 * 1024 * 1024),
        name=name,
    )(*operands)


def array(*shape):
    return jax.ShapeDtypeStruct(shape, F32)


def to_all(copies, axes):
    return lax.all_to_all(copies, axes, 0, 0, tiled=True)


def exchange_slabs(message):
    count = lax.axis_size("grp")
    upward = [(i, i + 1) for i in range(count - 1)]
    downward = [(i + 1, i) for i in range(count - 1)]
    return lax.ppermute(message, "grp", downward), lax.ppermute(message, "grp", upward)


def on_device(source, uptake, conductance, occupancy, assignment):
    slabs = lax.axis_size("grp")
    bricks = lax.axis_size("brick")
    place = (lax.axis_index("grp") * bricks + lax.axis_index("brick")).astype(jnp.int32).reshape(1)
    field = array(*FIELD)
    brick_pair = array(2, BS, BS * BS)
    copies = array(8 * slabs * bricks, 128)
    info, bonds, outer, diagonal, residual, sides, ends, tile = call(
        functools.partial(setup_kernel, slabs, bricks),
        "setup",
        [
            jax.ShapeDtypeStruct((8,), jnp.int32), array(3, *FIELD), array(B_ROWS, 128), field, field,
            array(XY_ROWS_FIRST, 128), array(Z_ROWS_FIRST, 128), copies,
        ],
        [pltpu.SMEM] * 3,
        [pltpu.SMEM],
        [
            place, assignment, jnp.transpose(occupancy, (1, 2, 0)),
            source[0, 0], uptake[0, 0], conductance[0, 0],
        ],
        [
            pltpu.VMEM(FIELD, F32), pltpu.VMEM(FIELD, F32),
        ],
    )
    mapped = residual
    directions = []
    state = {}
    for iteration in range(ITERS):
        first, last = iteration == 0, iteration == ITERS - 1
        tiles = to_all(tile, ("brick", "grp"))
        above, below = exchange_slabs(ends)
        gathered = lax.all_gather(sides, "brick", axis=0, tiled=False)
        operands = [info, gathered, above, below, tiles, bonds, outer, diagonal, residual]
        tall = array(H_S + 8 * slabs, 128)
        outs = {"smoothed": field if last else brick_pair, "mapped": field}
        if not first:
            operands += [mapped] + [state[k] for k in ("halo", "constant", "scalars")]
        if iteration > 1:
            operands += [state[k] for k in ("search", "search_halo")]
        if first:
            outs |= {"constant": array(C_F + 8 * slabs, 128), "halo": tall}
        else:
            outs |= {"residual": field, "search": field, "scalars": array(8, 128)}
            if not last:
                outs |= {"halo": tall, "search_halo": tall}
        outs["tile"] = array(slabs * bricks, 1, 128) if last else copies
        if not last:
            outs |= {"sides": array(XY_ROWS, 128), "ends": array(Z_ROWS, 128)}
        moved = ("smoothed",) if last else ("smoothed", "tile")
        results = call(
            functools.partial(step_kernel, iteration, slabs, bricks),
            f"step_{iteration}",
            list(outs.values()),
            [pltpu.SMEM],
            [pl.ANY if name in moved else pltpu.VMEM for name in outs],
            operands,
            [
                pltpu.VMEM(FIELD, F32),
                pltpu.VMEM(FIELD if last else (2, BS, BS * BS), F32),
                pltpu.SemaphoreType.DMA,
            ]
            + ([] if last else [pltpu.VMEM(copies.shape, F32), pltpu.SemaphoreType.DMA]),
        )
        state |= dict(zip(outs, results))
        if first:
            state["scalars"] = jnp.zeros((8, 128), F32)
        mapped, tile = state["mapped"], state["tile"]
        sides, ends = state.get("sides"), state.get("ends")
        residual = state.get("residual", residual)
        directions.append(state["smoothed"])
    tiles = to_all(tile, ("brick", "grp"))
    solution_field, residual = call(
        finish_kernel,
        "finish",
        [brick_pair, brick_pair],
        [pltpu.VMEM] * 6 + [pl.ANY] * 2,
        [pl.ANY] * 2,
        [tiles, state["scalars"], residual, mapped, state["search"], directions[2]] + directions[:2],
        [
            pltpu.VMEM(brick_pair.shape, F32), pltpu.VMEM(brick_pair.shape, F32),
            pltpu.VMEM(brick_pair.shape, F32), pltpu.SemaphoreType.DMA((2,)),
        ],
        {6: 0, 7: 1},
    )
    return solution_field[None, None], residual[None, None]


def solution(mesh):
    return jax.shard_map(
        on_device,
        mesh=mesh,
        in_specs=(
            P("grp", "brick", None, None, None),
            P("grp", "brick", None, None, None),
            P("grp", "brick", None, None, None, None),
            P(),
            P(),
        ),
        out_specs=(P("grp", "brick", None, None, None), P("grp", "brick", None, None, None)),
        check_vma=False,
    )
```
